32 devices in a mesh: dist: 2 (over core), rows: 16 (over z, y, x).
Axes of the slice: x: 2, y: 2, z: 4, core: 2. Of those that a mesh axis runs over, the one named last changes fastest.
Arguments:
- holograms: bfloat16 [1, 4, 4, 1024, 1024], P(None, None, 'dist', 'rows'), may hold values from -6 to 6
- propagation: float32 [4], replicated, may hold values from 100 to 1000
- weights: bfloat16 [4, 1024, 1024], P(None, None, 'dist'), may hold values from -0.09375 to 0.09375
- angle_order: int32 [1, 4], replicated, may hold values from 0 to 3, each once within a row
- slab_rows: int32 [16], replicated, may hold values from 0 to 128, as said below
Outputs:
- slab: bfloat16 [2048, 1024], P('rows', 'dist')
The draws below stay inside these ranges and needn't reach their ends.
Inputs may be any that keep to these rules, and one draw needn't show every extreme that they name: Owners 2j and 2j+1 together own 128 slices: slab_rows[2j] + slab_rows[2j+1] = 128, so owner 2j holds slices 2j 64 onward and owner 2j+1 the rest of that pair's range; in every draw some owner holds 128.
All inputs are finite; a program needn't handle non-finite values.
Results may differ from the reference program's by a relative error of at most 0.02.
Values may be sent and summed in bfloat16 or wider, within the bound.
No kernel may reach another device: no remote copies, remote signals or barrier semaphores. Data moves between devices by JAX's collectives and lax.ppermute only.
A program may use at most 128 MiB of HBM per device.

```python
import math
import jax
import jax.numpy as jnp
from jax import lax

DET = 1024
DIST = 4
ANG_MB = 4
MB = 1
ROWS_DEV = 64
CAP = 128
PAIRS = 8
PIXW = 1024
ANGLES = 4
N_ROWS = 16


def draw_slab_rows(key, part):
    first_key = jax.random.fold_in(key, 11)
    full_key = jax.random.fold_in(key, 12)
    first = jax.random.randint(first_key, (PAIRS,), 0, CAP + 1)
    full = jax.random.randint(full_key, (), 0, PAIRS)
    first = jnp.where(jnp.arange(PAIRS) == full, CAP, first)
    second = CAP - first
    return jnp.stack([first, second], axis=1).reshape(-1).astype(jnp.int32)


def shard_levels(stream_key, dims, shards, least, top_value):
    gain = 1.0
    for dim, parts in shards:
        draws = jax.random.uniform(jax.random.fold_in(jax.random.fold_in(stream_key, 6), dim), (parts,), jnp.float32, least / len(shards), top_value / len(shards))
        gain = gain * jnp.repeat(jnp.exp(draws), dims[dim] // parts).reshape((-1,) + (1,) * (len(dims) - 1 - dim))
    return gain


def noise(rng, dims, width, most, cuts=(), kind=jnp.bfloat16):
    level = shard_levels(rng, dims, cuts, -0.22, 0.18) if cuts else 1.0
    entries = jax.random.normal(rng, dims, jnp.float32) * width * level
    return jnp.minimum(jnp.maximum(entries, -most), most).astype(kind)


def setup_inputs(seed: int = 0) -> dict:
    key_of = jax.random.split(jax.random.key(seed), 6)
    return {
        "holograms": noise(key_of[0], (MB, ANG_MB, DIST, DET, DET), 1.0, 6.0, ((2, 2), (3, 16))),
        "propagation": jnp.clip(jnp.exp(jax.random.uniform(key_of[1], (DIST,), jnp.float32, math.log(100.0), math.log(1000.0))), 100.0, 1000.0),
        "weights": noise(key_of[2], (ANGLES, DET, PIXW), (ANGLES * DET) ** -0.5, 0.09375, ((2, 2),)),
        "angle_order": jax.vmap(lambda own: jax.random.permutation(own, ANG_MB))(jax.random.split(key_of[3], MB)).reshape((MB, ANG_MB)).astype(jnp.int32),
        "slab_rows": draw_slab_rows(jax.random.fold_in(key_of[5], 71), 0),
    }


absorb_ratio = 0.1
regularizer = 0.05


def to_half(value):
    return lax.optimization_barrier(value.astype(jnp.bfloat16)).astype(jnp.float32)


def reference(holograms, propagation, weights, angle_order, slab_rows):
    index = jnp.arange(DET, dtype=jnp.int32)
    signed = jnp.where(index < DET // 2, index, index - DET).astype(jnp.float32)
    radius = (signed[:, None] ** 2 + signed[None, :] ** 2) / float(DET * DET)
    chirp = propagation[:, None, None] * radius[None]
    transfer = 2.0 * (jnp.sin(chirp) + absorb_ratio * jnp.cos(chirp))
    denom = jnp.sum(transfer * transfer, axis=0) + regularizer
    recon = jnp.zeros((DET, PIXW), jnp.float32)
    for step in range(MB):
        for angle in range(ANG_MB):
            holo = holograms[step, angle].astype(jnp.float32)
            rows = jnp.fft.fft(holo, axis=-1, norm="ortho")
            rows = to_half(jnp.real(rows)) + 1j * to_half(jnp.imag(rows))
            spectra = jnp.fft.fft(rows, axis=-2, norm="ortho")
            numer = jnp.sum(transfer * spectra, axis=0) / denom
            numer = to_half(jnp.real(numer)) + 1j * to_half(jnp.imag(numer))
            half = jnp.fft.ifft(numer, axis=-2, norm="ortho")
            half = to_half(jnp.real(half)) + 1j * to_half(jnp.imag(half))
            phase = jnp.real(jnp.fft.ifft(half, axis=-1, norm="ortho")).astype(jnp.bfloat16)
            chosen = weights[step * ANG_MB + angle_order[step, angle]]
            recon = recon + jnp.dot(phase, chosen, preferred_element_type=jnp.float32)
    owner = jnp.arange(N_ROWS, dtype=jnp.int32)
    parity = owner % 2
    start = (owner - parity) * ROWS_DEV + parity * slab_rows[owner - parity]
    slot = jnp.arange(CAP, dtype=jnp.int32)
    where_rows = jnp.clip(start[:, None] + slot[None, :], 0, DET - 1).astype(jnp.int32)
    valid = (slot[None, :] < slab_rows[:, None]).astype(jnp.float32)
    picked = recon[where_rows] * valid[:, :, None]
    return picked.reshape(N_ROWS * CAP, PIXW).astype(jnp.bfloat16)
```

```python
import math

import jax
import jax.numpy as jnp
import numpy as np
from jax import lax
from jax.sharding import PartitionSpec as P

absorb_ratio = 0.1
regularizer = 0.05


def hartley(length):
    index = np.arange(length)
    turned = (index[:, None] * index[None, :] % length) * (2.0 * math.pi / length)
    table = (np.cos(turned) + np.sin(turned)) / math.sqrt(length)
    return table.astype(jnp.bfloat16)


def signed_square(index, length):
    signed = jnp.where(index < length // 2, index, index - length).astype(jnp.float32)
    return signed * signed / float(length * length)


def filters(propagation, rows_sq, cols_sq):
    first = propagation[:, None] * rows_sq[None]
    second = propagation[:, None] * cols_sq[None]
    sin_b, cos_b = jnp.sin(second), jnp.cos(second)
    with_sin = 2.0 * (cos_b - absorb_ratio * sin_b)
    with_cos = 2.0 * (sin_b + absorb_ratio * cos_b)
    transfer = (
        jnp.sin(first)[:, :, None] * with_sin[:, None, :]
        + jnp.cos(first)[:, :, None] * with_cos[:, None, :]
    )
    denom = jnp.sum(transfer * transfer, axis=0) + regularizer
    return transfer / denom


def on_device(holograms, propagation, weights, angle_order, slab_rows):
    mbatch, angles, dist_dev, rows_dev, width = holograms.shape
    groups = lax.axis_size("rows")
    cores = lax.axis_size("dist")
    capacity = 2 * rows_dev
    own = angles // cores
    cols = width // groups
    dists = dist_dev * cores
    device = lax.axis_index("rows")
    table = jnp.asarray(hartley(width))
    index = jnp.arange(width, dtype=jnp.int32)
    my_cols = device * cols + jnp.arange(cols, dtype=jnp.int32)
    gain = filters(propagation, signed_square(my_cols, width), signed_square(index, width))

    mine = lax.all_to_all(holograms[0], "dist", split_axis=0, concat_axis=1, tiled=True)
    flat = mine.reshape(own * dists * rows_dev, width)
    spec = jnp.einsum("kx,mx->km", table, flat, preferred_element_type=jnp.float32)
    spec = spec.astype(jnp.bfloat16).reshape(groups, cols, own * dists * rows_dev)
    spec = lax.all_to_all(spec, "rows", split_axis=0, concat_axis=0, tiled=True)
    spec = spec.reshape(groups, cols, own, dists, rows_dev).transpose(1, 2, 3, 0, 4)
    spec = spec.reshape(cols * own * dists, width)
    full = jnp.dot(spec, table, preferred_element_type=jnp.float32)
    full = full.reshape(cols, own, dists, width)
    full = jnp.sum(full * gain.transpose(1, 0, 2)[:, None], axis=2).astype(jnp.bfloat16)
    half = jnp.einsum("yq,akq->yak", table, full.transpose(1, 0, 2), preferred_element_type=jnp.float32)
    half = half.astype(jnp.bfloat16).reshape(groups, rows_dev, own * cols)
    half = lax.all_to_all(half, "rows", split_axis=0, concat_axis=0, tiled=True)
    half = half.reshape(groups, rows_dev, own, cols).transpose(2, 1, 0, 3)
    half = half.reshape(own * rows_dev, width)
    phase = jnp.dot(half, table, preferred_element_type=jnp.float32)
    phase = phase.astype(jnp.bfloat16).reshape(own, rows_dev, width)
    phase = lax.all_gather(phase, "dist", axis=0, tiled=True)
    place = (angle_order[0][None, :] == jnp.arange(angles)[:, None]).astype(jnp.bfloat16)
    phase = jnp.einsum("wa,ayx->wyx", place, phase, preferred_element_type=jnp.float32)
    recon = jnp.einsum(
        "wyx,wxp->yp",
        phase.astype(jnp.bfloat16),
        weights,
        preferred_element_type=jnp.float32,
    ).astype(jnp.bfloat16)
    parity = device % 2
    offset = parity * slab_rows[device - parity]
    count = slab_rows[device]
    pairs = [(source, source ^ 1) for source in range(groups)]
    partner = lax.ppermute(recon, "rows", pairs)
    lower = jnp.where(parity == 1, partner, recon)
    upper = jnp.where(parity == 1, recon, partner)
    paired = jnp.concatenate([lower, upper], axis=0)
    slot = jnp.arange(capacity, dtype=jnp.int32)[:, None]
    source = jnp.arange(capacity, dtype=jnp.int32)[None, :]
    select = ((source == offset + slot) & (slot < count)).astype(jnp.bfloat16)
    return jnp.dot(select, paired, preferred_element_type=jnp.float32).astype(jnp.bfloat16)


def solution(mesh):
    return jax.shard_map(
        on_device,
        mesh=mesh,
        in_specs=(P(None, None, "dist", "rows", None), P(), P(None, None, "dist"), P(), P()),
        out_specs=P("rows", "dist"),
        check_vma=False,
    )
```

```python
import math

import jax
import jax.numpy as jnp
import numpy as np
from jax import lax
from jax.experimental import pallas as pl
from jax.experimental.pallas import tpu as pltpu
from jax.sharding import PartitionSpec as P

absorb_ratio = 0.1
regularizer = 0.05
bf16 = jnp.bfloat16
f32 = jnp.float32


def hartley(length):
    index = np.arange(length)
    turned = (index[:, None] * index[None, :] % length) * (2.0 * math.pi / length)
    table = (np.cos(turned) + np.sin(turned)) / math.sqrt(length)
    return table.astype(bf16)


def signed_square(index, length):
    signed = jnp.where(index < length // 2, index, index - length).astype(f32)
    return signed * signed / float(length * length)


def filters(propagation, rows_sq, cols_sq):
    first = propagation[:, None] * rows_sq[None]
    second = propagation[:, None] * cols_sq[None]
    sin_b, cos_b = jnp.sin(second), jnp.cos(second)
    with_sin = 2.0 * (cos_b - absorb_ratio * sin_b)
    with_cos = 2.0 * (sin_b + absorb_ratio * cos_b)
    transfer = (
        jnp.sin(first)[:, :, None] * with_sin[:, None, :]
        + jnp.cos(first)[:, :, None] * with_cos[:, None, :]
    )
    denom = jnp.sum(transfer * transfer, axis=0) + regularizer
    return transfer / denom


def flat_plan(holograms, propagation, weights, angle_order, slab_rows):
    mbatch, angles, dist_dev, rows_dev, width = holograms.shape
    groups = lax.axis_size("rows")
    cores = lax.axis_size("dist")
    capacity = 2 * rows_dev
    own = angles // cores
    cols = width // groups
    dists = dist_dev * cores
    device = lax.axis_index("rows")
    table = jnp.asarray(hartley(width))
    index = jnp.arange(width, dtype=jnp.int32)
    my_cols = device * cols + jnp.arange(cols, dtype=jnp.int32)
    gain = filters(propagation, signed_square(my_cols, width), signed_square(index, width))

    mine = lax.all_to_all(holograms[0], "dist", split_axis=0, concat_axis=1, tiled=True)
    flat = mine.reshape(own * dists * rows_dev, width)
    spec = jnp.einsum("kx,mx->km", table, flat, preferred_element_type=f32)
    spec = spec.astype(bf16).reshape(groups, cols, own * dists * rows_dev)
    spec = lax.all_to_all(spec, "rows", split_axis=0, concat_axis=0, tiled=True)
    spec = spec.reshape(groups, cols, own, dists, rows_dev).transpose(1, 2, 3, 0, 4)
    spec = spec.reshape(cols * own * dists, width)
    full = jnp.dot(spec, table, preferred_element_type=f32)
    full = full.reshape(cols, own, dists, width)
    full = jnp.sum(full * gain.transpose(1, 0, 2)[:, None], axis=2).astype(bf16)
    half = jnp.einsum("yq,akq->yak", table, full.transpose(1, 0, 2), preferred_element_type=f32)
    half = half.astype(bf16).reshape(groups, rows_dev, own * cols)
    half = lax.all_to_all(half, "rows", split_axis=0, concat_axis=0, tiled=True)
    half = half.reshape(groups, rows_dev, own, cols).transpose(2, 1, 0, 3)
    half = half.reshape(own * rows_dev, width)
    phase = jnp.dot(half, table, preferred_element_type=f32)
    phase = phase.astype(bf16).reshape(own, rows_dev, width)
    phase = lax.all_gather(phase, "dist", axis=0, tiled=True)
    place = (angle_order[0][None, :] == jnp.arange(angles)[:, None]).astype(bf16)
    phase = jnp.einsum("wa,ayx->wyx", place, phase, preferred_element_type=f32)
    recon = jnp.einsum(
        "wyx,wxp->yp", phase.astype(bf16), weights, preferred_element_type=f32
    ).astype(bf16)
    parity = device % 2
    offset = parity * slab_rows[device - parity]
    count = slab_rows[device]
    pairs = [(source, source ^ 1) for source in range(groups)]
    partner = lax.ppermute(recon, "rows", pairs)
    lower = jnp.where(parity == 1, partner, recon)
    upper = jnp.where(parity == 1, recon, partner)
    paired = jnp.concatenate([lower, upper], axis=0)
    slot = jnp.arange(capacity, dtype=jnp.int32)[:, None]
    source = jnp.arange(capacity, dtype=jnp.int32)[None, :]
    select = ((source == offset + slot) & (slot < count)).astype(bf16)
    return jnp.dot(select, paired, preferred_element_type=f32).astype(bf16)


def row_kernel(inner, cores, own, chunk, place, holo, table, *outs):
    core, spot = place[0], place[1]
    block = table.shape[1] // inner
    dist_dev, rows_dev, width = holo.shape[1:]
    for rel in range(inner):
        start = pl.multiple_of((spot ^ rel) * block, block)
        part = table[:, pl.ds(start, block)]
        for other in range(cores):
            angle = (core ^ other) * own + chunk
            flat = holo[angle].reshape(dist_dev * rows_dev, width)
            got = jnp.dot(flat, part, preferred_element_type=f32)
            outs[rel * cores + other][...] = got.astype(bf16).reshape(dist_dev, rows_dev, block)


def column_kernel(inner, cores, outer, place, table, gain, *refs):
    pieces = refs[: inner * cores]
    out, first, last, stack, total, spectrum = refs[inner * cores :]
    spot, plane = place[1], place[2]
    dist_dev, rows_dev, block = pieces[0].shape
    depth = inner * rows_dev
    for rel in range(inner):
        start = pl.multiple_of((spot ^ rel) * rows_dev, rows_dev)
        for other in range(cores):
            for d in range(dist_dev):
                stack[other * dist_dev + d, pl.ds(start, rows_dev), :] = pieces[rel * cores + other][d]
    part = table[:, pl.ds(pl.multiple_of(plane * depth, depth), depth)]
    for d in range(cores * dist_dev):
        got = jnp.dot(part, stack[d], preferred_element_type=f32) * gain[d].astype(f32)
        if d == 0:
            total[...] = got
        else:
            total[...] += got
    spectrum[...] = total[...].astype(bf16)
    for z in range(outer):
        got = jnp.dot(
            table[z * depth : (z + 1) * depth, :], spectrum[...], preferred_element_type=f32
        ).astype(bf16)
        out[z] = got
        if z == 0:
            first[...] = got
        if z == outer - 1:
            last[...] = got


def recon_kernel(inner, cores, own, place, order, slabs, weights, *refs):
    halves = refs[: cores * own]
    outs = refs[cores * own :]
    core, spot, plane = place[0], place[1], place[2]
    depth, block = halves[0].shape
    capacity = 2 * depth // inner
    rows_dev = depth // inner
    joined = jnp.concatenate([half[...] for half in halves], axis=1)
    stacked = jnp.concatenate(
        [
            weights[order[0, (core ^ other) * own + chunk]]
            for other in range(cores)
            for chunk in range(own)
        ],
        axis=0,
    )
    slot = lax.broadcasted_iota(jnp.int32, (capacity, depth), 0)
    source = lax.broadcasted_iota(jnp.int32, (capacity, depth), 1)
    for rel in range(inner):
        there = spot ^ rel
        parity = there % 2
        owner = plane * inner + there
        offset = (there - parity) * rows_dev + parity * slabs[owner - parity]
        select = (source == slot + offset) & (slot < slabs[owner])
        select = jnp.where(select, 1.0, 0.0).astype(bf16)
        rows = jnp.dot(select, joined, preferred_element_type=f32).astype(bf16)
        got = jnp.dot(rows, stacked, preferred_element_type=f32)
        outs[rel][...] = got.astype(outs[rel].dtype)


def vmem(count):
    return [pl.BlockSpec(memory_space=pltpu.VMEM)] * count


def smem(count):
    return [pl.BlockSpec(memory_space=pltpu.SMEM)] * count


def plane_plan(inner, holograms, propagation, weights, angle_order, slab_rows):
    mbatch, angles, dist_dev, rows_dev, width = holograms.shape
    groups = lax.axis_size("rows")
    cores = lax.axis_size("dist")
    outer = groups // inner
    own = angles // cores
    block = width // inner
    depth = inner * rows_dev
    dists = cores * dist_dev
    pixels = weights.shape[2]
    capacity = 2 * rows_dev
    params = pltpu.CompilerParams(vmem_limit_bytes=40 * 2**20)

    device = lax.axis_index("rows")
    core = lax.axis_index("dist")
    plane, spot = device // inner, device % inner
    place = jnp.stack([core, spot, plane]).astype(jnp.int32)
    table = jnp.asarray(hartley(width))

    def sent(value, rel, other):
        if rel == 0 and other == 0:
            return value
        pairs = [
            (c * groups + r, (c ^ other) * groups + (r ^ rel))
            for c in range(cores)
            for r in range(groups)
        ]
        return lax.ppermute(value, ("dist", "rows"), pairs)

    arrived = []
    for chunk in range(own):
        pieces = pl.pallas_call(
            lambda *refs, chunk=chunk: row_kernel(inner, cores, own, chunk, *refs),
            out_shape=[jax.ShapeDtypeStruct((dist_dev, rows_dev, block), bf16)] * (inner * cores),
            in_specs=smem(1) + vmem(2),
            out_specs=vmem(inner * cores),
            compiler_params=params,
            cost_estimate=pl.CostEstimate(
                flops=2 * cores * dist_dev * rows_dev * width * width,
                bytes_accessed=2 * width * width + 4 * cores * dist_dev * rows_dev * width,
                transcendentals=0,
            ),
            name="row_spectra",
        )(place, holograms[0], table)
        arrived.append(
            [
                sent(pieces[rel * cores + other], rel, other)
                for rel in range(inner)
                for other in range(cores)
            ]
        )

    index = jnp.arange(width, dtype=jnp.int32)
    my_cols = spot * block + jnp.arange(block, dtype=jnp.int32)
    ordered = jnp.concatenate(
        [
            lax.dynamic_slice_in_dim(propagation, (core ^ other) * dist_dev, dist_dev, 0)
            for other in range(cores)
        ]
    )
    gain = filters(ordered, signed_square(index, width), signed_square(my_cols, width)).astype(bf16)

    my_table = lax.dynamic_slice_in_dim(table, spot * block, block, 0)
    turned = jnp.einsum("kx,wxp->wkp", my_table, weights, preferred_element_type=f32).astype(bf16)

    halves = []
    for chunk in range(own):
        parts, low, high = pl.pallas_call(
            lambda *refs: column_kernel(inner, cores, outer, *refs),
            out_shape=[jax.ShapeDtypeStruct((outer, depth, block), bf16)]
            + [jax.ShapeDtypeStruct((depth, block), bf16)] * 2,
            in_specs=smem(1) + vmem(2 + inner * cores),
            out_specs=vmem(3),
            scratch_shapes=[
                pltpu.VMEM((dists, depth, block), bf16),
                pltpu.VMEM((width, block), f32),
                pltpu.VMEM((width, block), bf16),
            ],
            compiler_params=params,
            cost_estimate=pl.CostEstimate(
                flops=2 * width * block * (dists * depth + width),
                bytes_accessed=2 * width * width + 2 * dists * width * block,
                transcendentals=0,
            ),
            name="columns",
        )(place, table, gain, *arrived[chunk])
        up = down = None
        for step in range(1, outer):
            if step == 1:
                to_up, to_down = high, low
            else:
                to_up = lax.dynamic_index_in_dim(parts, outer - step + plane, 0, False) + up
                to_down = lax.dynamic_index_in_dim(parts, step - outer + plane, 0, False) + down
            up_pairs = [
                (z * inner + i, (z + 1) * inner + i)
                for z in range(min(step, outer - 1))
                for i in range(inner)
            ]
            down_pairs = [(groups - 1 - a, groups - 1 - b) for a, b in up_pairs]
            up = lax.ppermute(to_up, "rows", up_pairs)
            down = lax.ppermute(to_down, "rows", down_pairs)
        mine = lax.dynamic_index_in_dim(parts, plane, 0, False).astype(f32)
        halves.append((mine + up.astype(f32) + down.astype(f32)).astype(bf16))
    halves = [sent(half, 0, other) for other in range(cores) for half in halves]

    slabs = pl.pallas_call(
        lambda *refs: recon_kernel(inner, cores, own, *refs),
        out_shape=[jax.ShapeDtypeStruct((capacity, pixels), f32)]
        + [jax.ShapeDtypeStruct((capacity, pixels), bf16)] * (inner - 1),
        in_specs=smem(3) + vmem(1 + cores * own),
        out_specs=vmem(inner),
        compiler_params=params,
        cost_estimate=pl.CostEstimate(
            flops=2 * inner * capacity * angles * block * (depth + pixels),
            bytes_accessed=2 * angles * block * (depth + pixels) + 2 * inner * capacity * pixels,
            transcendentals=0,
        ),
        name="recon_parts",
    )(place, angle_order, slab_rows, turned, *halves)
    total = slabs[0]
    for rel in range(1, inner):
        total = total + sent(slabs[rel], rel, 0).astype(f32)
    return total.astype(bf16)


def on_device(holograms, propagation, weights, angle_order, slab_rows):
    mbatch, angles, dist_dev, rows_dev, width = holograms.shape
    groups = lax.axis_size("rows")
    inner = 2 ** (int(math.log2(groups)) // 2)
    block = width // inner
    fits = (
        inner * (groups // inner) == groups
        and rows_dev % 16 == 0
        and block % 128 == 0
        and inner * rows_dev % 128 == 0
    )
    if fits:
        return plane_plan(inner, holograms, propagation, weights, angle_order, slab_rows)
    return flat_plan(holograms, propagation, weights, angle_order, slab_rows)


def solution(mesh):
    return jax.shard_map(
        on_device,
        mesh=mesh,
        in_specs=(P(None, None, "dist", "rows", None), P(), P(None, None, "dist"), P(), P()),
        out_specs=P("rows", "dist"),
        check_vma=False,
    )
```

```python
import math

import jax
import jax.numpy as jnp
import numpy as np
from jax import lax
from jax.experimental import pallas as pl
from jax.experimental.pallas import tpu as pltpu
from jax.sharding import PartitionSpec as P

absorb_ratio = 0.1
regularizer = 0.05
bf16 = jnp.bfloat16
f32 = jnp.float32


def hartley(length):
    index = np.arange(length)
    turned = (index[:, None] * index[None, :] % length) * (2.0 * math.pi / length)
    table = (np.cos(turned) + np.sin(turned)) / math.sqrt(length)
    return table.astype(bf16)


def signed_square(index, length):
    signed = jnp.where(index < length // 2, index, index - length).astype(f32)
    return signed * signed / float(length * length)


def filters(propagation, rows_sq, cols_sq):
    first = propagation[:, None] * rows_sq[None]
    second = propagation[:, None] * cols_sq[None]
    sin_b, cos_b = jnp.sin(second), jnp.cos(second)
    with_sin = 2.0 * (cos_b - absorb_ratio * sin_b)
    with_cos = 2.0 * (sin_b + absorb_ratio * cos_b)
    transfer = (
        jnp.sin(first)[:, :, None] * with_sin[:, None, :]
        + jnp.cos(first)[:, :, None] * with_cos[:, None, :]
    )
    denom = jnp.sum(transfer * transfer, axis=0) + regularizer
    return transfer / denom


def flat_plan(holograms, propagation, weights, angle_order, slab_rows):
    mbatch, angles, dist_dev, rows_dev, width = holograms.shape
    groups = lax.axis_size("rows")
    cores = lax.axis_size("dist")
    capacity = 2 * rows_dev
    own = angles // cores
    cols = width // groups
    dists = dist_dev * cores
    device = lax.axis_index("rows")
    table = jnp.asarray(hartley(width))
    index = jnp.arange(width, dtype=jnp.int32)
    my_cols = device * cols + jnp.arange(cols, dtype=jnp.int32)
    gain = filters(propagation, signed_square(my_cols, width), signed_square(index, width))

    mine = lax.all_to_all(holograms[0], "dist", split_axis=0, concat_axis=1, tiled=True)
    flat = mine.reshape(own * dists * rows_dev, width)
    spec = jnp.einsum("kx,mx->km", table, flat, preferred_element_type=f32)
    spec = spec.astype(bf16).reshape(groups, cols, own * dists * rows_dev)
    spec = lax.all_to_all(spec, "rows", split_axis=0, concat_axis=0, tiled=True)
    spec = spec.reshape(groups, cols, own, dists, rows_dev).transpose(1, 2, 3, 0, 4)
    spec = spec.reshape(cols * own * dists, width)
    full = jnp.dot(spec, table, preferred_element_type=f32)
    full = full.reshape(cols, own, dists, width)
    full = jnp.sum(full * gain.transpose(1, 0, 2)[:, None], axis=2).astype(bf16)
    half = jnp.einsum("yq,akq->yak", table, full.transpose(1, 0, 2), preferred_element_type=f32)
    half = half.astype(bf16).reshape(groups, rows_dev, own * cols)
    half = lax.all_to_all(half, "rows", split_axis=0, concat_axis=0, tiled=True)
    half = half.reshape(groups, rows_dev, own, cols).transpose(2, 1, 0, 3)
    half = half.reshape(own * rows_dev, width)
    phase = jnp.dot(half, table, preferred_element_type=f32)
    phase = phase.astype(bf16).reshape(own, rows_dev, width)
    phase = lax.all_gather(phase, "dist", axis=0, tiled=True)
    place = (angle_order[0][None, :] == jnp.arange(angles)[:, None]).astype(bf16)
    phase = jnp.einsum("wa,ayx->wyx", place, phase, preferred_element_type=f32)
    recon = jnp.einsum(
        "wyx,wxp->yp", phase.astype(bf16), weights, preferred_element_type=f32
    ).astype(bf16)
    parity = device % 2
    offset = parity * slab_rows[device - parity]
    count = slab_rows[device]
    pairs = [(source, source ^ 1) for source in range(groups)]
    partner = lax.ppermute(recon, "rows", pairs)
    lower = jnp.where(parity == 1, partner, recon)
    upper = jnp.where(parity == 1, recon, partner)
    paired = jnp.concatenate([lower, upper], axis=0)
    slot = jnp.arange(capacity, dtype=jnp.int32)[:, None]
    source = jnp.arange(capacity, dtype=jnp.int32)[None, :]
    select = ((source == offset + slot) & (slot < count)).astype(bf16)
    return jnp.dot(select, paired, preferred_element_type=f32).astype(bf16)


def row_kernel(inner, place, here, there, table, *outs):
    spot = place[1]
    block = table.shape[1] // inner
    for rel in range(inner):
        start = pl.multiple_of((spot ^ rel) * block, block)
        part = table[:, pl.ds(start, block)]
        at = 0
        for source in (here, there):
            dist_dev, rows_dev, width = source.shape[1:]
            flat = source[0].reshape(dist_dev * rows_dev, width)
            got = jnp.dot(flat, part, preferred_element_type=f32).astype(bf16)
            outs[rel][at : at + dist_dev] = got.reshape(dist_dev, rows_dev, block)
            at += dist_dev


def column_kernel(inner, outer, place, table, gain, *refs):
    pieces = refs[:inner]
    out, stack, total, spectrum = refs[inner:]
    spot, plane = place[1], place[2]
    dists, rows_dev, block = pieces[0].shape
    depth = inner * rows_dev
    for rel in range(inner):
        start = pl.multiple_of((spot ^ rel) * rows_dev, rows_dev)
        for d in range(dists):
            stack[d, pl.ds(start, rows_dev), :] = pieces[rel][d]
    part = table[:, pl.ds(pl.multiple_of(plane * depth, depth), depth)]
    for d in range(dists):
        got = jnp.dot(part, stack[d], preferred_element_type=f32) * gain[d].astype(f32)
        if d == 0:
            total[...] = got
        else:
            total[...] += got
    spectrum[...] = total[...].astype(bf16)
    for z in range(outer):
        got = jnp.dot(
            table[z * depth : (z + 1) * depth, :], spectrum[...], preferred_element_type=f32
        )
        out[z] = got.astype(bf16)


def phase_kernel(inner, place, table, *refs):
    pieces = refs[:inner]
    out, joined = refs[inner:]
    spot = place[1]
    block = table.shape[1] // inner
    for rel in range(inner):
        start = pl.multiple_of((spot ^ rel) * block, block)
        joined[:, pl.ds(start, block)] = pieces[rel][...]
    out[...] = jnp.dot(joined[...], table[...], preferred_element_type=f32).astype(bf16)


def recon_kernel(cores, own, chunk, place, order, slabs, weights, before, *refs):
    phases = refs[:cores]
    out = refs[cores]
    core = place[0]
    total = None if before is None else before[...]
    for other in range(cores):
        chosen = weights[order[0, (core ^ other) * own + chunk]]
        got = jnp.dot(phases[other][...], chosen, preferred_element_type=f32)
        total = got if total is None else total + got
    if slabs is None:
        out[...] = total
        return
    capacity = total.shape[0]
    device = place[3]
    parity = device % 2
    offset = parity * slabs[device - parity]
    slot = lax.broadcasted_iota(jnp.int32, (capacity, capacity), 0)
    source = lax.broadcasted_iota(jnp.int32, (capacity, capacity), 1)
    select = (source == slot + offset) & (slot < slabs[device])
    select = jnp.where(select, 1.0, 0.0).astype(bf16)
    got = jnp.dot(select, total.astype(bf16), preferred_element_type=f32)
    out[...] = got.astype(bf16)


def vmem(count):
    return [pl.BlockSpec(memory_space=pltpu.VMEM)] * count


def smem(count):
    return [pl.BlockSpec(memory_space=pltpu.SMEM)] * count


def plane_plan(inner, holograms, propagation, weights, angle_order, slab_rows):
    mbatch, angles, dist_dev, rows_dev, width = holograms.shape
    groups = lax.axis_size("rows")
    cores = lax.axis_size("dist")
    outer = groups // inner
    own = angles // cores
    block = width // inner
    depth = inner * rows_dev
    dists = cores * dist_dev
    pixels = weights.shape[2]
    capacity = 2 * rows_dev
    params = pltpu.CompilerParams(vmem_limit_bytes=20 * 2**20)

    device = lax.axis_index("rows")
    core = lax.axis_index("dist")
    plane, spot = device // inner, device % inner
    place = jnp.stack([core, spot, plane, device]).astype(jnp.int32)
    table = jnp.asarray(hartley(width))

    def sent(value, rel, other):
        if rel == 0 and other == 0:
            return value
        pairs = [
            (c * groups + r, (c ^ other) * groups + (r ^ rel))
            for c in range(cores)
            for r in range(groups)
        ]
        return lax.ppermute(value, ("dist", "rows"), pairs)

    other_angles = lax.dynamic_slice_in_dim(holograms[0], (core ^ 1) * own, own, 0)
    partner = sent(other_angles, 0, 1)

    arrived = []
    for chunk in range(own):
        pieces = pl.pallas_call(
            lambda *refs: row_kernel(inner, *refs),
            out_shape=[jax.ShapeDtypeStruct((dists, rows_dev, block), bf16)] * inner,
            grid_spec=pltpu.PrefetchScalarGridSpec(
                num_scalar_prefetch=1,
                grid=(1,),
                in_specs=[
                    pl.BlockSpec(
                        (1, dist_dev, rows_dev, width),
                        lambda i, place, chunk=chunk: (place[0] * own + chunk, 0, 0, 0),
                    ),
                    pl.BlockSpec(
                        (1, dist_dev, rows_dev, width), lambda i, place, chunk=chunk: (chunk, 0, 0, 0)
                    ),
                ]
                + vmem(1),
                out_specs=vmem(inner),
            ),
            compiler_params=params,
            cost_estimate=pl.CostEstimate(
                flops=2 * dists * rows_dev * width * width,
                bytes_accessed=2 * width * width + 4 * dists * rows_dev * width,
                transcendentals=0,
            ),
            name="row_spectra",
        )(place, holograms[0], partner, table)
        arrived.append([sent(pieces[rel], rel, 0) for rel in range(inner)])

    index = jnp.arange(width, dtype=jnp.int32)
    my_cols = spot * block + jnp.arange(block, dtype=jnp.int32)
    ordered = jnp.concatenate(
        [
            lax.dynamic_slice_in_dim(propagation, (core ^ other) * dist_dev, dist_dev, 0)
            for other in range(cores)
        ]
    )
    gain = filters(ordered, signed_square(index, width), signed_square(my_cols, width)).astype(bf16)

    def plane_sum(parts):
        if outer != 4:
            teams = [[z * inner + i for z in range(outer)] for i in range(inner)]
            return lax.psum_scatter(
                parts, "rows", scatter_dimension=0, axis_index_groups=teams, tiled=False
            ).astype(f32)

        def moved(value, steps):
            return lax.ppermute(
                value, "rows", [(a * inner + i, b * inner + i) for a, b in steps for i in range(inner)]
            )

        away = lax.dynamic_slice_in_dim(parts, jnp.where(plane < 2, 2, 0), 2, 0)
        got = moved(away, [(0, 1), (3, 2)])
        joint = (away.astype(f32) + got.astype(f32)).astype(bf16)
        across = moved(joint, [(1, 2), (2, 1)]).astype(f32)
        near = lax.dynamic_index_in_dim(parts, plane ^ 1, 0, False).astype(f32)
        near = (near + lax.dynamic_index_in_dim(across, (plane ^ 1) % 2, 0, False)).astype(bf16)
        last = moved(near, [(0, 1), (1, 0), (2, 3), (3, 2)]).astype(f32)
        mine = lax.dynamic_index_in_dim(parts, plane, 0, False).astype(f32)
        return mine + lax.dynamic_index_in_dim(across, plane % 2, 0, False) + last

    total = None
    for chunk in range(own):
        parts = pl.pallas_call(
            lambda *refs: column_kernel(inner, outer, *refs),
            out_shape=jax.ShapeDtypeStruct((outer, depth, block), bf16),
            in_specs=smem(1) + vmem(2 + inner),
            out_specs=pl.BlockSpec(memory_space=pltpu.VMEM),
            scratch_shapes=[
                pltpu.VMEM((dists, depth, block), bf16),
                pltpu.VMEM((width, block), f32),
                pltpu.VMEM((width, block), bf16),
            ],
            compiler_params=params,
            cost_estimate=pl.CostEstimate(
                flops=2 * width * block * (dists * depth + width),
                bytes_accessed=2 * width * width + 2 * dists * width * block,
                transcendentals=0,
            ),
            name="columns",
        )(place, table, gain, *arrived[chunk])
        half = plane_sum(parts).astype(bf16)
        pair_rows = {}
        for rel in range(0, inner, 2):
            start = ((spot ^ rel) // 2) * capacity
            pair_rows[rel] = lax.dynamic_slice_in_dim(half, start, capacity, 0)
        pieces = [sent(pair_rows[rel - rel % 2], rel, 0) for rel in range(inner)]
        phase = pl.pallas_call(
            lambda *refs: phase_kernel(inner, *refs),
            out_shape=jax.ShapeDtypeStruct((capacity, width), bf16),
            in_specs=smem(1) + vmem(1 + inner),
            out_specs=pl.BlockSpec(memory_space=pltpu.VMEM),
            scratch_shapes=[pltpu.VMEM((capacity, width), bf16)],
            compiler_params=params,
            cost_estimate=pl.CostEstimate(
                flops=2 * capacity * width * width,
                bytes_accessed=2 * width * width + 4 * capacity * width,
                transcendentals=0,
            ),
            name="phase",
        )(place, table, *pieces)
        phases = [sent(phase, 0, other) for other in range(cores)]
        first, final = chunk == 0, chunk == own - 1

        def recon(place, order, *refs, first=first, final=final, chunk=chunk):
            refs = list(refs)
            slabs = refs.pop(0) if final else None
            chosen = refs.pop(0)
            before = None if first else refs.pop(0)
            recon_kernel(cores, own, chunk, place, order, slabs, chosen, before, *refs)

        scalars = [place, angle_order] + ([slab_rows] if final else [])
        arrays = [weights] + ([] if first else [total]) + phases
        total = pl.pallas_call(
            recon,
            out_shape=jax.ShapeDtypeStruct((capacity, pixels), bf16 if final else f32),
            in_specs=smem(len(scalars)) + vmem(len(arrays)),
            out_specs=pl.BlockSpec(memory_space=pltpu.VMEM),
            compiler_params=params,
            cost_estimate=pl.CostEstimate(
                flops=2 * cores * capacity * width * pixels,
                bytes_accessed=2 * cores * width * (capacity + pixels),
                transcendentals=0,
            ),
            name="recon",
        )(*scalars, *arrays)
    return total


def on_device(holograms, propagation, weights, angle_order, slab_rows):
    mbatch, angles, dist_dev, rows_dev, width = holograms.shape
    groups = lax.axis_size("rows")
    inner = 2 ** (int(math.log2(groups)) // 2)
    block = width // inner
    fits = (
        inner * (groups // inner) == groups
        and rows_dev % 16 == 0
        and block % 128 == 0
        and inner * rows_dev % 128 == 0
        and inner % 2 == 0
        and lax.axis_size("dist") == 2
    )
    if fits:
        return plane_plan(inner, holograms, propagation, weights, angle_order, slab_rows)
    return flat_plan(holograms, propagation, weights, angle_order, slab_rows)


def solution(mesh):
    return jax.shard_map(
        on_device,
        mesh=mesh,
        in_specs=(P(None, None, "dist", "rows", None), P(), P(None, None, "dist"), P(), P()),
        out_specs=P("rows", "dist"),
        check_vma=False,
    )
```

```python
import math

import jax
import jax.numpy as jnp
import numpy as np
from jax import lax
from jax.experimental import pallas as pl
from jax.experimental.pallas import tpu as pltpu
from jax.sharding import PartitionSpec as P

absorb_ratio = 0.1
regularizer = 0.05
bf16 = jnp.bfloat16
f32 = jnp.float32


def hartley(length):
    index = np.arange(length)
    turned = (index[:, None] * index[None, :] % length) * (2.0 * math.pi / length)
    table = (np.cos(turned) + np.sin(turned)) / math.sqrt(length)
    return table.astype(bf16)


def signed_square(index, length):
    signed = jnp.where(index < length // 2, index, index - length).astype(f32)
    return signed * signed / float(length * length)


def filters(propagation, rows_sq, cols_sq):
    first = propagation[:, None] * rows_sq[None]
    second = propagation[:, None] * cols_sq[None]
    sin_b, cos_b = jnp.sin(second), jnp.cos(second)
    with_sin = 2.0 * (cos_b - absorb_ratio * sin_b)
    with_cos = 2.0 * (sin_b + absorb_ratio * cos_b)
    transfer = (
        jnp.sin(first)[:, :, None] * with_sin[:, None, :]
        + jnp.cos(first)[:, :, None] * with_cos[:, None, :]
    )
    denom = jnp.sum(transfer * transfer, axis=0) + regularizer
    return transfer / denom


def flat_plan(holograms, propagation, weights, angle_order, slab_rows):
    mbatch, angles, dist_dev, rows_dev, width = holograms.shape
    groups = lax.axis_size("rows")
    cores = lax.axis_size("dist")
    capacity = 2 * rows_dev
    own = angles // cores
    cols = width // groups
    dists = dist_dev * cores
    device = lax.axis_index("rows")
    table = jnp.asarray(hartley(width))
    index = jnp.arange(width, dtype=jnp.int32)
    my_cols = device * cols + jnp.arange(cols, dtype=jnp.int32)
    gain = filters(propagation, signed_square(my_cols, width), signed_square(index, width))

    mine = lax.all_to_all(holograms[0], "dist", split_axis=0, concat_axis=1, tiled=True)
    flat = mine.reshape(own * dists * rows_dev, width)
    spec = jnp.einsum("kx,mx->km", table, flat, preferred_element_type=f32)
    spec = spec.astype(bf16).reshape(groups, cols, own * dists * rows_dev)
    spec = lax.all_to_all(spec, "rows", split_axis=0, concat_axis=0, tiled=True)
    spec = spec.reshape(groups, cols, own, dists, rows_dev).transpose(1, 2, 3, 0, 4)
    spec = spec.reshape(cols * own * dists, width)
    full = jnp.dot(spec, table, preferred_element_type=f32)
    full = full.reshape(cols, own, dists, width)
    full = jnp.sum(full * gain.transpose(1, 0, 2)[:, None], axis=2).astype(bf16)
    half = jnp.einsum("yq,akq->yak", table, full.transpose(1, 0, 2), preferred_element_type=f32)
    half = half.astype(bf16).reshape(groups, rows_dev, own * cols)
    half = lax.all_to_all(half, "rows", split_axis=0, concat_axis=0, tiled=True)
    half = half.reshape(groups, rows_dev, own, cols).transpose(2, 1, 0, 3)
    half = half.reshape(own * rows_dev, width)
    phase = jnp.dot(half, table, preferred_element_type=f32)
    phase = phase.astype(bf16).reshape(own, rows_dev, width)
    phase = lax.all_gather(phase, "dist", axis=0, tiled=True)
    place = (angle_order[0][None, :] == jnp.arange(angles)[:, None]).astype(bf16)
    phase = jnp.einsum("wa,ayx->wyx", place, phase, preferred_element_type=f32)
    recon = jnp.einsum(
        "wyx,wxp->yp", phase.astype(bf16), weights, preferred_element_type=f32
    ).astype(bf16)
    parity = device % 2
    offset = parity * slab_rows[device - parity]
    count = slab_rows[device]
    pairs = [(source, source ^ 1) for source in range(groups)]
    partner = lax.ppermute(recon, "rows", pairs)
    lower = jnp.where(parity == 1, partner, recon)
    upper = jnp.where(parity == 1, recon, partner)
    paired = jnp.concatenate([lower, upper], axis=0)
    slot = jnp.arange(capacity, dtype=jnp.int32)[:, None]
    source = jnp.arange(capacity, dtype=jnp.int32)[None, :]
    select = ((source == offset + slot) & (slot < count)).astype(bf16)
    return jnp.dot(select, paired, preferred_element_type=f32).astype(bf16)


def row_kernel(inner, holo, table, out):
    cores, _, dist_dev, rows_dev, width = holo.shape
    block = width // inner
    flat = holo[...].reshape(cores * dist_dev * rows_dev, width)
    for spot in range(inner):
        part = table[:, spot * block : (spot + 1) * block]
        got = jnp.dot(flat, part, preferred_element_type=f32).astype(bf16)
        got = got.reshape(cores, dist_dev, rows_dev, block)
        for core in range(cores):
            out[core * inner + spot] = got[core]


def filter_kernel(sin_a, cos_a, with_sin, with_cos, out):
    dists, width, block = out.shape
    step = 128
    for at in range(0, width, step):
        rows = pl.ds(at, step)
        transfer = [
            sin_a[rows, d : d + 1] * with_sin[d : d + 1, :] + cos_a[rows, d : d + 1] * with_cos[d : d + 1, :]
            for d in range(dists)
        ]
        denom = transfer[0] * transfer[0]
        for value in transfer[1:]:
            denom = denom + value * value
        scale = 1.0 / (denom + regularizer)
        for d in range(dists):
            out[d, rows, :] = (transfer[d] * scale).astype(bf16)


def column_kernel(inner, outer, place, table, gain, pieces, out, stack, total, spectrum):
    plane = place[1]
    _, dist_dev, rows_dev, block = pieces.shape
    dists = gain.shape[0]
    depth = inner * rows_dev
    for d in range(dists):
        for spot in range(inner):
            stack[d, spot * rows_dev : (spot + 1) * rows_dev, :] = pieces[
                d // dist_dev * inner + spot, d % dist_dev
            ]
    part = table[:, pl.ds(pl.multiple_of(plane * depth, depth), depth)]
    for d in range(dists):
        got = jnp.dot(part, stack[d], preferred_element_type=f32) * gain[d].astype(f32)
        if d == 0:
            total[...] = got
        else:
            total[...] += got
    spectrum[...] = total[...].astype(bf16)
    for z in range(outer):
        got = jnp.dot(
            table[z * depth : (z + 1) * depth, :], spectrum[...], preferred_element_type=f32
        )
        out[z] = got.astype(bf16)


def half_kernel(inner, parts, out):
    outer, depth, block = parts.shape
    capacity = 2 * depth // inner
    for at in range(0, depth, capacity):
        rows = parts[0, at : at + capacity, :].astype(f32)
        for z in range(1, outer):
            rows = rows + parts[z, at : at + capacity, :].astype(f32)
        rows = rows.astype(bf16)
        for twin in range(2):
            out[at // capacity * 2 + twin] = rows


def phase_kernel(table, pieces, out, joined):
    inner, capacity, block = pieces.shape
    for spot in range(inner):
        joined[:, spot * block : (spot + 1) * block] = pieces[spot]
    out[...] = jnp.dot(joined[...], table[...], preferred_element_type=f32).astype(bf16)


def recon_kernel(cores, own, chunk, place, order, slabs, weights, before, *refs):
    phases = refs[:cores]
    out = refs[cores]
    core = place[0]
    total = None if before is None else before[...]
    for other in range(cores):
        chosen = weights[order[0, (core ^ other) * own + chunk]]
        got = jnp.dot(phases[other][...], chosen, preferred_element_type=f32)
        total = got if total is None else total + got
    if slabs is None:
        out[...] = total
        return
    capacity = total.shape[0]
    device = place[2]
    parity = device % 2
    offset = parity * slabs[device - parity]
    slot = lax.broadcasted_iota(jnp.int32, (capacity, capacity), 0)
    source = lax.broadcasted_iota(jnp.int32, (capacity, capacity), 1)
    select = (source == slot + offset) & (slot < slabs[device])
    select = jnp.where(select, 1.0, 0.0).astype(bf16)
    got = jnp.dot(select, total.astype(bf16), preferred_element_type=f32)
    out[...] = got.astype(bf16)


def vmem(count):
    return [pl.BlockSpec(memory_space=pltpu.VMEM)] * count


def smem(count):
    return [pl.BlockSpec(memory_space=pltpu.SMEM)] * count


def plane_plan(inner, holograms, propagation, weights, angle_order, slab_rows):
    mbatch, angles, dist_dev, rows_dev, width = holograms.shape
    groups = lax.axis_size("rows")
    cores = lax.axis_size("dist")
    outer = groups // inner
    own = angles // cores
    block = width // inner
    depth = inner * rows_dev
    dists = cores * dist_dev
    pixels = weights.shape[2]
    capacity = 2 * rows_dev
    params = pltpu.CompilerParams(vmem_limit_bytes=20 * 2**20)

    def cost(flops, *arrays):
        return pl.CostEstimate(
            flops=flops, bytes_accessed=sum(2 * math.prod(a) for a in arrays), transcendentals=0
        )

    device = lax.axis_index("rows")
    core = lax.axis_index("dist")
    plane, spot = device // inner, device % inner
    place = jnp.stack([core, plane, device]).astype(jnp.int32)
    table = jnp.asarray(hartley(width))
    in_plane = [[z * inner + i for i in range(inner)] for z in range(outer)]
    in_line = [[z * inner + i for z in range(outer)] for i in range(inner)]
    with_cores = [[c * groups + r for c in range(cores) for r in team] for team in in_plane]

    def exchanged(value, axes, teams):
        return lax.all_to_all(
            value, axes, split_axis=0, concat_axis=0, axis_index_groups=teams, tiled=True
        )

    by_core = holograms[0].reshape(cores, own, dist_dev, rows_dev, width)
    arrived = []
    for chunk in range(own):
        pieces = pl.pallas_call(
            lambda *refs: row_kernel(inner, *refs),
            out_shape=jax.ShapeDtypeStruct((cores * inner, dist_dev, rows_dev, block), bf16),
            grid=(1,),
            in_specs=[
                pl.BlockSpec(
                    (cores, 1, dist_dev, rows_dev, width),
                    lambda i, chunk=chunk: (0, chunk, 0, 0, 0),
                )
            ]
            + vmem(1),
            out_specs=pl.BlockSpec(memory_space=pltpu.VMEM),
            compiler_params=params,
            cost_estimate=cost(
                2 * dists * rows_dev * width * width, (width, width), (2, dists, rows_dev, width)
            ),
            name="row_spectra",
        )(by_core, table)
        arrived.append(exchanged(pieces, ("dist", "rows"), with_cores))

    index = jnp.arange(width, dtype=jnp.int32)
    my_cols = spot * block + jnp.arange(block, dtype=jnp.int32)
    first = signed_square(index, width)[:, None] * propagation[None]
    second = propagation[:, None] * signed_square(my_cols, width)[None]
    sin_b, cos_b = jnp.sin(second), jnp.cos(second)
    gain = pl.pallas_call(
        filter_kernel,
        out_shape=jax.ShapeDtypeStruct((dists, width, block), bf16),
        in_specs=vmem(4),
        out_specs=pl.BlockSpec(memory_space=pltpu.VMEM),
        compiler_params=params,
        cost_estimate=cost(32 * width * block, (dists, width, block)),
        name="filters",
    )(
        jnp.sin(first),
        jnp.cos(first),
        2.0 * (cos_b - absorb_ratio * sin_b),
        2.0 * (sin_b + absorb_ratio * cos_b),
    )

    total = None
    for chunk in range(own):
        parts = pl.pallas_call(
            lambda *refs: column_kernel(inner, outer, *refs),
            out_shape=jax.ShapeDtypeStruct((outer, depth, block), bf16),
            in_specs=smem(1) + vmem(3),
            out_specs=pl.BlockSpec(memory_space=pltpu.VMEM),
            scratch_shapes=[
                pltpu.VMEM((dists, depth, block), bf16),
                pltpu.VMEM((width, block), f32),
                pltpu.VMEM((width, block), bf16),
            ],
            compiler_params=params,
            cost_estimate=cost(
                2 * width * block * (dists * depth + width), (width, width), (dists, width, block)
            ),
            name="columns",
        )(place, table, gain, arrived[chunk])
        parts = exchanged(parts, "rows", in_line)
        halves = pl.pallas_call(
            lambda *refs: half_kernel(inner, *refs),
            out_shape=jax.ShapeDtypeStruct((inner, capacity, block), bf16),
            in_specs=vmem(1),
            out_specs=pl.BlockSpec(memory_space=pltpu.VMEM),
            compiler_params=params,
            cost_estimate=cost(outer * depth * block, (2, outer, depth, block)),
            name="half",
        )(parts)
        halves = exchanged(halves, "rows", in_plane)
        phase = pl.pallas_call(
            phase_kernel,
            out_shape=jax.ShapeDtypeStruct((capacity, width), bf16),
            in_specs=vmem(2),
            out_specs=pl.BlockSpec(memory_space=pltpu.VMEM),
            scratch_shapes=[pltpu.VMEM((capacity, width), bf16)],
            compiler_params=params,
            cost_estimate=cost(2 * capacity * width * width, (width, width), (2, capacity, width)),
            name="phase",
        )(table, halves)
        swaps = [(c, c ^ 1) for c in range(cores)]
        phases = [phase, lax.ppermute(phase, "dist", swaps)]
        opening, final = chunk == 0, chunk == own - 1

        def recon(place, order, *refs, opening=opening, final=final, chunk=chunk):
            refs = list(refs)
            slabs = refs.pop(0) if final else None
            chosen = refs.pop(0)
            before = None if opening else refs.pop(0)
            recon_kernel(cores, own, chunk, place, order, slabs, chosen, before, *refs)

        scalars = [place, angle_order] + ([slab_rows] if final else [])
        arrays = [weights] + ([] if opening else [total]) + phases
        total = pl.pallas_call(
            recon,
            out_shape=jax.ShapeDtypeStruct((capacity, pixels), bf16 if final else f32),
            in_specs=smem(len(scalars)) + vmem(len(arrays)),
            out_specs=pl.BlockSpec(memory_space=pltpu.VMEM),
            compiler_params=params,
            cost_estimate=cost(
                2 * cores * capacity * width * pixels, (cores, width, capacity + pixels)
            ),
            name="recon",
        )(*scalars, *arrays)
    return total


def on_device(holograms, propagation, weights, angle_order, slab_rows):
    mbatch, angles, dist_dev, rows_dev, width = holograms.shape
    groups = lax.axis_size("rows")
    inner = 2 ** (int(math.log2(groups)) // 2)
    block = width // inner
    fits = (
        inner * (groups // inner) == groups
        and rows_dev % 16 == 0
        and block % 128 == 0
        and inner * rows_dev % 128 == 0
        and inner % 2 == 0
        and lax.axis_size("dist") == 2
    )
    if fits:
        return plane_plan(inner, holograms, propagation, weights, angle_order, slab_rows)
    return flat_plan(holograms, propagation, weights, angle_order, slab_rows)


def solution(mesh):
    return jax.shard_map(
        on_device,
        mesh=mesh,
        in_specs=(P(None, None, "dist", "rows", None), P(), P(None, None, "dist"), P(), P()),
        out_specs=P("rows", "dist"),
        check_vma=False,
    )
```

```python
import math

import jax
import jax.numpy as jnp
import numpy as np
from jax import lax
from jax.experimental import pallas as pl
from jax.experimental.pallas import tpu as pltpu
from jax.sharding import PartitionSpec as P

absorb_ratio = 0.1
regularizer = 0.05
bf16 = jnp.bfloat16
f32 = jnp.float32


def hartley(length):
    index = np.arange(length)
    turned = (index[:, None] * index[None, :] % length) * (2.0 * math.pi / length)
    table = (np.cos(turned) + np.sin(turned)) / math.sqrt(length)
    return table.astype(bf16)


def signed_square(index, length):
    signed = jnp.where(index < length // 2, index, index - length).astype(f32)
    return signed * signed / float(length * length)


def filters(propagation, rows_sq, cols_sq):
    first = propagation[:, None] * rows_sq[None]
    second = propagation[:, None] * cols_sq[None]
    sin_b, cos_b = jnp.sin(second), jnp.cos(second)
    with_sin = 2.0 * (cos_b - absorb_ratio * sin_b)
    with_cos = 2.0 * (sin_b + absorb_ratio * cos_b)
    transfer = (
        jnp.sin(first)[:, :, None] * with_sin[:, None, :]
        + jnp.cos(first)[:, :, None] * with_cos[:, None, :]
    )
    denom = jnp.sum(transfer * transfer, axis=0) + regularizer
    return transfer / denom


def flat_plan(holograms, propagation, weights, angle_order, slab_rows):
    mbatch, angles, dist_dev, rows_dev, width = holograms.shape
    groups = lax.axis_size("rows")
    cores = lax.axis_size("dist")
    capacity = 2 * rows_dev
    own = angles // cores
    cols = width // groups
    dists = dist_dev * cores
    device = lax.axis_index("rows")
    table = jnp.asarray(hartley(width))
    index = jnp.arange(width, dtype=jnp.int32)
    my_cols = device * cols + jnp.arange(cols, dtype=jnp.int32)
    gain = filters(propagation, signed_square(my_cols, width), signed_square(index, width))

    mine = lax.all_to_all(holograms[0], "dist", split_axis=0, concat_axis=1, tiled=True)
    flat = mine.reshape(own * dists * rows_dev, width)
    spec = jnp.einsum("kx,mx->km", table, flat, preferred_element_type=f32)
    spec = spec.astype(bf16).reshape(groups, cols, own * dists * rows_dev)
    spec = lax.all_to_all(spec, "rows", split_axis=0, concat_axis=0, tiled=True)
    spec = spec.reshape(groups, cols, own, dists, rows_dev).transpose(1, 2, 3, 0, 4)
    spec = spec.reshape(cols * own * dists, width)
    full = jnp.dot(spec, table, preferred_element_type=f32)
    full = full.reshape(cols, own, dists, width)
    full = jnp.sum(full * gain.transpose(1, 0, 2)[:, None], axis=2).astype(bf16)
    half = jnp.einsum("yq,akq->yak", table, full.transpose(1, 0, 2), preferred_element_type=f32)
    half = half.astype(bf16).reshape(groups, rows_dev, own * cols)
    half = lax.all_to_all(half, "rows", split_axis=0, concat_axis=0, tiled=True)
    half = half.reshape(groups, rows_dev, own, cols).transpose(2, 1, 0, 3)
    half = half.reshape(own * rows_dev, width)
    phase = jnp.dot(half, table, preferred_element_type=f32)
    phase = phase.astype(bf16).reshape(own, rows_dev, width)
    phase = lax.all_gather(phase, "dist", axis=0, tiled=True)
    place = (angle_order[0][None, :] == jnp.arange(angles)[:, None]).astype(bf16)
    phase = jnp.einsum("wa,ayx->wyx", place, phase, preferred_element_type=f32)
    recon = jnp.einsum(
        "wyx,wxp->yp", phase.astype(bf16), weights, preferred_element_type=f32
    ).astype(bf16)
    parity = device % 2
    offset = parity * slab_rows[device - parity]
    count = slab_rows[device]
    pairs = [(source, source ^ 1) for source in range(groups)]
    partner = lax.ppermute(recon, "rows", pairs)
    lower = jnp.where(parity == 1, partner, recon)
    upper = jnp.where(parity == 1, recon, partner)
    paired = jnp.concatenate([lower, upper], axis=0)
    slot = jnp.arange(capacity, dtype=jnp.int32)[:, None]
    source = jnp.arange(capacity, dtype=jnp.int32)[None, :]
    select = ((source == offset + slot) & (slot < count)).astype(bf16)
    return jnp.dot(select, paired, preferred_element_type=f32).astype(bf16)


def take_kernel(holo, out):
    out[...] = holo[...]


def row_kernel(inner, place, here, there, table, *outs):
    spot = place[1]
    dist_dev, rows_dev, width = here.shape[1:]
    block = width // inner
    flat = jnp.concatenate(
        [source[0].reshape(dist_dev * rows_dev, width) for source in (here, there)], axis=0
    )
    for rel in range(inner):
        part = table[:, pl.ds(pl.multiple_of((spot ^ rel) * block, block), block)]
        got = jnp.dot(flat, part, preferred_element_type=f32).astype(bf16)
        outs[rel][...] = got.reshape(2 * dist_dev, rows_dev, block)


def filter_kernel(waves_a, with_sin, with_cos, out):
    dists, width, block = out.shape
    turned = waves_a[...].T
    step = 128
    for at in range(0, width, step):
        rows = turned[at : at + step]
        transfer = [
            rows[:, d : d + 1] * with_sin[d : d + 1, :]
            + rows[:, dists + d : dists + d + 1] * with_cos[d : d + 1, :]
            for d in range(dists)
        ]
        denom = transfer[0] * transfer[0]
        for value in transfer[1:]:
            denom = denom + value * value
        scale = 1.0 / (denom + regularizer)
        for d in range(dists):
            out[d, at : at + step, :] = (transfer[d] * scale).astype(bf16)


def column_kernel(inner, outer, place, table, gain, *refs):
    pieces = refs[:inner]
    away, keep, stack, total, spectrum = refs[inner:]
    spot, plane = place[1], place[2]
    dists, rows_dev, block = pieces[0].shape
    depth = inner * rows_dev
    for rel in range(inner):
        start = pl.multiple_of((spot ^ rel) * rows_dev, rows_dev)
        for d in range(dists):
            stack[d, pl.ds(start, rows_dev), :] = pieces[rel][d]
    part = table[:, pl.ds(pl.multiple_of(plane * depth, depth), depth)]
    for d in range(dists):
        got = jnp.dot(part, stack[d], preferred_element_type=f32) * gain[d].astype(f32)
        if d == 0:
            total[...] = got
        else:
            total[...] += got
    spectrum[...] = total[...].astype(bf16)
    half = outer // 2
    side = plane // half
    for out, first in ((away, (1 - side) * half), (keep, side * half)):
        rows = pl.ds(pl.multiple_of(first * depth, half * depth), half * depth)
        got = jnp.dot(table[rows, :], spectrum[...], preferred_element_type=f32)
        out[...] = got.astype(bf16).reshape(half, depth, block)


def add_kernel(one, two, out):
    out[...] = (one[...].astype(f32) + two[...].astype(f32)).astype(bf16)


def near_kernel(place, keep, across, out):
    plane = place[2]
    which = (plane ^ 1) % 2
    inside = (plane == 1) | (plane == 2)
    more = jnp.where(inside, across[which].astype(f32), 0.0)
    out[...] = (keep[which].astype(f32) + more).astype(bf16)


def half_kernel(inner, place, *refs):
    mine, other = refs[-2:]
    own = len(refs[:-2]) // 3
    spot, plane = place[1], place[2]
    which = plane % 2
    inside = (plane == 1) | (plane == 2)
    capacity = mine.shape[1]
    for chunk in range(own):
        keep, across, last = refs[3 * chunk : 3 * chunk + 3]
        for out, pair in ((mine, spot // 2), (other, 1 - spot // 2)):
            rows = pl.ds(pl.multiple_of(pair * capacity, capacity), capacity)
            more = jnp.where(inside, across[which, rows, :].astype(f32), 0.0)
            got = keep[which, rows, :].astype(f32) + more + last[rows, :].astype(f32)
            out[chunk] = got.astype(bf16)


def phase_kernel(inner, place, table, *refs):
    pieces = refs[:inner]
    out, joined = refs[inner:]
    spot = place[1]
    own, capacity, block = pieces[0].shape
    for rel in range(inner):
        columns = pl.ds(pl.multiple_of((spot ^ rel) * block, block), block)
        joined[:, columns] = pieces[rel][...].reshape(own * capacity, block)
    got = jnp.dot(joined[...], table[...], preferred_element_type=f32)
    out[...] = got.astype(bf16).reshape(own, capacity, inner * block)


def recon_kernel(own, place, order, slabs, here, there, weights, out, total):
    step = pl.program_id(0)
    phase = jnp.where(step < own, here[0], there[0])
    got = jnp.dot(phase, weights[0], preferred_element_type=f32)

    @pl.when(step == 0)
    def _():
        total[...] = got

    @pl.when(step > 0)
    def _():
        total[...] += got

    @pl.when(step == 2 * own - 1)
    def _():
        capacity = total.shape[0]
        device = place[3]
        parity = device % 2
        offset = parity * slabs[device - parity]
        slot = lax.broadcasted_iota(jnp.int32, (capacity, capacity), 0)
        source = lax.broadcasted_iota(jnp.int32, (capacity, capacity), 1)
        select = (source == slot + offset) & (slot < slabs[device])
        select = jnp.where(select, 1.0, 0.0).astype(bf16)
        picked = jnp.dot(select, total[...].astype(bf16), preferred_element_type=f32)
        out[...] = picked.astype(bf16)


def vmem(count):
    return [pl.BlockSpec(memory_space=pltpu.VMEM)] * count


def smem(count):
    return [pl.BlockSpec(memory_space=pltpu.SMEM)] * count


def plane_plan(inner, holograms, propagation, weights, angle_order, slab_rows):
    mbatch, angles, dist_dev, rows_dev, width = holograms.shape
    groups = lax.axis_size("rows")
    cores = lax.axis_size("dist")
    outer = groups // inner
    own = angles // cores
    block = width // inner
    depth = inner * rows_dev
    dists = cores * dist_dev
    pixels = weights.shape[2]
    capacity = 2 * rows_dev
    params = pltpu.CompilerParams(vmem_limit_bytes=16 * 2**20)
    one_out = pl.BlockSpec(memory_space=pltpu.VMEM)

    def cost(flops, *arrays):
        return pl.CostEstimate(
            flops=flops, bytes_accessed=sum(2 * math.prod(a) for a in arrays), transcendentals=0
        )

    def shaped(*shape):
        return jax.ShapeDtypeStruct(shape, bf16)

    device = lax.axis_index("rows")
    core = lax.axis_index("dist")
    plane, spot = device // inner, device % inner
    place = jnp.stack([core, spot, plane, device]).astype(jnp.int32)
    table = jnp.asarray(hartley(width))

    def sent(value, target):
        pairs = []
        for c in range(cores):
            for r in range(groups):
                to_core, to_row = target(c, r)
                pairs.append((c * groups + r, to_core * groups + to_row))
        return lax.ppermute(value, ("dist", "rows"), pairs)

    def to_other_core(c, r):
        return c ^ 1, r

    def to_spot(rel):
        return lambda c, r: (c, r ^ rel)

    def to_near_plane(c, r):
        return c, (r // inner ^ 1) * inner + r % inner

    def to_middle(c, r):
        z = r // inner
        return (c, (3 - z) * inner + r % inner) if z in (1, 2) else (c ^ 1, r)

    other_angles = pl.pallas_call(
        lambda place, holo, out: take_kernel(holo, out),
        out_shape=shaped(own, dist_dev, rows_dev, width),
        grid_spec=pltpu.PrefetchScalarGridSpec(
            num_scalar_prefetch=1,
            grid=(1,),
            in_specs=[
                pl.BlockSpec(
                    (own, dist_dev, rows_dev, width), lambda i, place: (place[0] ^ 1, 0, 0, 0)
                )
            ],
            out_specs=one_out,
        ),
        compiler_params=params,
        cost_estimate=cost(0, (2, own, dist_dev, rows_dev, width)),
        name="other_angles",
    )(place, holograms[0])
    partner = sent(other_angles, to_other_core)

    arrived = []
    for chunk in range(own):
        pieces = pl.pallas_call(
            lambda *refs: row_kernel(inner, *refs),
            out_shape=[shaped(dists, rows_dev, block)] * inner,
            grid_spec=pltpu.PrefetchScalarGridSpec(
                num_scalar_prefetch=1,
                grid=(1,),
                in_specs=[
                    pl.BlockSpec(
                        (1, dist_dev, rows_dev, width),
                        lambda i, place, chunk=chunk: (place[0] * own + chunk, 0, 0, 0),
                    ),
                    pl.BlockSpec(
                        (1, dist_dev, rows_dev, width), lambda i, place, chunk=chunk: (chunk, 0, 0, 0)
                    ),
                ]
                + vmem(1),
                out_specs=vmem(inner),
            ),
            compiler_params=params,
            cost_estimate=cost(
                2 * dists * rows_dev * width * width, (width, width), (2, dists, rows_dev, width)
            ),
            name="row_spectra",
        )(place, holograms[0], partner, table)
        arrived.append([pieces[0]] + [sent(pieces[rel], to_spot(rel)) for rel in range(1, inner)])

    index = jnp.arange(width, dtype=jnp.int32)
    my_cols = spot * block + jnp.arange(block, dtype=jnp.int32)
    ordered = jnp.concatenate(
        [
            lax.dynamic_slice_in_dim(propagation, (core ^ other) * dist_dev, dist_dev, 0)
            for other in range(cores)
        ]
    )
    first = ordered[:, None] * signed_square(index, width)[None]
    second = ordered[:, None] * signed_square(my_cols, width)[None]
    sin_b, cos_b = jnp.sin(second), jnp.cos(second)
    gain = pl.pallas_call(
        filter_kernel,
        out_shape=shaped(dists, width, block),
        in_specs=vmem(3),
        out_specs=one_out,
        compiler_params=params,
        cost_estimate=cost(32 * width * block, (dists, width, block)),
        name="filters",
    )(
        jnp.concatenate([jnp.sin(first), jnp.cos(first)], axis=0),
        2.0 * (cos_b - absorb_ratio * sin_b),
        2.0 * (sin_b + absorb_ratio * cos_b),
    )

    sums = []
    for chunk in range(own):
        away, keep = pl.pallas_call(
            lambda *refs: column_kernel(inner, outer, *refs),
            out_shape=[shaped(outer // 2, depth, block)] * 2,
            in_specs=smem(1) + vmem(2 + inner),
            out_specs=vmem(2),
            scratch_shapes=[
                pltpu.VMEM((dists, depth, block), bf16),
                pltpu.VMEM((width, block), f32),
                pltpu.VMEM((width, block), bf16),
            ],
            compiler_params=params,
            cost_estimate=cost(
                2 * width * block * (dists * depth + width), (width, width), (dists, width, block)
            ),
            name="columns",
        )(place, table, gain, *arrived[chunk])
        joint = pl.pallas_call(
            add_kernel,
            out_shape=shaped(outer // 2, depth, block),
            in_specs=vmem(2),
            out_specs=one_out,
            compiler_params=params,
            cost_estimate=cost(outer * depth * block, (3, outer // 2, depth, block)),
            name="joint",
        )(away, sent(away, to_near_plane))
        across = sent(joint, to_middle)
        near = pl.pallas_call(
            near_kernel,
            out_shape=shaped(depth, block),
            in_specs=smem(1) + vmem(2),
            out_specs=one_out,
            compiler_params=params,
            cost_estimate=cost(depth * block, (3, depth, block)),
            name="near",
        )(place, keep, across)
        sums += [keep, across, sent(near, to_near_plane)]

    mine, other = pl.pallas_call(
        lambda *refs: half_kernel(inner, *refs),
        out_shape=[shaped(own, capacity, block)] * 2,
        in_specs=smem(1) + vmem(len(sums)),
        out_specs=vmem(2),
        compiler_params=params,
        cost_estimate=cost(own * depth * block, (5, own, depth, block)),
        name="half",
    )(place, *sums)
    pieces = [mine] + [sent(mine if rel < 2 else other, to_spot(rel)) for rel in range(1, inner)]
    phase = pl.pallas_call(
        lambda *refs: phase_kernel(inner, *refs),
        out_shape=shaped(own, capacity, width),
        in_specs=smem(1) + vmem(1 + inner),
        out_specs=one_out,
        scratch_shapes=[pltpu.VMEM((own * capacity, width), bf16)],
        compiler_params=params,
        cost_estimate=cost(
            2 * own * capacity * width * width, (width, width), (2, own, capacity, width)
        ),
        name="phase",
    )(place, table, *pieces)
    there = sent(phase, to_other_core)

    def angle_of(step, place):
        return (place[0] ^ (step // own)) * own + step % own

    return pl.pallas_call(
        lambda *refs: recon_kernel(own, *refs),
        out_shape=shaped(capacity, pixels),
        grid_spec=pltpu.PrefetchScalarGridSpec(
            num_scalar_prefetch=3,
            grid=(angles,),
            in_specs=[
                pl.BlockSpec(
                    (1, capacity, width), lambda i, place, order, slabs: (jnp.minimum(i, own - 1), 0, 0)
                ),
                pl.BlockSpec(
                    (1, capacity, width), lambda i, place, order, slabs: (jnp.maximum(i - own, 0), 0, 0)
                ),
                pl.BlockSpec(
                    (1, width, pixels),
                    lambda i, place, order, slabs: (order[angle_of(i, place)], 0, 0),
                ),
            ],
            out_specs=one_out,
            scratch_shapes=[pltpu.VMEM((capacity, pixels), f32)],
        ),
        compiler_params=params,
        cost_estimate=cost(
            2 * angles * capacity * width * pixels, (angles, width, capacity + pixels)
        ),
        name="recon",
    )(place, angle_order[0], slab_rows, phase, there, weights)


def on_device(holograms, propagation, weights, angle_order, slab_rows):
    mbatch, angles, dist_dev, rows_dev, width = holograms.shape
    groups = lax.axis_size("rows")
    inner = 2 ** (int(math.log2(groups)) // 2)
    block = width // inner
    fits = (
        inner * (groups // inner) == groups
        and rows_dev % 16 == 0
        and block % 128 == 0
        and inner * rows_dev % 128 == 0
        and inner == 4
        and groups == inner * inner
        and lax.axis_size("dist") == 2
    )
    if fits:
        return plane_plan(inner, holograms, propagation, weights, angle_order, slab_rows)
    return flat_plan(holograms, propagation, weights, angle_order, slab_rows)


def solution(mesh):
    return jax.shard_map(
        on_device,
        mesh=mesh,
        in_specs=(P(None, None, "dist", "rows", None), P(), P(None, None, "dist"), P(), P()),
        out_specs=P("rows", "dist"),
        check_vma=False,
    )
```

```python
import math

import jax
import jax.numpy as jnp
import numpy as np
from jax import lax
from jax.experimental import pallas as pl
from jax.experimental.pallas import tpu as pltpu
from jax.sharding import PartitionSpec as P

absorb_ratio = 0.1
regularizer = 0.05
bf16 = jnp.bfloat16
f32 = jnp.float32


def hartley(length):
    index = np.arange(length)
    turned = (index[:, None] * index[None, :] % length) * (2.0 * math.pi / length)
    table = (np.cos(turned) + np.sin(turned)) / math.sqrt(length)
    return table.astype(bf16)


def signed_square(index, length):
    signed = jnp.where(index < length // 2, index, index - length).astype(f32)
    return signed * signed / float(length * length)


def filters(propagation, rows_sq, cols_sq):
    first = propagation[:, None] * rows_sq[None]
    second = propagation[:, None] * cols_sq[None]
    sin_b, cos_b = jnp.sin(second), jnp.cos(second)
    with_sin = 2.0 * (cos_b - absorb_ratio * sin_b)
    with_cos = 2.0 * (sin_b + absorb_ratio * cos_b)
    transfer = (
        jnp.sin(first)[:, :, None] * with_sin[:, None, :]
        + jnp.cos(first)[:, :, None] * with_cos[:, None, :]
    )
    denom = jnp.sum(transfer * transfer, axis=0) + regularizer
    return transfer / denom


def flat_plan(holograms, propagation, weights, angle_order, slab_rows):
    mbatch, angles, dist_dev, rows_dev, width = holograms.shape
    groups = lax.axis_size("rows")
    cores = lax.axis_size("dist")
    capacity = 2 * rows_dev
    own = angles // cores
    cols = width // groups
    dists = dist_dev * cores
    device = lax.axis_index("rows")
    table = jnp.asarray(hartley(width))
    index = jnp.arange(width, dtype=jnp.int32)
    my_cols = device * cols + jnp.arange(cols, dtype=jnp.int32)
    gain = filters(propagation, signed_square(my_cols, width), signed_square(index, width))

    mine = lax.all_to_all(holograms[0], "dist", split_axis=0, concat_axis=1, tiled=True)
    flat = mine.reshape(own * dists * rows_dev, width)
    spec = jnp.einsum("kx,mx->km", table, flat, preferred_element_type=f32)
    spec = spec.astype(bf16).reshape(groups, cols, own * dists * rows_dev)
    spec = lax.all_to_all(spec, "rows", split_axis=0, concat_axis=0, tiled=True)
    spec = spec.reshape(groups, cols, own, dists, rows_dev).transpose(1, 2, 3, 0, 4)
    spec = spec.reshape(cols * own * dists, width)
    full = jnp.dot(spec, table, preferred_element_type=f32)
    full = full.reshape(cols, own, dists, width)
    full = jnp.sum(full * gain.transpose(1, 0, 2)[:, None], axis=2).astype(bf16)
    half = jnp.einsum("yq,akq->yak", table, full.transpose(1, 0, 2), preferred_element_type=f32)
    half = half.astype(bf16).reshape(groups, rows_dev, own * cols)
    half = lax.all_to_all(half, "rows", split_axis=0, concat_axis=0, tiled=True)
    half = half.reshape(groups, rows_dev, own, cols).transpose(2, 1, 0, 3)
    half = half.reshape(own * rows_dev, width)
    phase = jnp.dot(half, table, preferred_element_type=f32)
    phase = phase.astype(bf16).reshape(own, rows_dev, width)
    phase = lax.all_gather(phase, "dist", axis=0, tiled=True)
    place = (angle_order[0][None, :] == jnp.arange(angles)[:, None]).astype(bf16)
    phase = jnp.einsum("wa,ayx->wyx", place, phase, preferred_element_type=f32)
    recon = jnp.einsum(
        "wyx,wxp->yp", phase.astype(bf16), weights, preferred_element_type=f32
    ).astype(bf16)
    parity = device % 2
    offset = parity * slab_rows[device - parity]
    count = slab_rows[device]
    pairs = [(source, source ^ 1) for source in range(groups)]
    partner = lax.ppermute(recon, "rows", pairs)
    lower = jnp.where(parity == 1, partner, recon)
    upper = jnp.where(parity == 1, recon, partner)
    paired = jnp.concatenate([lower, upper], axis=0)
    slot = jnp.arange(capacity, dtype=jnp.int32)[:, None]
    source = jnp.arange(capacity, dtype=jnp.int32)[None, :]
    select = ((source == offset + slot) & (slot < count)).astype(bf16)
    return jnp.dot(select, paired, preferred_element_type=f32).astype(bf16)


def row_kernel(inner, own, chunk, place, here, there, table, after, *outs):
    core, spot = place[0], place[1]
    dist_dev, rows_dev, width = here.shape[1:]
    block = width // inner
    angle = core * own + chunk
    flat = jnp.concatenate(
        [source[angle].reshape(dist_dev * rows_dev, width) for source in (here, there)], axis=0
    )
    for rel in range(inner):
        part = table[:, pl.ds(pl.multiple_of((spot ^ rel) * block, block), block)]
        got = jnp.dot(flat, part, preferred_element_type=f32).astype(bf16)
        outs[rel][...] = got.reshape(2 * dist_dev, rows_dev, block)


def filter_kernel(waves_a, with_sin, with_cos, out):
    dists, width, block = out.shape
    turned = waves_a[...].T
    step = 128
    for at in range(0, width, step):
        rows = turned[at : at + step]
        transfer = [
            rows[:, d : d + 1] * with_sin[d : d + 1, :]
            + rows[:, dists + d : dists + d + 1] * with_cos[d : d + 1, :]
            for d in range(dists)
        ]
        denom = transfer[0] * transfer[0]
        for value in transfer[1:]:
            denom = denom + value * value
        scale = 1.0 / (denom + regularizer)
        for d in range(dists):
            out[d, at : at + step, :] = (transfer[d] * scale).astype(bf16)


def column_kernel(inner, outer, place, table, gain, *refs):
    pieces = refs[:inner]
    away, keep, stack, total, spectrum = refs[inner:]
    spot, plane = place[1], place[2]
    dists, rows_dev, block = pieces[0].shape
    depth = inner * rows_dev
    for rel in range(inner):
        start = pl.multiple_of((spot ^ rel) * rows_dev, rows_dev)
        for d in range(dists):
            stack[d, pl.ds(start, rows_dev), :] = pieces[rel][d]
    part = table[:, pl.ds(pl.multiple_of(plane * depth, depth), depth)]
    for d in range(dists):
        got = jnp.dot(part, stack[d], preferred_element_type=f32) * gain[d].astype(f32)
        if d == 0:
            total[...] = got
        else:
            total[...] += got
    spectrum[...] = total[...].astype(bf16)
    half = outer // 2
    side = plane // half
    for out, first in ((away, (1 - side) * half), (keep, side * half)):
        rows = pl.ds(pl.multiple_of(first * depth, half * depth), half * depth)
        got = jnp.dot(table[rows, :], spectrum[...], preferred_element_type=f32)
        out[...] = got.astype(bf16).reshape(half, depth, block)


def add_kernel(one, two, out):
    out[...] = (one[...].astype(f32) + two[...].astype(f32)).astype(bf16)


def near_kernel(place, keep, across, out):
    plane = place[2]
    which = (plane ^ 1) % 2
    inside = (plane == 1) | (plane == 2)
    more = jnp.where(inside, across[which].astype(f32), 0.0)
    out[...] = (keep[which].astype(f32) + more).astype(bf16)


def half_kernel(place, keep, across, last, after, mine, other):
    spot, plane = place[1], place[2]
    which = plane % 2
    inside = (plane == 1) | (plane == 2)
    capacity = mine.shape[0]
    for out, pair in ((mine, spot // 2), (other, 1 - spot // 2)):
        rows = pl.ds(pl.multiple_of(pair * capacity, capacity), capacity)
        more = jnp.where(inside, across[which, rows, :].astype(f32), 0.0)
        got = keep[which, rows, :].astype(f32) + more + last[rows, :].astype(f32)
        out[...] = got.astype(bf16)


def phase_kernel(inner, place, table, *refs):
    pieces = refs[:inner]
    out, joined = refs[-2:]
    spot = place[1]
    block = pieces[0].shape[1]
    for rel in range(inner):
        columns = pl.ds(pl.multiple_of((spot ^ rel) * block, block), block)
        joined[:, columns] = pieces[rel][...]
    out[...] = jnp.dot(joined[...], table[...], preferred_element_type=f32).astype(bf16)


def recon_kernel(place, order, phase, weights, out):
    out[...] = jnp.dot(phase[...], weights[0], preferred_element_type=f32)


def recon_more_kernel(place, order, phase, weights, before, out):
    out[...] = before[...] + jnp.dot(phase[...], weights[0], preferred_element_type=f32)


def recon_last_kernel(place, order, slabs, phase, weights, before, out):
    total = before[...] + jnp.dot(phase[...], weights[0], preferred_element_type=f32)
    capacity = total.shape[0]
    device = place[3]
    parity = device % 2
    offset = parity * slabs[device - parity]
    slot = lax.broadcasted_iota(jnp.int32, (capacity, capacity), 0)
    source = lax.broadcasted_iota(jnp.int32, (capacity, capacity), 1)
    select = (source == slot + offset) & (slot < slabs[device])
    select = jnp.where(select, 1.0, 0.0).astype(bf16)
    picked = jnp.dot(select, total.astype(bf16), preferred_element_type=f32)
    out[...] = picked.astype(bf16)


def vmem(count):
    return [pl.BlockSpec(memory_space=pltpu.VMEM)] * count


def unread(count):
    return [pl.BlockSpec(memory_space=pl.ANY)] * count


def smem(count):
    return [pl.BlockSpec(memory_space=pltpu.SMEM)] * count


def plane_plan(inner, holograms, propagation, weights, angle_order, slab_rows):
    mbatch, angles, dist_dev, rows_dev, width = holograms.shape
    groups = lax.axis_size("rows")
    cores = lax.axis_size("dist")
    outer = groups // inner
    own = angles // cores
    block = width // inner
    depth = inner * rows_dev
    dists = cores * dist_dev
    pixels = weights.shape[2]
    capacity = 2 * rows_dev
    params = pltpu.CompilerParams(vmem_limit_bytes=16 * 2**20)
    one_out = pl.BlockSpec(memory_space=pltpu.VMEM)

    def cost(flops, *arrays):
        return pl.CostEstimate(
            flops=flops, bytes_accessed=sum(2 * math.prod(a) for a in arrays), transcendentals=0
        )

    def shaped(*shape):
        return jax.ShapeDtypeStruct(shape, bf16)

    device = lax.axis_index("rows")
    core = lax.axis_index("dist")
    plane, spot = device // inner, device % inner
    place = jnp.stack([core, spot, plane, device]).astype(jnp.int32)
    table = jnp.asarray(hartley(width))

    def sent(value, target):
        pairs = []
        for c in range(cores):
            for r in range(groups):
                to_core, to_row = target(c, r)
                pairs.append((c * groups + r, to_core * groups + to_row))
        return lax.ppermute(value, ("dist", "rows"), pairs)

    def to_other_core(c, r):
        return c ^ 1, r

    def to_spot(rel):
        return lambda c, r: (c, r ^ rel)

    def to_near_plane(c, r):
        return c, (r // inner ^ 1) * inner + r % inner

    def to_middle(c, r):
        z = r // inner
        return (c, (3 - z) * inner + r % inner) if z in (1, 2) else (c ^ 1, r)

    index = jnp.arange(width, dtype=jnp.int32)
    my_cols = spot * block + jnp.arange(block, dtype=jnp.int32)
    ordered = jnp.concatenate(
        [
            lax.dynamic_slice_in_dim(propagation, (core ^ other) * dist_dev, dist_dev, 0)
            for other in range(cores)
        ]
    )
    first = ordered[:, None] * signed_square(index, width)[None]
    second = ordered[:, None] * signed_square(my_cols, width)[None]
    sin_b, cos_b = jnp.sin(second), jnp.cos(second)
    gain = pl.pallas_call(
        filter_kernel,
        out_shape=shaped(dists, width, block),
        in_specs=vmem(3),
        out_specs=one_out,
        compiler_params=params,
        cost_estimate=cost(32 * width * block, (dists, width, block)),
        name="filters",
    )(
        jnp.concatenate([jnp.sin(first), jnp.cos(first)], axis=0),
        2.0 * (cos_b - absorb_ratio * sin_b),
        2.0 * (sin_b + absorb_ratio * cos_b),
    )

    partner = sent(holograms[0], to_other_core)
    arrived = []
    for chunk in range(own):
        pieces = pl.pallas_call(
            lambda *refs, chunk=chunk: row_kernel(inner, own, chunk, *refs),
            out_shape=[shaped(dists, rows_dev, block)] * inner,
            in_specs=smem(1) + vmem(3) + unread(1),
            out_specs=vmem(inner),
            compiler_params=params,
            cost_estimate=cost(
                2 * dists * rows_dev * width * width, (width, width), (2, dists, rows_dev, width)
            ),
            name="row_spectra",
        )(place, holograms[0], partner, table, gain)
        arrived.append([pieces[0]] + [sent(pieces[rel], to_spot(rel)) for rel in range(1, inner)])

    sums = []
    for chunk in range(own):
        away, keep = pl.pallas_call(
            lambda *refs: column_kernel(inner, outer, *refs),
            out_shape=[shaped(outer // 2, depth, block)] * 2,
            in_specs=smem(1) + vmem(2 + inner),
            out_specs=vmem(2),
            scratch_shapes=[
                pltpu.VMEM((dists, depth, block), bf16),
                pltpu.VMEM((width, block), f32),
                pltpu.VMEM((width, block), bf16),
            ],
            compiler_params=params,
            cost_estimate=cost(
                2 * width * block * (dists * depth + width), (width, width), (dists, width, block)
            ),
            name="columns",
        )(place, table, gain, *arrived[chunk])
        joint = pl.pallas_call(
            add_kernel,
            out_shape=shaped(outer // 2, depth, block),
            in_specs=vmem(2),
            out_specs=one_out,
            compiler_params=params,
            cost_estimate=cost(outer * depth * block, (3, outer // 2, depth, block)),
            name="joint",
        )(away, sent(away, to_near_plane))
        across = sent(joint, to_middle)
        near = pl.pallas_call(
            near_kernel,
            out_shape=shaped(depth, block),
            in_specs=smem(1) + vmem(2),
            out_specs=one_out,
            compiler_params=params,
            cost_estimate=cost(depth * block, (3, depth, block)),
            name="near",
        )(place, keep, across)
        sums.append((keep, across, sent(near, to_near_plane)))

    def recon(kernel, out_type, other, chunk, scalars, phase, *before):
        def angle(place):
            return (place[0] ^ other) * own + chunk

        return pl.pallas_call(
            kernel,
            out_shape=jax.ShapeDtypeStruct((capacity, pixels), out_type),
            grid_spec=pltpu.PrefetchScalarGridSpec(
                num_scalar_prefetch=len(scalars),
                grid=(1,),
                in_specs=vmem(1)
                + [
                    pl.BlockSpec(
                        (1, width, pixels),
                        lambda i, place, order, *slabs: (order[angle(place)], 0, 0),
                    )
                ]
                + vmem(len(before)),
                out_specs=one_out,
            ),
            compiler_params=params,
            cost_estimate=cost(2 * capacity * width * pixels, (width, capacity + pixels)),
            name="recon",
        )(*scalars, phase, weights, *before)

    total = None
    scalars = (place, angle_order[0])
    for chunk in range(own):
        mine, other = pl.pallas_call(
            half_kernel,
            out_shape=[shaped(capacity, block)] * 2,
            in_specs=smem(1) + vmem(3) + unread(1),
            out_specs=vmem(2),
            compiler_params=params,
            cost_estimate=cost(depth * block, (5, depth, block)),
            name="half",
        )(place, *sums[chunk], near)
        pieces = [mine] + [sent(mine if rel < 2 else other, to_spot(rel)) for rel in range(1, inner)]
        phase = pl.pallas_call(
            lambda *refs: phase_kernel(inner, *refs),
            out_shape=shaped(capacity, width),
            in_specs=smem(1) + vmem(1 + inner) + unread(0 if total is None else 1),
            out_specs=one_out,
            scratch_shapes=[pltpu.VMEM((capacity, width), bf16)],
            compiler_params=params,
            cost_estimate=cost(2 * capacity * width * width, (width, width), (2, capacity, width)),
            name="phase",
        )(place, table, *pieces, *([] if total is None else [total]))
        there = sent(phase, to_other_core)
        if total is None:
            total = recon(recon_kernel, f32, 0, chunk, scalars, phase)
        else:
            total = recon(recon_more_kernel, f32, 0, chunk, scalars, phase, total)
        if chunk < own - 1:
            total = recon(recon_more_kernel, f32, 1, chunk, scalars, there, total)
        else:
            total = recon(recon_last_kernel, bf16, 1, chunk, scalars + (slab_rows,), there, total)
    return total


def on_device(holograms, propagation, weights, angle_order, slab_rows):
    mbatch, angles, dist_dev, rows_dev, width = holograms.shape
    groups = lax.axis_size("rows")
    inner = 2 ** (int(math.log2(groups)) // 2)
    block = width // inner
    fits = (
        inner * (groups // inner) == groups
        and rows_dev % 16 == 0
        and block % 128 == 0
        and inner * rows_dev % 128 == 0
        and inner == 4
        and groups == inner * inner
        and lax.axis_size("dist") == 2
    )
    if fits:
        return plane_plan(inner, holograms, propagation, weights, angle_order, slab_rows)
    return flat_plan(holograms, propagation, weights, angle_order, slab_rows)


def solution(mesh):
    return jax.shard_map(
        on_device,
        mesh=mesh,
        in_specs=(P(None, None, "dist", "rows", None), P(), P(None, None, "dist"), P(), P()),
        out_specs=P("rows", "dist"),
        check_vma=False,
    )
```

```python
import math

import jax
import jax.numpy as jnp
import numpy as np
from jax import lax
from jax.experimental import pallas as pl
from jax.experimental.pallas import tpu as pltpu
from jax.sharding import PartitionSpec as P

absorb_ratio = 0.1
regularizer = 0.05
bf16 = jnp.bfloat16
f32 = jnp.float32


def hartley(length):
    index = np.arange(length)
    turned = (index[:, None] * index[None, :] % length) * (2.0 * math.pi / length)
    table = (np.cos(turned) + np.sin(turned)) / math.sqrt(length)
    return table.astype(bf16)


def signed_square(index, length):
    signed = jnp.where(index < length // 2, index, index - length).astype(f32)
    return signed * signed / float(length * length)


def filters(propagation, rows_sq, cols_sq):
    first = propagation[:, None] * rows_sq[None]
    second = propagation[:, None] * cols_sq[None]
    sin_b, cos_b = jnp.sin(second), jnp.cos(second)
    with_sin = 2.0 * (cos_b - absorb_ratio * sin_b)
    with_cos = 2.0 * (sin_b + absorb_ratio * cos_b)
    transfer = (
        jnp.sin(first)[:, :, None] * with_sin[:, None, :]
        + jnp.cos(first)[:, :, None] * with_cos[:, None, :]
    )
    denom = jnp.sum(transfer * transfer, axis=0) + regularizer
    return transfer / denom


def flat_plan(holograms, propagation, weights, angle_order, slab_rows):
    mbatch, angles, dist_dev, rows_dev, width = holograms.shape
    groups = lax.axis_size("rows")
    cores = lax.axis_size("dist")
    capacity = 2 * rows_dev
    own = angles // cores
    cols = width // groups
    dists = dist_dev * cores
    device = lax.axis_index("rows")
    table = jnp.asarray(hartley(width))
    index = jnp.arange(width, dtype=jnp.int32)
    my_cols = device * cols + jnp.arange(cols, dtype=jnp.int32)
    gain = filters(propagation, signed_square(my_cols, width), signed_square(index, width))

    mine = lax.all_to_all(holograms[0], "dist", split_axis=0, concat_axis=1, tiled=True)
    flat = mine.reshape(own * dists * rows_dev, width)
    spec = jnp.einsum("kx,mx->km", table, flat, preferred_element_type=f32)
    spec = spec.astype(bf16).reshape(groups, cols, own * dists * rows_dev)
    spec = lax.all_to_all(spec, "rows", split_axis=0, concat_axis=0, tiled=True)
    spec = spec.reshape(groups, cols, own, dists, rows_dev).transpose(1, 2, 3, 0, 4)
    spec = spec.reshape(cols * own * dists, width)
    full = jnp.dot(spec, table, preferred_element_type=f32)
    full = full.reshape(cols, own, dists, width)
    full = jnp.sum(full * gain.transpose(1, 0, 2)[:, None], axis=2).astype(bf16)
    half = jnp.einsum("yq,akq->yak", table, full.transpose(1, 0, 2), preferred_element_type=f32)
    half = half.astype(bf16).reshape(groups, rows_dev, own * cols)
    half = lax.all_to_all(half, "rows", split_axis=0, concat_axis=0, tiled=True)
    half = half.reshape(groups, rows_dev, own, cols).transpose(2, 1, 0, 3)
    half = half.reshape(own * rows_dev, width)
    phase = jnp.dot(half, table, preferred_element_type=f32)
    phase = phase.astype(bf16).reshape(own, rows_dev, width)
    phase = lax.all_gather(phase, "dist", axis=0, tiled=True)
    place = (angle_order[0][None, :] == jnp.arange(angles)[:, None]).astype(bf16)
    phase = jnp.einsum("wa,ayx->wyx", place, phase, preferred_element_type=f32)
    recon = jnp.einsum(
        "wyx,wxp->yp", phase.astype(bf16), weights, preferred_element_type=f32
    ).astype(bf16)
    parity = device % 2
    offset = parity * slab_rows[device - parity]
    count = slab_rows[device]
    pairs = [(source, source ^ 1) for source in range(groups)]
    partner = lax.ppermute(recon, "rows", pairs)
    lower = jnp.where(parity == 1, partner, recon)
    upper = jnp.where(parity == 1, recon, partner)
    paired = jnp.concatenate([lower, upper], axis=0)
    slot = jnp.arange(capacity, dtype=jnp.int32)[:, None]
    source = jnp.arange(capacity, dtype=jnp.int32)[None, :]
    select = ((source == offset + slot) & (slot < count)).astype(bf16)
    return jnp.dot(select, paired, preferred_element_type=f32).astype(bf16)


def row_kernel(inner, place, here, there, table, after, *outs):
    spot = place[1]
    dist_dev, rows_dev, width = here.shape[1:]
    block = width // inner
    flat = jnp.concatenate(
        [source[0].reshape(dist_dev * rows_dev, width) for source in (here, there)], axis=0
    )
    for rel in range(inner):
        part = table[:, pl.ds(pl.multiple_of((spot ^ rel) * block, block), block)]
        got = jnp.dot(flat, part, preferred_element_type=f32).astype(bf16)
        outs[rel][...] = got.reshape(2 * dist_dev, rows_dev, block)


def filter_kernel(waves_a, with_sin, with_cos, out):
    dists, width, block = out.shape
    turned = waves_a[...].T
    step = 128
    for at in range(0, width, step):
        rows = turned[at : at + step]
        transfer = [
            rows[:, d : d + 1] * with_sin[d : d + 1, :]
            + rows[:, dists + d : dists + d + 1] * with_cos[d : d + 1, :]
            for d in range(dists)
        ]
        denom = transfer[0] * transfer[0]
        for value in transfer[1:]:
            denom = denom + value * value
        scale = 1.0 / (denom + regularizer)
        for d in range(dists):
            out[d, at : at + step, :] = (transfer[d] * scale).astype(bf16)


def column_kernel(inner, outer, place, table, gain, *refs):
    pieces = refs[:inner]
    away, keep, stack, total, spectrum = refs[inner:]
    spot, plane = place[1], place[2]
    dists, rows_dev, block = pieces[0].shape
    depth = inner * rows_dev
    for rel in range(inner):
        start = pl.multiple_of((spot ^ rel) * rows_dev, rows_dev)
        for d in range(dists):
            stack[d, pl.ds(start, rows_dev), :] = pieces[rel][d]
    part = table[:, pl.ds(pl.multiple_of(plane * depth, depth), depth)]
    for d in range(dists):
        got = jnp.dot(part, stack[d], preferred_element_type=f32) * gain[d].astype(f32)
        if d == 0:
            total[...] = got
        else:
            total[...] += got
    spectrum[...] = total[...].astype(bf16)
    half = outer // 2
    side = plane // half
    for out, first in ((away, (1 - side) * half), (keep, side * half)):
        rows = pl.ds(pl.multiple_of(first * depth, half * depth), half * depth)
        got = jnp.dot(table[rows, :], spectrum[...], preferred_element_type=f32)
        out[...] = got.astype(bf16).reshape(half, depth, block)


def add_kernel(one, two, out):
    out[...] = (one[...].astype(f32) + two[...].astype(f32)).astype(bf16)


def near_kernel(place, keep, across, out):
    plane = place[2]
    which = (plane ^ 1) % 2
    inside = (plane == 1) | (plane == 2)
    more = jnp.where(inside, across[which].astype(f32), 0.0)
    out[...] = (keep[which].astype(f32) + more).astype(bf16)


def half_kernel(place, keep, across, last, after, mine, other):
    spot, plane = place[1], place[2]
    which = plane % 2
    inside = (plane == 1) | (plane == 2)
    capacity = mine.shape[0]
    for out, pair in ((mine, spot // 2), (other, 1 - spot // 2)):
        rows = pl.ds(pl.multiple_of(pair * capacity, capacity), capacity)
        more = jnp.where(inside, across[which, rows, :].astype(f32), 0.0)
        got = keep[which, rows, :].astype(f32) + more + last[rows, :].astype(f32)
        out[...] = got.astype(bf16)


def phase_kernel(inner, place, table, *refs):
    pieces = refs[:inner]
    out, joined = refs[-2:]
    spot = place[1]
    block = pieces[0].shape[1]
    for rel in range(inner):
        columns = pl.ds(pl.multiple_of((spot ^ rel) * block, block), block)
        joined[:, columns] = pieces[rel][...]
    out[...] = jnp.dot(joined[...], table[...], preferred_element_type=f32).astype(bf16)


def recon_kernel(own, chunk, cores, place, order, weights, *refs):
    phases, out = refs[: len(cores)], refs[-1]
    total = refs[-2][...] if len(refs) > len(cores) + 1 else None
    for other, phase in zip(cores, phases):
        chosen = weights[order[0, (place[0] ^ other) * own + chunk]]
        got = jnp.dot(phase[...], chosen, preferred_element_type=f32)
        total = got if total is None else total + got
    out[...] = total


def recon_last_kernel(own, chunk, other, place, order, slabs, weights, phase, before, out):
    chosen = weights[order[0, (place[0] ^ other) * own + chunk]]
    total = before[...] + jnp.dot(phase[...], chosen, preferred_element_type=f32)
    capacity = total.shape[0]
    device = place[3]
    parity = device % 2
    offset = parity * slabs[device - parity]
    turned = pltpu.roll(total, lax.rem(capacity - offset, capacity), 0)
    slot = lax.broadcasted_iota(jnp.int32, turned.shape, 0)
    out[...] = jnp.where(slot < slabs[device], turned, 0.0).astype(bf16)


def vmem(count):
    return [pl.BlockSpec(memory_space=pltpu.VMEM)] * count


def unread(count):
    return [pl.BlockSpec(memory_space=pl.ANY)] * count


def smem(count):
    return [pl.BlockSpec(memory_space=pltpu.SMEM)] * count


def plane_plan(inner, holograms, propagation, weights, angle_order, slab_rows):
    mbatch, angles, dist_dev, rows_dev, width = holograms.shape
    groups = lax.axis_size("rows")
    cores = lax.axis_size("dist")
    outer = groups // inner
    own = angles // cores
    block = width // inner
    depth = inner * rows_dev
    dists = cores * dist_dev
    pixels = weights.shape[2]
    capacity = 2 * rows_dev
    params = pltpu.CompilerParams(vmem_limit_bytes=16 * 2**20)
    one_out = pl.BlockSpec(memory_space=pltpu.VMEM)

    def cost(flops, *arrays):
        return pl.CostEstimate(
            flops=flops, bytes_accessed=sum(2 * math.prod(a) for a in arrays), transcendentals=0
        )

    def shaped(*shape):
        return jax.ShapeDtypeStruct(shape, bf16)

    device = lax.axis_index("rows")
    core = lax.axis_index("dist")
    plane, spot = device // inner, device % inner
    place = jnp.stack([core, spot, plane, device]).astype(jnp.int32)
    table = jnp.asarray(hartley(width))

    def sent(value, target):
        pairs = []
        for c in range(cores):
            for r in range(groups):
                to_core, to_row = target(c, r)
                pairs.append((c * groups + r, to_core * groups + to_row))
        return lax.ppermute(value, ("dist", "rows"), pairs)

    def to_other_core(c, r):
        return c ^ 1, r

    def to_spot(rel):
        return lambda c, r: (c, r ^ rel)

    def spread(pieces):
        got = {rel: sent(pieces[rel], to_spot(rel)) for rel in (2, 3, 1)}
        return [pieces[0]] + [got[rel] for rel in range(1, inner)]

    def to_near_plane(c, r):
        return c, (r // inner ^ 1) * inner + r % inner

    def to_middle(c, r):
        z = r // inner
        return (c, (3 - z) * inner + r % inner) if z in (1, 2) else (c ^ 1, r)

    index = jnp.arange(width, dtype=jnp.int32)
    my_cols = spot * block + jnp.arange(block, dtype=jnp.int32)
    ordered = jnp.concatenate(
        [
            lax.dynamic_slice_in_dim(propagation, (core ^ other) * dist_dev, dist_dev, 0)
            for other in range(cores)
        ]
    )
    first = ordered[:, None] * signed_square(index, width)[None]
    second = ordered[:, None] * signed_square(my_cols, width)[None]
    sin_b, cos_b = jnp.sin(second), jnp.cos(second)
    gain = pl.pallas_call(
        filter_kernel,
        out_shape=shaped(dists, width, block),
        in_specs=vmem(3),
        out_specs=one_out,
        compiler_params=params,
        cost_estimate=cost(32 * width * block, (dists, width, block)),
        name="filters",
    )(
        jnp.concatenate([jnp.sin(first), jnp.cos(first)], axis=0),
        2.0 * (cos_b - absorb_ratio * sin_b),
        2.0 * (sin_b + absorb_ratio * cos_b),
    )

    partner = sent(holograms[0], to_other_core)
    arrived = []
    for chunk in range(own):
        pieces = pl.pallas_call(
            lambda *refs: row_kernel(inner, *refs),
            out_shape=[shaped(dists, rows_dev, block)] * inner,
            grid_spec=pltpu.PrefetchScalarGridSpec(
                num_scalar_prefetch=1,
                grid=(1,),
                in_specs=[
                    pl.BlockSpec(
                        (1, dist_dev, rows_dev, width),
                        lambda i, place, chunk=chunk: (place[0] * own + chunk, 0, 0, 0),
                    )
                ]
                * 2
                + vmem(1)
                + unread(1),
                out_specs=vmem(inner),
            ),
            compiler_params=params,
            cost_estimate=cost(
                2 * dists * rows_dev * width * width, (width, width), (2, dists, rows_dev, width)
            ),
            name="row_spectra",
        )(place, holograms[0], partner, table, gain)
        arrived.append(spread(pieces))

    sums = []
    for chunk in range(own):
        away, keep = pl.pallas_call(
            lambda *refs: column_kernel(inner, outer, *refs),
            out_shape=[shaped(outer // 2, depth, block)] * 2,
            in_specs=smem(1) + vmem(2 + inner),
            out_specs=vmem(2),
            scratch_shapes=[
                pltpu.VMEM((dists, depth, block), bf16),
                pltpu.VMEM((width, block), f32),
                pltpu.VMEM((width, block), bf16),
            ],
            compiler_params=params,
            cost_estimate=cost(
                2 * width * block * (dists * depth + width), (width, width), (dists, width, block)
            ),
            name="columns",
        )(place, table, gain, *arrived[chunk])
        joint = pl.pallas_call(
            add_kernel,
            out_shape=shaped(outer // 2, depth, block),
            in_specs=vmem(2),
            out_specs=one_out,
            compiler_params=params,
            cost_estimate=cost(outer * depth * block, (3, outer // 2, depth, block)),
            name="joint",
        )(away, sent(away, to_near_plane))
        across = sent(joint, to_middle)
        near = pl.pallas_call(
            near_kernel,
            out_shape=shaped(depth, block),
            in_specs=smem(1) + vmem(2),
            out_specs=one_out,
            compiler_params=params,
            cost_estimate=cost(depth * block, (3, depth, block)),
            name="near",
        )(place, keep, across)
        sums.append((keep, across, sent(near, to_near_plane)))

    def recon(kernel, out_type, scalars, *arrays):
        return pl.pallas_call(
            kernel,
            out_shape=jax.ShapeDtypeStruct((capacity, pixels), out_type),
            in_specs=smem(len(scalars)) + vmem(1 + len(arrays)),
            out_specs=one_out,
            compiler_params=params,
            cost_estimate=cost(1, (8, pixels)),
            name="recon",
        )(*scalars, weights, *arrays)

    total = None
    scalars = (place, angle_order)
    for chunk in range(own):
        mine, other = pl.pallas_call(
            half_kernel,
            out_shape=[shaped(capacity, block)] * 2,
            in_specs=smem(1) + vmem(3) + unread(1),
            out_specs=vmem(2),
            compiler_params=params,
            cost_estimate=cost(1, (8, width)),
            name="half",
        )(place, *sums[chunk], near)
        pieces = spread([mine, mine, other, other])
        phase = pl.pallas_call(
            lambda *refs: phase_kernel(inner, *refs),
            out_shape=shaped(capacity, width),
            in_specs=smem(1) + vmem(1 + inner),
            out_specs=one_out,
            scratch_shapes=[pltpu.VMEM((capacity, width), bf16)],
            compiler_params=params,
            cost_estimate=cost(1, (8, width)),
            name="phase",
        )(place, table, *pieces)
        there = sent(phase, to_other_core)
        def part(cores, chunk=chunk):
            return lambda *refs: recon_kernel(own, chunk, cores, *refs)

        before = [] if total is None else [total]
        if chunk < own - 1:
            total = recon(part((0, 1)), f32, scalars, phase, there, *before)
        else:
            total = recon(part((0,)), f32, scalars, phase, *before)
            total = recon(
                lambda *refs, chunk=chunk: recon_last_kernel(own, chunk, 1, *refs),
                bf16,
                scalars + (slab_rows,),
                there,
                total,
            )
    return total


def on_device(holograms, propagation, weights, angle_order, slab_rows):
    mbatch, angles, dist_dev, rows_dev, width = holograms.shape
    groups = lax.axis_size("rows")
    inner = 2 ** (int(math.log2(groups)) // 2)
    block = width // inner
    fits = (
        inner * (groups // inner) == groups
        and rows_dev % 16 == 0
        and block % 128 == 0
        and inner * rows_dev % 128 == 0
        and inner == 4
        and groups == inner * inner
        and lax.axis_size("dist") == 2
    )
    if fits:
        return plane_plan(inner, holograms, propagation, weights, angle_order, slab_rows)
    return flat_plan(holograms, propagation, weights, angle_order, slab_rows)


def solution(mesh):
    return jax.shard_map(
        on_device,
        mesh=mesh,
        in_specs=(P(None, None, "dist", "rows", None), P(), P(None, None, "dist"), P(), P()),
        out_specs=P("rows", "dist"),
        check_vma=False,
    )
```

```python
import math

import jax
import jax.numpy as jnp
import numpy as np
from jax import lax
from jax.experimental import pallas as pl
from jax.experimental.pallas import tpu as pltpu
from jax.sharding import PartitionSpec as P

absorb_ratio = 0.1
regularizer = 0.05
bf16 = jnp.bfloat16
f32 = jnp.float32
send_order = (0, 2, 3, 1)
tail_order = (0, 1, 3, 2)


def hartley(length):
    index = np.arange(length)
    turned = (index[:, None] * index[None, :] % length) * (2.0 * math.pi / length)
    table = (np.cos(turned) + np.sin(turned)) / math.sqrt(length)
    return table.astype(bf16)


def signed_square(index, length):
    signed = jnp.where(index < length // 2, index, index - length).astype(f32)
    return signed * signed / float(length * length)


def filters(propagation, rows_sq, cols_sq):
    first = propagation[:, None] * rows_sq[None]
    second = propagation[:, None] * cols_sq[None]
    sin_b, cos_b = jnp.sin(second), jnp.cos(second)
    with_sin = 2.0 * (cos_b - absorb_ratio * sin_b)
    with_cos = 2.0 * (sin_b + absorb_ratio * cos_b)
    transfer = (
        jnp.sin(first)[:, :, None] * with_sin[:, None, :]
        + jnp.cos(first)[:, :, None] * with_cos[:, None, :]
    )
    denom = jnp.sum(transfer * transfer, axis=0) + regularizer
    return transfer / denom


def flat_plan(holograms, propagation, weights, angle_order, slab_rows):
    mbatch, angles, dist_dev, rows_dev, width = holograms.shape
    groups = lax.axis_size("rows")
    cores = lax.axis_size("dist")
    capacity = 2 * rows_dev
    own = angles // cores
    cols = width // groups
    dists = dist_dev * cores
    device = lax.axis_index("rows")
    table = jnp.asarray(hartley(width))
    index = jnp.arange(width, dtype=jnp.int32)
    my_cols = device * cols + jnp.arange(cols, dtype=jnp.int32)
    gain = filters(propagation, signed_square(my_cols, width), signed_square(index, width))

    mine = lax.all_to_all(holograms[0], "dist", split_axis=0, concat_axis=1, tiled=True)
    flat = mine.reshape(own * dists * rows_dev, width)
    spec = jnp.einsum("kx,mx->km", table, flat, preferred_element_type=f32)
    spec = spec.astype(bf16).reshape(groups, cols, own * dists * rows_dev)
    spec = lax.all_to_all(spec, "rows", split_axis=0, concat_axis=0, tiled=True)
    spec = spec.reshape(groups, cols, own, dists, rows_dev).transpose(1, 2, 3, 0, 4)
    spec = spec.reshape(cols * own * dists, width)
    full = jnp.dot(spec, table, preferred_element_type=f32)
    full = full.reshape(cols, own, dists, width)
    full = jnp.sum(full * gain.transpose(1, 0, 2)[:, None], axis=2).astype(bf16)
    half = jnp.einsum("yq,akq->yak", table, full.transpose(1, 0, 2), preferred_element_type=f32)
    half = half.astype(bf16).reshape(groups, rows_dev, own * cols)
    half = lax.all_to_all(half, "rows", split_axis=0, concat_axis=0, tiled=True)
    half = half.reshape(groups, rows_dev, own, cols).transpose(2, 1, 0, 3)
    half = half.reshape(own * rows_dev, width)
    phase = jnp.dot(half, table, preferred_element_type=f32)
    phase = phase.astype(bf16).reshape(own, rows_dev, width)
    phase = lax.all_gather(phase, "dist", axis=0, tiled=True)
    place = (angle_order[0][None, :] == jnp.arange(angles)[:, None]).astype(bf16)
    phase = jnp.einsum("wa,ayx->wyx", place, phase, preferred_element_type=f32)
    recon = jnp.einsum(
        "wyx,wxp->yp", phase.astype(bf16), weights, preferred_element_type=f32
    ).astype(bf16)
    parity = device % 2
    offset = parity * slab_rows[device - parity]
    count = slab_rows[device]
    pairs = [(source, source ^ 1) for source in range(groups)]
    partner = lax.ppermute(recon, "rows", pairs)
    lower = jnp.where(parity == 1, partner, recon)
    upper = jnp.where(parity == 1, recon, partner)
    paired = jnp.concatenate([lower, upper], axis=0)
    slot = jnp.arange(capacity, dtype=jnp.int32)[:, None]
    source = jnp.arange(capacity, dtype=jnp.int32)[None, :]
    select = ((source == offset + slot) & (slot < count)).astype(bf16)
    return jnp.dot(select, paired, preferred_element_type=f32).astype(bf16)


def position(inner):
    device = lax.axis_index("rows")
    return lax.axis_index("dist"), device // inner, device % inner


def row_kernel(inner, chunk, here, there, table, after, *outs):
    core, _, spot = position(inner)
    own, dist_dev, rows_dev, width = here.shape
    block = width // inner
    partner = there[core * own + chunk]
    flat = jnp.concatenate(
        [source.reshape(dist_dev * rows_dev, width) for source in (here[chunk], partner)], axis=0
    )
    for rel in range(inner):
        part = table[:, pl.ds(pl.multiple_of((spot ^ rel) * block, block), block)]
        got = jnp.dot(flat, part, preferred_element_type=f32).astype(bf16)
        outs[rel][...] = got.reshape(2 * dist_dev, rows_dev, block)


def filter_kernel(waves_a, with_sin, with_cos, holo, out, mine, arrived):
    dists, width, block = out.shape
    own = mine.shape[0]
    core = lax.axis_index("dist")
    copy = pltpu.make_async_copy(holo.at[pl.ds(core * own, own)], mine, arrived)
    copy.start()
    turned = waves_a[...].T
    step = 128
    for at in range(0, width, step):
        rows = turned[at : at + step]
        transfer = [
            rows[:, d : d + 1] * with_sin[d : d + 1, :]
            + rows[:, dists + d : dists + d + 1] * with_cos[d : d + 1, :]
            for d in range(dists)
        ]
        denom = transfer[0] * transfer[0]
        for value in transfer[1:]:
            denom = denom + value * value
        scale = 1.0 / (denom + regularizer)
        for d in range(dists):
            out[d, at : at + step, :] = (transfer[d] * scale).astype(bf16)
    copy.wait()


def column_kernel(inner, outer, table, gain, *refs):
    pieces = dict(zip(send_order, refs[:inner]))
    away, keep, stack, total, spectrum = refs[inner:]
    _, plane, spot = position(inner)
    dists, rows_dev, block = pieces[0].shape
    depth = inner * rows_dev
    for rel in range(inner):
        start = pl.multiple_of((spot ^ rel) * rows_dev, rows_dev)
        for d in range(dists):
            stack[d, pl.ds(start, rows_dev), :] = pieces[rel][d]
    part = table[:, pl.ds(pl.multiple_of(plane * depth, depth), depth)]
    for d in range(dists):
        got = jnp.dot(part, stack[d], preferred_element_type=f32) * gain[d].astype(f32)
        if d == 0:
            total[...] = got
        else:
            total[...] += got
    spectrum[...] = total[...].astype(bf16)
    half = outer // 2
    side = plane // half
    for out, first in ((away, (1 - side) * half), (keep, side * half)):
        rows = pl.ds(pl.multiple_of(first * depth, half * depth), half * depth)
        got = jnp.dot(table[rows, :], spectrum[...], preferred_element_type=f32)
        out[...] = got.astype(bf16).reshape(half, depth, block)


def add_kernel(one, two, out):
    out[...] = (one[...].astype(f32) + two[...].astype(f32)).astype(bf16)


def near_kernel(inner, keep, across, out):
    _, plane, _ = position(inner)
    which = (plane ^ 1) % 2
    inside = (plane == 1) | (plane == 2)
    more = jnp.where(inside, across[which].astype(f32), 0.0)
    out[...] = (keep[which].astype(f32) + more).astype(bf16)


def half_kernel(inner, keep, across, last, *refs):
    mine, other = refs[-2:]
    _, plane, spot = position(inner)
    which = plane % 2
    inside = (plane == 1) | (plane == 2)
    capacity = mine.shape[0]
    for out, pair in ((mine, spot // 2), (other, 1 - spot // 2)):
        rows = pl.ds(pl.multiple_of(pair * capacity, capacity), capacity)
        more = jnp.where(inside, across[which, rows, :].astype(f32), 0.0)
        got = keep[which, rows, :].astype(f32) + more + last[rows, :].astype(f32)
        out[...] = got.astype(bf16)


def phase_kernel(inner, table, *refs):
    pieces = dict(zip(tail_order, refs[:inner]))
    out, joined = refs[-2:]
    _, _, spot = position(inner)
    block = refs[0].shape[1]
    for rel in range(inner):
        columns = pl.ds(pl.multiple_of((spot ^ rel) * block, block), block)
        joined[:, columns] = pieces[rel][...]
    out[...] = jnp.dot(joined[...], table[...], preferred_element_type=f32).astype(bf16)


def recon_kernel(own, chunk, cores, info, weights, *refs):
    core = lax.axis_index("dist")
    phases, out = refs[: len(cores)], refs[-1]
    total = refs[-2][...] if len(refs) > len(cores) + 1 else None
    for other, phase in zip(cores, phases):
        chosen = weights[info[(core ^ other) * own + chunk]]
        got = jnp.dot(phase[...], chosen, preferred_element_type=f32)
        total = got if total is None else total + got
    out[...] = total


def recon_last_kernel(own, chunk, other, info, weights, phase, before, out):
    core = lax.axis_index("dist")
    chosen = weights[info[(core ^ other) * own + chunk]]
    total = before[...] + jnp.dot(phase[...], chosen, preferred_element_type=f32)
    capacity = total.shape[0]
    offset, count = info[weights.shape[0]], info[weights.shape[0] + 1]
    turned = pltpu.roll(total, lax.rem(capacity - offset, capacity), 0)
    slot = lax.broadcasted_iota(jnp.int32, turned.shape, 0)
    out[...] = jnp.where(slot < count, turned, 0.0).astype(bf16)


def vmem(count):
    return [pl.BlockSpec(memory_space=pltpu.VMEM)] * count


def unread(count):
    return [pl.BlockSpec(memory_space=pl.ANY)] * count


def smem(count):
    return [pl.BlockSpec(memory_space=pltpu.SMEM)] * count


def plane_plan(inner, holograms, propagation, weights, angle_order, slab_rows):
    mbatch, angles, dist_dev, rows_dev, width = holograms.shape
    groups = lax.axis_size("rows")
    cores = lax.axis_size("dist")
    outer = groups // inner
    own = angles // cores
    block = width // inner
    depth = inner * rows_dev
    dists = cores * dist_dev
    pixels = weights.shape[2]
    capacity = 2 * rows_dev
    params = pltpu.CompilerParams(vmem_limit_bytes=16 * 2**20)
    one_out = pl.BlockSpec(memory_space=pltpu.VMEM)

    def cost(flops, *arrays):
        return pl.CostEstimate(
            flops=flops, bytes_accessed=sum(2 * math.prod(a) for a in arrays), transcendentals=0
        )

    def shaped(*shape):
        return jax.ShapeDtypeStruct(shape, bf16)

    device = lax.axis_index("rows")
    core = lax.axis_index("dist")
    plane, spot = device // inner, device % inner
    parity = device % 2
    info = jnp.concatenate(
        [
            angle_order[0],
            (parity * slab_rows[device - parity])[None],
            slab_rows[device][None],
        ]
    )
    table = jnp.asarray(hartley(width))

    def sent(value, target):
        pairs = []
        for c in range(cores):
            for r in range(groups):
                to_core, to_row = target(c, r)
                pairs.append((c * groups + r, to_core * groups + to_row))
        return lax.ppermute(value, ("dist", "rows"), pairs)

    def to_other_core(c, r):
        return c ^ 1, r

    def to_spot(rel):
        return lambda c, r: (c, r ^ rel)

    def spread(pieces, order):
        return [sent(pieces[rel], to_spot(rel)) if rel else pieces[rel] for rel in order]

    def to_near_plane(c, r):
        return c, (r // inner ^ 1) * inner + r % inner

    def to_middle(c, r):
        z = r // inner
        return (c, (3 - z) * inner + r % inner) if z in (1, 2) else (c ^ 1, r)

    index = jnp.arange(width, dtype=jnp.int32)
    my_cols = spot * block + jnp.arange(block, dtype=jnp.int32)
    ordered = jnp.concatenate(
        [
            lax.dynamic_slice_in_dim(propagation, (core ^ other) * dist_dev, dist_dev, 0)
            for other in range(cores)
        ]
    )
    first = ordered[:, None] * signed_square(index, width)[None]
    second = ordered[:, None] * signed_square(my_cols, width)[None]
    sin_b, cos_b = jnp.sin(second), jnp.cos(second)
    gain, mine = pl.pallas_call(
        filter_kernel,
        out_shape=[shaped(dists, width, block), shaped(own, dist_dev, rows_dev, width)],
        in_specs=vmem(3) + unread(1),
        out_specs=vmem(2),
        scratch_shapes=[pltpu.SemaphoreType.DMA],
        compiler_params=params,
        cost_estimate=cost(32 * width * block, (dists, width, block)),
        name="filters",
    )(
        jnp.concatenate([jnp.sin(first), jnp.cos(first)], axis=0),
        2.0 * (cos_b - absorb_ratio * sin_b),
        2.0 * (sin_b + absorb_ratio * cos_b),
        holograms[0],
    )

    partner = sent(holograms[0], to_other_core)
    arrived = []
    for chunk in range(own):
        pieces = pl.pallas_call(
            lambda *refs, chunk=chunk: row_kernel(inner, chunk, *refs),
            out_shape=[shaped(dists, rows_dev, block)] * inner,
            in_specs=vmem(3) + unread(1),
            out_specs=vmem(inner),
            compiler_params=params,
            cost_estimate=cost(
                2 * dists * rows_dev * width * width, (width, width), (2, dists, rows_dev, width)
            ),
            name="row_spectra",
        )(mine, partner, table, gain)
        arrived.append(spread(pieces, send_order))

    sums = []
    for chunk in range(own):
        away, keep = pl.pallas_call(
            lambda *refs: column_kernel(inner, outer, *refs),
            out_shape=[shaped(outer // 2, depth, block)] * 2,
            in_specs=vmem(2 + inner),
            out_specs=vmem(2),
            scratch_shapes=[
                pltpu.VMEM((dists, depth, block), bf16),
                pltpu.VMEM((width, block), f32),
                pltpu.VMEM((width, block), bf16),
            ],
            compiler_params=params,
            cost_estimate=cost(
                2 * width * block * (dists * depth + width), (width, width), (dists, width, block)
            ),
            name="columns",
        )(table, gain, *arrived[chunk])
        joint = pl.pallas_call(
            add_kernel,
            out_shape=shaped(outer // 2, depth, block),
            in_specs=vmem(2),
            out_specs=one_out,
            compiler_params=params,
            cost_estimate=cost(outer * depth * block, (3, outer // 2, depth, block)),
            name="joint",
        )(away, sent(away, to_near_plane))
        across = sent(joint, to_middle)
        near = pl.pallas_call(
            lambda *refs: near_kernel(inner, *refs),
            out_shape=shaped(depth, block),
            in_specs=vmem(2),
            out_specs=one_out,
            compiler_params=params,
            cost_estimate=cost(depth * block, (3, depth, block)),
            name="near",
        )(keep, across)
        sums.append((keep, across, sent(near, to_near_plane)))

    def recon(kernel, out_type, *arrays):
        return pl.pallas_call(
            kernel,
            out_shape=jax.ShapeDtypeStruct((capacity, pixels), out_type),
            in_specs=smem(1) + vmem(1 + len(arrays)),
            out_specs=one_out,
            compiler_params=params,
            cost_estimate=cost(1, (8, pixels)),
            name="recon",
        )(info, weights, *arrays)

    total = None
    for chunk in range(own):
        first, second = pl.pallas_call(
            lambda *refs: half_kernel(inner, *refs),
            out_shape=[shaped(capacity, block)] * 2,
            in_specs=vmem(3) + unread(2),
            out_specs=vmem(2),
            compiler_params=params,
            cost_estimate=cost(1, (8, width)),
            name="half",
        )(*sums[chunk], near, info)
        pieces = spread([first, first, second, second], tail_order)
        phase = pl.pallas_call(
            lambda *refs: phase_kernel(inner, *refs),
            out_shape=shaped(capacity, width),
            in_specs=vmem(1 + inner),
            out_specs=one_out,
            scratch_shapes=[pltpu.VMEM((capacity, width), bf16)],
            compiler_params=params,
            cost_estimate=cost(1, (8, width)),
            name="phase",
        )(table, *pieces)
        there = sent(phase, to_other_core)
        def part(cores, chunk=chunk):
            return lambda *refs: recon_kernel(own, chunk, cores, *refs)

        before = [] if total is None else [total]
        if chunk < own - 1:
            total = recon(part((0, 1)), f32, phase, there, *before)
        else:
            total = recon(part((0,)), f32, phase, *before)
            total = recon(
                lambda *refs, chunk=chunk: recon_last_kernel(own, chunk, 1, *refs),
                bf16,
                there,
                total,
            )
    return total


def on_device(holograms, propagation, weights, angle_order, slab_rows):
    mbatch, angles, dist_dev, rows_dev, width = holograms.shape
    groups = lax.axis_size("rows")
    inner = 2 ** (int(math.log2(groups)) // 2)
    block = width // inner
    fits = (
        inner * (groups // inner) == groups
        and rows_dev % 16 == 0
        and block % 128 == 0
        and inner * rows_dev % 128 == 0
        and inner == 4
        and groups == inner * inner
        and lax.axis_size("dist") == 2
    )
    if fits:
        return plane_plan(inner, holograms, propagation, weights, angle_order, slab_rows)
    return flat_plan(holograms, propagation, weights, angle_order, slab_rows)


def solution(mesh):
    return jax.shard_map(
        on_device,
        mesh=mesh,
        in_specs=(P(None, None, "dist", "rows", None), P(), P(None, None, "dist"), P(), P()),
        out_specs=P("rows", "dist"),
        check_vma=False,
    )
```

```python
import math

import jax
import jax.numpy as jnp
import numpy as np
from jax import lax
from jax.experimental import pallas as pl
from jax.experimental.pallas import tpu as pltpu
from jax.sharding import PartitionSpec as P

absorb_ratio = 0.1
regularizer = 0.05
bf16 = jnp.bfloat16
f32 = jnp.float32


def hartley(length):
    index = np.arange(length)
    turned = (index[:, None] * index[None, :] % length) * (2.0 * math.pi / length)
    table = (np.cos(turned) + np.sin(turned)) / math.sqrt(length)
    return table.astype(bf16)


def signed_square(index, length):
    signed = jnp.where(index < length // 2, index, index - length).astype(f32)
    return signed * signed / float(length * length)


def filters(propagation, rows_sq, cols_sq):
    first = propagation[:, None] * rows_sq[None]
    second = propagation[:, None] * cols_sq[None]
    sin_b, cos_b = jnp.sin(second), jnp.cos(second)
    with_sin = 2.0 * (cos_b - absorb_ratio * sin_b)
    with_cos = 2.0 * (sin_b + absorb_ratio * cos_b)
    transfer = (
        jnp.sin(first)[:, :, None] * with_sin[:, None, :]
        + jnp.cos(first)[:, :, None] * with_cos[:, None, :]
    )
    denom = jnp.sum(transfer * transfer, axis=0) + regularizer
    return transfer / denom


def flat_plan(holograms, propagation, weights, angle_order, slab_rows):
    mbatch, angles, dist_dev, rows_dev, width = holograms.shape
    groups = lax.axis_size("rows")
    cores = lax.axis_size("dist")
    capacity = 2 * rows_dev
    own = angles // cores
    cols = width // groups
    dists = dist_dev * cores
    device = lax.axis_index("rows")
    table = jnp.asarray(hartley(width))
    index = jnp.arange(width, dtype=jnp.int32)
    my_cols = device * cols + jnp.arange(cols, dtype=jnp.int32)
    gain = filters(propagation, signed_square(my_cols, width), signed_square(index, width))

    mine = lax.all_to_all(holograms[0], "dist", split_axis=0, concat_axis=1, tiled=True)
    flat = mine.reshape(own * dists * rows_dev, width)
    spec = jnp.einsum("kx,mx->km", table, flat, preferred_element_type=f32)
    spec = spec.astype(bf16).reshape(groups, cols, own * dists * rows_dev)
    spec = lax.all_to_all(spec, "rows", split_axis=0, concat_axis=0, tiled=True)
    spec = spec.reshape(groups, cols, own, dists, rows_dev).transpose(1, 2, 3, 0, 4)
    spec = spec.reshape(cols * own * dists, width)
    full = jnp.dot(spec, table, preferred_element_type=f32)
    full = full.reshape(cols, own, dists, width)
    full = jnp.sum(full * gain.transpose(1, 0, 2)[:, None], axis=2).astype(bf16)
    half = jnp.einsum("yq,akq->yak", table, full.transpose(1, 0, 2), preferred_element_type=f32)
    half = half.astype(bf16).reshape(groups, rows_dev, own * cols)
    half = lax.all_to_all(half, "rows", split_axis=0, concat_axis=0, tiled=True)
    half = half.reshape(groups, rows_dev, own, cols).transpose(2, 1, 0, 3)
    half = half.reshape(own * rows_dev, width)
    phase = jnp.dot(half, table, preferred_element_type=f32)
    phase = phase.astype(bf16).reshape(own, rows_dev, width)
    phase = lax.all_gather(phase, "dist", axis=0, tiled=True)
    place = (angle_order[0][None, :] == jnp.arange(angles)[:, None]).astype(bf16)
    phase = jnp.einsum("wa,ayx->wyx", place, phase, preferred_element_type=f32)
    recon = jnp.einsum(
        "wyx,wxp->yp", phase.astype(bf16), weights, preferred_element_type=f32
    ).astype(bf16)
    parity = device % 2
    offset = parity * slab_rows[device - parity]
    count = slab_rows[device]
    pairs = [(source, source ^ 1) for source in range(groups)]
    partner = lax.ppermute(recon, "rows", pairs)
    lower = jnp.where(parity == 1, partner, recon)
    upper = jnp.where(parity == 1, recon, partner)
    paired = jnp.concatenate([lower, upper], axis=0)
    slot = jnp.arange(capacity, dtype=jnp.int32)[:, None]
    source = jnp.arange(capacity, dtype=jnp.int32)[None, :]
    select = ((source == offset + slot) & (slot < count)).astype(bf16)
    return jnp.dot(select, paired, preferred_element_type=f32).astype(bf16)


def position(inner):
    device = lax.axis_index("rows")
    return lax.axis_index("dist"), device // inner, device % inner


def steps_of(core):
    return 2 - core, 1 + core


def whole_turns(scale, square):
    turns = scale * square * (0.5 / math.pi)
    return (turns - jnp.round(turns)) * (2.0 * math.pi)


def filter_kernel(inner, propagation, holo, out, mine, arrived):
    dists, width, block = out.shape
    own, dist_dev = mine.shape[:2]
    core, _, spot = position(inner)
    copy = pltpu.make_async_copy(holo.at[pl.ds(core * own, own)], mine, arrived)
    copy.start()

    def square(first, length):
        index = lax.broadcasted_iota(jnp.int32, (1, length), 1) + first
        signed = jnp.where(index < width // 2, index, index - width).astype(f32)
        return signed * signed * (1.0 / (width * width))

    def phases(first, length):
        values = square(first, length)
        rows = []
        for d in range(dists):
            other = d // dist_dev
            scale = propagation[(core ^ other) * dist_dev + d % dist_dev]
            rows.append(whole_turns(scale, values))
        return jnp.concatenate(rows, axis=0)

    along = phases(0, width)
    across = phases(spot * block, block)
    sin_b, cos_b = jnp.sin(across), jnp.cos(across)
    with_sin = 2.0 * (cos_b - absorb_ratio * sin_b)
    with_cos = 2.0 * (sin_b + absorb_ratio * cos_b)
    turned = jnp.concatenate([jnp.sin(along), jnp.cos(along)], axis=0).T
    step = 128
    for at in range(0, width, step):
        rows = turned[at : at + step]
        transfer = [
            rows[:, d : d + 1] * with_sin[d : d + 1, :]
            + rows[:, dists + d : dists + d + 1] * with_cos[d : d + 1, :]
            for d in range(dists)
        ]
        denom = transfer[0] * transfer[0]
        for value in transfer[1:]:
            denom = denom + value * value
        scale = 1.0 / (denom + regularizer)
        for d in range(dists):
            out[d, at : at + step, :] = (transfer[d] * scale).astype(bf16)
    copy.wait()


def row_kernel(inner, chunk, here, there, table, after, stays, leaves, later):
    core, _, spot = position(inner)
    first, second = steps_of(core)
    own, dist_dev, rows_dev, width = here.shape
    block = width // inner
    partner = there[core * own + chunk]
    flat = jnp.concatenate(
        [source.reshape(dist_dev * rows_dev, width) for source in (here[chunk], partner)], axis=0
    )

    def part(rel):
        columns = pl.ds(pl.multiple_of((spot ^ rel) * block, block), block)
        got = jnp.dot(flat, table[:, columns], preferred_element_type=f32).astype(bf16)
        return got.reshape(2 * dist_dev, rows_dev, block)

    leaves[0] = part(first)
    leaves[1] = part(3)
    later[...] = part(second)
    stays[...] = part(0)


def relay_kernel(later, got, out):
    out[0] = later[...]
    out[1] = got[1]


def column_kernel(inner, outer, table, gain, stays, got, relayed, *refs):
    away, keep, stack, total, spectrum = refs
    core, plane, spot = position(inner)
    first, second = steps_of(core)
    dists, rows_dev, block = stays.shape
    depth = inner * rows_dev
    pieces = ((0, stays), (first, got.at[0]), (second, relayed.at[0]), (3, relayed.at[1]))
    for rel, piece in pieces:
        start = pl.multiple_of((spot ^ rel) * rows_dev, rows_dev)
        for d in range(dists):
            stack[d, pl.ds(start, rows_dev), :] = piece[d]
    part = table[:, pl.ds(pl.multiple_of(plane * depth, depth), depth)]
    for d in range(dists):
        value = jnp.dot(part, stack[d], preferred_element_type=f32) * gain[d].astype(f32)
        if d == 0:
            total[...] = value
        else:
            total[...] += value
    spectrum[...] = total[...].astype(bf16)
    half = outer // 2
    side = plane // half
    for out, low in ((away, (1 - side) * half), (keep, side * half)):
        rows = pl.ds(pl.multiple_of(low * depth, half * depth), half * depth)
        value = jnp.dot(table[rows, :], spectrum[...], preferred_element_type=f32)
        out[...] = value.astype(bf16).reshape(half, depth, block)


def add_kernel(one, two, out):
    out[...] = (one[...].astype(f32) + two[...].astype(f32)).astype(bf16)


def near_kernel(inner, keep, across, *refs):
    out = refs[-1]
    _, plane, _ = position(inner)
    which = (plane ^ 1) % 2
    inside = (plane == 1) | (plane == 2)
    more = jnp.where(inside, across[which].astype(f32), 0.0)
    out[...] = (keep[which].astype(f32) + more).astype(bf16)


def half_kernel(inner, keep, across, last, *refs):
    stays, leaves, later = refs[-3:]
    core, plane, spot = position(inner)
    which = plane % 2
    inside = (plane == 1) | (plane == 2)
    capacity = stays.shape[0]
    got = []
    for pair in (spot // 2, 1 - spot // 2):
        rows = pl.ds(pl.multiple_of(pair * capacity, capacity), capacity)
        more = jnp.where(inside, across[which, rows, :].astype(f32), 0.0)
        value = keep[which, rows, :].astype(f32) + more + last[rows, :].astype(f32)
        got.append(value.astype(bf16))
    near, far = got
    stays[...] = near
    leaves[0] = jnp.where(core == 0, far, near)
    leaves[1] = far
    later[...] = jnp.where(core == 0, near, far)


def phase_kernel(inner, table, stays, got, relayed, *refs):
    out, joined = refs[-2:]
    core, _, spot = position(inner)
    first, second = steps_of(core)
    block = stays.shape[1]
    pieces = ((0, stays), (first, got.at[0]), (second, relayed.at[0]), (3, relayed.at[1]))
    for rel, piece in pieces:
        columns = pl.ds(pl.multiple_of((spot ^ rel) * block, block), block)
        joined[:, columns] = piece[...]
    out[...] = jnp.dot(joined[...], table[...], preferred_element_type=f32).astype(bf16)


def choose_kernel(order, slabs, weights, after, chosen, select, arrived):
    angles = chosen.shape[0]
    core = lax.axis_index("dist")
    device = lax.axis_index("rows")
    own = angles // 2
    copies = [
        pltpu.make_async_copy(
            weights.at[order[0, (core ^ (step // own)) * own + step % own]],
            chosen.at[step],
            arrived.at[step],
        )
        for step in range(angles)
    ]
    for copy in copies:
        copy.start()
    parity = device % 2
    offset = parity * slabs[device - parity]
    slot = lax.broadcasted_iota(jnp.int32, select.shape, 0)
    source = lax.broadcasted_iota(jnp.int32, select.shape, 1)
    picked = (source == slot + offset) & (slot < slabs[device])
    select[...] = jnp.where(picked, 1.0, 0.0).astype(bf16)
    for copy in copies:
        copy.wait()


def recon_kernel(steps, weights, *refs):
    phases, out = refs[: len(steps)], refs[-1]
    total = refs[-2][...] if len(refs) > len(steps) + 1 else None
    for step, phase in zip(steps, phases):
        got = jnp.dot(phase[...], weights[step], preferred_element_type=f32)
        total = got if total is None else total + got
    out[...] = total


def recon_last_kernel(step, weights, phase, before, select, out):
    total = before[...] + jnp.dot(phase[...], weights[step], preferred_element_type=f32)
    got = jnp.dot(select[...], total.astype(bf16), preferred_element_type=f32)
    out[...] = got.astype(bf16)


def vmem(count):
    return [pl.BlockSpec(memory_space=pltpu.VMEM)] * count


def from_hbm(value):
    return pltpu.with_memory_space_constraint(value, pltpu.HBM)


def unread(count):
    return [pl.BlockSpec(memory_space=pl.ANY)] * count


def in_hbm(count):
    return [pl.BlockSpec(memory_space=pltpu.HBM)] * count


def smem(count):
    return [pl.BlockSpec(memory_space=pltpu.SMEM)] * count


def plane_plan(inner, holograms, propagation, weights, angle_order, slab_rows):
    mbatch, angles, dist_dev, rows_dev, width = holograms.shape
    groups = lax.axis_size("rows")
    cores = lax.axis_size("dist")
    outer = groups // inner
    own = angles // cores
    block = width // inner
    depth = inner * rows_dev
    dists = cores * dist_dev
    pixels = weights.shape[2]
    capacity = 2 * rows_dev
    params = pltpu.CompilerParams(vmem_limit_bytes=16 * 2**20)
    one_out = pl.BlockSpec(memory_space=pltpu.VMEM)

    def cost(flops, *arrays):
        return pl.CostEstimate(
            flops=flops, bytes_accessed=sum(2 * math.prod(a) for a in arrays), transcendentals=0
        )

    def shaped(*shape):
        return jax.ShapeDtypeStruct(shape, bf16)

    table = jnp.asarray(hartley(width))

    def sent(value, target):
        pairs = []
        for c in range(cores):
            for r in range(groups):
                to_core, to_row = target(c, r)
                pairs.append((c * groups + r, to_core * groups + to_row))
        return lax.ppermute(value, ("dist", "rows"), pairs)

    def to_other_core(c, r):
        return c ^ 1, r

    def to_first(c, r):
        return c, r ^ steps_of(c)[0]

    def to_second(c, r):
        return c, r ^ steps_of(c)[1]

    def spread(stays, leaves, later):
        got = sent(leaves, to_first)
        message = pl.pallas_call(
            relay_kernel,
            out_shape=shaped(*leaves.shape),
            in_specs=vmem(2),
            out_specs=one_out,
            compiler_params=params,
            cost_estimate=cost(1, (8, width)),
            name="relay",
        )(later, got)
        return stays, got, sent(message, to_second)

    def to_near_plane(c, r):
        return c, (r // inner ^ 1) * inner + r % inner

    def to_middle(c, r):
        z = r // inner
        return (c, (3 - z) * inner + r % inner) if z in (1, 2) else (c ^ 1, r)

    partner = sent(holograms[0], to_other_core)
    gain, mine = pl.pallas_call(
        lambda *refs: filter_kernel(inner, *refs),
        out_shape=[
            shaped(dists, width, block),
            shaped(own, dist_dev, rows_dev, width),
        ],
        in_specs=smem(1) + in_hbm(1),
        out_specs=vmem(2),
        scratch_shapes=[pltpu.SemaphoreType.DMA],
        compiler_params=params,
        cost_estimate=cost(32 * width * block, (dists, width, block)),
        name="filters",
    )(propagation, from_hbm(holograms[0]))

    arrived = []
    for chunk in range(own):
        pieces = pl.pallas_call(
            lambda *refs, chunk=chunk: row_kernel(inner, chunk, *refs),
            out_shape=[
                shaped(dists, rows_dev, block),
                shaped(2, dists, rows_dev, block),
                shaped(dists, rows_dev, block),
            ],
            in_specs=vmem(3) + unread(1),
            out_specs=vmem(3),
            compiler_params=params,
            cost_estimate=cost(
                2 * dists * rows_dev * width * width, (width, width), (2, dists, rows_dev, width)
            ),
            name="row_spectra",
        )(mine, partner, table, gain)
        arrived.append(spread(*pieces))

    sums = []
    for chunk in range(own):
        away, keep = pl.pallas_call(
            lambda *refs: column_kernel(inner, outer, *refs),
            out_shape=[shaped(outer // 2, depth, block)] * 2,
            in_specs=vmem(5),
            out_specs=vmem(2),
            scratch_shapes=[
                pltpu.VMEM((dists, depth, block), bf16),
                pltpu.VMEM((width, block), f32),
                pltpu.VMEM((width, block), bf16),
            ],
            compiler_params=params,
            cost_estimate=cost(
                2 * width * block * (dists * depth + width), (width, width), (dists, width, block)
            ),
            name="columns",
        )(table, gain, *arrived[chunk])
        joint = pl.pallas_call(
            add_kernel,
            out_shape=shaped(outer // 2, depth, block),
            in_specs=vmem(2),
            out_specs=one_out,
            compiler_params=params,
            cost_estimate=cost(outer * depth * block, (3, outer // 2, depth, block)),
            name="joint",
        )(away, sent(away, to_near_plane))
        across = sent(joint, to_middle)
        last = chunk == own - 1
        if last:
            chosen, select = pl.pallas_call(
                choose_kernel,
                out_shape=[shaped(angles, width, pixels), shaped(capacity, capacity)],
                in_specs=smem(2) + in_hbm(1) + unread(1),
                out_specs=vmem(2),
                scratch_shapes=[pltpu.SemaphoreType.DMA((angles,))],
                compiler_params=params,
                cost_estimate=cost(1, (8, width)),
                name="choose",
            )(angle_order, slab_rows, from_hbm(weights), near)
        near = pl.pallas_call(
            lambda *refs: near_kernel(inner, *refs),
            out_shape=shaped(depth, block),
            in_specs=vmem(2) + unread(last),
            out_specs=one_out,
            compiler_params=params,
            cost_estimate=cost(depth * block, (3, depth, block)),
            name="near",
        )(keep, across, *([select] if last else []))
        sums.append((keep, across, sent(near, to_near_plane)))

    def recon(kernel, out_type, *arrays):
        return pl.pallas_call(
            kernel,
            out_shape=jax.ShapeDtypeStruct((capacity, pixels), out_type),
            in_specs=vmem(1 + len(arrays)),
            out_specs=one_out,
            compiler_params=params,
            cost_estimate=cost(1, (8, pixels)),
            name="recon",
        )(chosen, *arrays)

    total = None
    for chunk in range(own):
        pieces = pl.pallas_call(
            lambda *refs: half_kernel(inner, *refs),
            out_shape=[
                shaped(capacity, block),
                shaped(2, capacity, block),
                shaped(capacity, block),
            ],
            in_specs=vmem(3) + unread(2),
            out_specs=vmem(3),
            compiler_params=params,
            cost_estimate=cost(1, (8, width)),
            name="half",
        )(*sums[chunk], near, select)
        phase = pl.pallas_call(
            lambda *refs: phase_kernel(inner, *refs),
            out_shape=shaped(capacity, width),
            in_specs=vmem(4),
            out_specs=one_out,
            scratch_shapes=[pltpu.VMEM((capacity, width), bf16)],
            compiler_params=params,
            cost_estimate=cost(1, (8, width)),
            name="phase",
        )(table, *spread(*pieces))
        there = sent(phase, to_other_core)

        def part(*steps):
            return lambda *refs: recon_kernel(steps, *refs)

        before = [] if total is None else [total]
        if chunk < own - 1:
            total = recon(part(chunk, own + chunk), f32, phase, there, *before)
        else:
            total = recon(part(chunk), f32, phase, *before)
            total = recon(
                lambda *refs, chunk=chunk: recon_last_kernel(own + chunk, *refs),
                bf16,
                there,
                total,
                select,
            )
    return total


def on_device(holograms, propagation, weights, angle_order, slab_rows):
    mbatch, angles, dist_dev, rows_dev, width = holograms.shape
    groups = lax.axis_size("rows")
    inner = 2 ** (int(math.log2(groups)) // 2)
    block = width // inner
    fits = (
        inner * (groups // inner) == groups
        and rows_dev % 16 == 0
        and block % 128 == 0
        and inner * rows_dev % 128 == 0
        and inner == 4
        and groups == inner * inner
        and lax.axis_size("dist") == 2
    )
    if fits:
        return plane_plan(inner, holograms, propagation, weights, angle_order, slab_rows)
    return flat_plan(holograms, propagation, weights, angle_order, slab_rows)


def solution(mesh):
    return jax.shard_map(
        on_device,
        mesh=mesh,
        in_specs=(P(None, None, "dist", "rows", None), P(), P(None, None, "dist"), P(), P()),
        out_specs=P("rows", "dist"),
        check_vma=False,
    )
```

```python
import math

import jax
import jax.numpy as jnp
import numpy as np
from jax import lax
from jax.experimental import pallas as pl
from jax.experimental.pallas import tpu as pltpu
from jax.sharding import PartitionSpec as P

absorb_ratio = 0.1
regularizer = 0.05
bf16 = jnp.bfloat16
f32 = jnp.float32
send_order = (0, 1, 2, 3)
tail_order = (0, 1, 3, 2)


def hartley(length):
    index = np.arange(length)
    turned = (index[:, None] * index[None, :] % length) * (2.0 * math.pi / length)
    table = (np.cos(turned) + np.sin(turned)) / math.sqrt(length)
    return table.astype(bf16)


def signed_square(index, length):
    signed = jnp.where(index < length // 2, index, index - length).astype(f32)
    return signed * signed / float(length * length)


def filters(propagation, rows_sq, cols_sq):
    first = propagation[:, None] * rows_sq[None]
    second = propagation[:, None] * cols_sq[None]
    sin_b, cos_b = jnp.sin(second), jnp.cos(second)
    with_sin = 2.0 * (cos_b - absorb_ratio * sin_b)
    with_cos = 2.0 * (sin_b + absorb_ratio * cos_b)
    transfer = (
        jnp.sin(first)[:, :, None] * with_sin[:, None, :]
        + jnp.cos(first)[:, :, None] * with_cos[:, None, :]
    )
    denom = jnp.sum(transfer * transfer, axis=0) + regularizer
    return transfer / denom


def flat_plan(holograms, propagation, weights, angle_order, slab_rows):
    mbatch, angles, dist_dev, rows_dev, width = holograms.shape
    groups = lax.axis_size("rows")
    cores = lax.axis_size("dist")
    capacity = 2 * rows_dev
    own = angles // cores
    cols = width // groups
    dists = dist_dev * cores
    device = lax.axis_index("rows")
    table = jnp.asarray(hartley(width))
    index = jnp.arange(width, dtype=jnp.int32)
    my_cols = device * cols + jnp.arange(cols, dtype=jnp.int32)
    gain = filters(propagation, signed_square(my_cols, width), signed_square(index, width))

    mine = lax.all_to_all(holograms[0], "dist", split_axis=0, concat_axis=1, tiled=True)
    flat = mine.reshape(own * dists * rows_dev, width)
    spec = jnp.einsum("kx,mx->km", table, flat, preferred_element_type=f32)
    spec = spec.astype(bf16).reshape(groups, cols, own * dists * rows_dev)
    spec = lax.all_to_all(spec, "rows", split_axis=0, concat_axis=0, tiled=True)
    spec = spec.reshape(groups, cols, own, dists, rows_dev).transpose(1, 2, 3, 0, 4)
    spec = spec.reshape(cols * own * dists, width)
    full = jnp.dot(spec, table, preferred_element_type=f32)
    full = full.reshape(cols, own, dists, width)
    full = jnp.sum(full * gain.transpose(1, 0, 2)[:, None], axis=2).astype(bf16)
    half = jnp.einsum("yq,akq->yak", table, full.transpose(1, 0, 2), preferred_element_type=f32)
    half = half.astype(bf16).reshape(groups, rows_dev, own * cols)
    half = lax.all_to_all(half, "rows", split_axis=0, concat_axis=0, tiled=True)
    half = half.reshape(groups, rows_dev, own, cols).transpose(2, 1, 0, 3)
    half = half.reshape(own * rows_dev, width)
    phase = jnp.dot(half, table, preferred_element_type=f32)
    phase = phase.astype(bf16).reshape(own, rows_dev, width)
    phase = lax.all_gather(phase, "dist", axis=0, tiled=True)
    place = (angle_order[0][None, :] == jnp.arange(angles)[:, None]).astype(bf16)
    phase = jnp.einsum("wa,ayx->wyx", place, phase, preferred_element_type=f32)
    recon = jnp.einsum(
        "wyx,wxp->yp", phase.astype(bf16), weights, preferred_element_type=f32
    ).astype(bf16)
    parity = device % 2
    offset = parity * slab_rows[device - parity]
    count = slab_rows[device]
    pairs = [(source, source ^ 1) for source in range(groups)]
    partner = lax.ppermute(recon, "rows", pairs)
    lower = jnp.where(parity == 1, partner, recon)
    upper = jnp.where(parity == 1, recon, partner)
    paired = jnp.concatenate([lower, upper], axis=0)
    slot = jnp.arange(capacity, dtype=jnp.int32)[:, None]
    source = jnp.arange(capacity, dtype=jnp.int32)[None, :]
    select = ((source == offset + slot) & (slot < count)).astype(bf16)
    return jnp.dot(select, paired, preferred_element_type=f32).astype(bf16)


def position(inner):
    device = lax.axis_index("rows")
    return lax.axis_index("dist"), device // inner, device % inner


def take_kernel(holo, after, out, arrived):
    own = out.shape[0]
    core = lax.axis_index("dist")
    copy = pltpu.make_async_copy(holo.at[pl.ds(core * own, own)], out, arrived)
    copy.start()
    copy.wait()


def row_kernel(inner, chunk, here, there, table, *outs):
    core, _, spot = position(inner)
    own, dist_dev, rows_dev, width = here.shape
    block = width // inner
    partner = there[core * own + chunk]
    flat = jnp.concatenate(
        [source.reshape(dist_dev * rows_dev, width) for source in (here[chunk], partner)], axis=0
    )
    for rel in range(inner):
        part = table[:, pl.ds(pl.multiple_of((spot ^ rel) * block, block), block)]
        got = jnp.dot(flat, part, preferred_element_type=f32).astype(bf16)
        outs[rel][...] = got.reshape(2 * dist_dev, rows_dev, block)


def whole_turns(scale, square):
    turns = scale * square * (0.5 / math.pi)
    return (turns - jnp.round(turns)) * (2.0 * math.pi)


def filter_kernel(inner, dist_dev, propagation, after, out):
    dists, width, block = out.shape
    core, _, spot = position(inner)

    def square(first, length):
        index = lax.broadcasted_iota(jnp.int32, (1, length), 1) + first
        signed = jnp.where(index < width // 2, index, index - width).astype(f32)
        return signed * signed * (1.0 / (width * width))

    def phases(first, length):
        values = square(first, length)
        rows = []
        for d in range(dists):
            other = d // dist_dev
            scale = propagation[(core ^ other) * dist_dev + d % dist_dev]
            rows.append(whole_turns(scale, values))
        return jnp.concatenate(rows, axis=0)

    along = phases(0, width)
    across = phases(spot * block, block)
    sin_b, cos_b = jnp.sin(across), jnp.cos(across)
    with_sin = 2.0 * (cos_b - absorb_ratio * sin_b)
    with_cos = 2.0 * (sin_b + absorb_ratio * cos_b)
    turned = jnp.concatenate([jnp.sin(along), jnp.cos(along)], axis=0).T
    step = 128
    for at in range(0, width, step):
        rows = turned[at : at + step]
        transfer = [
            rows[:, d : d + 1] * with_sin[d : d + 1, :]
            + rows[:, dists + d : dists + d + 1] * with_cos[d : d + 1, :]
            for d in range(dists)
        ]
        denom = transfer[0] * transfer[0]
        for value in transfer[1:]:
            denom = denom + value * value
        scale = 1.0 / (denom + regularizer)
        for d in range(dists):
            out[d, at : at + step, :] = (transfer[d] * scale).astype(bf16)


def column_kernel(inner, outer, table, gain, *refs):
    pieces = dict(zip(send_order, refs[:inner]))
    keep, *away = refs[inner:-3]
    stack, total, spectrum = refs[-3:]
    _, plane, spot = position(inner)
    dists, rows_dev, block = pieces[0].shape
    depth = inner * rows_dev
    for rel in range(inner):
        start = pl.multiple_of((spot ^ rel) * rows_dev, rows_dev)
        for d in range(dists):
            stack[d, pl.ds(start, rows_dev), :] = pieces[rel][d]
    part = table[:, pl.ds(pl.multiple_of(plane * depth, depth), depth)]
    for d in range(dists):
        got = jnp.dot(part, stack[d], preferred_element_type=f32) * gain[d].astype(f32)
        if d == 0:
            total[...] = got
        else:
            total[...] += got
    spectrum[...] = total[...].astype(bf16)
    half = outer // 2
    side = plane // half

    def rows_from(low):
        rows = pl.ds(pl.multiple_of(low * depth, half * depth), half * depth)
        value = jnp.dot(table[rows, :], spectrum[...], preferred_element_type=f32)
        return value.astype(bf16).reshape(half, depth, block)

    value = rows_from((1 - side) * half)
    wide = block // len(away)
    for split, out in enumerate(away):
        out[...] = value[:, :, split * wide : (split + 1) * wide]
    keep[...] = rows_from(side * half)


def add_kernel(one, two, out):
    out[...] = (one[...].astype(f32) + two[...].astype(f32)).astype(bf16)


def near_kernel(inner, split, keep, across, out):
    _, plane, _ = position(inner)
    which = (plane ^ 1) % 2
    inside = (plane == 1) | (plane == 2)
    more = jnp.where(inside, across[which].astype(f32), 0.0)
    wide = out.shape[1]
    here = keep[which, :, split * wide : (split + 1) * wide].astype(f32)
    out[...] = (here + more).astype(bf16)


def half_kernel(inner, keep, *refs):
    mine, other = refs[-2:]
    parts = refs[:-2]
    splits = len(parts) // 2
    _, plane, spot = position(inner)
    which = plane % 2
    inside = (plane == 1) | (plane == 2)
    capacity = mine.shape[0]
    wide = mine.shape[1] // splits
    for split in range(splits):
        across, last = parts[2 * split : 2 * split + 2]
        lanes = slice(split * wide, (split + 1) * wide)
        for out, pair in ((mine, spot // 2), (other, 1 - spot // 2)):
            rows = pl.ds(pl.multiple_of(pair * capacity, capacity), capacity)
            more = jnp.where(inside, across[which, rows, :].astype(f32), 0.0)
            got = keep[which, rows, lanes].astype(f32) + more + last[rows, :].astype(f32)
            out[:, lanes] = got.astype(bf16)


def phase_kernel(inner, table, *refs):
    pieces = dict(zip(tail_order, refs[:inner]))
    out, joined = refs[-2:]
    _, _, spot = position(inner)
    block = refs[0].shape[1]
    for rel in range(inner):
        columns = pl.ds(pl.multiple_of((spot ^ rel) * block, block), block)
        joined[:, columns] = pieces[rel][...]
    out[...] = jnp.dot(joined[...], table[...], preferred_element_type=f32).astype(bf16)


def recon_kernel(own, chunk, cores, order, weights, *refs):
    core = lax.axis_index("dist")
    phases, out = refs[: len(cores)], refs[-1]
    total = None
    for other, phase in zip(cores, phases):
        chosen = weights[order[0, (core ^ other) * own + chunk]]
        got = jnp.dot(phase[...], chosen, preferred_element_type=f32)
        total = got if total is None else total + got
    out[...] = total


def recon_next_kernel(own, chunk, order, slabs, weights, phase, before, out, chosen, select):
    core = lax.axis_index("dist")
    device = lax.axis_index("rows")
    here = weights[order[0, core * own + chunk]]
    out[...] = before[...] + jnp.dot(phase[...], here, preferred_element_type=f32)
    chosen[...] = weights[order[0, (core ^ 1) * own + chunk]]
    parity = device % 2
    offset = parity * slabs[device - parity]
    slot = lax.broadcasted_iota(jnp.int32, select.shape, 0)
    source = lax.broadcasted_iota(jnp.int32, select.shape, 1)
    picked = (source == slot + offset) & (slot < slabs[device])
    select[...] = jnp.where(picked, 1.0, 0.0).astype(bf16)


def recon_last_kernel(weights, phase, before, select, out):
    total = before[...] + jnp.dot(phase[...], weights[...], preferred_element_type=f32)
    got = jnp.dot(select[...], total.astype(bf16), preferred_element_type=f32)
    out[...] = got.astype(bf16)


def vmem(count):
    return [pl.BlockSpec(memory_space=pltpu.VMEM)] * count


def from_hbm(value):
    return pltpu.with_memory_space_constraint(value, pltpu.HBM)


def in_hbm(count):
    return [pl.BlockSpec(memory_space=pltpu.HBM)] * count


def unread(count):
    return [pl.BlockSpec(memory_space=pl.ANY)] * count


def smem(count):
    return [pl.BlockSpec(memory_space=pltpu.SMEM)] * count


def plane_plan(inner, holograms, propagation, weights, angle_order, slab_rows):
    mbatch, angles, dist_dev, rows_dev, width = holograms.shape
    groups = lax.axis_size("rows")
    cores = lax.axis_size("dist")
    outer = groups // inner
    own = angles // cores
    block = width // inner
    depth = inner * rows_dev
    dists = cores * dist_dev
    pixels = weights.shape[2]
    capacity = 2 * rows_dev
    splits = block // 128
    params = pltpu.CompilerParams(vmem_limit_bytes=16 * 2**20)
    one_out = pl.BlockSpec(memory_space=pltpu.VMEM)

    def cost(flops, *arrays):
        return pl.CostEstimate(
            flops=flops, bytes_accessed=sum(2 * math.prod(a) for a in arrays), transcendentals=0
        )

    def shaped(*shape):
        return jax.ShapeDtypeStruct(shape, bf16)

    table = jnp.asarray(hartley(width))

    def sent(value, target):
        pairs = []
        for c in range(cores):
            for r in range(groups):
                to_core, to_row = target(c, r)
                pairs.append((c * groups + r, to_core * groups + to_row))
        return lax.ppermute(value, ("dist", "rows"), pairs)

    def to_other_core(c, r):
        return c ^ 1, r

    def to_spot(rel):
        return lambda c, r: (c, r ^ rel)

    def spread(pieces, order):
        return [sent(pieces[rel], to_spot(rel)) if rel else pieces[rel] for rel in order]

    def to_near_plane(c, r):
        return c, (r // inner ^ 1) * inner + r % inner

    def to_middle(c, r):
        z = r // inner
        return (c, (3 - z) * inner + r % inner) if z in (1, 2) else (c ^ 1, r)

    partner = sent(holograms[0], to_other_core)
    mine = pl.pallas_call(
        take_kernel,
        out_shape=shaped(own, dist_dev, rows_dev, width),
        in_specs=in_hbm(1) + vmem(1),
        out_specs=one_out,
        scratch_shapes=[pltpu.SemaphoreType.DMA],
        compiler_params=params,
        cost_estimate=cost(1, (8, width)),
        name="take",
    )(from_hbm(holograms[0]), table)
    arrived = []
    for chunk in range(own):
        pieces = pl.pallas_call(
            lambda *refs, chunk=chunk: row_kernel(inner, chunk, *refs),
            out_shape=[shaped(dists, rows_dev, block)] * inner,
            in_specs=vmem(3),
            out_specs=vmem(inner),
            compiler_params=params,
            cost_estimate=cost(
                2 * dists * rows_dev * width * width, (width, width), (2, dists, rows_dev, width)
            ),
            name="row_spectra",
        )(mine, partner, table)
        arrived.append(spread(pieces, send_order))

    gain = pl.pallas_call(
        lambda *refs: filter_kernel(inner, dist_dev, *refs),
        out_shape=shaped(dists, width, block),
        in_specs=smem(1) + unread(1),
        out_specs=one_out,
        compiler_params=params,
        cost_estimate=cost(32 * width * block, (dists, width, block)),
        name="filters",
    )(propagation, pieces[0])

    sums = []
    for chunk in range(own):
        keep, *away = pl.pallas_call(
            lambda *refs: column_kernel(inner, outer, *refs),
            out_shape=[shaped(outer // 2, depth, block)]
            + [shaped(outer // 2, depth, block // splits)] * splits,
            in_specs=vmem(2 + inner),
            out_specs=vmem(1 + splits),
            scratch_shapes=[
                pltpu.VMEM((dists, depth, block), bf16),
                pltpu.VMEM((width, block), f32),
                pltpu.VMEM((width, block), bf16),
            ],
            compiler_params=params,
            cost_estimate=cost(
                2 * width * block * (dists * depth + width), (width, width), (dists, width, block)
            ),
            name="columns",
        )(table, gain, *arrived[chunk])
        parts = [keep]
        for split in range(splits):
            joint = pl.pallas_call(
                add_kernel,
                out_shape=shaped(outer // 2, depth, block // splits),
                in_specs=vmem(2),
                out_specs=one_out,
                compiler_params=params,
                cost_estimate=cost(1, (8, width)),
                name="joint",
            )(away[split], sent(away[split], to_near_plane))
            across = sent(joint, to_middle)
            near = pl.pallas_call(
                lambda *refs, split=split: near_kernel(inner, split, *refs),
                out_shape=shaped(depth, block // splits),
                in_specs=vmem(2),
                out_specs=one_out,
                compiler_params=params,
                cost_estimate=cost(1, (8, width)),
                name="near",
            )(keep, across)
            parts += [across, sent(near, to_near_plane)]
        sums.append(parts)

    total = None
    for chunk in range(own):
        first, second = pl.pallas_call(
            lambda *refs: half_kernel(inner, *refs),
            out_shape=[shaped(capacity, block)] * 2,
            in_specs=vmem(1 + 2 * splits),
            out_specs=vmem(2),
            compiler_params=params,
            cost_estimate=cost(1, (8, width)),
            name="half",
        )(*sums[chunk])
        pieces = spread([first, first, second, second], tail_order)
        phase = pl.pallas_call(
            lambda *refs: phase_kernel(inner, *refs),
            out_shape=shaped(capacity, width),
            in_specs=vmem(1 + inner),
            out_specs=one_out,
            scratch_shapes=[pltpu.VMEM((capacity, width), bf16)],
            compiler_params=params,
            cost_estimate=cost(1, (8, width)),
            name="phase",
        )(table, *pieces)
        there = sent(phase, to_other_core)
        if chunk < own - 1:
            total = pl.pallas_call(
                lambda *refs, chunk=chunk: recon_kernel(own, chunk, (0, 1), *refs),
                out_shape=jax.ShapeDtypeStruct((capacity, pixels), f32),
                in_specs=smem(1) + vmem(3),
                out_specs=one_out,
                compiler_params=params,
                cost_estimate=cost(1, (8, width)),
                name="recon",
            )(angle_order, weights, phase, there)
        else:
            total, chosen, select = pl.pallas_call(
                lambda *refs, chunk=chunk: recon_next_kernel(own, chunk, *refs),
                out_shape=[
                    jax.ShapeDtypeStruct((capacity, pixels), f32),
                    shaped(width, pixels),
                    shaped(capacity, capacity),
                ],
                in_specs=smem(2) + vmem(3),
                out_specs=vmem(3),
                compiler_params=params,
                cost_estimate=cost(1, (8, width)),
                name="recon",
            )(angle_order, slab_rows, weights, phase, total)
            total = pl.pallas_call(
                recon_last_kernel,
                out_shape=shaped(capacity, pixels),
                in_specs=vmem(4),
                out_specs=one_out,
                compiler_params=params,
                cost_estimate=cost(1, (8, width)),
                name="recon",
            )(chosen, there, total, select)
    return total


def on_device(holograms, propagation, weights, angle_order, slab_rows):
    mbatch, angles, dist_dev, rows_dev, width = holograms.shape
    groups = lax.axis_size("rows")
    inner = 2 ** (int(math.log2(groups)) // 2)
    block = width // inner
    fits = (
        inner * (groups // inner) == groups
        and rows_dev % 16 == 0
        and block % 128 == 0
        and inner * rows_dev % 128 == 0
        and inner == 4
        and groups == inner * inner
        and lax.axis_size("dist") == 2
        and angles == 2 * lax.axis_size("dist")
    )
    if fits:
        return plane_plan(inner, holograms, propagation, weights, angle_order, slab_rows)
    return flat_plan(holograms, propagation, weights, angle_order, slab_rows)


def solution(mesh):
    return jax.shard_map(
        on_device,
        mesh=mesh,
        in_specs=(P(None, None, "dist", "rows", None), P(), P(None, None, "dist"), P(), P()),
        out_specs=P("rows", "dist"),
        check_vma=False,
    )
```

```python
import math

import jax
import jax.numpy as jnp
import numpy as np
from jax import lax
from jax.experimental import pallas as pl
from jax.experimental.pallas import tpu as pltpu
from jax.sharding import PartitionSpec as P

absorb_ratio = 0.1
regularizer = 0.05
bf16 = jnp.bfloat16
f32 = jnp.float32
send_order = (0, 1, 2, 3)
tail_order = (0, 1, 3, 2)


def hartley(length):
    index = np.arange(length)
    turned = (index[:, None] * index[None, :] % length) * (2.0 * math.pi / length)
    table = (np.cos(turned) + np.sin(turned)) / math.sqrt(length)
    return table.astype(bf16)


def signed_square(index, length):
    signed = jnp.where(index < length // 2, index, index - length).astype(f32)
    return signed * signed / float(length * length)


def filters(propagation, rows_sq, cols_sq):
    first = propagation[:, None] * rows_sq[None]
    second = propagation[:, None] * cols_sq[None]
    sin_b, cos_b = jnp.sin(second), jnp.cos(second)
    with_sin = 2.0 * (cos_b - absorb_ratio * sin_b)
    with_cos = 2.0 * (sin_b + absorb_ratio * cos_b)
    transfer = (
        jnp.sin(first)[:, :, None] * with_sin[:, None, :]
        + jnp.cos(first)[:, :, None] * with_cos[:, None, :]
    )
    denom = jnp.sum(transfer * transfer, axis=0) + regularizer
    return transfer / denom


def flat_plan(holograms, propagation, weights, angle_order, slab_rows):
    mbatch, angles, dist_dev, rows_dev, width = holograms.shape
    groups = lax.axis_size("rows")
    cores = lax.axis_size("dist")
    capacity = 2 * rows_dev
    own = angles // cores
    cols = width // groups
    dists = dist_dev * cores
    device = lax.axis_index("rows")
    table = jnp.asarray(hartley(width))
    index = jnp.arange(width, dtype=jnp.int32)
    my_cols = device * cols + jnp.arange(cols, dtype=jnp.int32)
    gain = filters(propagation, signed_square(my_cols, width), signed_square(index, width))

    mine = lax.all_to_all(holograms[0], "dist", split_axis=0, concat_axis=1, tiled=True)
    flat = mine.reshape(own * dists * rows_dev, width)
    spec = jnp.einsum("kx,mx->km", table, flat, preferred_element_type=f32)
    spec = spec.astype(bf16).reshape(groups, cols, own * dists * rows_dev)
    spec = lax.all_to_all(spec, "rows", split_axis=0, concat_axis=0, tiled=True)
    spec = spec.reshape(groups, cols, own, dists, rows_dev).transpose(1, 2, 3, 0, 4)
    spec = spec.reshape(cols * own * dists, width)
    full = jnp.dot(spec, table, preferred_element_type=f32)
    full = full.reshape(cols, own, dists, width)
    full = jnp.sum(full * gain.transpose(1, 0, 2)[:, None], axis=2).astype(bf16)
    half = jnp.einsum("yq,akq->yak", table, full.transpose(1, 0, 2), preferred_element_type=f32)
    half = half.astype(bf16).reshape(groups, rows_dev, own * cols)
    half = lax.all_to_all(half, "rows", split_axis=0, concat_axis=0, tiled=True)
    half = half.reshape(groups, rows_dev, own, cols).transpose(2, 1, 0, 3)
    half = half.reshape(own * rows_dev, width)
    phase = jnp.dot(half, table, preferred_element_type=f32)
    phase = phase.astype(bf16).reshape(own, rows_dev, width)
    phase = lax.all_gather(phase, "dist", axis=0, tiled=True)
    place = (angle_order[0][None, :] == jnp.arange(angles)[:, None]).astype(bf16)
    phase = jnp.einsum("wa,ayx->wyx", place, phase, preferred_element_type=f32)
    recon = jnp.einsum(
        "wyx,wxp->yp", phase.astype(bf16), weights, preferred_element_type=f32
    ).astype(bf16)
    parity = device % 2
    offset = parity * slab_rows[device - parity]
    count = slab_rows[device]
    pairs = [(source, source ^ 1) for source in range(groups)]
    partner = lax.ppermute(recon, "rows", pairs)
    lower = jnp.where(parity == 1, partner, recon)
    upper = jnp.where(parity == 1, recon, partner)
    paired = jnp.concatenate([lower, upper], axis=0)
    slot = jnp.arange(capacity, dtype=jnp.int32)[:, None]
    source = jnp.arange(capacity, dtype=jnp.int32)[None, :]
    select = ((source == offset + slot) & (slot < count)).astype(bf16)
    return jnp.dot(select, paired, preferred_element_type=f32).astype(bf16)


def position(inner):
    device = lax.axis_index("rows")
    return lax.axis_index("dist"), device // inner, device % inner


def row_kernel(inner, chunk, here, there, table, *outs):
    core, _, spot = position(inner)
    own, dist_dev, rows_dev, width = here.shape
    block = width // inner
    partner = there[core * own + chunk]
    flat = jnp.concatenate(
        [source.reshape(dist_dev * rows_dev, width) for source in (here[chunk], partner)], axis=0
    )
    for rel in range(inner):
        part = table[:, pl.ds(pl.multiple_of((spot ^ rel) * block, block), block)]
        got = jnp.dot(flat, part, preferred_element_type=f32).astype(bf16)
        outs[rel][...] = got.reshape(2 * dist_dev, rows_dev, block)


def whole_turns(scale, square):
    turns = scale * square
    return (turns - jnp.round(turns)) * (2.0 * math.pi)


def filter_kernel(inner, turns, holo, out, mine, arrived):
    dists, width, block = out.shape
    own, dist_dev = mine.shape[:2]
    core, _, spot = position(inner)
    copy = pltpu.make_async_copy(holo.at[pl.ds(core * own, own)], mine, arrived)
    copy.start()

    def square(first, length):
        index = lax.broadcasted_iota(jnp.int32, (1, length), 1) + first
        signed = jnp.where(index < width // 2, index, index - width).astype(f32)
        return signed * signed * (1.0 / (width * width))

    def phases(first, length):
        values = square(first, length)
        rows = []
        for d in range(dists):
            other = d // dist_dev
            scale = turns[(core ^ other) * dist_dev + d % dist_dev]
            rows.append(whole_turns(scale, values))
        return jnp.concatenate(rows, axis=0)

    along = phases(0, width)
    across = phases(spot * block, block)
    sin_b, cos_b = jnp.sin(across), jnp.cos(across)
    with_sin = 2.0 * (cos_b - absorb_ratio * sin_b)
    with_cos = 2.0 * (sin_b + absorb_ratio * cos_b)
    turned = jnp.concatenate([jnp.sin(along), jnp.cos(along)], axis=0).T
    step = 128
    for at in range(0, width, step):
        rows = turned[at : at + step]
        transfer = [
            rows[:, d : d + 1] * with_sin[d : d + 1, :]
            + rows[:, dists + d : dists + d + 1] * with_cos[d : d + 1, :]
            for d in range(dists)
        ]
        denom = transfer[0] * transfer[0]
        for value in transfer[1:]:
            denom = denom + value * value
        scale = 1.0 / (denom + regularizer)
        for d in range(dists):
            out[d, at : at + step, :] = (transfer[d] * scale).astype(bf16)
    copy.wait()


def column_kernel(inner, outer, table, gain, *refs):
    pieces = dict(zip(send_order, refs[:inner]))
    keep, *away = refs[inner:-3]
    stack, total, spectrum = refs[-3:]
    _, plane, spot = position(inner)
    dists, rows_dev, block = pieces[0].shape
    depth = inner * rows_dev
    for rel in range(inner):
        start = pl.multiple_of((spot ^ rel) * rows_dev, rows_dev)
        for d in range(dists):
            stack[d, pl.ds(start, rows_dev), :] = pieces[rel][d]
    part = table[:, pl.ds(pl.multiple_of(plane * depth, depth), depth)]
    for d in range(dists):
        got = jnp.dot(part, stack[d], preferred_element_type=f32) * gain[d].astype(f32)
        if d == 0:
            total[...] = got
        else:
            total[...] += got
    spectrum[...] = total[...].astype(bf16)
    half = outer // 2
    side = plane // half

    def rows_from(low):
        rows = pl.ds(pl.multiple_of(low * depth, half * depth), half * depth)
        value = jnp.dot(table[rows, :], spectrum[...], preferred_element_type=f32)
        return value.astype(bf16).reshape(half, depth, block)

    value = rows_from((1 - side) * half)
    wide = block // len(away)
    for split, out in enumerate(away):
        out[...] = value[:, :, split * wide : (split + 1) * wide]
    keep[...] = rows_from(side * half)


def add_kernel(one, two, out):
    out[...] = (one[...].astype(f32) + two[...].astype(f32)).astype(bf16)


def near_kernel(inner, split, keep, across, out):
    _, plane, _ = position(inner)
    which = (plane ^ 1) % 2
    inside = (plane == 1) | (plane == 2)
    more = jnp.where(inside, across[which].astype(f32), 0.0)
    wide = out.shape[1]
    here = keep[which, :, split * wide : (split + 1) * wide].astype(f32)
    out[...] = (here + more).astype(bf16)


def half_kernel(inner, keep, *refs):
    mine, other = refs[-2:]
    parts = refs[:-2]
    splits = len(parts) // 2
    _, plane, spot = position(inner)
    which = plane % 2
    inside = (plane == 1) | (plane == 2)
    capacity = mine.shape[0]
    wide = mine.shape[1] // splits
    for split in range(splits):
        across, last = parts[2 * split : 2 * split + 2]
        lanes = slice(split * wide, (split + 1) * wide)
        for out, pair in ((mine, spot // 2), (other, 1 - spot // 2)):
            rows = pl.ds(pl.multiple_of(pair * capacity, capacity), capacity)
            more = jnp.where(inside, across[which, rows, :].astype(f32), 0.0)
            got = keep[which, rows, lanes].astype(f32) + more + last[rows, :].astype(f32)
            out[:, lanes] = got.astype(bf16)


def phase_kernel(inner, table, *refs):
    pieces = dict(zip(tail_order, refs[:inner]))
    out, joined = refs[-2:]
    _, _, spot = position(inner)
    block = refs[0].shape[1]
    for rel in range(inner):
        columns = pl.ds(pl.multiple_of((spot ^ rel) * block, block), block)
        joined[:, columns] = pieces[rel][...]
    out[...] = jnp.dot(joined[...], table[...], preferred_element_type=f32).astype(bf16)


def recon_kernel(own, order, slabs, weights, *refs):
    phases = refs[: 2 * own - 1]
    out, chosen, select = refs[2 * own - 1 :]
    core = lax.axis_index("dist")
    device = lax.axis_index("rows")
    total = None
    for step, phase in enumerate(phases):
        here = weights[order[0, (core ^ (step % 2)) * own + step // 2]]
        got = jnp.dot(phase[...], here, preferred_element_type=f32)
        total = got if total is None else total + got
    out[...] = total
    chosen[...] = weights[order[0, (core ^ 1) * own + own - 1]]
    parity = device % 2
    offset = parity * slabs[device - parity]
    slot = lax.broadcasted_iota(jnp.int32, select.shape, 0)
    source = lax.broadcasted_iota(jnp.int32, select.shape, 1)
    picked = (source == slot + offset) & (slot < slabs[device])
    select[...] = jnp.where(picked, 1.0, 0.0).astype(bf16)


def recon_last_kernel(weights, phase, before, select, out):
    total = before[...] + jnp.dot(phase[...], weights[...], preferred_element_type=f32)
    got = jnp.dot(select[...], total.astype(bf16), preferred_element_type=f32)
    out[...] = got.astype(bf16)


def vmem(count):
    return [pl.BlockSpec(memory_space=pltpu.VMEM)] * count


def from_hbm(value):
    return pltpu.with_memory_space_constraint(value, pltpu.HBM)


def in_hbm(count):
    return [pl.BlockSpec(memory_space=pltpu.HBM)] * count


def unread(count):
    return [pl.BlockSpec(memory_space=pl.ANY)] * count


def smem(count):
    return [pl.BlockSpec(memory_space=pltpu.SMEM)] * count


def plane_plan(inner, holograms, propagation, weights, angle_order, slab_rows):
    mbatch, angles, dist_dev, rows_dev, width = holograms.shape
    groups = lax.axis_size("rows")
    cores = lax.axis_size("dist")
    outer = groups // inner
    own = angles // cores
    block = width // inner
    depth = inner * rows_dev
    dists = cores * dist_dev
    pixels = weights.shape[2]
    capacity = 2 * rows_dev
    splits = block // 128
    params = pltpu.CompilerParams(vmem_limit_bytes=16 * 2**20)
    one_out = pl.BlockSpec(memory_space=pltpu.VMEM)

    cheap = pl.CostEstimate(flops=1, bytes_accessed=1, transcendentals=0)

    def shaped(*shape):
        return jax.ShapeDtypeStruct(shape, bf16)

    table = jnp.asarray(hartley(width))

    def sent(value, target):
        pairs = []
        for c in range(cores):
            for r in range(groups):
                to_core, to_row = target(c, r)
                pairs.append((c * groups + r, to_core * groups + to_row))
        return lax.ppermute(value, ("dist", "rows"), pairs)

    def to_other_core(c, r):
        return c ^ 1, r

    def to_spot(rel):
        return lambda c, r: (c, r ^ rel)

    def spread(pieces, order):
        return [sent(pieces[rel], to_spot(rel)) if rel else pieces[rel] for rel in order]

    def to_near_plane(c, r):
        return c, (r // inner ^ 1) * inner + r % inner

    def to_middle(c, r):
        z = r // inner
        return (c, (3 - z) * inner + r % inner) if z in (1, 2) else (c ^ 1, r)

    partner = sent(holograms[0], to_other_core)
    gain, mine = pl.pallas_call(
        lambda *refs: filter_kernel(inner, *refs),
        out_shape=[
            shaped(dists, width, block),
            shaped(own, dist_dev, rows_dev, width),
        ],
        in_specs=smem(1) + in_hbm(1),
        out_specs=vmem(2),
        scratch_shapes=[pltpu.SemaphoreType.DMA],
        compiler_params=params,
        cost_estimate=cheap,
        name="filters",
    )(propagation * (0.5 / math.pi), from_hbm(holograms[0]))
    arrived = []
    for chunk in range(own):
        pieces = pl.pallas_call(
            lambda *refs, chunk=chunk: row_kernel(inner, chunk, *refs),
            out_shape=[shaped(dists, rows_dev, block)] * inner,
            in_specs=vmem(3),
            out_specs=vmem(inner),
            compiler_params=params,
            cost_estimate=cheap,
            name="row_spectra",
        )(mine, partner, table)
        arrived.append(spread(pieces, send_order))

    sums = []
    for chunk in range(own):
        keep, *away = pl.pallas_call(
            lambda *refs: column_kernel(inner, outer, *refs),
            out_shape=[shaped(outer // 2, depth, block)]
            + [shaped(outer // 2, depth, block // splits)] * splits,
            in_specs=vmem(2 + inner),
            out_specs=vmem(1 + splits),
            scratch_shapes=[
                pltpu.VMEM((dists, depth, block), bf16),
                pltpu.VMEM((width, block), f32),
                pltpu.VMEM((width, block), bf16),
            ],
            compiler_params=params,
            cost_estimate=cheap,
            name="columns",
        )(table, gain, *arrived[chunk])
        parts = [keep]
        for split in range(splits):
            joint = pl.pallas_call(
                add_kernel,
                out_shape=shaped(outer // 2, depth, block // splits),
                in_specs=vmem(2),
                out_specs=one_out,
                compiler_params=params,
                cost_estimate=cheap,
                name="joint",
            )(away[split], sent(away[split], to_near_plane))
            across = sent(joint, to_middle)
            near = pl.pallas_call(
                lambda *refs, split=split: near_kernel(inner, split, *refs),
                out_shape=shaped(depth, block // splits),
                in_specs=vmem(2),
                out_specs=one_out,
                compiler_params=params,
                cost_estimate=cheap,
                name="near",
            )(keep, across)
            parts += [across, sent(near, to_near_plane)]
        sums.append(parts)

    phases = []
    for chunk in range(own):
        first, second = pl.pallas_call(
            lambda *refs: half_kernel(inner, *refs),
            out_shape=[shaped(capacity, block)] * 2,
            in_specs=vmem(1 + 2 * splits),
            out_specs=vmem(2),
            compiler_params=params,
            cost_estimate=cheap,
            name="half",
        )(*sums[chunk])
        pieces = spread([first, first, second, second], tail_order)
        phase = pl.pallas_call(
            lambda *refs: phase_kernel(inner, *refs),
            out_shape=shaped(capacity, width),
            in_specs=vmem(1 + inner),
            out_specs=one_out,
            scratch_shapes=[pltpu.VMEM((capacity, width), bf16)],
            compiler_params=params,
            cost_estimate=cheap,
            name="phase",
        )(table, *pieces)
        phases += [phase, sent(phase, to_other_core)]

    total, chosen, select = pl.pallas_call(
        lambda *refs: recon_kernel(own, *refs),
        out_shape=[
            jax.ShapeDtypeStruct((capacity, pixels), f32),
            shaped(width, pixels),
            shaped(capacity, capacity),
        ],
        in_specs=smem(2) + vmem(2 * own),
        out_specs=vmem(3),
        compiler_params=params,
        cost_estimate=cheap,
        name="recon",
    )(angle_order, slab_rows, weights, *phases[:-1])
    return pl.pallas_call(
        recon_last_kernel,
        out_shape=shaped(capacity, pixels),
        in_specs=vmem(4),
        out_specs=one_out,
        compiler_params=params,
        cost_estimate=cheap,
        name="recon",
    )(chosen, phases[-1], total, select)


def on_device(holograms, propagation, weights, angle_order, slab_rows):
    mbatch, angles, dist_dev, rows_dev, width = holograms.shape
    groups = lax.axis_size("rows")
    inner = 2 ** (int(math.log2(groups)) // 2)
    block = width // inner
    fits = (
        inner * (groups // inner) == groups
        and rows_dev % 16 == 0
        and block % 128 == 0
        and inner * rows_dev % 128 == 0
        and inner == 4
        and groups == inner * inner
        and lax.axis_size("dist") == 2
        and angles == 2 * lax.axis_size("dist")
    )
    if fits:
        return plane_plan(inner, holograms, propagation, weights, angle_order, slab_rows)
    return flat_plan(holograms, propagation, weights, angle_order, slab_rows)


def solution(mesh):
    return jax.shard_map(
        on_device,
        mesh=mesh,
        in_specs=(P(None, None, "dist", "rows", None), P(), P(None, None, "dist"), P(), P()),
        out_specs=P("rows", "dist"),
        check_vma=False,
    )
```

```python
import math

import jax
import jax.numpy as jnp
import numpy as np
from jax import lax
from jax.experimental import pallas as pl
from jax.experimental.pallas import tpu as pltpu
from jax.sharding import PartitionSpec as P

absorb_ratio = 0.1
regularizer = 0.05
bf16 = jnp.bfloat16
f32 = jnp.float32
send_order = (0, 2, 1, 3)
tail_order = (0, 1, 3, 2)


def hartley(length):
    index = np.arange(length)
    turned = (index[:, None] * index[None, :] % length) * (2.0 * math.pi / length)
    table = (np.cos(turned) + np.sin(turned)) / math.sqrt(length)
    return table.astype(bf16)


def signed_square(index, length):
    signed = jnp.where(index < length // 2, index, index - length).astype(f32)
    return signed * signed / float(length * length)


def filters(propagation, rows_sq, cols_sq):
    first = propagation[:, None] * rows_sq[None]
    second = propagation[:, None] * cols_sq[None]
    sin_b, cos_b = jnp.sin(second), jnp.cos(second)
    with_sin = 2.0 * (cos_b - absorb_ratio * sin_b)
    with_cos = 2.0 * (sin_b + absorb_ratio * cos_b)
    transfer = (
        jnp.sin(first)[:, :, None] * with_sin[:, None, :]
        + jnp.cos(first)[:, :, None] * with_cos[:, None, :]
    )
    denom = jnp.sum(transfer * transfer, axis=0) + regularizer
    return transfer / denom


def flat_plan(holograms, propagation, weights, angle_order, slab_rows):
    mbatch, angles, dist_dev, rows_dev, width = holograms.shape
    groups = lax.axis_size("rows")
    cores = lax.axis_size("dist")
    capacity = 2 * rows_dev
    own = angles // cores
    cols = width // groups
    dists = dist_dev * cores
    device = lax.axis_index("rows")
    table = jnp.asarray(hartley(width))
    index = jnp.arange(width, dtype=jnp.int32)
    my_cols = device * cols + jnp.arange(cols, dtype=jnp.int32)
    gain = filters(propagation, signed_square(my_cols, width), signed_square(index, width))

    mine = lax.all_to_all(holograms[0], "dist", split_axis=0, concat_axis=1, tiled=True)
    flat = mine.reshape(own * dists * rows_dev, width)
    spec = jnp.einsum("kx,mx->km", table, flat, preferred_element_type=f32)
    spec = spec.astype(bf16).reshape(groups, cols, own * dists * rows_dev)
    spec = lax.all_to_all(spec, "rows", split_axis=0, concat_axis=0, tiled=True)
    spec = spec.reshape(groups, cols, own, dists, rows_dev).transpose(1, 2, 3, 0, 4)
    spec = spec.reshape(cols * own * dists, width)
    full = jnp.dot(spec, table, preferred_element_type=f32)
    full = full.reshape(cols, own, dists, width)
    full = jnp.sum(full * gain.transpose(1, 0, 2)[:, None], axis=2).astype(bf16)
    half = jnp.einsum("yq,akq->yak", table, full.transpose(1, 0, 2), preferred_element_type=f32)
    half = half.astype(bf16).reshape(groups, rows_dev, own * cols)
    half = lax.all_to_all(half, "rows", split_axis=0, concat_axis=0, tiled=True)
    half = half.reshape(groups, rows_dev, own, cols).transpose(2, 1, 0, 3)
    half = half.reshape(own * rows_dev, width)
    phase = jnp.dot(half, table, preferred_element_type=f32)
    phase = phase.astype(bf16).reshape(own, rows_dev, width)
    phase = lax.all_gather(phase, "dist", axis=0, tiled=True)
    place = (angle_order[0][None, :] == jnp.arange(angles)[:, None]).astype(bf16)
    phase = jnp.einsum("wa,ayx->wyx", place, phase, preferred_element_type=f32)
    recon = jnp.einsum(
        "wyx,wxp->yp", phase.astype(bf16), weights, preferred_element_type=f32
    ).astype(bf16)
    parity = device % 2
    offset = parity * slab_rows[device - parity]
    count = slab_rows[device]
    pairs = [(source, source ^ 1) for source in range(groups)]
    partner = lax.ppermute(recon, "rows", pairs)
    lower = jnp.where(parity == 1, partner, recon)
    upper = jnp.where(parity == 1, recon, partner)
    paired = jnp.concatenate([lower, upper], axis=0)
    slot = jnp.arange(capacity, dtype=jnp.int32)[:, None]
    source = jnp.arange(capacity, dtype=jnp.int32)[None, :]
    select = ((source == offset + slot) & (slot < count)).astype(bf16)
    return jnp.dot(select, paired, preferred_element_type=f32).astype(bf16)


def position(inner):
    device = lax.axis_index("rows")
    return lax.axis_index("dist"), device // inner, device % inner


def row_kernel(inner, chunk, holo, there, table, after, *refs):
    outs, flat, loaded = refs[:inner], refs[inner], refs[inner + 1]
    core, _, spot = position(inner)
    angles, dist_dev, rows_dev, width = there.shape
    block = width // inner
    angle = core * (angles // 2) + chunk
    copy = pltpu.make_async_copy(holo.at[angle], flat.at[pl.ds(0, dist_dev)], loaded)
    copy.start()
    flat[dist_dev:] = there[angle]
    copy.wait()
    rows = flat[...].reshape(2 * dist_dev * rows_dev, width)
    for rel in range(inner):
        part = table[:, pl.ds(pl.multiple_of((spot ^ rel) * block, block), block)]
        got = jnp.dot(rows, part, preferred_element_type=f32).astype(bf16)
        outs[rel][...] = got.reshape(2 * dist_dev, rows_dev, block)


def whole_turns(scale, square):
    turns = scale * square
    return (turns - jnp.round(turns)) * (2.0 * math.pi)


def filter_kernel(inner, dist_dev, turns, out):
    dists, width, block = out.shape
    core, _, spot = position(inner)

    def square(first, length):
        index = lax.broadcasted_iota(jnp.int32, (1, length), 1) + first
        signed = jnp.where(index < width // 2, index, index - width).astype(f32)
        return signed * signed * (1.0 / (width * width))

    def phases(first, length):
        values = square(first, length)
        rows = []
        for d in range(dists):
            other = d // dist_dev
            scale = turns[(core ^ other) * dist_dev + d % dist_dev]
            rows.append(whole_turns(scale, values))
        return jnp.concatenate(rows, axis=0)

    along = phases(0, width)
    across = phases(spot * block, block)
    sin_b, cos_b = jnp.sin(across), jnp.cos(across)
    with_sin = 2.0 * (cos_b - absorb_ratio * sin_b)
    with_cos = 2.0 * (sin_b + absorb_ratio * cos_b)
    turned = jnp.concatenate([jnp.sin(along), jnp.cos(along)], axis=0).T
    step = 128
    for at in range(0, width, step):
        rows = turned[at : at + step]
        transfer = [
            rows[:, d : d + 1] * with_sin[d : d + 1, :]
            + rows[:, dists + d : dists + d + 1] * with_cos[d : d + 1, :]
            for d in range(dists)
        ]
        denom = transfer[0] * transfer[0]
        for value in transfer[1:]:
            denom = denom + value * value
        scale = 1.0 / (denom + regularizer)
        for d in range(dists):
            out[d, at : at + step, :] = (transfer[d] * scale).astype(bf16)


def column_kernel(inner, outer, table, gain, *refs):
    pieces = dict(zip(send_order, refs[:inner]))
    keep, *away = refs[inner:-3]
    stack, total, spectrum = refs[-3:]
    _, plane, spot = position(inner)
    dists, rows_dev, block = pieces[0].shape
    depth = inner * rows_dev
    for rel in range(inner):
        start = pl.multiple_of((spot ^ rel) * rows_dev, rows_dev)
        for d in range(dists):
            stack[d, pl.ds(start, rows_dev), :] = pieces[rel][d]
    part = table[:, pl.ds(pl.multiple_of(plane * depth, depth), depth)]
    for d in range(dists):
        got = jnp.dot(part, stack[d], preferred_element_type=f32) * gain[d].astype(f32)
        if d == 0:
            total[...] = got
        else:
            total[...] += got
    spectrum[...] = total[...].astype(bf16)
    half = outer // 2
    side = plane // half

    def rows_from(low):
        rows = pl.ds(pl.multiple_of(low * depth, half * depth), half * depth)
        value = jnp.dot(table[rows, :], spectrum[...], preferred_element_type=f32)
        return value.astype(bf16).reshape(half, depth, block)

    value = rows_from((1 - side) * half)
    wide = block // len(away)
    for split, out in enumerate(away):
        out[...] = value[:, :, split * wide : (split + 1) * wide]
    keep[...] = rows_from(side * half)


def add_kernel(one, two, out):
    out[...] = (one[...].astype(f32) + two[...].astype(f32)).astype(bf16)


def near_kernel(inner, split, keep, across, out):
    _, plane, _ = position(inner)
    which = (plane ^ 1) % 2
    inside = (plane == 1) | (plane == 2)
    more = jnp.where(inside, across[which].astype(f32), 0.0)
    wide = out.shape[1]
    here = keep[which, :, split * wide : (split + 1) * wide].astype(f32)
    out[...] = (here + more).astype(bf16)


def half_kernel(inner, keep, *refs):
    other, mine = refs[-2:]
    parts = refs[:-2]
    splits = len(parts) // 2
    _, plane, spot = position(inner)
    which = plane % 2
    inside = (plane == 1) | (plane == 2)
    capacity = mine.shape[0]
    wide = mine.shape[1] // splits
    for split in range(splits):
        across, last = parts[2 * split : 2 * split + 2]
        lanes = slice(split * wide, (split + 1) * wide)
        for out, pair in ((mine, spot // 2), (other, 1 - spot // 2)):
            rows = pl.ds(pl.multiple_of(pair * capacity, capacity), capacity)
            more = jnp.where(inside, across[which, rows, :].astype(f32), 0.0)
            got = keep[which, rows, lanes].astype(f32) + more + last[rows, :].astype(f32)
            out[:, lanes] = got.astype(bf16)


def phase_kernel(inner, table, *refs):
    pieces = dict(zip(tail_order, refs[:inner]))
    out, joined = refs[-2:]
    _, _, spot = position(inner)
    block = refs[0].shape[1]
    for rel in range(inner):
        columns = pl.ds(pl.multiple_of((spot ^ rel) * block, block), block)
        joined[:, columns] = pieces[rel][...]
    out[...] = jnp.dot(joined[...], table[...], preferred_element_type=f32).astype(bf16)


def recon_kernel(own, order, slabs, weights, *refs):
    phases = refs[: 2 * own - 1]
    out, chosen, select = refs[2 * own - 1 :]
    core = lax.axis_index("dist")
    device = lax.axis_index("rows")
    total = None
    for step, phase in enumerate(phases):
        here = weights[order[0, (core ^ (step % 2)) * own + step // 2]]
        got = jnp.dot(phase[...], here, preferred_element_type=f32)
        total = got if total is None else total + got
    out[...] = total
    chosen[...] = weights[order[0, (core ^ 1) * own + own - 1]]
    parity = device % 2
    offset = parity * slabs[device - parity]
    slot = lax.broadcasted_iota(jnp.int32, select.shape, 0)
    source = lax.broadcasted_iota(jnp.int32, select.shape, 1)
    picked = (source == slot + offset) & (slot < slabs[device])
    select[...] = jnp.where(picked, 1.0, 0.0).astype(bf16)


def recon_last_kernel(weights, phase, before, select, out):
    total = before[...] + jnp.dot(phase[...], weights[...], preferred_element_type=f32)
    got = jnp.dot(select[...], total.astype(bf16), preferred_element_type=f32)
    out[...] = got.astype(bf16)


def vmem(count):
    return [pl.BlockSpec(memory_space=pltpu.VMEM)] * count


def from_hbm(value):
    return pltpu.with_memory_space_constraint(value, pltpu.HBM)


def in_hbm(count):
    return [pl.BlockSpec(memory_space=pltpu.HBM)] * count


def unread(count):
    return [pl.BlockSpec(memory_space=pl.ANY)] * count


def smem(count):
    return [pl.BlockSpec(memory_space=pltpu.SMEM)] * count


def plane_plan(inner, holograms, propagation, weights, angle_order, slab_rows):
    mbatch, angles, dist_dev, rows_dev, width = holograms.shape
    groups = lax.axis_size("rows")
    cores = lax.axis_size("dist")
    outer = groups // inner
    own = angles // cores
    block = width // inner
    depth = inner * rows_dev
    dists = cores * dist_dev
    pixels = weights.shape[2]
    capacity = 2 * rows_dev
    splits = block // 128
    params = pltpu.CompilerParams(vmem_limit_bytes=16 * 2**20)
    one_out = pl.BlockSpec(memory_space=pltpu.VMEM)

    cheap = pl.CostEstimate(flops=1, bytes_accessed=1, transcendentals=0)

    def shaped(*shape):
        return jax.ShapeDtypeStruct(shape, bf16)

    table = jnp.asarray(hartley(width))

    def sent(value, target):
        pairs = []
        for c in range(cores):
            for r in range(groups):
                to_core, to_row = target(c, r)
                pairs.append((c * groups + r, to_core * groups + to_row))
        return lax.ppermute(value, ("dist", "rows"), pairs)

    def to_other_core(c, r):
        return c ^ 1, r

    def to_spot(rel):
        return lambda c, r: (c, r ^ rel)

    def spread(pieces, order):
        return [sent(pieces[rel], to_spot(rel)) if rel else pieces[rel] for rel in order]

    def to_near_plane(c, r):
        return c, (r // inner ^ 1) * inner + r % inner

    def to_middle(c, r):
        z = r // inner
        return (c, (3 - z) * inner + r % inner) if z in (1, 2) else (c ^ 1, r)

    partner = sent(holograms[0], to_other_core)
    gain = pl.pallas_call(
        lambda *refs: filter_kernel(inner, dist_dev, *refs),
        out_shape=shaped(dists, width, block),
        in_specs=smem(1),
        out_specs=one_out,
        compiler_params=params,
        cost_estimate=cheap,
        name="filters",
    )(propagation * (0.5 / math.pi))
    arrived = []
    for chunk in range(own):
        pieces = pl.pallas_call(
            lambda *refs, chunk=chunk: row_kernel(inner, chunk, *refs),
            out_shape=[shaped(dists, rows_dev, block)] * inner,
            in_specs=in_hbm(1) + vmem(2) + unread(1),
            out_specs=vmem(inner),
            scratch_shapes=[
                pltpu.VMEM((dists, rows_dev, width), bf16),
                pltpu.SemaphoreType.DMA,
            ],
            compiler_params=params,
            cost_estimate=cheap,
            name="row_spectra",
        )(from_hbm(holograms[0]), partner, table, gain)
        arrived.append(spread(pieces, send_order))

    sums = []
    for chunk in range(own):
        keep, *away = pl.pallas_call(
            lambda *refs: column_kernel(inner, outer, *refs),
            out_shape=[shaped(outer // 2, depth, block)]
            + [shaped(outer // 2, depth, block // splits)] * splits,
            in_specs=vmem(2 + inner),
            out_specs=vmem(1 + splits),
            scratch_shapes=[
                pltpu.VMEM((dists, depth, block), bf16),
                pltpu.VMEM((width, block), f32),
                pltpu.VMEM((width, block), bf16),
            ],
            compiler_params=params,
            cost_estimate=cheap,
            name="columns",
        )(table, gain, *arrived[chunk])
        parts = [keep]
        for split in range(splits):
            joint = pl.pallas_call(
                add_kernel,
                out_shape=shaped(outer // 2, depth, block // splits),
                in_specs=vmem(2),
                out_specs=one_out,
                compiler_params=params,
                cost_estimate=cheap,
                name="joint",
            )(away[split], sent(away[split], to_near_plane))
            across = sent(joint, to_middle)
            near = pl.pallas_call(
                lambda *refs, split=split: near_kernel(inner, split, *refs),
                out_shape=shaped(depth, block // splits),
                in_specs=vmem(2),
                out_specs=one_out,
                compiler_params=params,
                cost_estimate=cheap,
                name="near",
            )(keep, across)
            parts += [across, sent(near, to_near_plane)]
        sums.append(parts)

    phases = []
    for chunk in range(own):
        second, first = pl.pallas_call(
            lambda *refs: half_kernel(inner, *refs),
            out_shape=[shaped(capacity, block)] * 2,
            in_specs=vmem(1 + 2 * splits),
            out_specs=vmem(2),
            compiler_params=params,
            cost_estimate=cheap,
            name="half",
        )(*sums[chunk])
        pieces = spread([first, first, second, second], tail_order)
        phase = pl.pallas_call(
            lambda *refs: phase_kernel(inner, *refs),
            out_shape=shaped(capacity, width),
            in_specs=vmem(1 + inner),
            out_specs=one_out,
            scratch_shapes=[pltpu.VMEM((capacity, width), bf16)],
            compiler_params=params,
            cost_estimate=cheap,
            name="phase",
        )(table, *pieces)
        phases += [phase, sent(phase, to_other_core)]

    total, chosen, select = pl.pallas_call(
        lambda *refs: recon_kernel(own, *refs),
        out_shape=[
            jax.ShapeDtypeStruct((capacity, pixels), f32),
            shaped(width, pixels),
            shaped(capacity, capacity),
        ],
        in_specs=smem(2) + vmem(2 * own),
        out_specs=vmem(3),
        compiler_params=params,
        cost_estimate=cheap,
        name="recon",
    )(angle_order, slab_rows, weights, *phases[:-1])
    return pl.pallas_call(
        recon_last_kernel,
        out_shape=shaped(capacity, pixels),
        in_specs=vmem(4),
        out_specs=one_out,
        compiler_params=params,
        cost_estimate=cheap,
        name="recon",
    )(chosen, phases[-1], total, select)


def on_device(holograms, propagation, weights, angle_order, slab_rows):
    mbatch, angles, dist_dev, rows_dev, width = holograms.shape
    groups = lax.axis_size("rows")
    inner = 2 ** (int(math.log2(groups)) // 2)
    block = width // inner
    fits = (
        inner * (groups // inner) == groups
        and rows_dev % 16 == 0
        and block % 128 == 0
        and inner * rows_dev % 128 == 0
        and inner == 4
        and groups == inner * inner
        and lax.axis_size("dist") == 2
        and angles == 2 * lax.axis_size("dist")
    )
    if fits:
        return plane_plan(inner, holograms, propagation, weights, angle_order, slab_rows)
    return flat_plan(holograms, propagation, weights, angle_order, slab_rows)


def solution(mesh):
    return jax.shard_map(
        on_device,
        mesh=mesh,
        in_specs=(P(None, None, "dist", "rows", None), P(), P(None, None, "dist"), P(), P()),
        out_specs=P("rows", "dist"),
        check_vma=False,
    )
```

```python
import math

import jax
import jax.numpy as jnp
import numpy as np
from jax import lax
from jax.experimental import pallas as pl
from jax.experimental.pallas import tpu as pltpu
from jax.sharding import PartitionSpec as P

absorb_ratio = 0.1
regularizer = 0.05
bf16 = jnp.bfloat16
f32 = jnp.float32
send_order = (0, 2, 1, 3)
tail_order = (0, 2, 3, 1)


def hartley(length):
    index = np.arange(length)
    turned = (index[:, None] * index[None, :] % length) * (2.0 * math.pi / length)
    table = (np.cos(turned) + np.sin(turned)) / math.sqrt(length)
    return table.astype(bf16)


def signed_square(index, length):
    signed = jnp.where(index < length // 2, index, index - length).astype(f32)
    return signed * signed / float(length * length)


def filters(propagation, rows_sq, cols_sq):
    first = propagation[:, None] * rows_sq[None]
    second = propagation[:, None] * cols_sq[None]
    sin_b, cos_b = jnp.sin(second), jnp.cos(second)
    with_sin = 2.0 * (cos_b - absorb_ratio * sin_b)
    with_cos = 2.0 * (sin_b + absorb_ratio * cos_b)
    transfer = (
        jnp.sin(first)[:, :, None] * with_sin[:, None, :]
        + jnp.cos(first)[:, :, None] * with_cos[:, None, :]
    )
    denom = jnp.sum(transfer * transfer, axis=0) + regularizer
    return transfer / denom


def flat_plan(holograms, propagation, weights, angle_order, slab_rows):
    mbatch, angles, dist_dev, rows_dev, width = holograms.shape
    groups = lax.axis_size("rows")
    cores = lax.axis_size("dist")
    capacity = 2 * rows_dev
    own = angles // cores
    cols = width // groups
    dists = dist_dev * cores
    device = lax.axis_index("rows")
    table = jnp.asarray(hartley(width))
    index = jnp.arange(width, dtype=jnp.int32)
    my_cols = device * cols + jnp.arange(cols, dtype=jnp.int32)
    gain = filters(propagation, signed_square(my_cols, width), signed_square(index, width))

    mine = lax.all_to_all(holograms[0], "dist", split_axis=0, concat_axis=1, tiled=True)
    flat = mine.reshape(own * dists * rows_dev, width)
    spec = jnp.einsum("kx,mx->km", table, flat, preferred_element_type=f32)
    spec = spec.astype(bf16).reshape(groups, cols, own * dists * rows_dev)
    spec = lax.all_to_all(spec, "rows", split_axis=0, concat_axis=0, tiled=True)
    spec = spec.reshape(groups, cols, own, dists, rows_dev).transpose(1, 2, 3, 0, 4)
    spec = spec.reshape(cols * own * dists, width)
    full = jnp.dot(spec, table, preferred_element_type=f32)
    full = full.reshape(cols, own, dists, width)
    full = jnp.sum(full * gain.transpose(1, 0, 2)[:, None], axis=2).astype(bf16)
    half = jnp.einsum("yq,akq->yak", table, full.transpose(1, 0, 2), preferred_element_type=f32)
    half = half.astype(bf16).reshape(groups, rows_dev, own * cols)
    half = lax.all_to_all(half, "rows", split_axis=0, concat_axis=0, tiled=True)
    half = half.reshape(groups, rows_dev, own, cols).transpose(2, 1, 0, 3)
    half = half.reshape(own * rows_dev, width)
    phase = jnp.dot(half, table, preferred_element_type=f32)
    phase = phase.astype(bf16).reshape(own, rows_dev, width)
    phase = lax.all_gather(phase, "dist", axis=0, tiled=True)
    place = (angle_order[0][None, :] == jnp.arange(angles)[:, None]).astype(bf16)
    phase = jnp.einsum("wa,ayx->wyx", place, phase, preferred_element_type=f32)
    recon = jnp.einsum(
        "wyx,wxp->yp", phase.astype(bf16), weights, preferred_element_type=f32
    ).astype(bf16)
    parity = device % 2
    offset = parity * slab_rows[device - parity]
    count = slab_rows[device]
    pairs = [(source, source ^ 1) for source in range(groups)]
    partner = lax.ppermute(recon, "rows", pairs)
    lower = jnp.where(parity == 1, partner, recon)
    upper = jnp.where(parity == 1, recon, partner)
    paired = jnp.concatenate([lower, upper], axis=0)
    slot = jnp.arange(capacity, dtype=jnp.int32)[:, None]
    source = jnp.arange(capacity, dtype=jnp.int32)[None, :]
    select = ((source == offset + slot) & (slot < count)).astype(bf16)
    return jnp.dot(select, paired, preferred_element_type=f32).astype(bf16)


def position(inner):
    device = lax.axis_index("rows")
    return lax.axis_index("dist"), device // inner, device % inner


def row_kernel(inner, holo, there, table, after, *refs):
    outs, mine, loaded = refs[:-2], refs[-2], refs[-1]
    own = len(outs) // inner
    core, _, spot = position(inner)
    _, dist_dev, rows_dev, width = there.shape
    block = width // inner
    copy = pltpu.make_async_copy(holo.at[pl.ds(core * own, own)], mine, loaded)
    copy.start()
    for first, source in ((dist_dev, there.at[pl.ds(core * own, own)]), (0, mine)):
        if first == 0:
            copy.wait()
        rows = source[...].reshape(own * dist_dev * rows_dev, width)
        for rel in range(inner):
            part = table[:, pl.ds(pl.multiple_of((spot ^ rel) * block, block), block)]
            got = jnp.dot(rows, part, preferred_element_type=f32).astype(bf16)
            got = got.reshape(own, dist_dev, rows_dev, block)
            for chunk in range(own):
                outs[chunk * inner + rel][first : first + dist_dev] = got[chunk]


def whole_turns(scale, square):
    turns = scale * square
    return (turns - jnp.round(turns)) * (2.0 * math.pi)


def filter_kernel(inner, dist_dev, turns, out):
    dists, width, block = out.shape
    core, _, spot = position(inner)

    def square(first, length):
        index = lax.broadcasted_iota(jnp.int32, (1, length), 1) + first
        signed = jnp.where(index < width // 2, index, index - width).astype(f32)
        return signed * signed * (1.0 / (width * width))

    def phases(first, length):
        values = square(first, length)
        rows = []
        for d in range(dists):
            other = d // dist_dev
            scale = turns[(core ^ other) * dist_dev + d % dist_dev]
            rows.append(whole_turns(scale, values))
        return jnp.concatenate(rows, axis=0)

    along = phases(0, width)
    across = phases(spot * block, block)
    sin_b, cos_b = jnp.sin(across), jnp.cos(across)
    with_sin = 2.0 * (cos_b - absorb_ratio * sin_b)
    with_cos = 2.0 * (sin_b + absorb_ratio * cos_b)
    turned = jnp.concatenate([jnp.sin(along), jnp.cos(along)], axis=0).T
    step = 128
    for at in range(0, width, step):
        rows = turned[at : at + step]
        transfer = [
            rows[:, d : d + 1] * with_sin[d : d + 1, :]
            + rows[:, dists + d : dists + d + 1] * with_cos[d : d + 1, :]
            for d in range(dists)
        ]
        denom = transfer[0] * transfer[0]
        for value in transfer[1:]:
            denom = denom + value * value
        scale = 1.0 / (denom + regularizer)
        for d in range(dists):
            out[d, at : at + step, :] = (transfer[d] * scale).astype(bf16)


def column_kernel(inner, outer, table, gain, *refs):
    pieces = dict(zip(send_order, refs[:inner]))
    keep, *away = refs[inner:-3]
    stack, total, spectrum = refs[-3:]
    _, plane, spot = position(inner)
    dists, rows_dev, block = pieces[0].shape
    depth = inner * rows_dev
    for rel in range(inner):
        start = pl.multiple_of((spot ^ rel) * rows_dev, rows_dev)
        for d in range(dists):
            stack[d, pl.ds(start, rows_dev), :] = pieces[rel][d]
    part = table[:, pl.ds(pl.multiple_of(plane * depth, depth), depth)]
    for d in range(dists):
        got = jnp.dot(part, stack[d], preferred_element_type=f32) * gain[d].astype(f32)
        if d == 0:
            total[...] = got
        else:
            total[...] += got
    spectrum[...] = total[...].astype(bf16)
    half = outer // 2
    side = plane // half

    def rows_from(low):
        rows = pl.ds(pl.multiple_of(low * depth, half * depth), half * depth)
        value = jnp.dot(table[rows, :], spectrum[...], preferred_element_type=f32)
        return value.astype(bf16).reshape(half, depth, block)

    value = rows_from((1 - side) * half)
    wide = block // len(away)
    for split, out in enumerate(away):
        out[...] = value[:, :, split * wide : (split + 1) * wide]
    keep[...] = rows_from(side * half)


def add_kernel(one, two, out):
    out[...] = (one[...].astype(f32) + two[...].astype(f32)).astype(bf16)


def near_kernel(inner, split, keep, across, out):
    _, plane, _ = position(inner)
    which = (plane ^ 1) % 2
    inside = (plane == 1) | (plane == 2)
    more = jnp.where(inside, across[which].astype(f32), 0.0)
    wide = out.shape[1]
    here = keep[which, :, split * wide : (split + 1) * wide].astype(f32)
    out[...] = (here + more).astype(bf16)


def half_kernel(inner, keep, *refs):
    other, mine = refs[-2:]
    parts = refs[:-2]
    splits = len(parts) // 2
    _, plane, spot = position(inner)
    which = plane % 2
    inside = (plane == 1) | (plane == 2)
    capacity = mine.shape[0]
    wide = mine.shape[1] // splits
    for split in range(splits):
        across, last = parts[2 * split : 2 * split + 2]
        lanes = slice(split * wide, (split + 1) * wide)
        for out, pair in ((mine, spot // 2), (other, 1 - spot // 2)):
            rows = pl.ds(pl.multiple_of(pair * capacity, capacity), capacity)
            more = jnp.where(inside, across[which, rows, :].astype(f32), 0.0)
            got = keep[which, rows, lanes].astype(f32) + more + last[rows, :].astype(f32)
            out[:, lanes] = got.astype(bf16)


def phase_kernel(inner, table, *refs):
    pieces = dict(zip(tail_order, refs[:inner]))
    out, joined = refs[-2:]
    _, _, spot = position(inner)
    block = refs[0].shape[1]
    for rel in range(inner):
        columns = pl.ds(pl.multiple_of((spot ^ rel) * block, block), block)
        joined[:, columns] = pieces[rel][...]
    out[...] = jnp.dot(joined[...], table[...], preferred_element_type=f32).astype(bf16)


def recon_kernel(own, order, slabs, weights, *refs):
    phases = refs[: 2 * own - 1]
    out, chosen, select = refs[2 * own - 1 :]
    core = lax.axis_index("dist")
    device = lax.axis_index("rows")
    total = None
    for step, phase in enumerate(phases):
        here = weights[order[0, (core ^ (step % 2)) * own + step // 2]]
        got = jnp.dot(phase[...], here, preferred_element_type=f32)
        total = got if total is None else total + got
    out[...] = total
    chosen[...] = weights[order[0, (core ^ 1) * own + own - 1]]
    parity = device % 2
    offset = parity * slabs[device - parity]
    slot = lax.broadcasted_iota(jnp.int32, select.shape, 0)
    source = lax.broadcasted_iota(jnp.int32, select.shape, 1)
    picked = (source == slot + offset) & (slot < slabs[device])
    select[...] = jnp.where(picked, 1.0, 0.0).astype(bf16)


def recon_last_kernel(weights, phase, before, select, out):
    total = before[...] + jnp.dot(phase[...], weights[...], preferred_element_type=f32)
    got = jnp.dot(select[...], total.astype(bf16), preferred_element_type=f32)
    out[...] = got.astype(bf16)


def vmem(count):
    return [pl.BlockSpec(memory_space=pltpu.VMEM)] * count


def from_hbm(value):
    return pltpu.with_memory_space_constraint(value, pltpu.HBM)


def in_hbm(count):
    return [pl.BlockSpec(memory_space=pltpu.HBM)] * count


def unread(count):
    return [pl.BlockSpec(memory_space=pl.ANY)] * count


def smem(count):
    return [pl.BlockSpec(memory_space=pltpu.SMEM)] * count


def plane_plan(inner, holograms, propagation, weights, angle_order, slab_rows):
    mbatch, angles, dist_dev, rows_dev, width = holograms.shape
    groups = lax.axis_size("rows")
    cores = lax.axis_size("dist")
    outer = groups // inner
    own = angles // cores
    block = width // inner
    depth = inner * rows_dev
    dists = cores * dist_dev
    pixels = weights.shape[2]
    capacity = 2 * rows_dev
    splits = block // 128
    params = pltpu.CompilerParams(vmem_limit_bytes=16 * 2**20)
    one_out = pl.BlockSpec(memory_space=pltpu.VMEM)

    cheap = pl.CostEstimate(flops=1, bytes_accessed=1, transcendentals=0)

    def shaped(*shape):
        return jax.ShapeDtypeStruct(shape, bf16)

    table = jnp.asarray(hartley(width))

    def sent(value, target):
        pairs = []
        for c in range(cores):
            for r in range(groups):
                to_core, to_row = target(c, r)
                pairs.append((c * groups + r, to_core * groups + to_row))
        return lax.ppermute(value, ("dist", "rows"), pairs)

    def to_other_core(c, r):
        return c ^ 1, r

    def to_spot(rel):
        return lambda c, r: (c, r ^ rel)

    def spread(pieces, order):
        return [sent(pieces[rel], to_spot(rel)) if rel else pieces[rel] for rel in order]

    def to_near_plane(c, r):
        return c, (r // inner ^ 1) * inner + r % inner

    def to_middle(c, r):
        z = r // inner
        return (c, (3 - z) * inner + r % inner) if z in (1, 2) else (c ^ 1, r)

    partner = sent(holograms[0], to_other_core)
    gain = pl.pallas_call(
        lambda *refs: filter_kernel(inner, dist_dev, *refs),
        out_shape=shaped(dists, width, block),
        in_specs=smem(1),
        out_specs=one_out,
        compiler_params=params,
        cost_estimate=cheap,
        name="filters",
    )(propagation * (0.5 / math.pi))
    pieces = pl.pallas_call(
        lambda *refs: row_kernel(inner, *refs),
        out_shape=[shaped(dists, rows_dev, block)] * (own * inner),
        in_specs=in_hbm(1) + vmem(2) + unread(1),
        out_specs=vmem(own * inner),
        scratch_shapes=[
            pltpu.VMEM((own, dist_dev, rows_dev, width), bf16),
            pltpu.SemaphoreType.DMA,
        ],
        compiler_params=params,
        cost_estimate=cheap,
        name="row_spectra",
    )(from_hbm(holograms[0]), partner, table, gain)
    arrived = [
        spread(pieces[chunk * inner : (chunk + 1) * inner], send_order) for chunk in range(own)
    ]

    sums = []
    for chunk in range(own):
        keep, *away = pl.pallas_call(
            lambda *refs: column_kernel(inner, outer, *refs),
            out_shape=[shaped(outer // 2, depth, block)]
            + [shaped(outer // 2, depth, block // splits)] * splits,
            in_specs=vmem(2 + inner),
            out_specs=vmem(1 + splits),
            scratch_shapes=[
                pltpu.VMEM((dists, depth, block), bf16),
                pltpu.VMEM((width, block), f32),
                pltpu.VMEM((width, block), bf16),
            ],
            compiler_params=params,
            cost_estimate=cheap,
            name="columns",
        )(table, gain, *arrived[chunk])
        parts = [keep]
        for split in range(splits):
            joint = pl.pallas_call(
                add_kernel,
                out_shape=shaped(outer // 2, depth, block // splits),
                in_specs=vmem(2),
                out_specs=one_out,
                compiler_params=params,
                cost_estimate=cheap,
                name="joint",
            )(away[split], sent(away[split], to_near_plane))
            across = sent(joint, to_middle)
            near = pl.pallas_call(
                lambda *refs, split=split: near_kernel(inner, split, *refs),
                out_shape=shaped(depth, block // splits),
                in_specs=vmem(2),
                out_specs=one_out,
                compiler_params=params,
                cost_estimate=cheap,
                name="near",
            )(keep, across)
            parts += [across, sent(near, to_near_plane)]
        sums.append(parts)

    phases = []
    for chunk in range(own):
        second, first = pl.pallas_call(
            lambda *refs: half_kernel(inner, *refs),
            out_shape=[shaped(capacity, block)] * 2,
            in_specs=vmem(1 + 2 * splits),
            out_specs=vmem(2),
            compiler_params=params,
            cost_estimate=cheap,
            name="half",
        )(*sums[chunk])
        pieces = spread([first, first, second, second], tail_order)
        phase = pl.pallas_call(
            lambda *refs: phase_kernel(inner, *refs),
            out_shape=shaped(capacity, width),
            in_specs=vmem(1 + inner),
            out_specs=one_out,
            scratch_shapes=[pltpu.VMEM((capacity, width), bf16)],
            compiler_params=params,
            cost_estimate=cheap,
            name="phase",
        )(table, *pieces)
        phases += [phase, sent(phase, to_other_core)]

    total, chosen, select = pl.pallas_call(
        lambda *refs: recon_kernel(own, *refs),
        out_shape=[
            jax.ShapeDtypeStruct((capacity, pixels), f32),
            shaped(width, pixels),
            shaped(capacity, capacity),
        ],
        in_specs=smem(2) + vmem(2 * own),
        out_specs=vmem(3),
        compiler_params=params,
        cost_estimate=cheap,
        name="recon",
    )(angle_order, slab_rows, weights, *phases[:-1])
    return pl.pallas_call(
        recon_last_kernel,
        out_shape=shaped(capacity, pixels),
        in_specs=vmem(4),
        out_specs=one_out,
        compiler_params=params,
        cost_estimate=cheap,
        name="recon",
    )(chosen, phases[-1], total, select)


def on_device(holograms, propagation, weights, angle_order, slab_rows):
    mbatch, angles, dist_dev, rows_dev, width = holograms.shape
    groups = lax.axis_size("rows")
    inner = 2 ** (int(math.log2(groups)) // 2)
    block = width // inner
    fits = (
        inner * (groups // inner) == groups
        and rows_dev % 16 == 0
        and block % 128 == 0
        and inner * rows_dev % 128 == 0
        and inner == 4
        and groups == inner * inner
        and lax.axis_size("dist") == 2
        and angles == 2 * lax.axis_size("dist")
    )
    if fits:
        return plane_plan(inner, holograms, propagation, weights, angle_order, slab_rows)
    return flat_plan(holograms, propagation, weights, angle_order, slab_rows)


def solution(mesh):
    return jax.shard_map(
        on_device,
        mesh=mesh,
        in_specs=(P(None, None, "dist", "rows", None), P(), P(None, None, "dist"), P(), P()),
        out_specs=P("rows", "dist"),
        check_vma=False,
    )
```

```python
import math

import jax
import jax.numpy as jnp
import numpy as np
from jax import lax
from jax.experimental import pallas as pl
from jax.experimental.pallas import tpu as pltpu
from jax.sharding import PartitionSpec as P

absorb_ratio = 0.1
regularizer = 0.05
bf16 = jnp.bfloat16
f32 = jnp.float32


def hartley(length):
    index = np.arange(length)
    turned = (index[:, None] * index[None, :] % length) * (2.0 * math.pi / length)
    table = (np.cos(turned) + np.sin(turned)) / math.sqrt(length)
    return table.astype(bf16)


def signed_square(index, length):
    signed = jnp.where(index < length // 2, index, index - length).astype(f32)
    return signed * signed / float(length * length)


def filters(propagation, rows_sq, cols_sq):
    first = propagation[:, None] * rows_sq[None]
    second = propagation[:, None] * cols_sq[None]
    sin_b, cos_b = jnp.sin(second), jnp.cos(second)
    with_sin = 2.0 * (cos_b - absorb_ratio * sin_b)
    with_cos = 2.0 * (sin_b + absorb_ratio * cos_b)
    transfer = (
        jnp.sin(first)[:, :, None] * with_sin[:, None, :]
        + jnp.cos(first)[:, :, None] * with_cos[:, None, :]
    )
    denom = jnp.sum(transfer * transfer, axis=0) + regularizer
    return transfer / denom


def flat_plan(holograms, propagation, weights, angle_order, slab_rows):
    mbatch, angles, dist_dev, rows_dev, width = holograms.shape
    groups = lax.axis_size("rows")
    cores = lax.axis_size("dist")
    capacity = 2 * rows_dev
    own = angles // cores
    cols = width // groups
    dists = dist_dev * cores
    device = lax.axis_index("rows")
    table = jnp.asarray(hartley(width))
    index = jnp.arange(width, dtype=jnp.int32)
    my_cols = device * cols + jnp.arange(cols, dtype=jnp.int32)
    gain = filters(propagation, signed_square(my_cols, width), signed_square(index, width))

    mine = lax.all_to_all(holograms[0], "dist", split_axis=0, concat_axis=1, tiled=True)
    flat = mine.reshape(own * dists * rows_dev, width)
    spec = jnp.einsum("kx,mx->km", table, flat, preferred_element_type=f32)
    spec = spec.astype(bf16).reshape(groups, cols, own * dists * rows_dev)
    spec = lax.all_to_all(spec, "rows", split_axis=0, concat_axis=0, tiled=True)
    spec = spec.reshape(groups, cols, own, dists, rows_dev).transpose(1, 2, 3, 0, 4)
    spec = spec.reshape(cols * own * dists, width)
    full = jnp.dot(spec, table, preferred_element_type=f32)
    full = full.reshape(cols, own, dists, width)
    full = jnp.sum(full * gain.transpose(1, 0, 2)[:, None], axis=2).astype(bf16)
    half = jnp.einsum("yq,akq->yak", table, full.transpose(1, 0, 2), preferred_element_type=f32)
    half = half.astype(bf16).reshape(groups, rows_dev, own * cols)
    half = lax.all_to_all(half, "rows", split_axis=0, concat_axis=0, tiled=True)
    half = half.reshape(groups, rows_dev, own, cols).transpose(2, 1, 0, 3)
    half = half.reshape(own * rows_dev, width)
    phase = jnp.dot(half, table, preferred_element_type=f32)
    phase = phase.astype(bf16).reshape(own, rows_dev, width)
    phase = lax.all_gather(phase, "dist", axis=0, tiled=True)
    place = (angle_order[0][None, :] == jnp.arange(angles)[:, None]).astype(bf16)
    phase = jnp.einsum("wa,ayx->wyx", place, phase, preferred_element_type=f32)
    recon = jnp.einsum(
        "wyx,wxp->yp", phase.astype(bf16), weights, preferred_element_type=f32
    ).astype(bf16)
    parity = device % 2
    offset = parity * slab_rows[device - parity]
    count = slab_rows[device]
    pairs = [(source, source ^ 1) for source in range(groups)]
    partner = lax.ppermute(recon, "rows", pairs)
    lower = jnp.where(parity == 1, partner, recon)
    upper = jnp.where(parity == 1, recon, partner)
    paired = jnp.concatenate([lower, upper], axis=0)
    slot = jnp.arange(capacity, dtype=jnp.int32)[:, None]
    source = jnp.arange(capacity, dtype=jnp.int32)[None, :]
    select = ((source == offset + slot) & (slot < count)).astype(bf16)
    return jnp.dot(select, paired, preferred_element_type=f32).astype(bf16)


def position(inner):
    device = lax.axis_index("rows")
    return lax.axis_index("dist"), device // inner, device % inner


def row_kernel(inner, holo, there, table, after, *refs):
    outs, mine, loaded = refs[:-2], refs[-2], refs[-1]
    own = len(outs) // inner
    core, _, spot = position(inner)
    _, dist_dev, rows_dev, width = there.shape
    block = width // inner
    copy = pltpu.make_async_copy(holo.at[pl.ds(core * own, own)], mine, loaded)
    copy.start()
    for first, source in ((dist_dev, there.at[pl.ds(core * own, own)]), (0, mine)):
        if first == 0:
            copy.wait()
        rows = source[...].reshape(own * dist_dev * rows_dev, width)
        for rel in range(inner):
            part = table[:, pl.ds(pl.multiple_of((spot ^ rel) * block, block), block)]
            got = jnp.dot(rows, part, preferred_element_type=f32).astype(bf16)
            got = got.reshape(own, dist_dev, rows_dev, block)
            for chunk in range(own):
                outs[chunk * inner + rel][first : first + dist_dev] = got[chunk]


def whole_turns(scale, square):
    turns = scale * square * (0.5 / math.pi)
    return (turns - jnp.round(turns)) * (2.0 * math.pi)


def filter_kernel(inner, dist_dev, turns, out):
    dists, width, block = out.shape
    core, _, spot = position(inner)

    def square(first, length):
        index = lax.broadcasted_iota(jnp.int32, (1, length), 1) + first
        signed = jnp.where(index < width // 2, index, index - width).astype(f32)
        return signed * signed * (1.0 / (width * width))

    def phases(first, length):
        values = square(first, length)
        rows = []
        for d in range(dists):
            other = d // dist_dev
            scale = turns[(core ^ other) * dist_dev + d % dist_dev]
            rows.append(whole_turns(scale, values))
        return jnp.concatenate(rows, axis=0)

    along = phases(0, width)
    across = phases(spot * block, block)
    sin_b, cos_b = jnp.sin(across), jnp.cos(across)
    with_sin = 2.0 * (cos_b - absorb_ratio * sin_b)
    with_cos = 2.0 * (sin_b + absorb_ratio * cos_b)
    turned = jnp.concatenate([jnp.sin(along), jnp.cos(along)], axis=0).T
    step = 128
    for at in range(0, width, step):
        rows = turned[at : at + step]
        transfer = [
            rows[:, d : d + 1] * with_sin[d : d + 1, :]
            + rows[:, dists + d : dists + d + 1] * with_cos[d : d + 1, :]
            for d in range(dists)
        ]
        denom = transfer[0] * transfer[0]
        for value in transfer[1:]:
            denom = denom + value * value
        scale = 1.0 / (denom + regularizer)
        for d in range(dists):
            out[d, at : at + step, :] = (transfer[d] * scale).astype(bf16)


def column_kernel(inner, outer, table, gain, *refs):
    pieces = refs[:inner]
    keep, *away = refs[inner:-3]
    stack, total, spectrum = refs[-3:]
    _, plane, spot = position(inner)
    dists, rows_dev, block = pieces[0].shape
    depth = inner * rows_dev
    for rel in range(inner):
        start = pl.multiple_of((spot ^ rel) * rows_dev, rows_dev)
        for d in range(dists):
            stack[d, pl.ds(start, rows_dev), :] = pieces[rel][d]
    part = table[:, pl.ds(pl.multiple_of(plane * depth, depth), depth)]
    for d in range(dists):
        got = jnp.dot(part, stack[d], preferred_element_type=f32) * gain[d].astype(f32)
        if d == 0:
            total[...] = got
        else:
            total[...] += got
    spectrum[...] = total[...].astype(bf16)
    half = outer // 2
    side = plane // half

    def rows_from(low):
        rows = pl.ds(pl.multiple_of(low * depth, half * depth), half * depth)
        value = jnp.dot(table[rows, :], spectrum[...], preferred_element_type=f32)
        return value.astype(bf16).reshape(half, depth, block)

    value = rows_from((1 - side) * half)
    wide = block // len(away)
    for split, out in enumerate(away):
        out[...] = value[:, :, split * wide : (split + 1) * wide]
    keep[...] = rows_from(side * half)


def add_kernel(one, two, out):
    out[...] = (one[...].astype(f32) + two[...].astype(f32)).astype(bf16)


def near_kernel(inner, split, keep, across, out):
    _, plane, _ = position(inner)
    which = (plane ^ 1) % 2
    inside = (plane == 1) | (plane == 2)
    more = jnp.where(inside, across[which].astype(f32), 0.0)
    wide = out.shape[1]
    here = keep[which, :, split * wide : (split + 1) * wide].astype(f32)
    out[...] = (here + more).astype(bf16)


def half_kernel(inner, keep, *refs):
    other, mine = refs[-2:]
    parts = refs[:-2]
    splits = len(parts) // 2
    _, plane, spot = position(inner)
    which = plane % 2
    inside = (plane == 1) | (plane == 2)
    capacity = mine.shape[0]
    wide = mine.shape[1] // splits
    for split in range(splits):
        across, last = parts[2 * split : 2 * split + 2]
        lanes = slice(split * wide, (split + 1) * wide)
        for out, pair in ((mine, spot // 2), (other, 1 - spot // 2)):
            rows = pl.ds(pl.multiple_of(pair * capacity, capacity), capacity)
            more = jnp.where(inside, across[which, rows, :].astype(f32), 0.0)
            got = keep[which, rows, lanes].astype(f32) + more + last[rows, :].astype(f32)
            out[:, lanes] = got.astype(bf16)


def phase_kernel(inner, table, *refs):
    pieces = refs[:inner]
    out, joined = refs[-2:]
    _, _, spot = position(inner)
    block = refs[0].shape[1]
    for rel in range(inner):
        columns = pl.ds(pl.multiple_of((spot ^ rel) * block, block), block)
        joined[:, columns] = pieces[rel][...]
    out[...] = jnp.dot(joined[...], table[...], preferred_element_type=f32).astype(bf16)


def recon_kernel(own, order, slabs, weights, *refs):
    phases = refs[: 2 * own - 1]
    out, chosen, select = refs[2 * own - 1 :]
    core = lax.axis_index("dist")
    device = lax.axis_index("rows")
    total = None
    for step, phase in enumerate(phases):
        here = weights[order[0, (core ^ (step % 2)) * own + step // 2]]
        got = jnp.dot(phase[...], here, preferred_element_type=f32)
        total = got if total is None else total + got
    out[...] = total
    chosen[...] = weights[order[0, (core ^ 1) * own + own - 1]]
    parity = device % 2
    offset = parity * slabs[device - parity]
    slot = lax.broadcasted_iota(jnp.int32, select.shape, 0)
    source = lax.broadcasted_iota(jnp.int32, select.shape, 1)
    picked = (source == slot + offset) & (slot < slabs[device])
    select[...] = jnp.where(picked, 1.0, 0.0).astype(bf16)


def recon_last_kernel(weights, phase, before, select, out):
    total = before[...] + jnp.dot(phase[...], weights[...], preferred_element_type=f32)
    got = jnp.dot(select[...], total.astype(bf16), preferred_element_type=f32)
    out[...] = got.astype(bf16)


def vmem(count):
    return [pl.BlockSpec(memory_space=pltpu.VMEM)] * count


def from_hbm(value):
    return pltpu.with_memory_space_constraint(value, pltpu.HBM)


def in_hbm(count):
    return [pl.BlockSpec(memory_space=pltpu.HBM)] * count


def unread(count):
    return [pl.BlockSpec(memory_space=pl.ANY)] * count


def smem(count):
    return [pl.BlockSpec(memory_space=pltpu.SMEM)] * count


def plane_plan(inner, holograms, propagation, weights, angle_order, slab_rows):
    mbatch, angles, dist_dev, rows_dev, width = holograms.shape
    groups = lax.axis_size("rows")
    cores = lax.axis_size("dist")
    outer = groups // inner
    own = angles // cores
    block = width // inner
    depth = inner * rows_dev
    dists = cores * dist_dev
    pixels = weights.shape[2]
    capacity = 2 * rows_dev
    splits = block // 128
    params = pltpu.CompilerParams(vmem_limit_bytes=16 * 2**20)
    one_out = pl.BlockSpec(memory_space=pltpu.VMEM)

    cheap = pl.CostEstimate(flops=1, bytes_accessed=1, transcendentals=0)

    def shaped(*shape):
        return jax.ShapeDtypeStruct(shape, bf16)

    table = jnp.asarray(hartley(width))

    def sent(value, target):
        pairs = []
        for c in range(cores):
            for r in range(groups):
                to_core, to_row = target(c, r)
                pairs.append((c * groups + r, to_core * groups + to_row))
        return lax.ppermute(value, ("dist", "rows"), pairs)

    def to_other_core(c, r):
        return c ^ 1, r

    def to_spot(rel):
        return lambda c, r: (c, r ^ rel)

    def spread(stays, along_x, along_y, diagonal):
        first = sent(diagonal, to_spot(2))
        other = first if along_y is diagonal else sent(along_y, to_spot(2))
        return [stays, sent(along_x, to_spot(1)), other, sent(first, to_spot(1))]

    def to_near_plane(c, r):
        return c, (r // inner ^ 1) * inner + r % inner

    def to_middle(c, r):
        z = r // inner
        return (c, (3 - z) * inner + r % inner) if z in (1, 2) else (c ^ 1, r)

    partner = sent(holograms[0], to_other_core)
    gain = pl.pallas_call(
        lambda *refs: filter_kernel(inner, dist_dev, *refs),
        out_shape=shaped(dists, width, block),
        in_specs=smem(1),
        out_specs=one_out,
        compiler_params=params,
        cost_estimate=cheap,
        name="filters",
    )(from_hbm(propagation))
    pieces = pl.pallas_call(
        lambda *refs: row_kernel(inner, *refs),
        out_shape=[shaped(dists, rows_dev, block)] * (own * inner),
        in_specs=in_hbm(1) + vmem(2) + unread(1),
        out_specs=vmem(own * inner),
        scratch_shapes=[
            pltpu.VMEM((own, dist_dev, rows_dev, width), bf16),
            pltpu.SemaphoreType.DMA,
        ],
        compiler_params=params,
        cost_estimate=cheap,
        name="row_spectra",
    )(from_hbm(holograms[0]), partner, table, gain)
    arrived = [
        spread(*pieces[chunk * inner : (chunk + 1) * inner]) for chunk in range(own)
    ]

    sums = []
    for chunk in range(own):
        keep, *away = pl.pallas_call(
            lambda *refs: column_kernel(inner, outer, *refs),
            out_shape=[shaped(outer // 2, depth, block)]
            + [shaped(outer // 2, depth, block // splits)] * splits,
            in_specs=vmem(2 + inner),
            out_specs=vmem(1 + splits),
            scratch_shapes=[
                pltpu.VMEM((dists, depth, block), bf16),
                pltpu.VMEM((width, block), f32),
                pltpu.VMEM((width, block), bf16),
            ],
            compiler_params=params,
            cost_estimate=cheap,
            name="columns",
        )(table, gain, *arrived[chunk])
        parts = [keep]
        for split in range(splits):
            joint = pl.pallas_call(
                add_kernel,
                out_shape=shaped(outer // 2, depth, block // splits),
                in_specs=vmem(2),
                out_specs=one_out,
                compiler_params=params,
                cost_estimate=cheap,
                name="joint",
            )(away[split], sent(away[split], to_near_plane))
            across = sent(joint, to_middle)
            near = pl.pallas_call(
                lambda *refs, split=split: near_kernel(inner, split, *refs),
                out_shape=shaped(depth, block // splits),
                in_specs=vmem(2),
                out_specs=one_out,
                compiler_params=params,
                cost_estimate=cheap,
                name="near",
            )(keep, across)
            parts += [across, sent(near, to_near_plane)]
        sums.append(parts)

    phases = []
    for chunk in range(own):
        second, first = pl.pallas_call(
            lambda *refs: half_kernel(inner, *refs),
            out_shape=[shaped(capacity, block)] * 2,
            in_specs=vmem(1 + 2 * splits),
            out_specs=vmem(2),
            compiler_params=params,
            cost_estimate=cheap,
            name="half",
        )(*sums[chunk])
        pieces = spread(first, first, second, second)
        phase = pl.pallas_call(
            lambda *refs: phase_kernel(inner, *refs),
            out_shape=shaped(capacity, width),
            in_specs=vmem(1 + inner),
            out_specs=one_out,
            scratch_shapes=[pltpu.VMEM((capacity, width), bf16)],
            compiler_params=params,
            cost_estimate=cheap,
            name="phase",
        )(table, *pieces)
        phases += [phase, sent(phase, to_other_core)]

    total, chosen, select = pl.pallas_call(
        lambda *refs: recon_kernel(own, *refs),
        out_shape=[
            jax.ShapeDtypeStruct((capacity, pixels), f32),
            shaped(width, pixels),
            shaped(capacity, capacity),
        ],
        in_specs=smem(2) + vmem(2 * own),
        out_specs=vmem(3),
        compiler_params=params,
        cost_estimate=cheap,
        name="recon",
    )(angle_order, slab_rows, weights, *phases[:-1])
    return pl.pallas_call(
        recon_last_kernel,
        out_shape=shaped(capacity, pixels),
        in_specs=vmem(4),
        out_specs=one_out,
        compiler_params=params,
        cost_estimate=cheap,
        name="recon",
    )(chosen, phases[-1], total, select)


def on_device(holograms, propagation, weights, angle_order, slab_rows):
    mbatch, angles, dist_dev, rows_dev, width = holograms.shape
    groups = lax.axis_size("rows")
    inner = 2 ** (int(math.log2(groups)) // 2)
    block = width // inner
    fits = (
        inner * (groups // inner) == groups
        and rows_dev % 16 == 0
        and block % 128 == 0
        and inner * rows_dev % 128 == 0
        and inner == 4
        and groups == inner * inner
        and lax.axis_size("dist") == 2
        and angles == 2 * lax.axis_size("dist")
    )
    if fits:
        return plane_plan(inner, holograms, propagation, weights, angle_order, slab_rows)
    return flat_plan(holograms, propagation, weights, angle_order, slab_rows)


def solution(mesh):
    return jax.shard_map(
        on_device,
        mesh=mesh,
        in_specs=(P(None, None, "dist", "rows", None), P(), P(None, None, "dist"), P(), P()),
        out_specs=P("rows", "dist"),
        check_vma=False,
    )
```

```python
import math

import jax
import jax.numpy as jnp
import numpy as np
from jax import lax
from jax.experimental import pallas as pl
from jax.experimental.pallas import tpu as pltpu
from jax.sharding import PartitionSpec as P

absorb_ratio = 0.1
regularizer = 0.05
bf16 = jnp.bfloat16
f32 = jnp.float32


def hartley(length):
    index = np.arange(length)
    turned = (index[:, None] * index[None, :] % length) * (2.0 * math.pi / length)
    table = (np.cos(turned) + np.sin(turned)) / math.sqrt(length)
    return table.astype(bf16)


def signed_square(index, length):
    signed = jnp.where(index < length // 2, index, index - length).astype(f32)
    return signed * signed / float(length * length)


def filters(propagation, rows_sq, cols_sq):
    first = propagation[:, None] * rows_sq[None]
    second = propagation[:, None] * cols_sq[None]
    sin_b, cos_b = jnp.sin(second), jnp.cos(second)
    with_sin = 2.0 * (cos_b - absorb_ratio * sin_b)
    with_cos = 2.0 * (sin_b + absorb_ratio * cos_b)
    transfer = (
        jnp.sin(first)[:, :, None] * with_sin[:, None, :]
        + jnp.cos(first)[:, :, None] * with_cos[:, None, :]
    )
    denom = jnp.sum(transfer * transfer, axis=0) + regularizer
    return transfer / denom


def flat_plan(holograms, propagation, weights, angle_order, slab_rows):
    mbatch, angles, dist_dev, rows_dev, width = holograms.shape
    groups = lax.axis_size("rows")
    cores = lax.axis_size("dist")
    capacity = 2 * rows_dev
    own = angles // cores
    cols = width // groups
    dists = dist_dev * cores
    device = lax.axis_index("rows")
    table = jnp.asarray(hartley(width))
    index = jnp.arange(width, dtype=jnp.int32)
    my_cols = device * cols + jnp.arange(cols, dtype=jnp.int32)
    gain = filters(propagation, signed_square(my_cols, width), signed_square(index, width))

    mine = lax.all_to_all(holograms[0], "dist", split_axis=0, concat_axis=1, tiled=True)
    flat = mine.reshape(own * dists * rows_dev, width)
    spec = jnp.einsum("kx,mx->km", table, flat, preferred_element_type=f32)
    spec = spec.astype(bf16).reshape(groups, cols, own * dists * rows_dev)
    spec = lax.all_to_all(spec, "rows", split_axis=0, concat_axis=0, tiled=True)
    spec = spec.reshape(groups, cols, own, dists, rows_dev).transpose(1, 2, 3, 0, 4)
    spec = spec.reshape(cols * own * dists, width)
    full = jnp.dot(spec, table, preferred_element_type=f32)
    full = full.reshape(cols, own, dists, width)
    full = jnp.sum(full * gain.transpose(1, 0, 2)[:, None], axis=2).astype(bf16)
    half = jnp.einsum("yq,akq->yak", table, full.transpose(1, 0, 2), preferred_element_type=f32)
    half = half.astype(bf16).reshape(groups, rows_dev, own * cols)
    half = lax.all_to_all(half, "rows", split_axis=0, concat_axis=0, tiled=True)
    half = half.reshape(groups, rows_dev, own, cols).transpose(2, 1, 0, 3)
    half = half.reshape(own * rows_dev, width)
    phase = jnp.dot(half, table, preferred_element_type=f32)
    phase = phase.astype(bf16).reshape(own, rows_dev, width)
    phase = lax.all_gather(phase, "dist", axis=0, tiled=True)
    place = (angle_order[0][None, :] == jnp.arange(angles)[:, None]).astype(bf16)
    phase = jnp.einsum("wa,ayx->wyx", place, phase, preferred_element_type=f32)
    recon = jnp.einsum(
        "wyx,wxp->yp", phase.astype(bf16), weights, preferred_element_type=f32
    ).astype(bf16)
    parity = device % 2
    offset = parity * slab_rows[device - parity]
    count = slab_rows[device]
    pairs = [(source, source ^ 1) for source in range(groups)]
    partner = lax.ppermute(recon, "rows", pairs)
    lower = jnp.where(parity == 1, partner, recon)
    upper = jnp.where(parity == 1, recon, partner)
    paired = jnp.concatenate([lower, upper], axis=0)
    slot = jnp.arange(capacity, dtype=jnp.int32)[:, None]
    source = jnp.arange(capacity, dtype=jnp.int32)[None, :]
    select = ((source == offset + slot) & (slot < count)).astype(bf16)
    return jnp.dot(select, paired, preferred_element_type=f32).astype(bf16)


def position(inner):
    device = lax.axis_index("rows")
    return lax.axis_index("dist"), device // inner, device % inner


def row_kernel(inner, holo, there, table, after, *refs):
    outs, mine, loaded = refs[:-2], refs[-2], refs[-1]
    own = len(outs) // inner
    core, _, spot = position(inner)
    _, dist_dev, rows_dev, width = there.shape
    block = width // inner
    copy = pltpu.make_async_copy(holo.at[pl.ds(core * own, own)], mine, loaded)
    copy.start()
    for first, source in ((dist_dev, there.at[pl.ds(core * own, own)]), (0, mine)):
        if first == 0:
            copy.wait()
        rows = source[...].reshape(own * dist_dev * rows_dev, width)
        for rel in range(inner):
            part = table[:, pl.ds(pl.multiple_of((spot ^ rel) * block, block), block)]
            got = jnp.dot(rows, part, preferred_element_type=f32).astype(bf16)
            got = got.reshape(own, dist_dev, rows_dev, block)
            for chunk in range(own):
                outs[chunk * inner + rel][first : first + dist_dev] = got[chunk]


def whole_turns(scale, square):
    turns = scale * square * (0.5 / math.pi)
    return (turns - jnp.round(turns)) * (2.0 * math.pi)


def filter_kernel(inner, dist_dev, turns, out):
    dists, width, block = out.shape
    core, _, spot = position(inner)

    def square(first, length):
        index = lax.broadcasted_iota(jnp.int32, (1, length), 1) + first
        signed = jnp.where(index < width // 2, index, index - width).astype(f32)
        return signed * signed * (1.0 / (width * width))

    def phases(first, length):
        values = square(first, length)
        rows = []
        for d in range(dists):
            other = d // dist_dev
            scale = turns[(core ^ other) * dist_dev + d % dist_dev]
            rows.append(whole_turns(scale, values))
        return jnp.concatenate(rows, axis=0)

    along = phases(0, width)
    across = phases(spot * block, block)
    sin_b, cos_b = jnp.sin(across), jnp.cos(across)
    with_sin = 2.0 * (cos_b - absorb_ratio * sin_b)
    with_cos = 2.0 * (sin_b + absorb_ratio * cos_b)
    turned = jnp.concatenate([jnp.sin(along), jnp.cos(along)], axis=0).T
    step = 128
    for at in range(0, width, step):
        rows = turned[at : at + step]
        transfer = [
            rows[:, d : d + 1] * with_sin[d : d + 1, :]
            + rows[:, dists + d : dists + d + 1] * with_cos[d : d + 1, :]
            for d in range(dists)
        ]
        denom = transfer[0] * transfer[0]
        for value in transfer[1:]:
            denom = denom + value * value
        scale = 1.0 / (denom + regularizer)
        for d in range(dists):
            out[d, at : at + step, :] = (transfer[d] * scale).astype(bf16)


def column_kernel(inner, outer, table, gain, *refs):
    pieces = refs[:inner]
    out, stack, total, spectrum = refs[inner:]
    _, plane, spot = position(inner)
    dists, rows_dev, block = pieces[0].shape
    depth = inner * rows_dev
    for rel in range(inner):
        start = pl.multiple_of((spot ^ rel) * rows_dev, rows_dev)
        for d in range(dists):
            stack[d, pl.ds(start, rows_dev), :] = pieces[rel][d]
    part = table[:, pl.ds(pl.multiple_of(plane * depth, depth), depth)]
    for d in range(dists):
        got = jnp.dot(part, stack[d], preferred_element_type=f32) * gain[d].astype(f32)
        if d == 0:
            total[...] = got
        else:
            total[...] += got
    spectrum[...] = total[...].astype(bf16)
    value = jnp.dot(table[...], spectrum[...], preferred_element_type=f32)
    out[...] = value.astype(bf16).reshape(outer, depth, block)


def half_kernel(inner, half, other, mine):
    _, _, spot = position(inner)
    capacity = mine.shape[0]
    for out, pair in ((mine, spot // 2), (other, 1 - spot // 2)):
        out[...] = half[pl.ds(pl.multiple_of(pair * capacity, capacity), capacity), :]


def phase_kernel(inner, table, *refs):
    pieces = refs[:inner]
    out, joined = refs[-2:]
    _, _, spot = position(inner)
    block = refs[0].shape[1]
    for rel in range(inner):
        columns = pl.ds(pl.multiple_of((spot ^ rel) * block, block), block)
        joined[:, columns] = pieces[rel][...]
    out[...] = jnp.dot(joined[...], table[...], preferred_element_type=f32).astype(bf16)


def recon_kernel(own, order, slabs, weights, *refs):
    phases = refs[: 2 * own - 1]
    out, chosen, select = refs[2 * own - 1 :]
    core = lax.axis_index("dist")
    device = lax.axis_index("rows")
    total = None
    for step, phase in enumerate(phases):
        here = weights[order[0, (core ^ (step % 2)) * own + step // 2]]
        got = jnp.dot(phase[...], here, preferred_element_type=f32)
        total = got if total is None else total + got
    out[...] = total
    chosen[...] = weights[order[0, (core ^ 1) * own + own - 1]]
    parity = device % 2
    offset = parity * slabs[device - parity]
    slot = lax.broadcasted_iota(jnp.int32, select.shape, 0)
    source = lax.broadcasted_iota(jnp.int32, select.shape, 1)
    picked = (source == slot + offset) & (slot < slabs[device])
    select[...] = jnp.where(picked, 1.0, 0.0).astype(bf16)


def recon_last_kernel(weights, phase, before, select, out):
    total = before[...] + jnp.dot(phase[...], weights[...], preferred_element_type=f32)
    got = jnp.dot(select[...], total.astype(bf16), preferred_element_type=f32)
    out[...] = got.astype(bf16)


def vmem(count):
    return [pl.BlockSpec(memory_space=pltpu.VMEM)] * count


def from_hbm(value):
    return pltpu.with_memory_space_constraint(value, pltpu.HBM)


def in_hbm(count):
    return [pl.BlockSpec(memory_space=pltpu.HBM)] * count


def unread(count):
    return [pl.BlockSpec(memory_space=pl.ANY)] * count


def smem(count):
    return [pl.BlockSpec(memory_space=pltpu.SMEM)] * count


def plane_plan(inner, holograms, propagation, weights, angle_order, slab_rows):
    mbatch, angles, dist_dev, rows_dev, width = holograms.shape
    groups = lax.axis_size("rows")
    cores = lax.axis_size("dist")
    outer = groups // inner
    own = angles // cores
    block = width // inner
    depth = inner * rows_dev
    dists = cores * dist_dev
    pixels = weights.shape[2]
    capacity = 2 * rows_dev
    params = pltpu.CompilerParams(vmem_limit_bytes=16 * 2**20)
    one_out = pl.BlockSpec(memory_space=pltpu.VMEM)

    cheap = pl.CostEstimate(flops=1, bytes_accessed=1, transcendentals=0)

    def shaped(*shape):
        return jax.ShapeDtypeStruct(shape, bf16)

    table = jnp.asarray(hartley(width))

    def sent(value, target):
        pairs = []
        for c in range(cores):
            for r in range(groups):
                to_core, to_row = target(c, r)
                pairs.append((c * groups + r, to_core * groups + to_row))
        return lax.ppermute(value, ("dist", "rows"), pairs)

    def to_other_core(c, r):
        return c ^ 1, r

    def to_spot(rel):
        return lambda c, r: (c, r ^ rel)

    def spread(stays, along_x, along_y, diagonal):
        first = sent(diagonal, to_spot(2))
        other = first if along_y is diagonal else sent(along_y, to_spot(2))
        return [stays, sent(along_x, to_spot(1)), other, sent(first, to_spot(1))]

    def direct(stays, along_x, along_y, diagonal):
        first = sent(along_y, to_spot(2))
        return [stays, sent(along_x, to_spot(1)), first, sent(diagonal, to_spot(3))]

    partner = sent(holograms[0], to_other_core)
    gain = pl.pallas_call(
        lambda *refs: filter_kernel(inner, dist_dev, *refs),
        out_shape=shaped(dists, width, block),
        in_specs=smem(1),
        out_specs=one_out,
        compiler_params=params,
        cost_estimate=cheap,
        name="filters",
    )(from_hbm(propagation))
    pieces = pl.pallas_call(
        lambda *refs: row_kernel(inner, *refs),
        out_shape=[shaped(dists, rows_dev, block)] * (own * inner),
        in_specs=in_hbm(1) + vmem(2) + unread(1),
        out_specs=vmem(own * inner),
        scratch_shapes=[
            pltpu.VMEM((own, dist_dev, rows_dev, width), bf16),
            pltpu.SemaphoreType.DMA,
        ],
        compiler_params=params,
        cost_estimate=cheap,
        name="row_spectra",
    )(from_hbm(holograms[0]), partner, table, gain)
    arrived = [
        direct(*pieces[chunk * inner : (chunk + 1) * inner]) for chunk in range(own)
    ]

    sums = []
    lines = [[z * inner + i for z in range(outer)] for i in range(inner)]
    for chunk in range(own):
        parts = pl.pallas_call(
            lambda *refs: column_kernel(inner, outer, *refs),
            out_shape=shaped(outer, depth, block),
            in_specs=vmem(2 + inner),
            out_specs=one_out,
            scratch_shapes=[
                pltpu.VMEM((dists, depth, block), bf16),
                pltpu.VMEM((width, block), f32),
                pltpu.VMEM((width, block), bf16),
            ],
            compiler_params=params,
            cost_estimate=cheap,
            name="columns",
        )(table, gain, *arrived[chunk])
        sums.append(
            lax.psum_scatter(
                parts, "rows", scatter_dimension=0, axis_index_groups=lines, tiled=False
            )
        )

    phases = []
    for chunk in range(own):
        second, first = pl.pallas_call(
            lambda *refs: half_kernel(inner, *refs),
            out_shape=[shaped(capacity, block)] * 2,
            in_specs=vmem(1),
            out_specs=vmem(2),
            compiler_params=params,
            cost_estimate=cheap,
            name="half",
        )(sums[chunk])
        pieces = spread(first, first, second, second)
        phase = pl.pallas_call(
            lambda *refs: phase_kernel(inner, *refs),
            out_shape=shaped(capacity, width),
            in_specs=vmem(1 + inner),
            out_specs=one_out,
            scratch_shapes=[pltpu.VMEM((capacity, width), bf16)],
            compiler_params=params,
            cost_estimate=cheap,
            name="phase",
        )(table, *pieces)
        phases += [phase, sent(phase, to_other_core)]

    total, chosen, select = pl.pallas_call(
        lambda *refs: recon_kernel(own, *refs),
        out_shape=[
            jax.ShapeDtypeStruct((capacity, pixels), f32),
            shaped(width, pixels),
            shaped(capacity, capacity),
        ],
        in_specs=smem(2) + vmem(2 * own),
        out_specs=vmem(3),
        compiler_params=params,
        cost_estimate=cheap,
        name="recon",
    )(angle_order, slab_rows, weights, *phases[:-1])
    return pl.pallas_call(
        recon_last_kernel,
        out_shape=shaped(capacity, pixels),
        in_specs=vmem(4),
        out_specs=one_out,
        compiler_params=params,
        cost_estimate=cheap,
        name="recon",
    )(chosen, phases[-1], total, select)


def on_device(holograms, propagation, weights, angle_order, slab_rows):
    mbatch, angles, dist_dev, rows_dev, width = holograms.shape
    groups = lax.axis_size("rows")
    inner = 2 ** (int(math.log2(groups)) // 2)
    block = width // inner
    fits = (
        inner * (groups // inner) == groups
        and rows_dev % 16 == 0
        and block % 128 == 0
        and inner * rows_dev % 128 == 0
        and inner == 4
        and groups == inner * inner
        and lax.axis_size("dist") == 2
        and angles == 2 * lax.axis_size("dist")
    )
    if fits:
        return plane_plan(inner, holograms, propagation, weights, angle_order, slab_rows)
    return flat_plan(holograms, propagation, weights, angle_order, slab_rows)


def solution(mesh):
    return jax.shard_map(
        on_device,
        mesh=mesh,
        in_specs=(P(None, None, "dist", "rows", None), P(), P(None, None, "dist"), P(), P()),
        out_specs=P("rows", "dist"),
        check_vma=False,
    )
```

```python
import math

import jax
import jax.numpy as jnp
import numpy as np
from jax import lax
from jax.experimental import pallas as pl
from jax.experimental.pallas import tpu as pltpu
from jax.sharding import PartitionSpec as P

absorb_ratio = 0.1
regularizer = 0.05
bf16 = jnp.bfloat16
f32 = jnp.float32
send_order = (0, 2, 1, 3)
tail_order = (0, 2, 3, 1)


def hartley(length):
    index = np.arange(length)
    turned = (index[:, None] * index[None, :] % length) * (2.0 * math.pi / length)
    table = (np.cos(turned) + np.sin(turned)) / math.sqrt(length)
    return table.astype(bf16)


def signed_square(index, length):
    signed = jnp.where(index < length // 2, index, index - length).astype(f32)
    return signed * signed / float(length * length)


def filters(propagation, rows_sq, cols_sq):
    first = propagation[:, None] * rows_sq[None]
    second = propagation[:, None] * cols_sq[None]
    sin_b, cos_b = jnp.sin(second), jnp.cos(second)
    with_sin = 2.0 * (cos_b - absorb_ratio * sin_b)
    with_cos = 2.0 * (sin_b + absorb_ratio * cos_b)
    transfer = (
        jnp.sin(first)[:, :, None] * with_sin[:, None, :]
        + jnp.cos(first)[:, :, None] * with_cos[:, None, :]
    )
    denom = jnp.sum(transfer * transfer, axis=0) + regularizer
    return transfer / denom


def flat_plan(holograms, propagation, weights, angle_order, slab_rows):
    mbatch, angles, dist_dev, rows_dev, width = holograms.shape
    groups = lax.axis_size("rows")
    cores = lax.axis_size("dist")
    capacity = 2 * rows_dev
    own = angles // cores
    cols = width // groups
    dists = dist_dev * cores
    device = lax.axis_index("rows")
    table = jnp.asarray(hartley(width))
    index = jnp.arange(width, dtype=jnp.int32)
    my_cols = device * cols + jnp.arange(cols, dtype=jnp.int32)
    gain = filters(propagation, signed_square(my_cols, width), signed_square(index, width))

    mine = lax.all_to_all(holograms[0], "dist", split_axis=0, concat_axis=1, tiled=True)
    flat = mine.reshape(own * dists * rows_dev, width)
    spec = jnp.einsum("kx,mx->km", table, flat, preferred_element_type=f32)
    spec = spec.astype(bf16).reshape(groups, cols, own * dists * rows_dev)
    spec = lax.all_to_all(spec, "rows", split_axis=0, concat_axis=0, tiled=True)
    spec = spec.reshape(groups, cols, own, dists, rows_dev).transpose(1, 2, 3, 0, 4)
    spec = spec.reshape(cols * own * dists, width)
    full = jnp.dot(spec, table, preferred_element_type=f32)
    full = full.reshape(cols, own, dists, width)
    full = jnp.sum(full * gain.transpose(1, 0, 2)[:, None], axis=2).astype(bf16)
    half = jnp.einsum("yq,akq->yak", table, full.transpose(1, 0, 2), preferred_element_type=f32)
    half = half.astype(bf16).reshape(groups, rows_dev, own * cols)
    half = lax.all_to_all(half, "rows", split_axis=0, concat_axis=0, tiled=True)
    half = half.reshape(groups, rows_dev, own, cols).transpose(2, 1, 0, 3)
    half = half.reshape(own * rows_dev, width)
    phase = jnp.dot(half, table, preferred_element_type=f32)
    phase = phase.astype(bf16).reshape(own, rows_dev, width)
    phase = lax.all_gather(phase, "dist", axis=0, tiled=True)
    place = (angle_order[0][None, :] == jnp.arange(angles)[:, None]).astype(bf16)
    phase = jnp.einsum("wa,ayx->wyx", place, phase, preferred_element_type=f32)
    recon = jnp.einsum(
        "wyx,wxp->yp", phase.astype(bf16), weights, preferred_element_type=f32
    ).astype(bf16)
    parity = device % 2
    offset = parity * slab_rows[device - parity]
    count = slab_rows[device]
    pairs = [(source, source ^ 1) for source in range(groups)]
    partner = lax.ppermute(recon, "rows", pairs)
    lower = jnp.where(parity == 1, partner, recon)
    upper = jnp.where(parity == 1, recon, partner)
    paired = jnp.concatenate([lower, upper], axis=0)
    slot = jnp.arange(capacity, dtype=jnp.int32)[:, None]
    source = jnp.arange(capacity, dtype=jnp.int32)[None, :]
    select = ((source == offset + slot) & (slot < count)).astype(bf16)
    return jnp.dot(select, paired, preferred_element_type=f32).astype(bf16)


def position(inner):
    device = lax.axis_index("rows")
    return lax.axis_index("dist"), device // inner, device % inner


def row_kernel(inner, holo, there, table, *refs):
    outs, mine, loaded = refs[:-2], refs[-2], refs[-1]
    own = len(outs) // inner
    core, _, spot = position(inner)
    _, dist_dev, rows_dev, width = there.shape
    block = width // inner
    copy = pltpu.make_async_copy(holo.at[pl.ds(core * own, own)], mine, loaded)
    copy.start()
    for first, source in ((dist_dev, there.at[pl.ds(core * own, own)]), (0, mine)):
        if first == 0:
            copy.wait()
        rows = source[...].reshape(own * dist_dev * rows_dev, width)
        for rel in range(inner):
            part = table[:, pl.ds(pl.multiple_of((spot ^ rel) * block, block), block)]
            got = jnp.dot(rows, part, preferred_element_type=f32).astype(bf16)
            got = got.reshape(own, dist_dev, rows_dev, block)
            for chunk in range(own):
                outs[chunk * inner + rel][first : first + dist_dev] = got[chunk]


def whole_turns(scale, square):
    turns = scale * square * (0.5 / math.pi)
    return (turns - jnp.round(turns)) * (2.0 * math.pi)


def filter_kernel(inner, dist_dev, turns, after, out):
    dists, width, block = out.shape
    core, _, spot = position(inner)

    def square(first, length):
        index = lax.broadcasted_iota(jnp.int32, (1, length), 1) + first
        signed = jnp.where(index < width // 2, index, index - width).astype(f32)
        return signed * signed * (1.0 / (width * width))

    def phases(first, length):
        values = square(first, length)
        rows = []
        for d in range(dists):
            other = d // dist_dev
            scale = turns[(core ^ other) * dist_dev + d % dist_dev]
            rows.append(whole_turns(scale, values))
        return jnp.concatenate(rows, axis=0)

    along = phases(0, width)
    across = phases(spot * block, block)
    sin_b, cos_b = jnp.sin(across), jnp.cos(across)
    with_sin = 2.0 * (cos_b - absorb_ratio * sin_b)
    with_cos = 2.0 * (sin_b + absorb_ratio * cos_b)
    turned = jnp.concatenate([jnp.sin(along), jnp.cos(along)], axis=0).T
    step = 128
    for at in range(0, width, step):
        rows = turned[at : at + step]
        transfer = [
            rows[:, d : d + 1] * with_sin[d : d + 1, :]
            + rows[:, dists + d : dists + d + 1] * with_cos[d : d + 1, :]
            for d in range(dists)
        ]
        denom = transfer[0] * transfer[0]
        for value in transfer[1:]:
            denom = denom + value * value
        scale = 1.0 / (denom + regularizer)
        for d in range(dists):
            out[d, at : at + step, :] = (transfer[d] * scale).astype(bf16)


def column_kernel(inner, outer, table, gain, *refs):
    pieces = dict(zip(send_order, refs[:inner]))
    keep, *away = refs[inner:-3]
    stack, total, spectrum = refs[-3:]
    _, plane, spot = position(inner)
    dists, rows_dev, block = pieces[0].shape
    depth = inner * rows_dev
    for rel in range(inner):
        start = pl.multiple_of((spot ^ rel) * rows_dev, rows_dev)
        for d in range(dists):
            stack[d, pl.ds(start, rows_dev), :] = pieces[rel][d]
    part = table[:, pl.ds(pl.multiple_of(plane * depth, depth), depth)]
    for d in range(dists):
        got = jnp.dot(part, stack[d], preferred_element_type=f32) * gain[d].astype(f32)
        if d == 0:
            total[...] = got
        else:
            total[...] += got
    spectrum[...] = total[...].astype(bf16)
    half = outer // 2
    side = plane // half

    def rows_from(low):
        rows = pl.ds(pl.multiple_of(low * depth, half * depth), half * depth)
        value = jnp.dot(table[rows, :], spectrum[...], preferred_element_type=f32)
        return value.astype(bf16).reshape(half, depth, block)

    value = rows_from((1 - side) * half)
    wide = block // len(away)
    for split, out in enumerate(away):
        out[...] = value[:, :, split * wide : (split + 1) * wide]
    keep[...] = rows_from(side * half)


def add_kernel(one, two, out):
    out[...] = (one[...].astype(f32) + two[...].astype(f32)).astype(bf16)


def near_kernel(inner, split, keep, across, out):
    _, plane, _ = position(inner)
    which = (plane ^ 1) % 2
    inside = (plane == 1) | (plane == 2)
    more = jnp.where(inside, across[which].astype(f32), 0.0)
    wide = out.shape[1]
    here = keep[which, :, split * wide : (split + 1) * wide].astype(f32)
    out[...] = (here + more).astype(bf16)


def half_kernel(inner, own, *refs):
    other, mine, again = refs[-3:]
    each = (len(refs) - 3) // own
    _, plane, spot = position(inner)
    which = plane % 2
    inside = (plane == 1) | (plane == 2)
    _, capacity, block = mine.shape
    wide = block // (each // 2)
    for chunk in range(own):
        keep, *parts = refs[chunk * each : (chunk + 1) * each]
        for split in range(each // 2):
            across, last = parts[2 * split : 2 * split + 2]
            lanes = slice(split * wide, (split + 1) * wide)
            for out, pair in ((mine, spot // 2), (other, 1 - spot // 2)):
                rows = pl.ds(pl.multiple_of(pair * capacity, capacity), capacity)
                more = jnp.where(inside, across[which, rows, :].astype(f32), 0.0)
                got = keep[which, rows, lanes].astype(f32) + more + last[rows, :].astype(f32)
                out[chunk, :, lanes] = got.astype(bf16)
    again[...] = other[...]


def phase_kernel(inner, table, *refs):
    pieces = dict(zip(tail_order, refs[:inner]))
    *outs, joined = refs[inner:]
    _, _, spot = position(inner)
    own, capacity, block = refs[0].shape
    for rel in range(inner):
        columns = pl.ds(pl.multiple_of((spot ^ rel) * block, block), block)
        joined[:, columns] = pieces[rel][...].reshape(own * capacity, block)
    got = jnp.dot(joined[...], table[...], preferred_element_type=f32).astype(bf16)
    for chunk in range(own):
        outs[chunk][...] = got[chunk * capacity : (chunk + 1) * capacity]


def recon_kernel(own, order, slabs, weights, *refs):
    phases = refs[: 2 * own - 1]
    out, chosen, select = refs[2 * own - 1 :]
    core = lax.axis_index("dist")
    device = lax.axis_index("rows")
    total = None
    for step, phase in enumerate(phases):
        here = weights[order[0, (core ^ (step % 2)) * own + step // 2]]
        got = jnp.dot(phase[...], here, preferred_element_type=f32)
        total = got if total is None else total + got
    out[...] = total
    chosen[...] = weights[order[0, (core ^ 1) * own + own - 1]]
    parity = device % 2
    offset = parity * slabs[device - parity]
    slot = lax.broadcasted_iota(jnp.int32, select.shape, 0)
    source = lax.broadcasted_iota(jnp.int32, select.shape, 1)
    picked = (source == slot + offset) & (slot < slabs[device])
    select[...] = jnp.where(picked, 1.0, 0.0).astype(bf16)


def recon_last_kernel(weights, phase, before, select, out):
    total = before[...] + jnp.dot(phase[...], weights[...], preferred_element_type=f32)
    got = jnp.dot(select[...], total.astype(bf16), preferred_element_type=f32)
    out[...] = got.astype(bf16)


def vmem(count):
    return [pl.BlockSpec(memory_space=pltpu.VMEM)] * count


def from_hbm(value):
    return pltpu.with_memory_space_constraint(value, pltpu.HBM)


def in_hbm(count):
    return [pl.BlockSpec(memory_space=pltpu.HBM)] * count


def unread(count):
    return [pl.BlockSpec(memory_space=pl.ANY)] * count


def smem(count):
    return [pl.BlockSpec(memory_space=pltpu.SMEM)] * count


def plane_plan(inner, holograms, propagation, weights, angle_order, slab_rows):
    mbatch, angles, dist_dev, rows_dev, width = holograms.shape
    groups = lax.axis_size("rows")
    cores = lax.axis_size("dist")
    outer = groups // inner
    own = angles // cores
    block = width // inner
    depth = inner * rows_dev
    dists = cores * dist_dev
    pixels = weights.shape[2]
    capacity = 2 * rows_dev
    splits = block // 128
    params = pltpu.CompilerParams(vmem_limit_bytes=16 * 2**20)
    one_out = pl.BlockSpec(memory_space=pltpu.VMEM)

    cheap = pl.CostEstimate(flops=1, bytes_accessed=1, transcendentals=0)

    def shaped(*shape):
        return jax.ShapeDtypeStruct(shape, bf16)

    table = jnp.asarray(hartley(width))

    def sent(value, target):
        pairs = []
        for c in range(cores):
            for r in range(groups):
                to_core, to_row = target(c, r)
                pairs.append((c * groups + r, to_core * groups + to_row))
        return lax.ppermute(value, ("dist", "rows"), pairs)

    def to_other_core(c, r):
        return c ^ 1, r

    def to_spot(rel):
        return lambda c, r: (c, r ^ rel)

    def spread(pieces, order):
        return [sent(pieces[rel], to_spot(rel)) if rel else pieces[rel] for rel in order]

    def to_near_plane(c, r):
        return c, (r // inner ^ 1) * inner + r % inner

    def to_middle(c, r):
        z = r // inner
        return (c, (3 - z) * inner + r % inner) if z in (1, 2) else (c ^ 1, r)

    partner = sent(holograms[0], to_other_core)
    pieces = pl.pallas_call(
        lambda *refs: row_kernel(inner, *refs),
        out_shape=[shaped(dists, rows_dev, block)] * (own * inner),
        in_specs=in_hbm(1) + vmem(2),
        out_specs=vmem(own * inner),
        scratch_shapes=[
            pltpu.VMEM((own, dist_dev, rows_dev, width), bf16),
            pltpu.SemaphoreType.DMA,
        ],
        compiler_params=params,
        cost_estimate=cheap,
        name="row_spectra",
    )(from_hbm(holograms[0]), partner, table)
    arrived = [
        spread(pieces[chunk * inner : (chunk + 1) * inner], send_order) for chunk in range(own)
    ]

    gain = pl.pallas_call(
        lambda *refs: filter_kernel(inner, dist_dev, *refs),
        out_shape=shaped(dists, width, block),
        in_specs=smem(1) + unread(1),
        out_specs=one_out,
        compiler_params=params,
        cost_estimate=cheap,
        name="filters",
    )(from_hbm(propagation), pieces[0])

    sums = []
    for chunk in range(own):
        keep, *away = pl.pallas_call(
            lambda *refs: column_kernel(inner, outer, *refs),
            out_shape=[shaped(outer // 2, depth, block)]
            + [shaped(outer // 2, depth, block // splits)] * splits,
            in_specs=vmem(2 + inner),
            out_specs=vmem(1 + splits),
            scratch_shapes=[
                pltpu.VMEM((dists, depth, block), bf16),
                pltpu.VMEM((width, block), f32),
                pltpu.VMEM((width, block), bf16),
            ],
            compiler_params=params,
            cost_estimate=cheap,
            name="columns",
        )(table, gain, *arrived[chunk])
        parts = [keep]
        for split in range(splits):
            joint = pl.pallas_call(
                add_kernel,
                out_shape=shaped(outer // 2, depth, block // splits),
                in_specs=vmem(2),
                out_specs=one_out,
                compiler_params=params,
                cost_estimate=cheap,
                name="joint",
            )(away[split], sent(away[split], to_near_plane))
            across = sent(joint, to_middle)
            near = pl.pallas_call(
                lambda *refs, split=split: near_kernel(inner, split, *refs),
                out_shape=shaped(depth, block // splits),
                in_specs=vmem(2),
                out_specs=one_out,
                compiler_params=params,
                cost_estimate=cheap,
                name="near",
            )(keep, across)
            parts += [across, sent(near, to_near_plane)]
        sums.append(parts)

    parts = [part for chunk in sums for part in chunk]
    second, first, again = pl.pallas_call(
        lambda *refs: half_kernel(inner, own, *refs),
        out_shape=[shaped(own, capacity, block)] * 3,
        in_specs=vmem(len(parts)),
        out_specs=vmem(3),
        compiler_params=params,
        cost_estimate=cheap,
        name="half",
    )(*parts)
    ours = pl.pallas_call(
        lambda *refs: phase_kernel(inner, *refs),
        out_shape=[shaped(capacity, width)] * own,
        in_specs=vmem(1 + inner),
        out_specs=vmem(own),
        scratch_shapes=[pltpu.VMEM((own * capacity, width), bf16)],
        compiler_params=params,
        cost_estimate=cheap,
        name="phase",
    )(table, *spread([first, first, second, again], tail_order))
    phases = [value for phase in ours for value in (phase, sent(phase, to_other_core))]

    total, chosen, select = pl.pallas_call(
        lambda *refs: recon_kernel(own, *refs),
        out_shape=[
            jax.ShapeDtypeStruct((capacity, pixels), f32),
            shaped(width, pixels),
            shaped(capacity, capacity),
        ],
        in_specs=smem(2) + vmem(2 * own),
        out_specs=vmem(3),
        compiler_params=params,
        cost_estimate=cheap,
        name="recon",
    )(angle_order, slab_rows, weights, *phases[:-1])
    return pl.pallas_call(
        recon_last_kernel,
        out_shape=shaped(capacity, pixels),
        in_specs=vmem(4),
        out_specs=one_out,
        compiler_params=params,
        cost_estimate=cheap,
        name="recon",
    )(chosen, phases[-1], total, select)


def on_device(holograms, propagation, weights, angle_order, slab_rows):
    mbatch, angles, dist_dev, rows_dev, width = holograms.shape
    groups = lax.axis_size("rows")
    inner = 2 ** (int(math.log2(groups)) // 2)
    block = width // inner
    fits = (
        inner * (groups // inner) == groups
        and rows_dev % 16 == 0
        and block % 128 == 0
        and inner * rows_dev % 128 == 0
        and inner == 4
        and groups == inner * inner
        and lax.axis_size("dist") == 2
        and angles == 2 * lax.axis_size("dist")
    )
    if fits:
        return plane_plan(inner, holograms, propagation, weights, angle_order, slab_rows)
    return flat_plan(holograms, propagation, weights, angle_order, slab_rows)


def solution(mesh):
    return jax.shard_map(
        on_device,
        mesh=mesh,
        in_specs=(P(None, None, "dist", "rows", None), P(), P(None, None, "dist"), P(), P()),
        out_specs=P("rows", "dist"),
        check_vma=False,
    )
```

```python
import math

import jax
import jax.numpy as jnp
import numpy as np
from jax import lax
from jax.experimental import pallas as pl
from jax.experimental.pallas import tpu as pltpu
from jax.sharding import PartitionSpec as P

absorb_ratio = 0.1
regularizer = 0.05
bf16 = jnp.bfloat16
f32 = jnp.float32
send_order = (0, 2, 1, 3)
tail_order = (0, 2, 3, 1)


def hartley(length):
    index = np.arange(length)
    turned = (index[:, None] * index[None, :] % length) * (2.0 * math.pi / length)
    table = (np.cos(turned) + np.sin(turned)) / math.sqrt(length)
    return table.astype(bf16)


def signed_square(index, length):
    signed = jnp.where(index < length // 2, index, index - length).astype(f32)
    return signed * signed / float(length * length)


def filters(propagation, rows_sq, cols_sq):
    first = propagation[:, None] * rows_sq[None]
    second = propagation[:, None] * cols_sq[None]
    sin_b, cos_b = jnp.sin(second), jnp.cos(second)
    with_sin = 2.0 * (cos_b - absorb_ratio * sin_b)
    with_cos = 2.0 * (sin_b + absorb_ratio * cos_b)
    transfer = (
        jnp.sin(first)[:, :, None] * with_sin[:, None, :]
        + jnp.cos(first)[:, :, None] * with_cos[:, None, :]
    )
    denom = jnp.sum(transfer * transfer, axis=0) + regularizer
    return transfer / denom


def flat_plan(holograms, propagation, weights, angle_order, slab_rows):
    mbatch, angles, dist_dev, rows_dev, width = holograms.shape
    groups = lax.axis_size("rows")
    cores = lax.axis_size("dist")
    capacity = 2 * rows_dev
    own = angles // cores
    cols = width // groups
    dists = dist_dev * cores
    device = lax.axis_index("rows")
    table = jnp.asarray(hartley(width))
    index = jnp.arange(width, dtype=jnp.int32)
    my_cols = device * cols + jnp.arange(cols, dtype=jnp.int32)
    gain = filters(propagation, signed_square(my_cols, width), signed_square(index, width))

    mine = lax.all_to_all(holograms[0], "dist", split_axis=0, concat_axis=1, tiled=True)
    flat = mine.reshape(own * dists * rows_dev, width)
    spec = jnp.einsum("kx,mx->km", table, flat, preferred_element_type=f32)
    spec = spec.astype(bf16).reshape(groups, cols, own * dists * rows_dev)
    spec = lax.all_to_all(spec, "rows", split_axis=0, concat_axis=0, tiled=True)
    spec = spec.reshape(groups, cols, own, dists, rows_dev).transpose(1, 2, 3, 0, 4)
    spec = spec.reshape(cols * own * dists, width)
    full = jnp.dot(spec, table, preferred_element_type=f32)
    full = full.reshape(cols, own, dists, width)
    full = jnp.sum(full * gain.transpose(1, 0, 2)[:, None], axis=2).astype(bf16)
    half = jnp.einsum("yq,akq->yak", table, full.transpose(1, 0, 2), preferred_element_type=f32)
    half = half.astype(bf16).reshape(groups, rows_dev, own * cols)
    half = lax.all_to_all(half, "rows", split_axis=0, concat_axis=0, tiled=True)
    half = half.reshape(groups, rows_dev, own, cols).transpose(2, 1, 0, 3)
    half = half.reshape(own * rows_dev, width)
    phase = jnp.dot(half, table, preferred_element_type=f32)
    phase = phase.astype(bf16).reshape(own, rows_dev, width)
    phase = lax.all_gather(phase, "dist", axis=0, tiled=True)
    place = (angle_order[0][None, :] == jnp.arange(angles)[:, None]).astype(bf16)
    phase = jnp.einsum("wa,ayx->wyx", place, phase, preferred_element_type=f32)
    recon = jnp.einsum(
        "wyx,wxp->yp", phase.astype(bf16), weights, preferred_element_type=f32
    ).astype(bf16)
    parity = device % 2
    offset = parity * slab_rows[device - parity]
    count = slab_rows[device]
    pairs = [(source, source ^ 1) for source in range(groups)]
    partner = lax.ppermute(recon, "rows", pairs)
    lower = jnp.where(parity == 1, partner, recon)
    upper = jnp.where(parity == 1, recon, partner)
    paired = jnp.concatenate([lower, upper], axis=0)
    slot = jnp.arange(capacity, dtype=jnp.int32)[:, None]
    source = jnp.arange(capacity, dtype=jnp.int32)[None, :]
    select = ((source == offset + slot) & (slot < count)).astype(bf16)
    return jnp.dot(select, paired, preferred_element_type=f32).astype(bf16)


def position(inner):
    device = lax.axis_index("rows")
    return lax.axis_index("dist"), device // inner, device % inner


def row_kernel(inner, holo, there, table, after, *refs):
    outs, mine, loaded = refs[:-2], refs[-2], refs[-1]
    own = len(outs) // inner
    core, _, spot = position(inner)
    _, dist_dev, rows_dev, width = there.shape
    block = width // inner
    copy = pltpu.make_async_copy(holo.at[pl.ds(core * own, own)], mine, loaded)
    copy.start()
    for first, source in ((dist_dev, there.at[pl.ds(core * own, own)]), (0, mine)):
        if first == 0:
            copy.wait()
        rows = source[...].reshape(own * dist_dev * rows_dev, width)
        for rel in range(inner):
            part = table[:, pl.ds(pl.multiple_of((spot ^ rel) * block, block), block)]
            got = jnp.dot(rows, part, preferred_element_type=f32).astype(bf16)
            got = got.reshape(own, dist_dev, rows_dev, block)
            for chunk in range(own):
                outs[chunk * inner + rel][first : first + dist_dev] = got[chunk]


def whole_turns(scale, square):
    turns = scale * square * (0.5 / math.pi)
    return (turns - jnp.round(turns)) * (2.0 * math.pi)


def filter_kernel(inner, dist_dev, turns, out):
    dists, width, block = out.shape
    core, _, spot = position(inner)

    def square(first, length):
        index = lax.broadcasted_iota(jnp.int32, (1, length), 1) + first
        signed = jnp.where(index < width // 2, index, index - width).astype(f32)
        return signed * signed * (1.0 / (width * width))

    def phases(first, length):
        values = square(first, length)
        rows = []
        for d in range(dists):
            other = d // dist_dev
            scale = turns[(core ^ other) * dist_dev + d % dist_dev]
            rows.append(whole_turns(scale, values))
        return jnp.concatenate(rows, axis=0)

    along = phases(0, width)
    across = phases(spot * block, block)
    sin_b, cos_b = jnp.sin(across), jnp.cos(across)
    with_sin = 2.0 * (cos_b - absorb_ratio * sin_b)
    with_cos = 2.0 * (sin_b + absorb_ratio * cos_b)
    turned = jnp.concatenate([jnp.sin(along), jnp.cos(along)], axis=0).T
    step = 128
    for at in range(0, width, step):
        rows = turned[at : at + step]
        transfer = [
            rows[:, d : d + 1] * with_sin[d : d + 1, :]
            + rows[:, dists + d : dists + d + 1] * with_cos[d : d + 1, :]
            for d in range(dists)
        ]
        denom = transfer[0] * transfer[0]
        for value in transfer[1:]:
            denom = denom + value * value
        scale = 1.0 / (denom + regularizer)
        for d in range(dists):
            out[d, at : at + step, :] = (transfer[d] * scale).astype(bf16)


def column_kernel(inner, outer, table, gain, *refs):
    pieces = dict(zip(send_order, refs[:inner]))
    *outs, stack, total, spectrum = refs[inner:]
    _, plane, spot = position(inner)
    dists, rows_dev, block = pieces[0].shape
    depth = inner * rows_dev
    for rel in range(inner):
        start = pl.multiple_of((spot ^ rel) * rows_dev, rows_dev)
        for d in range(dists):
            stack[d, pl.ds(start, rows_dev), :] = pieces[rel][d]
    part = table[:, pl.ds(pl.multiple_of(plane * depth, depth), depth)]
    for d in range(dists):
        got = jnp.dot(part, stack[d], preferred_element_type=f32) * gain[d].astype(f32)
        if d == 0:
            total[...] = got
        else:
            total[...] += got
    spectrum[...] = total[...].astype(bf16)
    for rel, out in enumerate(outs):
        rows = pl.ds(pl.multiple_of((plane ^ rel) * depth, depth), depth)
        value = jnp.dot(table[rows, :], spectrum[...], preferred_element_type=f32)
        out[...] = value.astype(bf16)


def half_kernel(inner, *refs):
    parts, (other, mine) = refs[:-2], refs[-2:]
    _, _, spot = position(inner)
    capacity = mine.shape[0]
    for out, pair in ((mine, spot // 2), (other, 1 - spot // 2)):
        rows = pl.ds(pl.multiple_of(pair * capacity, capacity), capacity)
        got = parts[0][rows, :].astype(f32)
        for part in parts[1:]:
            got = got + part[rows, :].astype(f32)
        out[...] = got.astype(bf16)


def phase_kernel(inner, table, *refs):
    pieces = dict(zip(tail_order, refs[:inner]))
    out, joined = refs[-2:]
    _, _, spot = position(inner)
    block = refs[0].shape[1]
    for rel in range(inner):
        columns = pl.ds(pl.multiple_of((spot ^ rel) * block, block), block)
        joined[:, columns] = pieces[rel][...]
    out[...] = jnp.dot(joined[...], table[...], preferred_element_type=f32).astype(bf16)


def recon_kernel(own, order, slabs, weights, *refs):
    phases = refs[: 2 * own - 1]
    out, chosen, select = refs[2 * own - 1 :]
    core = lax.axis_index("dist")
    device = lax.axis_index("rows")
    total = None
    for step, phase in enumerate(phases):
        here = weights[order[0, (core ^ (step % 2)) * own + step // 2]]
        got = jnp.dot(phase[...], here, preferred_element_type=f32)
        total = got if total is None else total + got
    out[...] = total
    chosen[...] = weights[order[0, (core ^ 1) * own + own - 1]]
    parity = device % 2
    offset = parity * slabs[device - parity]
    slot = lax.broadcasted_iota(jnp.int32, select.shape, 0)
    source = lax.broadcasted_iota(jnp.int32, select.shape, 1)
    picked = (source == slot + offset) & (slot < slabs[device])
    select[...] = jnp.where(picked, 1.0, 0.0).astype(bf16)


def recon_last_kernel(weights, phase, before, select, out):
    total = before[...] + jnp.dot(phase[...], weights[...], preferred_element_type=f32)
    got = jnp.dot(select[...], total.astype(bf16), preferred_element_type=f32)
    out[...] = got.astype(bf16)


def vmem(count):
    return [pl.BlockSpec(memory_space=pltpu.VMEM)] * count


def from_hbm(value):
    return pltpu.with_memory_space_constraint(value, pltpu.HBM)


def in_hbm(count):
    return [pl.BlockSpec(memory_space=pltpu.HBM)] * count


def unread(count):
    return [pl.BlockSpec(memory_space=pl.ANY)] * count


def smem(count):
    return [pl.BlockSpec(memory_space=pltpu.SMEM)] * count


def plane_plan(inner, holograms, propagation, weights, angle_order, slab_rows):
    mbatch, angles, dist_dev, rows_dev, width = holograms.shape
    groups = lax.axis_size("rows")
    cores = lax.axis_size("dist")
    outer = groups // inner
    own = angles // cores
    block = width // inner
    depth = inner * rows_dev
    dists = cores * dist_dev
    pixels = weights.shape[2]
    capacity = 2 * rows_dev
    params = pltpu.CompilerParams(vmem_limit_bytes=16 * 2**20)
    one_out = pl.BlockSpec(memory_space=pltpu.VMEM)

    cheap = pl.CostEstimate(flops=1, bytes_accessed=1, transcendentals=0)

    def shaped(*shape):
        return jax.ShapeDtypeStruct(shape, bf16)

    table = jnp.asarray(hartley(width))

    def sent(value, target):
        pairs = []
        for c in range(cores):
            for r in range(groups):
                to_core, to_row = target(c, r)
                pairs.append((c * groups + r, to_core * groups + to_row))
        return lax.ppermute(value, ("dist", "rows"), pairs)

    def to_other_core(c, r):
        return c ^ 1, r

    def to_spot(rel):
        return lambda c, r: (c, r ^ rel)

    def spread(pieces, order):
        return [sent(pieces[rel], to_spot(rel)) if rel else pieces[rel] for rel in order]

    def to_plane(rel):
        return lambda c, r: (c, (r // inner ^ rel) * inner + r % inner)

    partner = sent(holograms[0], to_other_core)
    gain = pl.pallas_call(
        lambda *refs: filter_kernel(inner, dist_dev, *refs),
        out_shape=shaped(dists, width, block),
        in_specs=smem(1),
        out_specs=one_out,
        compiler_params=params,
        cost_estimate=cheap,
        name="filters",
    )(from_hbm(propagation))
    pieces = pl.pallas_call(
        lambda *refs: row_kernel(inner, *refs),
        out_shape=[shaped(dists, rows_dev, block)] * (own * inner),
        in_specs=in_hbm(1) + vmem(2) + unread(1),
        out_specs=vmem(own * inner),
        scratch_shapes=[
            pltpu.VMEM((own, dist_dev, rows_dev, width), bf16),
            pltpu.SemaphoreType.DMA,
        ],
        compiler_params=params,
        cost_estimate=cheap,
        name="row_spectra",
    )(from_hbm(holograms[0]), partner, table, gain)
    arrived = [
        spread(pieces[chunk * inner : (chunk + 1) * inner], send_order) for chunk in range(own)
    ]

    sums = []
    for chunk in range(own):
        blocks = pl.pallas_call(
            lambda *refs: column_kernel(inner, outer, *refs),
            out_shape=[shaped(depth, block)] * outer,
            in_specs=vmem(2 + inner),
            out_specs=vmem(outer),
            scratch_shapes=[
                pltpu.VMEM((dists, depth, block), bf16),
                pltpu.VMEM((width, block), f32),
                pltpu.VMEM((width, block), bf16),
            ],
            compiler_params=params,
            cost_estimate=cheap,
            name="columns",
        )(table, gain, *arrived[chunk])
        sums.append([sent(blocks[rel], to_plane(rel)) if rel else blocks[0] for rel in (3, 2, 1, 0)])

    phases = []
    for chunk in range(own):
        second, first = pl.pallas_call(
            lambda *refs: half_kernel(inner, *refs),
            out_shape=[shaped(capacity, block)] * 2,
            in_specs=vmem(outer),
            out_specs=vmem(2),
            compiler_params=params,
            cost_estimate=cheap,
            name="half",
        )(*sums[chunk])
        pieces = spread([first, first, second, second], tail_order)
        phase = pl.pallas_call(
            lambda *refs: phase_kernel(inner, *refs),
            out_shape=shaped(capacity, width),
            in_specs=vmem(1 + inner),
            out_specs=one_out,
            scratch_shapes=[pltpu.VMEM((capacity, width), bf16)],
            compiler_params=params,
            cost_estimate=cheap,
            name="phase",
        )(table, *pieces)
        phases += [phase, sent(phase, to_other_core)]

    total, chosen, select = pl.pallas_call(
        lambda *refs: recon_kernel(own, *refs),
        out_shape=[
            jax.ShapeDtypeStruct((capacity, pixels), f32),
            shaped(width, pixels),
            shaped(capacity, capacity),
        ],
        in_specs=smem(2) + vmem(2 * own),
        out_specs=vmem(3),
        compiler_params=params,
        cost_estimate=cheap,
        name="recon",
    )(angle_order, slab_rows, weights, *phases[:-1])
    return pl.pallas_call(
        recon_last_kernel,
        out_shape=shaped(capacity, pixels),
        in_specs=vmem(4),
        out_specs=one_out,
        compiler_params=params,
        cost_estimate=cheap,
        name="recon",
    )(chosen, phases[-1], total, select)


def on_device(holograms, propagation, weights, angle_order, slab_rows):
    mbatch, angles, dist_dev, rows_dev, width = holograms.shape
    groups = lax.axis_size("rows")
    inner = 2 ** (int(math.log2(groups)) // 2)
    block = width // inner
    fits = (
        inner * (groups // inner) == groups
        and rows_dev % 16 == 0
        and block % 128 == 0
        and inner * rows_dev % 128 == 0
        and inner == 4
        and groups == inner * inner
        and lax.axis_size("dist") == 2
        and angles == 2 * lax.axis_size("dist")
    )
    if fits:
        return plane_plan(inner, holograms, propagation, weights, angle_order, slab_rows)
    return flat_plan(holograms, propagation, weights, angle_order, slab_rows)


def solution(mesh):
    return jax.shard_map(
        on_device,
        mesh=mesh,
        in_specs=(P(None, None, "dist", "rows", None), P(), P(None, None, "dist"), P(), P()),
        out_specs=P("rows", "dist"),
        check_vma=False,
    )
```

```python
import math

import jax
import jax.numpy as jnp
import numpy as np
from jax import lax
from jax.experimental import pallas as pl
from jax.experimental.pallas import tpu as pltpu
from jax.sharding import PartitionSpec as P

absorb_ratio = 0.1
regularizer = 0.05
bf16 = jnp.bfloat16
f32 = jnp.float32
send_order = (0, 2, 1, 3)
tail_order = (0, 2, 3, 1)


def hartley(length):
    index = np.arange(length)
    turned = (index[:, None] * index[None, :] % length) * (2.0 * math.pi / length)
    table = (np.cos(turned) + np.sin(turned)) / math.sqrt(length)
    return table.astype(bf16)


def signed_square(index, length):
    signed = jnp.where(index < length // 2, index, index - length).astype(f32)
    return signed * signed / float(length * length)


def filters(propagation, rows_sq, cols_sq):
    first = propagation[:, None] * rows_sq[None]
    second = propagation[:, None] * cols_sq[None]
    sin_b, cos_b = jnp.sin(second), jnp.cos(second)
    with_sin = 2.0 * (cos_b - absorb_ratio * sin_b)
    with_cos = 2.0 * (sin_b + absorb_ratio * cos_b)
    transfer = (
        jnp.sin(first)[:, :, None] * with_sin[:, None, :]
        + jnp.cos(first)[:, :, None] * with_cos[:, None, :]
    )
    denom = jnp.sum(transfer * transfer, axis=0) + regularizer
    return transfer / denom


def flat_plan(holograms, propagation, weights, angle_order, slab_rows):
    mbatch, angles, dist_dev, rows_dev, width = holograms.shape
    groups = lax.axis_size("rows")
    cores = lax.axis_size("dist")
    capacity = 2 * rows_dev
    own = angles // cores
    cols = width // groups
    dists = dist_dev * cores
    device = lax.axis_index("rows")
    table = jnp.asarray(hartley(width))
    index = jnp.arange(width, dtype=jnp.int32)
    my_cols = device * cols + jnp.arange(cols, dtype=jnp.int32)
    gain = filters(propagation, signed_square(my_cols, width), signed_square(index, width))

    mine = lax.all_to_all(holograms[0], "dist", split_axis=0, concat_axis=1, tiled=True)
    flat = mine.reshape(own * dists * rows_dev, width)
    spec = jnp.einsum("kx,mx->km", table, flat, preferred_element_type=f32)
    spec = spec.astype(bf16).reshape(groups, cols, own * dists * rows_dev)
    spec = lax.all_to_all(spec, "rows", split_axis=0, concat_axis=0, tiled=True)
    spec = spec.reshape(groups, cols, own, dists, rows_dev).transpose(1, 2, 3, 0, 4)
    spec = spec.reshape(cols * own * dists, width)
    full = jnp.dot(spec, table, preferred_element_type=f32)
    full = full.reshape(cols, own, dists, width)
    full = jnp.sum(full * gain.transpose(1, 0, 2)[:, None], axis=2).astype(bf16)
    half = jnp.einsum("yq,akq->yak", table, full.transpose(1, 0, 2), preferred_element_type=f32)
    half = half.astype(bf16).reshape(groups, rows_dev, own * cols)
    half = lax.all_to_all(half, "rows", split_axis=0, concat_axis=0, tiled=True)
    half = half.reshape(groups, rows_dev, own, cols).transpose(2, 1, 0, 3)
    half = half.reshape(own * rows_dev, width)
    phase = jnp.dot(half, table, preferred_element_type=f32)
    phase = phase.astype(bf16).reshape(own, rows_dev, width)
    phase = lax.all_gather(phase, "dist", axis=0, tiled=True)
    place = (angle_order[0][None, :] == jnp.arange(angles)[:, None]).astype(bf16)
    phase = jnp.einsum("wa,ayx->wyx", place, phase, preferred_element_type=f32)
    recon = jnp.einsum(
        "wyx,wxp->yp", phase.astype(bf16), weights, preferred_element_type=f32
    ).astype(bf16)
    parity = device % 2
    offset = parity * slab_rows[device - parity]
    count = slab_rows[device]
    pairs = [(source, source ^ 1) for source in range(groups)]
    partner = lax.ppermute(recon, "rows", pairs)
    lower = jnp.where(parity == 1, partner, recon)
    upper = jnp.where(parity == 1, recon, partner)
    paired = jnp.concatenate([lower, upper], axis=0)
    slot = jnp.arange(capacity, dtype=jnp.int32)[:, None]
    source = jnp.arange(capacity, dtype=jnp.int32)[None, :]
    select = ((source == offset + slot) & (slot < count)).astype(bf16)
    return jnp.dot(select, paired, preferred_element_type=f32).astype(bf16)


def position(inner):
    device = lax.axis_index("rows")
    return lax.axis_index("dist"), device // inner, device % inner


def row_kernel(inner, holo, there, table, after, *refs):
    outs, mine, loaded = refs[:-2], refs[-2], refs[-1]
    own = len(outs) // inner
    core, _, spot = position(inner)
    _, dist_dev, rows_dev, width = there.shape
    block = width // inner
    copy = pltpu.make_async_copy(holo.at[pl.ds(core * own, own)], mine, loaded)
    copy.start()
    for first, source in ((dist_dev, there.at[pl.ds(core * own, own)]), (0, mine)):
        if first == 0:
            copy.wait()
        rows = source[...].reshape(own * dist_dev * rows_dev, width)
        for rel in range(inner):
            part = table[:, pl.ds(pl.multiple_of((spot ^ rel) * block, block), block)]
            got = jnp.dot(rows, part, preferred_element_type=f32).astype(bf16)
            got = got.reshape(own, dist_dev, rows_dev, block)
            for chunk in range(own):
                outs[chunk * inner + rel][first : first + dist_dev] = got[chunk]


def whole_turns(scale, square):
    turns = scale * square * (0.5 / math.pi)
    return (turns - jnp.round(turns)) * (2.0 * math.pi)


def filter_kernel(inner, dist_dev, turns, out):
    dists, width, block = out.shape
    core, _, spot = position(inner)

    def square(first, length):
        index = lax.broadcasted_iota(jnp.int32, (1, length), 1) + first
        signed = jnp.where(index < width // 2, index, index - width).astype(f32)
        return signed * signed * (1.0 / (width * width))

    def phases(first, length):
        values = square(first, length)
        rows = []
        for d in range(dists):
            other = d // dist_dev
            scale = turns[(core ^ other) * dist_dev + d % dist_dev]
            rows.append(whole_turns(scale, values))
        return jnp.concatenate(rows, axis=0)

    along = phases(0, width)
    across = phases(spot * block, block)
    sin_b, cos_b = jnp.sin(across), jnp.cos(across)
    with_sin = 2.0 * (cos_b - absorb_ratio * sin_b)
    with_cos = 2.0 * (sin_b + absorb_ratio * cos_b)
    turned = jnp.concatenate([jnp.sin(along), jnp.cos(along)], axis=0).T
    step = 128
    for at in range(0, width, step):
        rows = turned[at : at + step]
        transfer = [
            rows[:, d : d + 1] * with_sin[d : d + 1, :]
            + rows[:, dists + d : dists + d + 1] * with_cos[d : d + 1, :]
            for d in range(dists)
        ]
        denom = transfer[0] * transfer[0]
        for value in transfer[1:]:
            denom = denom + value * value
        scale = 1.0 / (denom + regularizer)
        for d in range(dists):
            out[d, at : at + step, :] = (transfer[d] * scale).astype(bf16)


def column_kernel(inner, outer, table, gain, *refs):
    pieces = dict(zip(send_order, refs[:inner]))
    *outs, stack, total, spectrum = refs[inner:]
    _, plane, spot = position(inner)
    dists, rows_dev, block = pieces[0].shape
    depth = inner * rows_dev
    for rel in range(inner):
        start = pl.multiple_of((spot ^ rel) * rows_dev, rows_dev)
        for d in range(dists):
            stack[d, pl.ds(start, rows_dev), :] = pieces[rel][d]
    part = table[:, pl.ds(pl.multiple_of(plane * depth, depth), depth)]
    for d in range(dists):
        got = jnp.dot(part, stack[d], preferred_element_type=f32) * gain[d].astype(f32)
        if d == 0:
            total[...] = got
        else:
            total[...] += got
    spectrum[...] = total[...].astype(bf16)
    middle = (plane == 1) | (plane == 2)
    first = jnp.where(middle, 1, 3)
    for rel, out in zip((0, first, 4 - first, 2), outs):
        rows = pl.ds(pl.multiple_of((plane ^ rel) * depth, depth), depth)
        value = jnp.dot(table[rows, :], spectrum[...], preferred_element_type=f32)
        out[...] = value.astype(bf16)


def far_kernel(inner, *refs):
    ours, got, out = refs[-3:]
    _, plane, _ = position(inner)
    middle = (plane == 1) | (plane == 2)
    more = jnp.where(middle, got[...].astype(f32), 0.0)
    out[...] = (ours[...].astype(f32) + more).astype(bf16)


def half_kernel(inner, ours, far, near, next_near, across, other, mine):
    _, plane, spot = position(inner)
    middle = (plane == 1) | (plane == 2)
    capacity = mine.shape[0]
    for out, pair in ((mine, spot // 2), (other, 1 - spot // 2)):
        rows = pl.ds(pl.multiple_of(pair * capacity, capacity), capacity)
        inside = next_near[rows, :].astype(f32) + across[rows, :].astype(f32)
        more = jnp.where(middle, inside, near[rows, :].astype(f32))
        got = ours[rows, :].astype(f32) + far[rows, :].astype(f32) + more
        out[...] = got.astype(bf16)


def phase_kernel(inner, table, *refs):
    pieces = dict(zip(tail_order, refs[:inner]))
    out, joined = refs[-2:]
    _, _, spot = position(inner)
    block = refs[0].shape[1]
    for rel in range(inner):
        columns = pl.ds(pl.multiple_of((spot ^ rel) * block, block), block)
        joined[:, columns] = pieces[rel][...]
    out[...] = jnp.dot(joined[...], table[...], preferred_element_type=f32).astype(bf16)


def recon_kernel(own, order, slabs, weights, *refs):
    phases = refs[: 2 * own - 1]
    out, chosen, select = refs[2 * own - 1 :]
    core = lax.axis_index("dist")
    device = lax.axis_index("rows")
    total = None
    for step, phase in enumerate(phases):
        here = weights[order[0, (core ^ (step % 2)) * own + step // 2]]
        got = jnp.dot(phase[...], here, preferred_element_type=f32)
        total = got if total is None else total + got
    out[...] = total
    chosen[...] = weights[order[0, (core ^ 1) * own + own - 1]]
    parity = device % 2
    offset = parity * slabs[device - parity]
    slot = lax.broadcasted_iota(jnp.int32, select.shape, 0)
    source = lax.broadcasted_iota(jnp.int32, select.shape, 1)
    picked = (source == slot + offset) & (slot < slabs[device])
    select[...] = jnp.where(picked, 1.0, 0.0).astype(bf16)


def recon_last_kernel(weights, phase, before, select, out):
    total = before[...] + jnp.dot(phase[...], weights[...], preferred_element_type=f32)
    got = jnp.dot(select[...], total.astype(bf16), preferred_element_type=f32)
    out[...] = got.astype(bf16)


def vmem(count):
    return [pl.BlockSpec(memory_space=pltpu.VMEM)] * count


def from_hbm(value):
    return pltpu.with_memory_space_constraint(value, pltpu.HBM)


def in_hbm(count):
    return [pl.BlockSpec(memory_space=pltpu.HBM)] * count


def unread(count):
    return [pl.BlockSpec(memory_space=pl.ANY)] * count


def smem(count):
    return [pl.BlockSpec(memory_space=pltpu.SMEM)] * count


def plane_plan(inner, holograms, propagation, weights, angle_order, slab_rows):
    mbatch, angles, dist_dev, rows_dev, width = holograms.shape
    groups = lax.axis_size("rows")
    cores = lax.axis_size("dist")
    outer = groups // inner
    own = angles // cores
    block = width // inner
    depth = inner * rows_dev
    dists = cores * dist_dev
    pixels = weights.shape[2]
    capacity = 2 * rows_dev
    params = pltpu.CompilerParams(vmem_limit_bytes=16 * 2**20)
    one_out = pl.BlockSpec(memory_space=pltpu.VMEM)

    cheap = pl.CostEstimate(flops=1, bytes_accessed=1, transcendentals=0)

    def shaped(*shape):
        return jax.ShapeDtypeStruct(shape, bf16)

    table = jnp.asarray(hartley(width))

    def sent(value, target):
        pairs = []
        for c in range(cores):
            for r in range(groups):
                to_core, to_row = target(c, r)
                pairs.append((c * groups + r, to_core * groups + to_row))
        return lax.ppermute(value, ("dist", "rows"), pairs)

    def to_other_core(c, r):
        return c ^ 1, r

    def to_spot(rel):
        return lambda c, r: (c, r ^ rel)

    def spread(pieces, order):
        return [sent(pieces[rel], to_spot(rel)) if rel else pieces[rel] for rel in order]

    def to_plane(rel):
        return lambda c, r: (c, (r // inner ^ rel) * inner + r % inner)

    def to_middle(c, r):
        z = r // inner
        return (c, (3 - z) * inner + r % inner) if z in (1, 2) else (c ^ 1, r)

    partner = sent(holograms[0], to_other_core)
    gain = pl.pallas_call(
        lambda *refs: filter_kernel(inner, dist_dev, *refs),
        out_shape=shaped(dists, width, block),
        in_specs=smem(1),
        out_specs=one_out,
        compiler_params=params,
        cost_estimate=cheap,
        name="filters",
    )(from_hbm(propagation))
    pieces = pl.pallas_call(
        lambda *refs: row_kernel(inner, *refs),
        out_shape=[shaped(dists, rows_dev, block)] * (own * inner),
        in_specs=in_hbm(1) + vmem(2) + unread(1),
        out_specs=vmem(own * inner),
        scratch_shapes=[
            pltpu.VMEM((own, dist_dev, rows_dev, width), bf16),
            pltpu.SemaphoreType.DMA,
        ],
        compiler_params=params,
        cost_estimate=cheap,
        name="row_spectra",
    )(from_hbm(holograms[0]), partner, table, gain)
    arrived = [
        spread(pieces[chunk * inner : (chunk + 1) * inner], send_order) for chunk in range(own)
    ]

    sums = []
    for chunk in range(own):
        blocks = pl.pallas_call(
            lambda *refs: column_kernel(inner, outer, *refs),
            out_shape=[shaped(depth, block)] * outer,
            in_specs=vmem(2 + inner),
            out_specs=vmem(outer),
            scratch_shapes=[
                pltpu.VMEM((dists, depth, block), bf16),
                pltpu.VMEM((width, block), f32),
                pltpu.VMEM((width, block), bf16),
            ],
            compiler_params=params,
            cost_estimate=cheap,
            name="columns",
        )(table, gain, *arrived[chunk])
        ours, first, second, third = blocks
        near = sent(first, to_plane(1))
        earlier = sums[-1][3:] if sums else []
        message = pl.pallas_call(
            lambda *refs: far_kernel(inner, *refs),
            out_shape=shaped(depth, block),
            in_specs=unread(len(earlier)) + vmem(2),
            out_specs=one_out,
            compiler_params=params,
            cost_estimate=cheap,
            name="far",
        )(*earlier, third, near)
        far = sent(message, to_plane(2))
        sums.append([ours, far, near, sent(second, to_plane(1)), sent(second, to_middle)])

    phases = []
    for chunk in range(own):
        second, first = pl.pallas_call(
            lambda *refs: half_kernel(inner, *refs),
            out_shape=[shaped(capacity, block)] * 2,
            in_specs=vmem(5),
            out_specs=vmem(2),
            compiler_params=params,
            cost_estimate=cheap,
            name="half",
        )(*sums[chunk])
        pieces = spread([first, first, second, second], tail_order)
        phase = pl.pallas_call(
            lambda *refs: phase_kernel(inner, *refs),
            out_shape=shaped(capacity, width),
            in_specs=vmem(1 + inner),
            out_specs=one_out,
            scratch_shapes=[pltpu.VMEM((capacity, width), bf16)],
            compiler_params=params,
            cost_estimate=cheap,
            name="phase",
        )(table, *pieces)
        phases += [phase, sent(phase, to_other_core)]

    total, chosen, select = pl.pallas_call(
        lambda *refs: recon_kernel(own, *refs),
        out_shape=[
            jax.ShapeDtypeStruct((capacity, pixels), f32),
            shaped(width, pixels),
            shaped(capacity, capacity),
        ],
        in_specs=smem(2) + vmem(2 * own),
        out_specs=vmem(3),
        compiler_params=params,
        cost_estimate=cheap,
        name="recon",
    )(angle_order, slab_rows, weights, *phases[:-1])
    return pl.pallas_call(
        recon_last_kernel,
        out_shape=shaped(capacity, pixels),
        in_specs=vmem(4),
        out_specs=one_out,
        compiler_params=params,
        cost_estimate=cheap,
        name="recon",
    )(chosen, phases[-1], total, select)


def on_device(holograms, propagation, weights, angle_order, slab_rows):
    mbatch, angles, dist_dev, rows_dev, width = holograms.shape
    groups = lax.axis_size("rows")
    inner = 2 ** (int(math.log2(groups)) // 2)
    block = width // inner
    fits = (
        inner * (groups // inner) == groups
        and rows_dev % 16 == 0
        and block % 128 == 0
        and inner * rows_dev % 128 == 0
        and inner == 4
        and groups == inner * inner
        and lax.axis_size("dist") == 2
        and angles == 2 * lax.axis_size("dist")
    )
    if fits:
        return plane_plan(inner, holograms, propagation, weights, angle_order, slab_rows)
    return flat_plan(holograms, propagation, weights, angle_order, slab_rows)


def solution(mesh):
    return jax.shard_map(
        on_device,
        mesh=mesh,
        in_specs=(P(None, None, "dist", "rows", None), P(), P(None, None, "dist"), P(), P()),
        out_specs=P("rows", "dist"),
        check_vma=False,
    )
```

```python
import math

import jax
import jax.numpy as jnp
import numpy as np
from jax import lax
from jax.experimental import pallas as pl
from jax.experimental.pallas import tpu as pltpu
from jax.sharding import PartitionSpec as P

absorb_ratio = 0.1
regularizer = 0.05
bf16 = jnp.bfloat16
f32 = jnp.float32
send_order = (0, 2, 1, 3)
tail_order = (0, 2, 3, 1)


def hartley(length):
    index = np.arange(length)
    turned = (index[:, None] * index[None, :] % length) * (2.0 * math.pi / length)
    table = (np.cos(turned) + np.sin(turned)) / math.sqrt(length)
    return table.astype(bf16)


def signed_square(index, length):
    signed = jnp.where(index < length // 2, index, index - length).astype(f32)
    return signed * signed / float(length * length)


def filters(propagation, rows_sq, cols_sq):
    first = propagation[:, None] * rows_sq[None]
    second = propagation[:, None] * cols_sq[None]
    sin_b, cos_b = jnp.sin(second), jnp.cos(second)
    with_sin = 2.0 * (cos_b - absorb_ratio * sin_b)
    with_cos = 2.0 * (sin_b + absorb_ratio * cos_b)
    transfer = (
        jnp.sin(first)[:, :, None] * with_sin[:, None, :]
        + jnp.cos(first)[:, :, None] * with_cos[:, None, :]
    )
    denom = jnp.sum(transfer * transfer, axis=0) + regularizer
    return transfer / denom


def flat_plan(holograms, propagation, weights, angle_order, slab_rows):
    mbatch, angles, dist_dev, rows_dev, width = holograms.shape
    groups = lax.axis_size("rows")
    cores = lax.axis_size("dist")
    capacity = 2 * rows_dev
    own = angles // cores
    cols = width // groups
    dists = dist_dev * cores
    device = lax.axis_index("rows")
    table = jnp.asarray(hartley(width))
    index = jnp.arange(width, dtype=jnp.int32)
    my_cols = device * cols + jnp.arange(cols, dtype=jnp.int32)
    gain = filters(propagation, signed_square(my_cols, width), signed_square(index, width))

    mine = lax.all_to_all(holograms[0], "dist", split_axis=0, concat_axis=1, tiled=True)
    flat = mine.reshape(own * dists * rows_dev, width)
    spec = jnp.einsum("kx,mx->km", table, flat, preferred_element_type=f32)
    spec = spec.astype(bf16).reshape(groups, cols, own * dists * rows_dev)
    spec = lax.all_to_all(spec, "rows", split_axis=0, concat_axis=0, tiled=True)
    spec = spec.reshape(groups, cols, own, dists, rows_dev).transpose(1, 2, 3, 0, 4)
    spec = spec.reshape(cols * own * dists, width)
    full = jnp.dot(spec, table, preferred_element_type=f32)
    full = full.reshape(cols, own, dists, width)
    full = jnp.sum(full * gain.transpose(1, 0, 2)[:, None], axis=2).astype(bf16)
    half = jnp.einsum("yq,akq->yak", table, full.transpose(1, 0, 2), preferred_element_type=f32)
    half = half.astype(bf16).reshape(groups, rows_dev, own * cols)
    half = lax.all_to_all(half, "rows", split_axis=0, concat_axis=0, tiled=True)
    half = half.reshape(groups, rows_dev, own, cols).transpose(2, 1, 0, 3)
    half = half.reshape(own * rows_dev, width)
    phase = jnp.dot(half, table, preferred_element_type=f32)
    phase = phase.astype(bf16).reshape(own, rows_dev, width)
    phase = lax.all_gather(phase, "dist", axis=0, tiled=True)
    place = (angle_order[0][None, :] == jnp.arange(angles)[:, None]).astype(bf16)
    phase = jnp.einsum("wa,ayx->wyx", place, phase, preferred_element_type=f32)
    recon = jnp.einsum(
        "wyx,wxp->yp", phase.astype(bf16), weights, preferred_element_type=f32
    ).astype(bf16)
    parity = device % 2
    offset = parity * slab_rows[device - parity]
    count = slab_rows[device]
    pairs = [(source, source ^ 1) for source in range(groups)]
    partner = lax.ppermute(recon, "rows", pairs)
    lower = jnp.where(parity == 1, partner, recon)
    upper = jnp.where(parity == 1, recon, partner)
    paired = jnp.concatenate([lower, upper], axis=0)
    slot = jnp.arange(capacity, dtype=jnp.int32)[:, None]
    source = jnp.arange(capacity, dtype=jnp.int32)[None, :]
    select = ((source == offset + slot) & (slot < count)).astype(bf16)
    return jnp.dot(select, paired, preferred_element_type=f32).astype(bf16)


def position(inner):
    device = lax.axis_index("rows")
    return lax.axis_index("dist"), device // inner, device % inner


def row_kernel(inner, holo, there, table, after, *refs):
    outs, mine, loaded = refs[:-2], refs[-2], refs[-1]
    own = len(outs) // inner
    core, _, spot = position(inner)
    _, dist_dev, rows_dev, width = there.shape
    block = width // inner
    copy = pltpu.make_async_copy(holo.at[pl.ds(core * own, own)], mine, loaded)
    copy.start()
    for first, source in ((dist_dev, there.at[pl.ds(core * own, own)]), (0, mine)):
        if first == 0:
            copy.wait()
        rows = source[...].reshape(own * dist_dev * rows_dev, width)
        for rel in range(inner):
            part = table[:, pl.ds(pl.multiple_of((spot ^ rel) * block, block), block)]
            got = jnp.dot(rows, part, preferred_element_type=f32).astype(bf16)
            got = got.reshape(own, dist_dev, rows_dev, block)
            for chunk in range(own):
                outs[chunk * inner + rel][first : first + dist_dev] = got[chunk]


def whole_turns(scale, square):
    turns = scale * square * (0.5 / math.pi)
    return (turns - jnp.round(turns)) * (2.0 * math.pi)


def filter_kernel(inner, dist_dev, turns, out):
    dists, width, block = out.shape
    core, _, spot = position(inner)

    def square(first, length):
        index = lax.broadcasted_iota(jnp.int32, (1, length), 1) + first
        signed = jnp.where(index < width // 2, index, index - width).astype(f32)
        return signed * signed * (1.0 / (width * width))

    def phases(first, length):
        values = square(first, length)
        rows = []
        for d in range(dists):
            other = d // dist_dev
            scale = turns[(core ^ other) * dist_dev + d % dist_dev]
            rows.append(whole_turns(scale, values))
        return jnp.concatenate(rows, axis=0)

    along = phases(0, width)
    across = phases(spot * block, block)
    sin_b, cos_b = jnp.sin(across), jnp.cos(across)
    with_sin = 2.0 * (cos_b - absorb_ratio * sin_b)
    with_cos = 2.0 * (sin_b + absorb_ratio * cos_b)
    turned = jnp.concatenate([jnp.sin(along), jnp.cos(along)], axis=0).T
    step = 128
    for at in range(0, width, step):
        rows = turned[at : at + step]
        transfer = [
            rows[:, d : d + 1] * with_sin[d : d + 1, :]
            + rows[:, dists + d : dists + d + 1] * with_cos[d : d + 1, :]
            for d in range(dists)
        ]
        denom = transfer[0] * transfer[0]
        for value in transfer[1:]:
            denom = denom + value * value
        scale = 1.0 / (denom + regularizer)
        for d in range(dists):
            out[d, at : at + step, :] = (transfer[d] * scale).astype(bf16)


def column_kernel(inner, outer, table, gain, *refs):
    pieces = dict(zip(send_order, refs[:inner]))
    *outs, stack, total, spectrum = refs[inner:]
    _, plane, spot = position(inner)
    dists, rows_dev, block = pieces[0].shape
    depth = inner * rows_dev
    for rel in range(inner):
        start = pl.multiple_of((spot ^ rel) * rows_dev, rows_dev)
        for d in range(dists):
            stack[d, pl.ds(start, rows_dev), :] = pieces[rel][d]
    part = table[:, pl.ds(pl.multiple_of(plane * depth, depth), depth)]
    for d in range(dists):
        got = jnp.dot(part, stack[d], preferred_element_type=f32) * gain[d].astype(f32)
        if d == 0:
            total[...] = got
        else:
            total[...] += got
    spectrum[...] = total[...].astype(bf16)
    middle = (plane == 1) | (plane == 2)
    first = jnp.where(middle, 1, 3)
    for rel, out in zip((0, first, 4 - first, 2), outs):
        rows = pl.ds(pl.multiple_of((plane ^ rel) * depth, depth), depth)
        value = jnp.dot(table[rows, :], spectrum[...], preferred_element_type=f32)
        out[...] = value.astype(bf16)


def far_kernel(inner, *refs):
    ours, got, out = refs[-3:]
    _, plane, _ = position(inner)
    middle = (plane == 1) | (plane == 2)
    more = jnp.where(middle, got[...].astype(f32), 0.0)
    out[...] = (ours[...].astype(f32) + more).astype(bf16)


def half_kernel(inner, ours, far, near, next_near, across, other, mine, again):
    _, plane, spot = position(inner)
    middle = (plane == 1) | (plane == 2)
    capacity = mine.shape[0]
    for out, pair in ((mine, spot // 2), (other, 1 - spot // 2)):
        rows = pl.ds(pl.multiple_of(pair * capacity, capacity), capacity)
        inside = next_near[rows, :].astype(f32) + across[rows, :].astype(f32)
        more = jnp.where(middle, inside, near[rows, :].astype(f32))
        got = ours[rows, :].astype(f32) + far[rows, :].astype(f32) + more
        out[...] = got.astype(bf16)
    again[...] = other[...]


def phase_kernel(inner, table, *refs):
    pieces = dict(zip(tail_order, refs[:inner]))
    out, joined = refs[-2:]
    _, _, spot = position(inner)
    block = refs[0].shape[1]
    for rel in range(inner):
        columns = pl.ds(pl.multiple_of((spot ^ rel) * block, block), block)
        joined[:, columns] = pieces[rel][...]
    out[...] = jnp.dot(joined[...], table[...], preferred_element_type=f32).astype(bf16)


def recon_kernel(own, order, slabs, weights, *refs):
    phases = refs[: 2 * own - 1]
    out, chosen, select = refs[2 * own - 1 :]
    core = lax.axis_index("dist")
    device = lax.axis_index("rows")
    total = None
    for step, phase in enumerate(phases):
        here = weights[order[0, (core ^ (step % 2)) * own + step // 2]]
        got = jnp.dot(phase[...], here, preferred_element_type=f32)
        total = got if total is None else total + got
    out[...] = total
    chosen[...] = weights[order[0, (core ^ 1) * own + own - 1]]
    parity = device % 2
    offset = parity * slabs[device - parity]
    slot = lax.broadcasted_iota(jnp.int32, select.shape, 0)
    source = lax.broadcasted_iota(jnp.int32, select.shape, 1)
    picked = (source == slot + offset) & (slot < slabs[device])
    select[...] = jnp.where(picked, 1.0, 0.0).astype(bf16)


def recon_last_kernel(weights, phase, before, select, out):
    total = before[...] + jnp.dot(phase[...], weights[...], preferred_element_type=f32)
    got = jnp.dot(select[...], total.astype(bf16), preferred_element_type=f32)
    out[...] = got.astype(bf16)


def vmem(count):
    return [pl.BlockSpec(memory_space=pltpu.VMEM)] * count


def from_hbm(value):
    return pltpu.with_memory_space_constraint(value, pltpu.HBM)


def in_hbm(count):
    return [pl.BlockSpec(memory_space=pltpu.HBM)] * count


def unread(count):
    return [pl.BlockSpec(memory_space=pl.ANY)] * count


def smem(count):
    return [pl.BlockSpec(memory_space=pltpu.SMEM)] * count


def plane_plan(inner, holograms, propagation, weights, angle_order, slab_rows):
    mbatch, angles, dist_dev, rows_dev, width = holograms.shape
    groups = lax.axis_size("rows")
    cores = lax.axis_size("dist")
    outer = groups // inner
    own = angles // cores
    block = width // inner
    depth = inner * rows_dev
    dists = cores * dist_dev
    pixels = weights.shape[2]
    capacity = 2 * rows_dev
    params = pltpu.CompilerParams(vmem_limit_bytes=16 * 2**20)
    one_out = pl.BlockSpec(memory_space=pltpu.VMEM)

    cheap = pl.CostEstimate(flops=1, bytes_accessed=1, transcendentals=0)

    def shaped(*shape):
        return jax.ShapeDtypeStruct(shape, bf16)

    table = jnp.asarray(hartley(width))

    def sent(value, target):
        pairs = []
        for c in range(cores):
            for r in range(groups):
                to_core, to_row = target(c, r)
                pairs.append((c * groups + r, to_core * groups + to_row))
        return lax.ppermute(value, ("dist", "rows"), pairs)

    def to_other_core(c, r):
        return c ^ 1, r

    def to_spot(rel):
        return lambda c, r: (c, r ^ rel)

    def spread(pieces, order):
        return [sent(pieces[rel], to_spot(rel)) if rel else pieces[rel] for rel in order]

    def to_plane(rel):
        return lambda c, r: (c, (r // inner ^ rel) * inner + r % inner)

    def to_middle(c, r):
        z = r // inner
        return (c, (3 - z) * inner + r % inner) if z in (1, 2) else (c ^ 1, r)

    partner = sent(holograms[0], to_other_core)
    gain = pl.pallas_call(
        lambda *refs: filter_kernel(inner, dist_dev, *refs),
        out_shape=shaped(dists, width, block),
        in_specs=smem(1),
        out_specs=one_out,
        compiler_params=params,
        cost_estimate=cheap,
        name="filters",
    )(from_hbm(propagation))
    pieces = pl.pallas_call(
        lambda *refs: row_kernel(inner, *refs),
        out_shape=[shaped(dists, rows_dev, block)] * (own * inner),
        in_specs=in_hbm(1) + vmem(2) + unread(1),
        out_specs=vmem(own * inner),
        scratch_shapes=[
            pltpu.VMEM((own, dist_dev, rows_dev, width), bf16),
            pltpu.SemaphoreType.DMA,
        ],
        compiler_params=params,
        cost_estimate=cheap,
        name="row_spectra",
    )(from_hbm(holograms[0]), partner, table, gain)
    arrived = [
        spread(pieces[chunk * inner : (chunk + 1) * inner], send_order) for chunk in range(own)
    ]

    sums = []
    for chunk in range(own):
        blocks = pl.pallas_call(
            lambda *refs: column_kernel(inner, outer, *refs),
            out_shape=[shaped(depth, block)] * outer,
            in_specs=vmem(2 + inner),
            out_specs=vmem(outer),
            scratch_shapes=[
                pltpu.VMEM((dists, depth, block), bf16),
                pltpu.VMEM((width, block), f32),
                pltpu.VMEM((width, block), bf16),
            ],
            compiler_params=params,
            cost_estimate=cheap,
            name="columns",
        )(table, gain, *arrived[chunk])
        ours, first, second, third = blocks
        near = sent(first, to_plane(1))
        earlier = sums[-1][3:] if sums else []
        message = pl.pallas_call(
            lambda *refs: far_kernel(inner, *refs),
            out_shape=shaped(depth, block),
            in_specs=unread(len(earlier)) + vmem(2),
            out_specs=one_out,
            compiler_params=params,
            cost_estimate=cheap,
            name="far",
        )(*earlier, third, near)
        far = sent(message, to_plane(2))
        sums.append([ours, far, near, sent(second, to_plane(1)), sent(second, to_middle)])

    phases = []
    for chunk in range(own):
        second, first, again = pl.pallas_call(
            lambda *refs: half_kernel(inner, *refs),
            out_shape=[shaped(capacity, block)] * 3,
            in_specs=vmem(5),
            out_specs=vmem(3),
            compiler_params=params,
            cost_estimate=cheap,
            name="half",
        )(*sums[chunk])
        pieces = spread([first, first, second, again], tail_order)
        phase = pl.pallas_call(
            lambda *refs: phase_kernel(inner, *refs),
            out_shape=shaped(capacity, width),
            in_specs=vmem(1 + inner),
            out_specs=one_out,
            scratch_shapes=[pltpu.VMEM((capacity, width), bf16)],
            compiler_params=params,
            cost_estimate=cheap,
            name="phase",
        )(table, *pieces)
        phases += [phase, sent(phase, to_other_core)]

    total, chosen, select = pl.pallas_call(
        lambda *refs: recon_kernel(own, *refs),
        out_shape=[
            jax.ShapeDtypeStruct((capacity, pixels), f32),
            shaped(width, pixels),
            shaped(capacity, capacity),
        ],
        in_specs=smem(2) + vmem(2 * own),
        out_specs=vmem(3),
        compiler_params=params,
        cost_estimate=cheap,
        name="recon",
    )(angle_order, slab_rows, weights, *phases[:-1])
    return pl.pallas_call(
        recon_last_kernel,
        out_shape=shaped(capacity, pixels),
        in_specs=vmem(4),
        out_specs=one_out,
        compiler_params=params,
        cost_estimate=cheap,
        name="recon",
    )(chosen, phases[-1], total, select)


def on_device(holograms, propagation, weights, angle_order, slab_rows):
    mbatch, angles, dist_dev, rows_dev, width = holograms.shape
    groups = lax.axis_size("rows")
    inner = 2 ** (int(math.log2(groups)) // 2)
    block = width // inner
    fits = (
        inner * (groups // inner) == groups
        and rows_dev % 16 == 0
        and block % 128 == 0
        and inner * rows_dev % 128 == 0
        and inner == 4
        and groups == inner * inner
        and lax.axis_size("dist") == 2
        and angles == 2 * lax.axis_size("dist")
    )
    if fits:
        return plane_plan(inner, holograms, propagation, weights, angle_order, slab_rows)
    return flat_plan(holograms, propagation, weights, angle_order, slab_rows)


def solution(mesh):
    return jax.shard_map(
        on_device,
        mesh=mesh,
        in_specs=(P(None, None, "dist", "rows", None), P(), P(None, None, "dist"), P(), P()),
        out_specs=P("rows", "dist"),
        check_vma=False,
    )
```

```python
import math

import jax
import jax.numpy as jnp
import numpy as np
from jax import lax
from jax.experimental import pallas as pl
from jax.experimental.pallas import tpu as pltpu
from jax.sharding import PartitionSpec as P

absorb_ratio = 0.1
regularizer = 0.05
bf16 = jnp.bfloat16
f32 = jnp.float32
send_order = (0, 2, 1, 3)
tail_order = (0, 2, 3, 1)


def hartley(length):
    index = np.arange(length)
    turned = (index[:, None] * index[None, :] % length) * (2.0 * math.pi / length)
    table = (np.cos(turned) + np.sin(turned)) / math.sqrt(length)
    return table.astype(bf16)


def signed_square(index, length):
    signed = jnp.where(index < length // 2, index, index - length).astype(f32)
    return signed * signed / float(length * length)


def filters(propagation, rows_sq, cols_sq):
    first = propagation[:, None] * rows_sq[None]
    second = propagation[:, None] * cols_sq[None]
    sin_b, cos_b = jnp.sin(second), jnp.cos(second)
    with_sin = 2.0 * (cos_b - absorb_ratio * sin_b)
    with_cos = 2.0 * (sin_b + absorb_ratio * cos_b)
    transfer = (
        jnp.sin(first)[:, :, None] * with_sin[:, None, :]
        + jnp.cos(first)[:, :, None] * with_cos[:, None, :]
    )
    denom = jnp.sum(transfer * transfer, axis=0) + regularizer
    return transfer / denom


def flat_plan(holograms, propagation, weights, angle_order, slab_rows):
    mbatch, angles, dist_dev, rows_dev, width = holograms.shape
    groups = lax.axis_size("rows")
    cores = lax.axis_size("dist")
    capacity = 2 * rows_dev
    own = angles // cores
    cols = width // groups
    dists = dist_dev * cores
    device = lax.axis_index("rows")
    table = jnp.asarray(hartley(width))
    index = jnp.arange(width, dtype=jnp.int32)
    my_cols = device * cols + jnp.arange(cols, dtype=jnp.int32)
    gain = filters(propagation, signed_square(my_cols, width), signed_square(index, width))

    mine = lax.all_to_all(holograms[0], "dist", split_axis=0, concat_axis=1, tiled=True)
    flat = mine.reshape(own * dists * rows_dev, width)
    spec = jnp.einsum("kx,mx->km", table, flat, preferred_element_type=f32)
    spec = spec.astype(bf16).reshape(groups, cols, own * dists * rows_dev)
    spec = lax.all_to_all(spec, "rows", split_axis=0, concat_axis=0, tiled=True)
    spec = spec.reshape(groups, cols, own, dists, rows_dev).transpose(1, 2, 3, 0, 4)
    spec = spec.reshape(cols * own * dists, width)
    full = jnp.dot(spec, table, preferred_element_type=f32)
    full = full.reshape(cols, own, dists, width)
    full = jnp.sum(full * gain.transpose(1, 0, 2)[:, None], axis=2).astype(bf16)
    half = jnp.einsum("yq,akq->yak", table, full.transpose(1, 0, 2), preferred_element_type=f32)
    half = half.astype(bf16).reshape(groups, rows_dev, own * cols)
    half = lax.all_to_all(half, "rows", split_axis=0, concat_axis=0, tiled=True)
    half = half.reshape(groups, rows_dev, own, cols).transpose(2, 1, 0, 3)
    half = half.reshape(own * rows_dev, width)
    phase = jnp.dot(half, table, preferred_element_type=f32)
    phase = phase.astype(bf16).reshape(own, rows_dev, width)
    phase = lax.all_gather(phase, "dist", axis=0, tiled=True)
    place = (angle_order[0][None, :] == jnp.arange(angles)[:, None]).astype(bf16)
    phase = jnp.einsum("wa,ayx->wyx", place, phase, preferred_element_type=f32)
    recon = jnp.einsum(
        "wyx,wxp->yp", phase.astype(bf16), weights, preferred_element_type=f32
    ).astype(bf16)
    parity = device % 2
    offset = parity * slab_rows[device - parity]
    count = slab_rows[device]
    pairs = [(source, source ^ 1) for source in range(groups)]
    partner = lax.ppermute(recon, "rows", pairs)
    lower = jnp.where(parity == 1, partner, recon)
    upper = jnp.where(parity == 1, recon, partner)
    paired = jnp.concatenate([lower, upper], axis=0)
    slot = jnp.arange(capacity, dtype=jnp.int32)[:, None]
    source = jnp.arange(capacity, dtype=jnp.int32)[None, :]
    select = ((source == offset + slot) & (slot < count)).astype(bf16)
    return jnp.dot(select, paired, preferred_element_type=f32).astype(bf16)


def position(inner):
    device = lax.axis_index("rows")
    return lax.axis_index("dist"), device // inner, device % inner


def row_kernel(inner, holo, there, table, after, *refs):
    outs, mine, loaded = refs[:-2], refs[-2], refs[-1]
    own = len(outs) // inner
    core, _, spot = position(inner)
    _, dist_dev, rows_dev, width = there.shape
    block = width // inner
    copy = pltpu.make_async_copy(holo.at[pl.ds(core * own, own)], mine, loaded)
    copy.start()
    for first, source in ((dist_dev, there.at[pl.ds(core * own, own)]), (0, mine)):
        if first == 0:
            copy.wait()
        rows = source[...].reshape(own * dist_dev * rows_dev, width)
        for rel in range(inner):
            part = table[:, pl.ds(pl.multiple_of((spot ^ rel) * block, block), block)]
            got = jnp.dot(rows, part, preferred_element_type=f32).astype(bf16)
            got = got.reshape(own, dist_dev, rows_dev, block)
            for chunk in range(own):
                outs[chunk * inner + rel][first : first + dist_dev] = got[chunk]


def whole_turns(scale, square):
    turns = scale * square * (0.5 / math.pi)
    return (turns - jnp.round(turns)) * (2.0 * math.pi)


def filter_kernel(inner, dist_dev, turns, out):
    dists, width, block = out.shape
    core, _, spot = position(inner)

    def square(first, length):
        index = lax.broadcasted_iota(jnp.int32, (1, length), 1) + first
        signed = jnp.where(index < width // 2, index, index - width).astype(f32)
        return signed * signed * (1.0 / (width * width))

    def phases(first, length):
        values = square(first, length)
        rows = []
        for d in range(dists):
            other = d // dist_dev
            scale = turns[(core ^ other) * dist_dev + d % dist_dev]
            rows.append(whole_turns(scale, values))
        return jnp.concatenate(rows, axis=0)

    along = phases(0, width)
    across = phases(spot * block, block)
    sin_b, cos_b = jnp.sin(across), jnp.cos(across)
    with_sin = 2.0 * (cos_b - absorb_ratio * sin_b)
    with_cos = 2.0 * (sin_b + absorb_ratio * cos_b)
    turned = jnp.concatenate([jnp.sin(along), jnp.cos(along)], axis=0).T
    step = 128
    for at in range(0, width, step):
        rows = turned[at : at + step]
        transfer = [
            rows[:, d : d + 1] * with_sin[d : d + 1, :]
            + rows[:, dists + d : dists + d + 1] * with_cos[d : d + 1, :]
            for d in range(dists)
        ]
        denom = transfer[0] * transfer[0]
        for value in transfer[1:]:
            denom = denom + value * value
        scale = 1.0 / (denom + regularizer)
        for d in range(dists):
            out[d, at : at + step, :] = (transfer[d] * scale).astype(bf16)


def column_kernel(inner, outer, table, gain, *refs):
    pieces = dict(zip(send_order, refs[:inner]))
    *outs, stack, total, spectrum = refs[inner:]
    _, plane, spot = position(inner)
    dists, rows_dev, block = pieces[0].shape
    depth = inner * rows_dev
    for rel in range(inner):
        start = pl.multiple_of((spot ^ rel) * rows_dev, rows_dev)
        for d in range(dists):
            stack[d, pl.ds(start, rows_dev), :] = pieces[rel][d]
    part = table[:, pl.ds(pl.multiple_of(plane * depth, depth), depth)]
    for d in range(dists):
        got = jnp.dot(part, stack[d], preferred_element_type=f32) * gain[d].astype(f32)
        if d == 0:
            total[...] = got
        else:
            total[...] += got
    spectrum[...] = total[...].astype(bf16)
    middle = (plane == 1) | (plane == 2)
    first = jnp.where(middle, 1, 3)
    for rel, out in zip((0, first, 4 - first, 2), outs):
        rows = pl.ds(pl.multiple_of((plane ^ rel) * depth, depth), depth)
        value = jnp.dot(table[rows, :], spectrum[...], preferred_element_type=f32)
        out[...] = value.astype(bf16)


def hold_kernel(value, after, out):
    out[...] = value[...]


def far_kernel(inner, *refs):
    ours, got, out = refs[-3:]
    _, plane, _ = position(inner)
    middle = (plane == 1) | (plane == 2)
    more = jnp.where(middle, got[...].astype(f32), 0.0)
    out[...] = (ours[...].astype(f32) + more).astype(bf16)


def half_kernel(inner, ours, far, near, next_near, across, other, mine, again):
    _, plane, spot = position(inner)
    middle = (plane == 1) | (plane == 2)
    capacity = mine.shape[0]
    for out, pair in ((mine, spot // 2), (other, 1 - spot // 2)):
        rows = pl.ds(pl.multiple_of(pair * capacity, capacity), capacity)
        inside = next_near[rows, :].astype(f32) + across[rows, :].astype(f32)
        more = jnp.where(middle, inside, near[rows, :].astype(f32))
        got = ours[rows, :].astype(f32) + far[rows, :].astype(f32) + more
        out[...] = got.astype(bf16)
    again[...] = other[...]


def phase_kernel(inner, table, *refs):
    pieces = dict(zip(tail_order, refs[:inner]))
    out, joined = refs[-2:]
    _, _, spot = position(inner)
    block = refs[0].shape[1]
    for rel in range(inner):
        columns = pl.ds(pl.multiple_of((spot ^ rel) * block, block), block)
        joined[:, columns] = pieces[rel][...]
    out[...] = jnp.dot(joined[...], table[...], preferred_element_type=f32).astype(bf16)


def recon_kernel(own, order, slabs, weights, *refs):
    phases = refs[: 2 * own - 1]
    out, chosen, select = refs[2 * own - 1 :]
    core = lax.axis_index("dist")
    device = lax.axis_index("rows")
    total = None
    for step, phase in enumerate(phases):
        here = weights[order[0, (core ^ (step % 2)) * own + step // 2]]
        got = jnp.dot(phase[...], here, preferred_element_type=f32)
        total = got if total is None else total + got
    out[...] = total
    chosen[...] = weights[order[0, (core ^ 1) * own + own - 1]]
    parity = device % 2
    offset = parity * slabs[device - parity]
    slot = lax.broadcasted_iota(jnp.int32, select.shape, 0)
    source = lax.broadcasted_iota(jnp.int32, select.shape, 1)
    picked = (source == slot + offset) & (slot < slabs[device])
    select[...] = jnp.where(picked, 1.0, 0.0).astype(bf16)


def recon_last_kernel(weights, phase, before, select, out):
    total = before[...] + jnp.dot(phase[...], weights[...], preferred_element_type=f32)
    got = jnp.dot(select[...], total.astype(bf16), preferred_element_type=f32)
    out[...] = got.astype(bf16)


def vmem(count):
    return [pl.BlockSpec(memory_space=pltpu.VMEM)] * count


def from_hbm(value):
    return pltpu.with_memory_space_constraint(value, pltpu.HBM)


def in_hbm(count):
    return [pl.BlockSpec(memory_space=pltpu.HBM)] * count


def unread(count):
    return [pl.BlockSpec(memory_space=pl.ANY)] * count


def smem(count):
    return [pl.BlockSpec(memory_space=pltpu.SMEM)] * count


def plane_plan(inner, holograms, propagation, weights, angle_order, slab_rows):
    mbatch, angles, dist_dev, rows_dev, width = holograms.shape
    groups = lax.axis_size("rows")
    cores = lax.axis_size("dist")
    outer = groups // inner
    own = angles // cores
    block = width // inner
    depth = inner * rows_dev
    dists = cores * dist_dev
    pixels = weights.shape[2]
    capacity = 2 * rows_dev
    params = pltpu.CompilerParams(vmem_limit_bytes=16 * 2**20)
    one_out = pl.BlockSpec(memory_space=pltpu.VMEM)

    cheap = pl.CostEstimate(flops=1, bytes_accessed=1, transcendentals=0)

    def shaped(*shape):
        return jax.ShapeDtypeStruct(shape, bf16)

    table = jnp.asarray(hartley(width))

    def sent(value, target):
        pairs = []
        for c in range(cores):
            for r in range(groups):
                to_core, to_row = target(c, r)
                pairs.append((c * groups + r, to_core * groups + to_row))
        return lax.ppermute(value, ("dist", "rows"), pairs)

    def to_other_core(c, r):
        return c ^ 1, r

    def to_spot(rel):
        return lambda c, r: (c, r ^ rel)

    def spread(pieces, order):
        return [sent(pieces[rel], to_spot(rel)) if rel else pieces[rel] for rel in order]

    def to_plane(rel):
        return lambda c, r: (c, (r // inner ^ rel) * inner + r % inner)

    def to_middle(c, r):
        z = r // inner
        return (c, (3 - z) * inner + r % inner) if z in (1, 2) else (c ^ 1, r)

    partner = sent(holograms[0], to_other_core)
    gain = pl.pallas_call(
        lambda *refs: filter_kernel(inner, dist_dev, *refs),
        out_shape=shaped(dists, width, block),
        in_specs=smem(1),
        out_specs=one_out,
        compiler_params=params,
        cost_estimate=cheap,
        name="filters",
    )(from_hbm(propagation))
    pieces = pl.pallas_call(
        lambda *refs: row_kernel(inner, *refs),
        out_shape=[shaped(dists, rows_dev, block)] * (own * inner),
        in_specs=in_hbm(1) + vmem(2) + unread(1),
        out_specs=vmem(own * inner),
        scratch_shapes=[
            pltpu.VMEM((own, dist_dev, rows_dev, width), bf16),
            pltpu.SemaphoreType.DMA,
        ],
        compiler_params=params,
        cost_estimate=cheap,
        name="row_spectra",
    )(from_hbm(holograms[0]), partner, table, gain)
    arrived = [
        spread(pieces[chunk * inner : (chunk + 1) * inner], send_order) for chunk in range(own)
    ]

    sums = []
    for chunk in range(own):
        blocks = pl.pallas_call(
            lambda *refs: column_kernel(inner, outer, *refs),
            out_shape=[shaped(depth, block)] * outer,
            in_specs=vmem(2 + inner),
            out_specs=vmem(outer),
            scratch_shapes=[
                pltpu.VMEM((dists, depth, block), bf16),
                pltpu.VMEM((width, block), f32),
                pltpu.VMEM((width, block), bf16),
            ],
            compiler_params=params,
            cost_estimate=cheap,
            name="columns",
        )(table, gain, *arrived[chunk])
        ours, first, second, third = blocks
        near = sent(first, to_plane(1))
        earlier = sums[-1][3:] if sums else []
        message = pl.pallas_call(
            lambda *refs: far_kernel(inner, *refs),
            out_shape=shaped(depth, block),
            in_specs=unread(len(earlier)) + vmem(2),
            out_specs=one_out,
            compiler_params=params,
            cost_estimate=cheap,
            name="far",
        )(*earlier, third, near)
        far = sent(message, to_plane(2))
        late = second
        if sums:
            late = pl.pallas_call(
                hold_kernel,
                out_shape=shaped(depth, block),
                in_specs=vmem(1) + unread(1),
                out_specs=one_out,
                compiler_params=params,
                cost_estimate=cheap,
                name="hold",
            )(second, sums[0][1])
        sums.append([ours, far, near, sent(late, to_plane(1)), sent(second, to_middle)])

    phases = []
    for chunk in range(own):
        second, first, again = pl.pallas_call(
            lambda *refs: half_kernel(inner, *refs),
            out_shape=[shaped(capacity, block)] * 3,
            in_specs=vmem(5),
            out_specs=vmem(3),
            compiler_params=params,
            cost_estimate=cheap,
            name="half",
        )(*sums[chunk])
        pieces = spread([first, first, second, again], tail_order)
        phase = pl.pallas_call(
            lambda *refs: phase_kernel(inner, *refs),
            out_shape=shaped(capacity, width),
            in_specs=vmem(1 + inner),
            out_specs=one_out,
            scratch_shapes=[pltpu.VMEM((capacity, width), bf16)],
            compiler_params=params,
            cost_estimate=cheap,
            name="phase",
        )(table, *pieces)
        phases += [phase, sent(phase, to_other_core)]

    total, chosen, select = pl.pallas_call(
        lambda *refs: recon_kernel(own, *refs),
        out_shape=[
            jax.ShapeDtypeStruct((capacity, pixels), f32),
            shaped(width, pixels),
            shaped(capacity, capacity),
        ],
        in_specs=smem(2) + vmem(2 * own),
        out_specs=vmem(3),
        compiler_params=params,
        cost_estimate=cheap,
        name="recon",
    )(angle_order, slab_rows, weights, *phases[:-1])
    return pl.pallas_call(
        recon_last_kernel,
        out_shape=shaped(capacity, pixels),
        in_specs=vmem(4),
        out_specs=one_out,
        compiler_params=params,
        cost_estimate=cheap,
        name="recon",
    )(chosen, phases[-1], total, select)


def on_device(holograms, propagation, weights, angle_order, slab_rows):
    mbatch, angles, dist_dev, rows_dev, width = holograms.shape
    groups = lax.axis_size("rows")
    inner = 2 ** (int(math.log2(groups)) // 2)
    block = width // inner
    fits = (
        inner * (groups // inner) == groups
        and rows_dev % 16 == 0
        and block % 128 == 0
        and inner * rows_dev % 128 == 0
        and inner == 4
        and groups == inner * inner
        and lax.axis_size("dist") == 2
        and angles == 2 * lax.axis_size("dist")
    )
    if fits:
        return plane_plan(inner, holograms, propagation, weights, angle_order, slab_rows)
    return flat_plan(holograms, propagation, weights, angle_order, slab_rows)


def solution(mesh):
    return jax.shard_map(
        on_device,
        mesh=mesh,
        in_specs=(P(None, None, "dist", "rows", None), P(), P(None, None, "dist"), P(), P()),
        out_specs=P("rows", "dist"),
        check_vma=False,
    )
```

```python
import math

import jax
import jax.numpy as jnp
import numpy as np
from jax import lax
from jax.experimental import pallas as pl
from jax.experimental.pallas import tpu as pltpu
from jax.sharding import PartitionSpec as P

absorb_ratio = 0.1
regularizer = 0.05
bf16 = jnp.bfloat16
f32 = jnp.float32
send_order = (0, 2, 1, 3)
tail_order = (0, 2, 3, 1)


def hartley(length):
    index = np.arange(length)
    turned = (index[:, None] * index[None, :] % length) * (2.0 * math.pi / length)
    table = (np.cos(turned) + np.sin(turned)) / math.sqrt(length)
    return table.astype(bf16)


def signed_square(index, length):
    signed = jnp.where(index < length // 2, index, index - length).astype(f32)
    return signed * signed / float(length * length)


def filters(propagation, rows_sq, cols_sq):
    first = propagation[:, None] * rows_sq[None]
    second = propagation[:, None] * cols_sq[None]
    sin_b, cos_b = jnp.sin(second), jnp.cos(second)
    with_sin = 2.0 * (cos_b - absorb_ratio * sin_b)
    with_cos = 2.0 * (sin_b + absorb_ratio * cos_b)
    transfer = (
        jnp.sin(first)[:, :, None] * with_sin[:, None, :]
        + jnp.cos(first)[:, :, None] * with_cos[:, None, :]
    )
    denom = jnp.sum(transfer * transfer, axis=0) + regularizer
    return transfer / denom


def flat_plan(holograms, propagation, weights, angle_order, slab_rows):
    mbatch, angles, dist_dev, rows_dev, width = holograms.shape
    groups = lax.axis_size("rows")
    cores = lax.axis_size("dist")
    capacity = 2 * rows_dev
    own = angles // cores
    cols = width // groups
    dists = dist_dev * cores
    device = lax.axis_index("rows")
    table = jnp.asarray(hartley(width))
    index = jnp.arange(width, dtype=jnp.int32)
    my_cols = device * cols + jnp.arange(cols, dtype=jnp.int32)
    gain = filters(propagation, signed_square(my_cols, width), signed_square(index, width))

    mine = lax.all_to_all(holograms[0], "dist", split_axis=0, concat_axis=1, tiled=True)
    flat = mine.reshape(own * dists * rows_dev, width)
    spec = jnp.einsum("kx,mx->km", table, flat, preferred_element_type=f32)
    spec = spec.astype(bf16).reshape(groups, cols, own * dists * rows_dev)
    spec = lax.all_to_all(spec, "rows", split_axis=0, concat_axis=0, tiled=True)
    spec = spec.reshape(groups, cols, own, dists, rows_dev).transpose(1, 2, 3, 0, 4)
    spec = spec.reshape(cols * own * dists, width)
    full = jnp.dot(spec, table, preferred_element_type=f32)
    full = full.reshape(cols, own, dists, width)
    full = jnp.sum(full * gain.transpose(1, 0, 2)[:, None], axis=2).astype(bf16)
    half = jnp.einsum("yq,akq->yak", table, full.transpose(1, 0, 2), preferred_element_type=f32)
    half = half.astype(bf16).reshape(groups, rows_dev, own * cols)
    half = lax.all_to_all(half, "rows", split_axis=0, concat_axis=0, tiled=True)
    half = half.reshape(groups, rows_dev, own, cols).transpose(2, 1, 0, 3)
    half = half.reshape(own * rows_dev, width)
    phase = jnp.dot(half, table, preferred_element_type=f32)
    phase = phase.astype(bf16).reshape(own, rows_dev, width)
    phase = lax.all_gather(phase, "dist", axis=0, tiled=True)
    place = (angle_order[0][None, :] == jnp.arange(angles)[:, None]).astype(bf16)
    phase = jnp.einsum("wa,ayx->wyx", place, phase, preferred_element_type=f32)
    recon = jnp.einsum(
        "wyx,wxp->yp", phase.astype(bf16), weights, preferred_element_type=f32
    ).astype(bf16)
    parity = device % 2
    offset = parity * slab_rows[device - parity]
    count = slab_rows[device]
    pairs = [(source, source ^ 1) for source in range(groups)]
    partner = lax.ppermute(recon, "rows", pairs)
    lower = jnp.where(parity == 1, partner, recon)
    upper = jnp.where(parity == 1, recon, partner)
    paired = jnp.concatenate([lower, upper], axis=0)
    slot = jnp.arange(capacity, dtype=jnp.int32)[:, None]
    source = jnp.arange(capacity, dtype=jnp.int32)[None, :]
    select = ((source == offset + slot) & (slot < count)).astype(bf16)
    return jnp.dot(select, paired, preferred_element_type=f32).astype(bf16)


def position(inner):
    device = lax.axis_index("rows")
    return lax.axis_index("dist"), device // inner, device % inner


def row_kernel(inner, holo, there, table, after, *refs):
    outs, mine, loaded = refs[:-2], refs[-2], refs[-1]
    own = len(outs) // inner
    core, _, spot = position(inner)
    _, dist_dev, rows_dev, width = there.shape
    block = width // inner
    copy = pltpu.make_async_copy(holo.at[pl.ds(core * own, own)], mine, loaded)
    copy.start()
    for first, source in ((dist_dev, there.at[pl.ds(core * own, own)]), (0, mine)):
        if first == 0:
            copy.wait()
        rows = source[...].reshape(own * dist_dev * rows_dev, width)
        for rel in range(inner):
            part = table[:, pl.ds(pl.multiple_of((spot ^ rel) * block, block), block)]
            got = jnp.dot(rows, part, preferred_element_type=f32).astype(bf16)
            got = got.reshape(own, dist_dev, rows_dev, block)
            for chunk in range(own):
                outs[chunk * inner + rel][first : first + dist_dev] = got[chunk]


def whole_turns(scale, square):
    turns = scale * square * (0.5 / math.pi)
    return (turns - jnp.round(turns)) * (2.0 * math.pi)


def filter_kernel(inner, dist_dev, turns, out):
    dists, width, block = out.shape
    core, _, spot = position(inner)

    def square(first, length):
        index = lax.broadcasted_iota(jnp.int32, (1, length), 1) + first
        signed = jnp.where(index < width // 2, index, index - width).astype(f32)
        return signed * signed * (1.0 / (width * width))

    def phases(first, length):
        values = square(first, length)
        rows = []
        for d in range(dists):
            other = d // dist_dev
            scale = turns[(core ^ other) * dist_dev + d % dist_dev]
            rows.append(whole_turns(scale, values))
        return jnp.concatenate(rows, axis=0)

    along = phases(0, width)
    across = phases(spot * block, block)
    sin_b, cos_b = jnp.sin(across), jnp.cos(across)
    with_sin = 2.0 * (cos_b - absorb_ratio * sin_b)
    with_cos = 2.0 * (sin_b + absorb_ratio * cos_b)
    turned = jnp.concatenate([jnp.sin(along), jnp.cos(along)], axis=0).T
    step = 128
    for at in range(0, width, step):
        rows = turned[at : at + step]
        transfer = [
            rows[:, d : d + 1] * with_sin[d : d + 1, :]
            + rows[:, dists + d : dists + d + 1] * with_cos[d : d + 1, :]
            for d in range(dists)
        ]
        denom = transfer[0] * transfer[0]
        for value in transfer[1:]:
            denom = denom + value * value
        scale = 1.0 / (denom + regularizer)
        for d in range(dists):
            out[d, at : at + step, :] = (transfer[d] * scale).astype(bf16)


def column_kernel(inner, outer, table, gain, *refs):
    pieces = dict(zip(send_order, refs[:inner]))
    *outs, stack, total, spectrum = refs[inner:]
    _, plane, spot = position(inner)
    dists, rows_dev, block = pieces[0].shape
    depth = inner * rows_dev
    for rel in range(inner):
        start = pl.multiple_of((spot ^ rel) * rows_dev, rows_dev)
        for d in range(dists):
            stack[d, pl.ds(start, rows_dev), :] = pieces[rel][d]
    part = table[:, pl.ds(pl.multiple_of(plane * depth, depth), depth)]
    for d in range(dists):
        got = jnp.dot(part, stack[d], preferred_element_type=f32) * gain[d].astype(f32)
        if d == 0:
            total[...] = got
        else:
            total[...] += got
    spectrum[...] = total[...].astype(bf16)
    middle = (plane == 1) | (plane == 2)
    first = jnp.where(middle, 1, 3)
    for rel, out in zip((0, first, 4 - first, 2), outs):
        rows = pl.ds(pl.multiple_of((plane ^ rel) * depth, depth), depth)
        value = jnp.dot(table[rows, :], spectrum[...], preferred_element_type=f32)
        out[...] = value.astype(bf16)


def far_kernel(inner, *refs):
    ours, got, out = refs[-3:]
    _, plane, _ = position(inner)
    middle = (plane == 1) | (plane == 2)
    more = jnp.where(middle, got[...].astype(f32), 0.0)
    out[...] = (ours[...].astype(f32) + more).astype(bf16)


def half_kernel(inner, ours, far, near, next_near, across, other, mine, again):
    _, plane, spot = position(inner)
    middle = (plane == 1) | (plane == 2)
    capacity = mine.shape[0]
    for out, pair in ((mine, spot // 2), (other, 1 - spot // 2)):
        rows = pl.ds(pl.multiple_of(pair * capacity, capacity), capacity)
        inside = next_near[rows, :].astype(f32) + across[rows, :].astype(f32)
        more = jnp.where(middle, inside, near[rows, :].astype(f32))
        got = ours[rows, :].astype(f32) + far[rows, :].astype(f32) + more
        out[...] = got.astype(bf16)
    again[...] = other[...]


def phase_kernel(inner, table, *refs):
    pieces = dict(zip(tail_order, refs[:inner]))
    out, joined = refs[-2:]
    _, _, spot = position(inner)
    block = refs[0].shape[1]
    for rel in range(inner):
        columns = pl.ds(pl.multiple_of((spot ^ rel) * block, block), block)
        joined[:, columns] = pieces[rel][...]
    out[...] = jnp.dot(joined[...], table[...], preferred_element_type=f32).astype(bf16)


def recon_kernel(own, order, slabs, weights, *refs):
    phases = refs[: 2 * own - 1]
    out, chosen, select = refs[2 * own - 1 :]
    core = lax.axis_index("dist")
    device = lax.axis_index("rows")
    total = None
    for step, phase in enumerate(phases):
        here = weights[order[0, (core ^ (step % 2)) * own + step // 2]]
        got = jnp.dot(phase[...], here, preferred_element_type=f32)
        total = got if total is None else total + got
    out[...] = total
    chosen[...] = weights[order[0, (core ^ 1) * own + own - 1]]
    parity = device % 2
    offset = parity * slabs[device - parity]
    slot = lax.broadcasted_iota(jnp.int32, select.shape, 0)
    source = lax.broadcasted_iota(jnp.int32, select.shape, 1)
    picked = (source == slot + offset) & (slot < slabs[device])
    select[...] = jnp.where(picked, 1.0, 0.0).astype(bf16)


def recon_last_kernel(weights, phase, before, select, out):
    total = before[...] + jnp.dot(phase[...], weights[...], preferred_element_type=f32)
    got = jnp.dot(select[...], total.astype(bf16), preferred_element_type=f32)
    out[...] = got.astype(bf16)


def vmem(count):
    return [pl.BlockSpec(memory_space=pltpu.VMEM)] * count


def from_hbm(value):
    return pltpu.with_memory_space_constraint(value, pltpu.HBM)


def in_hbm(count):
    return [pl.BlockSpec(memory_space=pltpu.HBM)] * count


def unread(count):
    return [pl.BlockSpec(memory_space=pl.ANY)] * count


def smem(count):
    return [pl.BlockSpec(memory_space=pltpu.SMEM)] * count


def plane_plan(inner, holograms, propagation, weights, angle_order, slab_rows):
    mbatch, angles, dist_dev, rows_dev, width = holograms.shape
    groups = lax.axis_size("rows")
    cores = lax.axis_size("dist")
    outer = groups // inner
    own = angles // cores
    block = width // inner
    depth = inner * rows_dev
    dists = cores * dist_dev
    pixels = weights.shape[2]
    capacity = 2 * rows_dev
    params = pltpu.CompilerParams(vmem_limit_bytes=16 * 2**20)
    one_out = pl.BlockSpec(memory_space=pltpu.VMEM)

    cheap = pl.CostEstimate(flops=1, bytes_accessed=1, transcendentals=0)

    def shaped(*shape):
        return jax.ShapeDtypeStruct(shape, bf16)

    table = jnp.asarray(hartley(width))

    def sent(value, target):
        pairs = []
        for c in range(cores):
            for r in range(groups):
                to_core, to_row = target(c, r)
                if to_row is not None:
                    pairs.append((c * groups + r, to_core * groups + to_row))
        return lax.ppermute(value, ("dist", "rows"), pairs)

    def to_other_core(c, r):
        return c ^ 1, r

    def to_spot(rel):
        return lambda c, r: (c, r ^ rel)

    def spread(pieces, order):
        return [sent(pieces[rel], to_spot(rel)) if rel else pieces[rel] for rel in order]

    def to_plane(rel):
        return lambda c, r: (c, (r // inner ^ rel) * inner + r % inner)

    def from_ends(c, r):
        z = r // inner
        return c, None if z in (1, 2) else (z ^ 1) * inner + r % inner

    def to_middle(c, r):
        z = r // inner
        return (c, (3 - z) * inner + r % inner) if z in (1, 2) else (c ^ 1, r)

    partner = sent(holograms[0], to_other_core)
    gain = pl.pallas_call(
        lambda *refs: filter_kernel(inner, dist_dev, *refs),
        out_shape=shaped(dists, width, block),
        in_specs=smem(1),
        out_specs=one_out,
        compiler_params=params,
        cost_estimate=cheap,
        name="filters",
    )(from_hbm(propagation))
    pieces = pl.pallas_call(
        lambda *refs: row_kernel(inner, *refs),
        out_shape=[shaped(dists, rows_dev, block)] * (own * inner),
        in_specs=in_hbm(1) + vmem(2) + unread(1),
        out_specs=vmem(own * inner),
        scratch_shapes=[
            pltpu.VMEM((own, dist_dev, rows_dev, width), bf16),
            pltpu.SemaphoreType.DMA,
        ],
        compiler_params=params,
        cost_estimate=cheap,
        name="row_spectra",
    )(from_hbm(holograms[0]), partner, table, gain)
    arrived = [
        spread(pieces[chunk * inner : (chunk + 1) * inner], send_order) for chunk in range(own)
    ]

    sums = []
    for chunk in range(own):
        blocks = pl.pallas_call(
            lambda *refs: column_kernel(inner, outer, *refs),
            out_shape=[shaped(depth, block)] * outer,
            in_specs=vmem(2 + inner),
            out_specs=vmem(outer),
            scratch_shapes=[
                pltpu.VMEM((dists, depth, block), bf16),
                pltpu.VMEM((width, block), f32),
                pltpu.VMEM((width, block), bf16),
            ],
            compiler_params=params,
            cost_estimate=cheap,
            name="columns",
        )(table, gain, *arrived[chunk])
        ours, first, second, third = blocks
        near = sent(first, to_plane(1))
        earlier = sums[-1][3:] if sums else []
        message = pl.pallas_call(
            lambda *refs: far_kernel(inner, *refs),
            out_shape=shaped(depth, block),
            in_specs=unread(len(earlier)) + vmem(2),
            out_specs=one_out,
            compiler_params=params,
            cost_estimate=cheap,
            name="far",
        )(*earlier, third, near)
        far = sent(message, to_plane(2))
        sums.append([ours, far, near, sent(second, from_ends), sent(second, to_middle)])

    phases = []
    for chunk in range(own):
        second, first, again = pl.pallas_call(
            lambda *refs: half_kernel(inner, *refs),
            out_shape=[shaped(capacity, block)] * 3,
            in_specs=vmem(5),
            out_specs=vmem(3),
            compiler_params=params,
            cost_estimate=cheap,
            name="half",
        )(*sums[chunk])
        pieces = spread([first, first, second, again], tail_order)
        phase = pl.pallas_call(
            lambda *refs: phase_kernel(inner, *refs),
            out_shape=shaped(capacity, width),
            in_specs=vmem(1 + inner),
            out_specs=one_out,
            scratch_shapes=[pltpu.VMEM((capacity, width), bf16)],
            compiler_params=params,
            cost_estimate=cheap,
            name="phase",
        )(table, *pieces)
        phases += [phase, sent(phase, to_other_core)]

    total, chosen, select = pl.pallas_call(
        lambda *refs: recon_kernel(own, *refs),
        out_shape=[
            jax.ShapeDtypeStruct((capacity, pixels), f32),
            shaped(width, pixels),
            shaped(capacity, capacity),
        ],
        in_specs=smem(2) + vmem(2 * own),
        out_specs=vmem(3),
        compiler_params=params,
        cost_estimate=cheap,
        name="recon",
    )(angle_order, slab_rows, weights, *phases[:-1])
    return pl.pallas_call(
        recon_last_kernel,
        out_shape=shaped(capacity, pixels),
        in_specs=vmem(4),
        out_specs=one_out,
        compiler_params=params,
        cost_estimate=cheap,
        name="recon",
    )(chosen, phases[-1], total, select)


def on_device(holograms, propagation, weights, angle_order, slab_rows):
    mbatch, angles, dist_dev, rows_dev, width = holograms.shape
    groups = lax.axis_size("rows")
    inner = 2 ** (int(math.log2(groups)) // 2)
    block = width // inner
    fits = (
        inner * (groups // inner) == groups
        and rows_dev % 16 == 0
        and block % 128 == 0
        and inner * rows_dev % 128 == 0
        and inner == 4
        and groups == inner * inner
        and lax.axis_size("dist") == 2
        and angles == 2 * lax.axis_size("dist")
    )
    if fits:
        return plane_plan(inner, holograms, propagation, weights, angle_order, slab_rows)
    return flat_plan(holograms, propagation, weights, angle_order, slab_rows)


def solution(mesh):
    return jax.shard_map(
        on_device,
        mesh=mesh,
        in_specs=(P(None, None, "dist", "rows", None), P(), P(None, None, "dist"), P(), P()),
        out_specs=P("rows", "dist"),
        check_vma=False,
    )
```

```python
import math

import jax
import jax.numpy as jnp
import numpy as np
from jax import lax
from jax.experimental import pallas as pl
from jax.experimental.pallas import tpu as pltpu
from jax.sharding import PartitionSpec as P

absorb_ratio = 0.1
regularizer = 0.05
bf16 = jnp.bfloat16
f32 = jnp.float32
send_order = (0, 2, 1, 3)
tail_order = (0, 2, 3, 1)


def hartley(length):
    index = np.arange(length)
    turned = (index[:, None] * index[None, :] % length) * (2.0 * math.pi / length)
    table = (np.cos(turned) + np.sin(turned)) / math.sqrt(length)
    return table.astype(bf16)


def signed_square(index, length):
    signed = jnp.where(index < length // 2, index, index - length).astype(f32)
    return signed * signed / float(length * length)


def filters(propagation, rows_sq, cols_sq):
    first = propagation[:, None] * rows_sq[None]
    second = propagation[:, None] * cols_sq[None]
    sin_b, cos_b = jnp.sin(second), jnp.cos(second)
    with_sin = 2.0 * (cos_b - absorb_ratio * sin_b)
    with_cos = 2.0 * (sin_b + absorb_ratio * cos_b)
    transfer = (
        jnp.sin(first)[:, :, None] * with_sin[:, None, :]
        + jnp.cos(first)[:, :, None] * with_cos[:, None, :]
    )
    denom = jnp.sum(transfer * transfer, axis=0) + regularizer
    return transfer / denom


def flat_plan(holograms, propagation, weights, angle_order, slab_rows):
    mbatch, angles, dist_dev, rows_dev, width = holograms.shape
    groups = lax.axis_size("rows")
    cores = lax.axis_size("dist")
    capacity = 2 * rows_dev
    own = angles // cores
    cols = width // groups
    dists = dist_dev * cores
    device = lax.axis_index("rows")
    table = jnp.asarray(hartley(width))
    index = jnp.arange(width, dtype=jnp.int32)
    my_cols = device * cols + jnp.arange(cols, dtype=jnp.int32)
    gain = filters(propagation, signed_square(my_cols, width), signed_square(index, width))

    mine = lax.all_to_all(holograms[0], "dist", split_axis=0, concat_axis=1, tiled=True)
    flat = mine.reshape(own * dists * rows_dev, width)
    spec = jnp.einsum("kx,mx->km", table, flat, preferred_element_type=f32)
    spec = spec.astype(bf16).reshape(groups, cols, own * dists * rows_dev)
    spec = lax.all_to_all(spec, "rows", split_axis=0, concat_axis=0, tiled=True)
    spec = spec.reshape(groups, cols, own, dists, rows_dev).transpose(1, 2, 3, 0, 4)
    spec = spec.reshape(cols * own * dists, width)
    full = jnp.dot(spec, table, preferred_element_type=f32)
    full = full.reshape(cols, own, dists, width)
    full = jnp.sum(full * gain.transpose(1, 0, 2)[:, None], axis=2).astype(bf16)
    half = jnp.einsum("yq,akq->yak", table, full.transpose(1, 0, 2), preferred_element_type=f32)
    half = half.astype(bf16).reshape(groups, rows_dev, own * cols)
    half = lax.all_to_all(half, "rows", split_axis=0, concat_axis=0, tiled=True)
    half = half.reshape(groups, rows_dev, own, cols).transpose(2, 1, 0, 3)
    half = half.reshape(own * rows_dev, width)
    phase = jnp.dot(half, table, preferred_element_type=f32)
    phase = phase.astype(bf16).reshape(own, rows_dev, width)
    phase = lax.all_gather(phase, "dist", axis=0, tiled=True)
    place = (angle_order[0][None, :] == jnp.arange(angles)[:, None]).astype(bf16)
    phase = jnp.einsum("wa,ayx->wyx", place, phase, preferred_element_type=f32)
    recon = jnp.einsum(
        "wyx,wxp->yp", phase.astype(bf16), weights, preferred_element_type=f32
    ).astype(bf16)
    parity = device % 2
    offset = parity * slab_rows[device - parity]
    count = slab_rows[device]
    pairs = [(source, source ^ 1) for source in range(groups)]
    partner = lax.ppermute(recon, "rows", pairs)
    lower = jnp.where(parity == 1, partner, recon)
    upper = jnp.where(parity == 1, recon, partner)
    paired = jnp.concatenate([lower, upper], axis=0)
    slot = jnp.arange(capacity, dtype=jnp.int32)[:, None]
    source = jnp.arange(capacity, dtype=jnp.int32)[None, :]
    select = ((source == offset + slot) & (slot < count)).astype(bf16)
    return jnp.dot(select, paired, preferred_element_type=f32).astype(bf16)


def position(inner):
    device = lax.axis_index("rows")
    return lax.axis_index("dist"), device // inner, device % inner


def row_kernel(inner, holo, there, table, after, *refs):
    outs, mine, loaded = refs[:-2], refs[-2], refs[-1]
    own = len(outs) // inner
    core, _, spot = position(inner)
    _, dist_dev, rows_dev, width = there.shape
    block = width // inner
    copy = pltpu.make_async_copy(holo.at[pl.ds(core * own, own)], mine, loaded)
    copy.start()
    for first, source in ((dist_dev, there.at[pl.ds(core * own, own)]), (0, mine)):
        if first == 0:
            copy.wait()
        rows = source[...].reshape(own * dist_dev * rows_dev, width)
        for rel in range(inner):
            part = table[:, pl.ds(pl.multiple_of((spot ^ rel) * block, block), block)]
            got = jnp.dot(rows, part, preferred_element_type=f32).astype(bf16)
            got = got.reshape(own, dist_dev, rows_dev, block)
            for chunk in range(own):
                outs[chunk * inner + rel][first : first + dist_dev] = got[chunk]


def whole_turns(scale, square):
    turns = scale * square * (0.5 / math.pi)
    return (turns - jnp.round(turns)) * (2.0 * math.pi)


def filter_kernel(inner, dist_dev, turns, out):
    dists, width, block = out.shape
    core, _, spot = position(inner)

    def square(first, length):
        index = lax.broadcasted_iota(jnp.int32, (1, length), 1) + first
        signed = jnp.where(index < width // 2, index, index - width).astype(f32)
        return signed * signed * (1.0 / (width * width))

    def phases(first, length):
        values = square(first, length)
        rows = []
        for d in range(dists):
            other = d // dist_dev
            scale = turns[(core ^ other) * dist_dev + d % dist_dev]
            rows.append(whole_turns(scale, values))
        return jnp.concatenate(rows, axis=0)

    along = phases(0, width)
    across = phases(spot * block, block)
    sin_b, cos_b = jnp.sin(across), jnp.cos(across)
    with_sin = 2.0 * (cos_b - absorb_ratio * sin_b)
    with_cos = 2.0 * (sin_b + absorb_ratio * cos_b)
    turned = jnp.concatenate([jnp.sin(along), jnp.cos(along)], axis=0).T
    step = 128
    for at in range(0, width, step):
        rows = turned[at : at + step]
        transfer = [
            rows[:, d : d + 1] * with_sin[d : d + 1, :]
            + rows[:, dists + d : dists + d + 1] * with_cos[d : d + 1, :]
            for d in range(dists)
        ]
        denom = transfer[0] * transfer[0]
        for value in transfer[1:]:
            denom = denom + value * value
        scale = 1.0 / (denom + regularizer)
        for d in range(dists):
            out[d, at : at + step, :] = (transfer[d] * scale).astype(bf16)


def column_kernel(inner, outer, table, gain, *refs):
    pieces = dict(zip(send_order, refs[:inner]))
    *outs, stack, total, spectrum = refs[inner:]
    _, plane, spot = position(inner)
    dists, rows_dev, block = pieces[0].shape
    depth = inner * rows_dev
    for rel in range(inner):
        start = pl.multiple_of((spot ^ rel) * rows_dev, rows_dev)
        for d in range(dists):
            stack[d, pl.ds(start, rows_dev), :] = pieces[rel][d]
    part = table[:, pl.ds(pl.multiple_of(plane * depth, depth), depth)]
    for d in range(dists):
        got = jnp.dot(part, stack[d], preferred_element_type=f32) * gain[d].astype(f32)
        if d == 0:
            total[...] = got
        else:
            total[...] += got
    spectrum[...] = total[...].astype(bf16)
    middle = (plane == 1) | (plane == 2)

    def rows_of(rel):
        rows = pl.ds(pl.multiple_of((plane ^ rel) * depth, depth), depth)
        return jnp.dot(table[rows, :], spectrum[...], preferred_element_type=f32)

    ours, lead, third, fourth = outs
    two, one, three = rows_of(2), rows_of(1), rows_of(3)
    lead[0] = jnp.where(middle, one, three).astype(bf16)
    lead[1] = two.astype(bf16)
    third[...] = jnp.where(middle, two, one).astype(bf16)
    fourth[...] = three.astype(bf16)
    ours[...] = rows_of(0).astype(bf16)


def far_kernel(inner, third, fourth, got, out_third, out_fourth):
    _, plane, _ = position(inner)
    middle = (plane == 1) | (plane == 2)
    for slot, ours, out in ((0, third, out_third), (1, fourth, out_fourth)):
        more = jnp.where(middle, got[slot].astype(f32), 0.0)
        out[...] = (ours[...].astype(f32) + more).astype(bf16)


def half_kernel(inner, ours, far, near, across, other, mine, again):
    _, plane, spot = position(inner)
    middle = (plane == 1) | (plane == 2)
    capacity = mine.shape[0]
    for out, pair in ((mine, spot // 2), (other, 1 - spot // 2)):
        rows = pl.ds(pl.multiple_of(pair * capacity, capacity), capacity)
        more = jnp.where(middle, across[rows, :].astype(f32), near[0, rows, :].astype(f32))
        got = ours[rows, :].astype(f32) + far[rows, :].astype(f32) + more
        out[...] = got.astype(bf16)
    again[...] = other[...]


def phase_kernel(inner, table, *refs):
    pieces = dict(zip(tail_order, refs[:inner]))
    out, joined = refs[-2:]
    _, _, spot = position(inner)
    block = refs[0].shape[1]
    for rel in range(inner):
        columns = pl.ds(pl.multiple_of((spot ^ rel) * block, block), block)
        joined[:, columns] = pieces[rel][...]
    out[...] = jnp.dot(joined[...], table[...], preferred_element_type=f32).astype(bf16)


def recon_kernel(own, order, slabs, weights, *refs):
    phases = refs[: 2 * own - 1]
    out, chosen, select = refs[2 * own - 1 :]
    core = lax.axis_index("dist")
    device = lax.axis_index("rows")
    total = None
    for step, phase in enumerate(phases):
        here = weights[order[0, (core ^ (step % 2)) * own + step // 2]]
        got = jnp.dot(phase[...], here, preferred_element_type=f32)
        total = got if total is None else total + got
    out[...] = total
    chosen[...] = weights[order[0, (core ^ 1) * own + own - 1]]
    parity = device % 2
    offset = parity * slabs[device - parity]
    slot = lax.broadcasted_iota(jnp.int32, select.shape, 0)
    source = lax.broadcasted_iota(jnp.int32, select.shape, 1)
    picked = (source == slot + offset) & (slot < slabs[device])
    select[...] = jnp.where(picked, 1.0, 0.0).astype(bf16)


def recon_last_kernel(weights, phase, before, select, out):
    total = before[...] + jnp.dot(phase[...], weights[...], preferred_element_type=f32)
    got = jnp.dot(select[...], total.astype(bf16), preferred_element_type=f32)
    out[...] = got.astype(bf16)


def vmem(count):
    return [pl.BlockSpec(memory_space=pltpu.VMEM)] * count


def from_hbm(value):
    return pltpu.with_memory_space_constraint(value, pltpu.HBM)


def in_hbm(count):
    return [pl.BlockSpec(memory_space=pltpu.HBM)] * count


def unread(count):
    return [pl.BlockSpec(memory_space=pl.ANY)] * count


def smem(count):
    return [pl.BlockSpec(memory_space=pltpu.SMEM)] * count


def plane_plan(inner, holograms, propagation, weights, angle_order, slab_rows):
    mbatch, angles, dist_dev, rows_dev, width = holograms.shape
    groups = lax.axis_size("rows")
    cores = lax.axis_size("dist")
    outer = groups // inner
    own = angles // cores
    block = width // inner
    depth = inner * rows_dev
    dists = cores * dist_dev
    pixels = weights.shape[2]
    capacity = 2 * rows_dev
    params = pltpu.CompilerParams(vmem_limit_bytes=16 * 2**20)
    one_out = pl.BlockSpec(memory_space=pltpu.VMEM)

    cheap = pl.CostEstimate(flops=1, bytes_accessed=1, transcendentals=0)

    def shaped(*shape):
        return jax.ShapeDtypeStruct(shape, bf16)

    table = jnp.asarray(hartley(width))

    def sent(value, target):
        pairs = []
        for c in range(cores):
            for r in range(groups):
                to_core, to_row = target(c, r)
                pairs.append((c * groups + r, to_core * groups + to_row))
        return lax.ppermute(value, ("dist", "rows"), pairs)

    def to_other_core(c, r):
        return c ^ 1, r

    def to_spot(rel):
        return lambda c, r: (c, r ^ rel)

    def spread(pieces, order):
        return [sent(pieces[rel], to_spot(rel)) if rel else pieces[rel] for rel in order]

    def to_plane(rel):
        return lambda c, r: (c, (r // inner ^ rel) * inner + r % inner)

    def around(c, r):
        return c, (1, 3, 0, 2)[r // inner] * inner + r % inner

    def to_middle(c, r):
        z = r // inner
        return (c, (3 - z) * inner + r % inner) if z in (1, 2) else (c ^ 1, r)

    partner = sent(holograms[0], to_other_core)
    gain = pl.pallas_call(
        lambda *refs: filter_kernel(inner, dist_dev, *refs),
        out_shape=shaped(dists, width, block),
        in_specs=smem(1),
        out_specs=one_out,
        compiler_params=params,
        cost_estimate=cheap,
        name="filters",
    )(from_hbm(propagation))
    pieces = pl.pallas_call(
        lambda *refs: row_kernel(inner, *refs),
        out_shape=[shaped(dists, rows_dev, block)] * (own * inner),
        in_specs=in_hbm(1) + vmem(2) + unread(1),
        out_specs=vmem(own * inner),
        scratch_shapes=[
            pltpu.VMEM((own, dist_dev, rows_dev, width), bf16),
            pltpu.SemaphoreType.DMA,
        ],
        compiler_params=params,
        cost_estimate=cheap,
        name="row_spectra",
    )(from_hbm(holograms[0]), partner, table, gain)
    arrived = [
        spread(pieces[chunk * inner : (chunk + 1) * inner], send_order) for chunk in range(own)
    ]

    sums = []
    for chunk in range(own):
        blocks = pl.pallas_call(
            lambda *refs: column_kernel(inner, outer, *refs),
            out_shape=[shaped(depth, block), shaped(2, depth, block)] + [shaped(depth, block)] * 2,
            in_specs=vmem(2 + inner),
            out_specs=vmem(outer),
            scratch_shapes=[
                pltpu.VMEM((dists, depth, block), bf16),
                pltpu.VMEM((width, block), f32),
                pltpu.VMEM((width, block), bf16),
            ],
            compiler_params=params,
            cost_estimate=cheap,
            name="columns",
        )(table, gain, *arrived[chunk])
        ours, lead, third, fourth = blocks
        near = sent(lead, to_plane(1))
        third, fourth = pl.pallas_call(
            lambda *refs: far_kernel(inner, *refs),
            out_shape=[shaped(depth, block)] * 2,
            in_specs=vmem(3),
            out_specs=vmem(2),
            compiler_params=params,
            cost_estimate=cheap,
            name="far",
        )(third, fourth, near)
        sums.append([ours, sent(third, around), near, sent(fourth, to_middle)])

    phases = []
    for chunk in range(own):
        second, first, again = pl.pallas_call(
            lambda *refs: half_kernel(inner, *refs),
            out_shape=[shaped(capacity, block)] * 3,
            in_specs=vmem(4),
            out_specs=vmem(3),
            compiler_params=params,
            cost_estimate=cheap,
            name="half",
        )(*sums[chunk])
        pieces = spread([first, first, second, again], tail_order)
        phase = pl.pallas_call(
            lambda *refs: phase_kernel(inner, *refs),
            out_shape=shaped(capacity, width),
            in_specs=vmem(1 + inner),
            out_specs=one_out,
            scratch_shapes=[pltpu.VMEM((capacity, width), bf16)],
            compiler_params=params,
            cost_estimate=cheap,
            name="phase",
        )(table, *pieces)
        phases += [phase, sent(phase, to_other_core)]

    total, chosen, select = pl.pallas_call(
        lambda *refs: recon_kernel(own, *refs),
        out_shape=[
            jax.ShapeDtypeStruct((capacity, pixels), f32),
            shaped(width, pixels),
            shaped(capacity, capacity),
        ],
        in_specs=smem(2) + vmem(2 * own),
        out_specs=vmem(3),
        compiler_params=params,
        cost_estimate=cheap,
        name="recon",
    )(angle_order, slab_rows, weights, *phases[:-1])
    return pl.pallas_call(
        recon_last_kernel,
        out_shape=shaped(capacity, pixels),
        in_specs=vmem(4),
        out_specs=one_out,
        compiler_params=params,
        cost_estimate=cheap,
        name="recon",
    )(chosen, phases[-1], total, select)


def on_device(holograms, propagation, weights, angle_order, slab_rows):
    mbatch, angles, dist_dev, rows_dev, width = holograms.shape
    groups = lax.axis_size("rows")
    inner = 2 ** (int(math.log2(groups)) // 2)
    block = width // inner
    fits = (
        inner * (groups // inner) == groups
        and rows_dev % 16 == 0
        and block % 128 == 0
        and inner * rows_dev % 128 == 0
        and inner == 4
        and groups == inner * inner
        and lax.axis_size("dist") == 2
        and angles == 2 * lax.axis_size("dist")
    )
    if fits:
        return plane_plan(inner, holograms, propagation, weights, angle_order, slab_rows)
    return flat_plan(holograms, propagation, weights, angle_order, slab_rows)


def solution(mesh):
    return jax.shard_map(
        on_device,
        mesh=mesh,
        in_specs=(P(None, None, "dist", "rows", None), P(), P(None, None, "dist"), P(), P()),
        out_specs=P("rows", "dist"),
        check_vma=False,
    )
```

```python
import math

import jax
import jax.numpy as jnp
import numpy as np
from jax import lax
from jax.experimental import pallas as pl
from jax.experimental.pallas import tpu as pltpu
from jax.sharding import PartitionSpec as P

absorb_ratio = 0.1
regularizer = 0.05
bf16 = jnp.bfloat16
f32 = jnp.float32
send_order = (0, 3, 2, 1)
tail_order = (0, 3, 2, 1)


def hartley(length):
    index = np.arange(length)
    turned = (index[:, None] * index[None, :] % length) * (2.0 * math.pi / length)
    table = (np.cos(turned) + np.sin(turned)) / math.sqrt(length)
    return table.astype(bf16)


def signed_square(index, length):
    signed = jnp.where(index < length // 2, index, index - length).astype(f32)
    return signed * signed / float(length * length)


def filters(propagation, rows_sq, cols_sq):
    first = propagation[:, None] * rows_sq[None]
    second = propagation[:, None] * cols_sq[None]
    sin_b, cos_b = jnp.sin(second), jnp.cos(second)
    with_sin = 2.0 * (cos_b - absorb_ratio * sin_b)
    with_cos = 2.0 * (sin_b + absorb_ratio * cos_b)
    transfer = (
        jnp.sin(first)[:, :, None] * with_sin[:, None, :]
        + jnp.cos(first)[:, :, None] * with_cos[:, None, :]
    )
    denom = jnp.sum(transfer * transfer, axis=0) + regularizer
    return transfer / denom


def flat_plan(holograms, propagation, weights, angle_order, slab_rows):
    mbatch, angles, dist_dev, rows_dev, width = holograms.shape
    groups = lax.axis_size("rows")
    cores = lax.axis_size("dist")
    capacity = 2 * rows_dev
    own = angles // cores
    cols = width // groups
    dists = dist_dev * cores
    device = lax.axis_index("rows")
    table = jnp.asarray(hartley(width))
    index = jnp.arange(width, dtype=jnp.int32)
    my_cols = device * cols + jnp.arange(cols, dtype=jnp.int32)
    gain = filters(propagation, signed_square(my_cols, width), signed_square(index, width))

    mine = lax.all_to_all(holograms[0], "dist", split_axis=0, concat_axis=1, tiled=True)
    flat = mine.reshape(own * dists * rows_dev, width)
    spec = jnp.einsum("kx,mx->km", table, flat, preferred_element_type=f32)
    spec = spec.astype(bf16).reshape(groups, cols, own * dists * rows_dev)
    spec = lax.all_to_all(spec, "rows", split_axis=0, concat_axis=0, tiled=True)
    spec = spec.reshape(groups, cols, own, dists, rows_dev).transpose(1, 2, 3, 0, 4)
    spec = spec.reshape(cols * own * dists, width)
    full = jnp.dot(spec, table, preferred_element_type=f32)
    full = full.reshape(cols, own, dists, width)
    full = jnp.sum(full * gain.transpose(1, 0, 2)[:, None], axis=2).astype(bf16)
    half = jnp.einsum("yq,akq->yak", table, full.transpose(1, 0, 2), preferred_element_type=f32)
    half = half.astype(bf16).reshape(groups, rows_dev, own * cols)
    half = lax.all_to_all(half, "rows", split_axis=0, concat_axis=0, tiled=True)
    half = half.reshape(groups, rows_dev, own, cols).transpose(2, 1, 0, 3)
    half = half.reshape(own * rows_dev, width)
    phase = jnp.dot(half, table, preferred_element_type=f32)
    phase = phase.astype(bf16).reshape(own, rows_dev, width)
    phase = lax.all_gather(phase, "dist", axis=0, tiled=True)
    place = (angle_order[0][None, :] == jnp.arange(angles)[:, None]).astype(bf16)
    phase = jnp.einsum("wa,ayx->wyx", place, phase, preferred_element_type=f32)
    recon = jnp.einsum(
        "wyx,wxp->yp", phase.astype(bf16), weights, preferred_element_type=f32
    ).astype(bf16)
    parity = device % 2
    offset = parity * slab_rows[device - parity]
    count = slab_rows[device]
    pairs = [(source, source ^ 1) for source in range(groups)]
    partner = lax.ppermute(recon, "rows", pairs)
    lower = jnp.where(parity == 1, partner, recon)
    upper = jnp.where(parity == 1, recon, partner)
    paired = jnp.concatenate([lower, upper], axis=0)
    slot = jnp.arange(capacity, dtype=jnp.int32)[:, None]
    source = jnp.arange(capacity, dtype=jnp.int32)[None, :]
    select = ((source == offset + slot) & (slot < count)).astype(bf16)
    return jnp.dot(select, paired, preferred_element_type=f32).astype(bf16)


def position(inner):
    device = lax.axis_index("rows")
    return lax.axis_index("dist"), device // inner, device % inner


def row_kernel(inner, holo, there, table, after, *refs):
    outs, mine, loaded = refs[:-2], refs[-2], refs[-1]
    own = len(outs) // inner
    core, _, spot = position(inner)
    _, dist_dev, rows_dev, width = there.shape
    block = width // inner
    copy = pltpu.make_async_copy(holo.at[pl.ds(core * own, own)], mine, loaded)
    copy.start()
    for first, source in ((dist_dev, there.at[pl.ds(core * own, own)]), (0, mine)):
        if first == 0:
            copy.wait()
        rows = source[...].reshape(own * dist_dev * rows_dev, width)
        for rel in range(inner):
            part = table[:, pl.ds(pl.multiple_of((spot ^ rel) * block, block), block)]
            got = jnp.dot(rows, part, preferred_element_type=f32).astype(bf16)
            got = got.reshape(own, dist_dev, rows_dev, block)
            for chunk in range(own):
                outs[chunk * inner + rel][first : first + dist_dev] = got[chunk]


def whole_turns(scale, square):
    turns = scale * square * (0.5 / math.pi)
    return (turns - jnp.round(turns)) * (2.0 * math.pi)


def filter_kernel(inner, dist_dev, turns, out):
    dists, width, block = out.shape
    core, _, spot = position(inner)

    def square(first, length):
        index = lax.broadcasted_iota(jnp.int32, (1, length), 1) + first
        signed = jnp.where(index < width // 2, index, index - width).astype(f32)
        return signed * signed * (1.0 / (width * width))

    def phases(first, length):
        values = square(first, length)
        rows = []
        for d in range(dists):
            other = d // dist_dev
            scale = turns[(core ^ other) * dist_dev + d % dist_dev]
            rows.append(whole_turns(scale, values))
        return jnp.concatenate(rows, axis=0)

    along = phases(0, width)
    across = phases(spot * block, block)
    sin_b, cos_b = jnp.sin(across), jnp.cos(across)
    with_sin = 2.0 * (cos_b - absorb_ratio * sin_b)
    with_cos = 2.0 * (sin_b + absorb_ratio * cos_b)
    turned = jnp.concatenate([jnp.sin(along), jnp.cos(along)], axis=0).T
    step = 128
    for at in range(0, width, step):
        rows = turned[at : at + step]
        transfer = [
            rows[:, d : d + 1] * with_sin[d : d + 1, :]
            + rows[:, dists + d : dists + d + 1] * with_cos[d : d + 1, :]
            for d in range(dists)
        ]
        denom = transfer[0] * transfer[0]
        for value in transfer[1:]:
            denom = denom + value * value
        scale = 1.0 / (denom + regularizer)
        for d in range(dists):
            out[d, at : at + step, :] = (transfer[d] * scale).astype(bf16)


def column_kernel(inner, outer, table, gain, *refs):
    pieces = dict(zip(send_order, refs[:inner]))
    *outs, stack, total, spectrum = refs[inner:]
    _, plane, spot = position(inner)
    dists, rows_dev, block = pieces[0].shape
    depth = inner * rows_dev
    for rel in range(inner):
        start = pl.multiple_of((spot ^ rel) * rows_dev, rows_dev)
        for d in range(dists):
            stack[d, pl.ds(start, rows_dev), :] = pieces[rel][d]
    part = table[:, pl.ds(pl.multiple_of(plane * depth, depth), depth)]
    for d in range(dists):
        got = jnp.dot(part, stack[d], preferred_element_type=f32) * gain[d].astype(f32)
        if d == 0:
            total[...] = got
        else:
            total[...] += got
    spectrum[...] = total[...].astype(bf16)
    middle = (plane == 1) | (plane == 2)
    first = jnp.where(middle, 1, 3)
    for rel, out in zip((0, first, 4 - first, 2), outs):
        rows = pl.ds(pl.multiple_of((plane ^ rel) * depth, depth), depth)
        value = jnp.dot(table[rows, :], spectrum[...], preferred_element_type=f32)
        out[...] = value.astype(bf16)


def far_kernel(inner, *refs):
    ours, got, out = refs[-3:]
    _, plane, _ = position(inner)
    middle = (plane == 1) | (plane == 2)
    more = jnp.where(middle, got[...].astype(f32), 0.0)
    out[...] = (ours[...].astype(f32) + more).astype(bf16)


def half_kernel(inner, ours, far, near, next_near, across, other, mine, again):
    _, plane, spot = position(inner)
    middle = (plane == 1) | (plane == 2)
    capacity = mine.shape[0]
    for out, pair in ((mine, spot // 2), (other, 1 - spot // 2)):
        rows = pl.ds(pl.multiple_of(pair * capacity, capacity), capacity)
        inside = next_near[rows, :].astype(f32) + across[rows, :].astype(f32)
        more = jnp.where(middle, inside, near[rows, :].astype(f32))
        got = ours[rows, :].astype(f32) + far[rows, :].astype(f32) + more
        out[...] = got.astype(bf16)
    again[...] = other[...]


def phase_kernel(inner, table, *refs):
    pieces = dict(zip(tail_order, refs[:inner]))
    out, joined = refs[-2:]
    _, _, spot = position(inner)
    block = refs[0].shape[1]
    for rel in range(inner):
        columns = pl.ds(pl.multiple_of((spot ^ rel) * block, block), block)
        joined[:, columns] = pieces[rel][...]
    out[...] = jnp.dot(joined[...], table[...], preferred_element_type=f32).astype(bf16)


def recon_kernel(own, order, slabs, weights, *refs):
    phases = refs[: 2 * own - 1]
    out, chosen, select = refs[2 * own - 1 :]
    core = lax.axis_index("dist")
    device = lax.axis_index("rows")
    total = None
    for step, phase in enumerate(phases):
        here = weights[order[0, (core ^ (step % 2)) * own + step // 2]]
        got = jnp.dot(phase[...], here, preferred_element_type=f32)
        total = got if total is None else total + got
    out[...] = total
    chosen[...] = weights[order[0, (core ^ 1) * own + own - 1]]
    parity = device % 2
    offset = parity * slabs[device - parity]
    slot = lax.broadcasted_iota(jnp.int32, select.shape, 0)
    source = lax.broadcasted_iota(jnp.int32, select.shape, 1)
    picked = (source == slot + offset) & (slot < slabs[device])
    select[...] = jnp.where(picked, 1.0, 0.0).astype(bf16)


def recon_last_kernel(weights, phase, before, select, out):
    total = before[...] + jnp.dot(phase[...], weights[...], preferred_element_type=f32)
    got = jnp.dot(select[...], total.astype(bf16), preferred_element_type=f32)
    out[...] = got.astype(bf16)


def vmem(count):
    return [pl.BlockSpec(memory_space=pltpu.VMEM)] * count


def from_hbm(value):
    return pltpu.with_memory_space_constraint(value, pltpu.HBM)


def in_hbm(count):
    return [pl.BlockSpec(memory_space=pltpu.HBM)] * count


def unread(count):
    return [pl.BlockSpec(memory_space=pl.ANY)] * count


def smem(count):
    return [pl.BlockSpec(memory_space=pltpu.SMEM)] * count


def plane_plan(inner, holograms, propagation, weights, angle_order, slab_rows):
    mbatch, angles, dist_dev, rows_dev, width = holograms.shape
    groups = lax.axis_size("rows")
    cores = lax.axis_size("dist")
    outer = groups // inner
    own = angles // cores
    block = width // inner
    depth = inner * rows_dev
    dists = cores * dist_dev
    pixels = weights.shape[2]
    capacity = 2 * rows_dev
    params = pltpu.CompilerParams(vmem_limit_bytes=16 * 2**20)
    one_out = pl.BlockSpec(memory_space=pltpu.VMEM)

    cheap = pl.CostEstimate(flops=1, bytes_accessed=1, transcendentals=0)

    def shaped(*shape):
        return jax.ShapeDtypeStruct(shape, bf16)

    table = jnp.asarray(hartley(width))

    def sent(value, target):
        pairs = []
        for c in range(cores):
            for r in range(groups):
                to_core, to_row = target(c, r)
                pairs.append((c * groups + r, to_core * groups + to_row))
        return lax.ppermute(value, ("dist", "rows"), pairs)

    def to_other_core(c, r):
        return c ^ 1, r

    def to_spot(rel):
        return lambda c, r: (c, r ^ rel)

    def spread(pieces, order):
        return [sent(pieces[rel], to_spot(rel)) if rel else pieces[rel] for rel in order]

    def to_plane(rel):
        return lambda c, r: (c, (r // inner ^ rel) * inner + r % inner)

    def to_middle(c, r):
        z = r // inner
        return (c, (3 - z) * inner + r % inner) if z in (1, 2) else (c ^ 1, r)

    partner = sent(holograms[0], to_other_core)
    gain = pl.pallas_call(
        lambda *refs: filter_kernel(inner, dist_dev, *refs),
        out_shape=shaped(dists, width, block),
        in_specs=smem(1),
        out_specs=one_out,
        compiler_params=params,
        cost_estimate=cheap,
        name="filters",
    )(from_hbm(propagation))
    pieces = pl.pallas_call(
        lambda *refs: row_kernel(inner, *refs),
        out_shape=[shaped(dists, rows_dev, block)] * (own * inner),
        in_specs=in_hbm(1) + vmem(2) + unread(1),
        out_specs=vmem(own * inner),
        scratch_shapes=[
            pltpu.VMEM((own, dist_dev, rows_dev, width), bf16),
            pltpu.SemaphoreType.DMA,
        ],
        compiler_params=params,
        cost_estimate=cheap,
        name="row_spectra",
    )(from_hbm(holograms[0]), partner, table, gain)
    arrived = [
        spread(pieces[chunk * inner : (chunk + 1) * inner], send_order) for chunk in range(own)
    ]

    sums = []
    for chunk in range(own):
        blocks = pl.pallas_call(
            lambda *refs: column_kernel(inner, outer, *refs),
            out_shape=[shaped(depth, block)] * outer,
            in_specs=vmem(2 + inner),
            out_specs=vmem(outer),
            scratch_shapes=[
                pltpu.VMEM((dists, depth, block), bf16),
                pltpu.VMEM((width, block), f32),
                pltpu.VMEM((width, block), bf16),
            ],
            compiler_params=params,
            cost_estimate=cheap,
            name="columns",
        )(table, gain, *arrived[chunk])
        ours, first, second, third = blocks
        near = sent(first, to_plane(1))
        earlier = sums[-1][3:] if sums else []
        message = pl.pallas_call(
            lambda *refs: far_kernel(inner, *refs),
            out_shape=shaped(depth, block),
            in_specs=unread(len(earlier)) + vmem(2),
            out_specs=one_out,
            compiler_params=params,
            cost_estimate=cheap,
            name="far",
        )(*earlier, third, near)
        far = sent(message, to_plane(2))
        sums.append([ours, far, near, sent(second, to_plane(1)), sent(second, to_middle)])

    phases = []
    for chunk in range(own):
        second, first, again = pl.pallas_call(
            lambda *refs: half_kernel(inner, *refs),
            out_shape=[shaped(capacity, block)] * 3,
            in_specs=vmem(5),
            out_specs=vmem(3),
            compiler_params=params,
            cost_estimate=cheap,
            name="half",
        )(*sums[chunk])
        pieces = spread([first, first, second, again], tail_order)
        phase = pl.pallas_call(
            lambda *refs: phase_kernel(inner, *refs),
            out_shape=shaped(capacity, width),
            in_specs=vmem(1 + inner),
            out_specs=one_out,
            scratch_shapes=[pltpu.VMEM((capacity, width), bf16)],
            compiler_params=params,
            cost_estimate=cheap,
            name="phase",
        )(table, *pieces)
        phases += [phase, sent(phase, to_other_core)]

    total, chosen, select = pl.pallas_call(
        lambda *refs: recon_kernel(own, *refs),
        out_shape=[
            jax.ShapeDtypeStruct((capacity, pixels), f32),
            shaped(width, pixels),
            shaped(capacity, capacity),
        ],
        in_specs=smem(2) + vmem(2 * own),
        out_specs=vmem(3),
        compiler_params=params,
        cost_estimate=cheap,
        name="recon",
    )(angle_order, slab_rows, weights, *phases[:-1])
    return pl.pallas_call(
        recon_last_kernel,
        out_shape=shaped(capacity, pixels),
        in_specs=vmem(4),
        out_specs=one_out,
        compiler_params=params,
        cost_estimate=cheap,
        name="recon",
    )(chosen, phases[-1], total, select)


def on_device(holograms, propagation, weights, angle_order, slab_rows):
    mbatch, angles, dist_dev, rows_dev, width = holograms.shape
    groups = lax.axis_size("rows")
    inner = 2 ** (int(math.log2(groups)) // 2)
    block = width // inner
    fits = (
        inner * (groups // inner) == groups
        and rows_dev % 16 == 0
        and block % 128 == 0
        and inner * rows_dev % 128 == 0
        and inner == 4
        and groups == inner * inner
        and lax.axis_size("dist") == 2
        and angles == 2 * lax.axis_size("dist")
    )
    if fits:
        return plane_plan(inner, holograms, propagation, weights, angle_order, slab_rows)
    return flat_plan(holograms, propagation, weights, angle_order, slab_rows)


def solution(mesh):
    return jax.shard_map(
        on_device,
        mesh=mesh,
        in_specs=(P(None, None, "dist", "rows", None), P(), P(None, None, "dist"), P(), P()),
        out_specs=P("rows", "dist"),
        check_vma=False,
    )
```

```python
import math

import jax
import jax.numpy as jnp
import numpy as np
from jax import lax
from jax.experimental import pallas as pl
from jax.experimental.pallas import tpu as pltpu
from jax.sharding import PartitionSpec as P

absorb_ratio = 0.1
regularizer = 0.05
bf16 = jnp.bfloat16
f32 = jnp.float32
send_order = (0, 2, 1, 3)
tail_order = (0, 2, 3, 1)


def hartley(length):
    index = np.arange(length)
    turned = (index[:, None] * index[None, :] % length) * (2.0 * math.pi / length)
    table = (np.cos(turned) + np.sin(turned)) / math.sqrt(length)
    return table.astype(bf16)


def signed_square(index, length):
    signed = jnp.where(index < length // 2, index, index - length).astype(f32)
    return signed * signed / float(length * length)


def filters(propagation, rows_sq, cols_sq):
    first = propagation[:, None] * rows_sq[None]
    second = propagation[:, None] * cols_sq[None]
    sin_b, cos_b = jnp.sin(second), jnp.cos(second)
    with_sin = 2.0 * (cos_b - absorb_ratio * sin_b)
    with_cos = 2.0 * (sin_b + absorb_ratio * cos_b)
    transfer = (
        jnp.sin(first)[:, :, None] * with_sin[:, None, :]
        + jnp.cos(first)[:, :, None] * with_cos[:, None, :]
    )
    denom = jnp.sum(transfer * transfer, axis=0) + regularizer
    return transfer / denom


def flat_plan(holograms, propagation, weights, angle_order, slab_rows):
    mbatch, angles, dist_dev, rows_dev, width = holograms.shape
    groups = lax.axis_size("rows")
    cores = lax.axis_size("dist")
    capacity = 2 * rows_dev
    own = angles // cores
    cols = width // groups
    dists = dist_dev * cores
    device = lax.axis_index("rows")
    table = jnp.asarray(hartley(width))
    index = jnp.arange(width, dtype=jnp.int32)
    my_cols = device * cols + jnp.arange(cols, dtype=jnp.int32)
    gain = filters(propagation, signed_square(my_cols, width), signed_square(index, width))

    mine = lax.all_to_all(holograms[0], "dist", split_axis=0, concat_axis=1, tiled=True)
    flat = mine.reshape(own * dists * rows_dev, width)
    spec = jnp.einsum("kx,mx->km", table, flat, preferred_element_type=f32)
    spec = spec.astype(bf16).reshape(groups, cols, own * dists * rows_dev)
    spec = lax.all_to_all(spec, "rows", split_axis=0, concat_axis=0, tiled=True)
    spec = spec.reshape(groups, cols, own, dists, rows_dev).transpose(1, 2, 3, 0, 4)
    spec = spec.reshape(cols * own * dists, width)
    full = jnp.dot(spec, table, preferred_element_type=f32)
    full = full.reshape(cols, own, dists, width)
    full = jnp.sum(full * gain.transpose(1, 0, 2)[:, None], axis=2).astype(bf16)
    half = jnp.einsum("yq,akq->yak", table, full.transpose(1, 0, 2), preferred_element_type=f32)
    half = half.astype(bf16).reshape(groups, rows_dev, own * cols)
    half = lax.all_to_all(half, "rows", split_axis=0, concat_axis=0, tiled=True)
    half = half.reshape(groups, rows_dev, own, cols).transpose(2, 1, 0, 3)
    half = half.reshape(own * rows_dev, width)
    phase = jnp.dot(half, table, preferred_element_type=f32)
    phase = phase.astype(bf16).reshape(own, rows_dev, width)
    phase = lax.all_gather(phase, "dist", axis=0, tiled=True)
    place = (angle_order[0][None, :] == jnp.arange(angles)[:, None]).astype(bf16)
    phase = jnp.einsum("wa,ayx->wyx", place, phase, preferred_element_type=f32)
    recon = jnp.einsum(
        "wyx,wxp->yp", phase.astype(bf16), weights, preferred_element_type=f32
    ).astype(bf16)
    parity = device % 2
    offset = parity * slab_rows[device - parity]
    count = slab_rows[device]
    pairs = [(source, source ^ 1) for source in range(groups)]
    partner = lax.ppermute(recon, "rows", pairs)
    lower = jnp.where(parity == 1, partner, recon)
    upper = jnp.where(parity == 1, recon, partner)
    paired = jnp.concatenate([lower, upper], axis=0)
    slot = jnp.arange(capacity, dtype=jnp.int32)[:, None]
    source = jnp.arange(capacity, dtype=jnp.int32)[None, :]
    select = ((source == offset + slot) & (slot < count)).astype(bf16)
    return jnp.dot(select, paired, preferred_element_type=f32).astype(bf16)


def position(inner):
    device = lax.axis_index("rows")
    return lax.axis_index("dist"), device // inner, device % inner


def take_kernel(holo, after, out, arrived):
    own = out.shape[0]
    core = lax.axis_index("dist")
    copy = pltpu.make_async_copy(holo.at[pl.ds(core * own, own)], out, arrived)
    copy.start()
    copy.wait()


def row_kernel(inner, mine, there, table, *outs):
    own = len(outs) // inner
    core, _, spot = position(inner)
    _, dist_dev, rows_dev, width = there.shape
    block = width // inner
    rows = jnp.concatenate(
        [
            source.reshape(own * dist_dev * rows_dev, width)
            for source in (mine[...], there[pl.ds(core * own, own)])
        ],
        axis=0,
    )
    for rel in range(inner):
        part = table[:, pl.ds(pl.multiple_of((spot ^ rel) * block, block), block)]
        got = jnp.dot(rows, part, preferred_element_type=f32).astype(bf16)
        got = got.reshape(2, own, dist_dev, rows_dev, block)
        for chunk in range(own):
            out = outs[chunk * inner + rel]
            out[0:dist_dev] = got[0, chunk]
            out[dist_dev:] = got[1, chunk]


def whole_turns(scale, square):
    turns = scale * square * (0.5 / math.pi)
    return (turns - jnp.round(turns)) * (2.0 * math.pi)


def filter_kernel(inner, dist_dev, turns, after, out):
    dists, height, block = out.shape
    width = height
    core, _, spot = position(inner)

    def square(first, length):
        index = lax.broadcasted_iota(jnp.int32, (1, length), 1) + first
        signed = jnp.where(index < width // 2, index, index - width).astype(f32)
        return signed * signed * (1.0 / (width * width))

    def phases(first, length):
        values = square(first, length)
        rows = []
        for d in range(dists):
            other = d // dist_dev
            scale = turns[(core ^ other) * dist_dev + d % dist_dev]
            rows.append(whole_turns(scale, values))
        return jnp.concatenate(rows, axis=0)

    along = phases(0, height)
    across = phases(spot * block, block)
    sin_b, cos_b = jnp.sin(across), jnp.cos(across)
    with_sin = 2.0 * (cos_b - absorb_ratio * sin_b)
    with_cos = 2.0 * (sin_b + absorb_ratio * cos_b)
    turned = jnp.concatenate([jnp.sin(along), jnp.cos(along)], axis=0).T
    step = 128
    for at in range(0, height, step):
        rows = turned[at : at + step]
        transfer = [
            rows[:, d : d + 1] * with_sin[d : d + 1, :]
            + rows[:, dists + d : dists + d + 1] * with_cos[d : d + 1, :]
            for d in range(dists)
        ]
        denom = transfer[0] * transfer[0]
        for value in transfer[1:]:
            denom = denom + value * value
        scale = 1.0 / (denom + regularizer)
        for d in range(dists):
            out[d, at : at + step, :] = (transfer[d] * scale).astype(bf16)


def column_kernel(inner, outer, table, gain, *refs):
    pieces = dict(zip(send_order, refs[:inner]))
    *outs, stack, total, spectrum = refs[inner:]
    core, plane, spot = position(inner)
    dists, rows_dev, block = pieces[0].shape
    depth = inner * rows_dev
    for rel in range(inner):
        start = pl.multiple_of((spot ^ rel) * rows_dev, rows_dev)
        for d in range(dists):
            stack[d, pl.ds(start, rows_dev), :] = pieces[rel][d]
    part = table[:, pl.ds(pl.multiple_of(plane * depth, depth), depth)]
    for d in range(dists):
        value = jnp.dot(part, stack[d], preferred_element_type=f32) * gain[d].astype(f32)
        if d == 0:
            total[...] = value
        else:
            total[...] += value
    spectrum[...] = total[...].astype(bf16)
    middle = (plane == 1) | (plane == 2)
    first = jnp.where(middle, 1, 3)
    for rel, out in zip((0, first, 4 - first, 2), outs):
        rows = pl.ds(pl.multiple_of((plane ^ rel) * depth, depth), depth)
        value = jnp.dot(table[rows, :], spectrum[...], preferred_element_type=f32)
        out[...] = value.astype(bf16)


def far_kernel(inner, *refs):
    ours, got, out = refs[-3:]
    _, plane, _ = position(inner)
    middle = (plane == 1) | (plane == 2)
    more = jnp.where(middle, got[...].astype(f32), 0.0)
    out[...] = (ours[...].astype(f32) + more).astype(bf16)


def half_kernel(inner, ours, far, near, next_near, across, other, mine, again):
    _, plane, spot = position(inner)
    middle = (plane == 1) | (plane == 2)
    capacity = mine.shape[0]
    for out, pair in ((mine, spot // 2), (other, 1 - spot // 2)):
        rows = pl.ds(pl.multiple_of(pair * capacity, capacity), capacity)
        inside = next_near[rows, :].astype(f32) + across[rows, :].astype(f32)
        more = jnp.where(middle, inside, near[rows, :].astype(f32))
        got = ours[rows, :].astype(f32) + far[rows, :].astype(f32) + more
        out[...] = got.astype(bf16)
    again[...] = other[...]


def phase_kernel(inner, table, *refs):
    pieces = dict(zip(tail_order, refs[:inner]))
    out, joined = refs[-2:]
    _, _, spot = position(inner)
    block = refs[0].shape[1]
    for rel in range(inner):
        columns = pl.ds(pl.multiple_of((spot ^ rel) * block, block), block)
        joined[:, columns] = pieces[rel][...]
    out[...] = jnp.dot(joined[...], table[...], preferred_element_type=f32).astype(bf16)


def recon_kernel(own, order, slabs, weights, *refs):
    phases = refs[: 2 * own - 1]
    out, chosen, select = refs[2 * own - 1 :]
    core = lax.axis_index("dist")
    device = lax.axis_index("rows")
    total = None
    for step, phase in enumerate(phases):
        here = weights[order[0, (core ^ (step % 2)) * own + step // 2]]
        got = jnp.dot(phase[...], here, preferred_element_type=f32)
        total = got if total is None else total + got
    out[...] = total
    chosen[...] = weights[order[0, (core ^ 1) * own + own - 1]]
    parity = device % 2
    offset = parity * slabs[device - parity]
    slot = lax.broadcasted_iota(jnp.int32, select.shape, 0)
    source = lax.broadcasted_iota(jnp.int32, select.shape, 1)
    picked = (source == slot + offset) & (slot < slabs[device])
    select[...] = jnp.where(picked, 1.0, 0.0).astype(bf16)


def recon_last_kernel(weights, phase, before, select, out):
    total = before[...] + jnp.dot(phase[...], weights[...], preferred_element_type=f32)
    got = jnp.dot(select[...], total.astype(bf16), preferred_element_type=f32)
    out[...] = got.astype(bf16)


def vmem(count):
    return [pl.BlockSpec(memory_space=pltpu.VMEM)] * count


def from_hbm(value):
    return pltpu.with_memory_space_constraint(value, pltpu.HBM)


def in_hbm(count):
    return [pl.BlockSpec(memory_space=pltpu.HBM)] * count


def unread(count):
    return [pl.BlockSpec(memory_space=pl.ANY)] * count


def smem(count):
    return [pl.BlockSpec(memory_space=pltpu.SMEM)] * count


def plane_plan(inner, holograms, propagation, weights, angle_order, slab_rows):
    mbatch, angles, dist_dev, rows_dev, width = holograms.shape
    groups = lax.axis_size("rows")
    cores = lax.axis_size("dist")
    outer = groups // inner
    own = angles // cores
    block = width // inner
    depth = inner * rows_dev
    dists = cores * dist_dev
    pixels = weights.shape[2]
    capacity = 2 * rows_dev
    params = pltpu.CompilerParams(vmem_limit_bytes=16 * 2**20)
    one_out = pl.BlockSpec(memory_space=pltpu.VMEM)

    cheap = pl.CostEstimate(flops=1, bytes_accessed=1, transcendentals=0)

    def shaped(*shape):
        return jax.ShapeDtypeStruct(shape, bf16)

    table = jnp.asarray(hartley(width))

    def sent(value, target):
        pairs = []
        for c in range(cores):
            for r in range(groups):
                to_core, to_row = target(c, r)
                pairs.append((c * groups + r, to_core * groups + to_row))
        return lax.ppermute(value, ("dist", "rows"), pairs)

    def to_other_core(c, r):
        return c ^ 1, r

    def to_spot(rel):
        return lambda c, r: (c, r ^ rel)

    def spread(pieces, order):
        return [sent(pieces[rel], to_spot(rel)) if rel else pieces[rel] for rel in order]

    def to_plane(rel):
        return lambda c, r: (c, (r // inner ^ rel) * inner + r % inner)

    def to_middle(c, r):
        z = r // inner
        return (c, (3 - z) * inner + r % inner) if z in (1, 2) else (c ^ 1, r)

    partner = sent(holograms[0], to_other_core)
    mine = pl.pallas_call(
        take_kernel,
        out_shape=shaped(own, dist_dev, rows_dev, width),
        in_specs=in_hbm(1) + vmem(1),
        out_specs=one_out,
        scratch_shapes=[pltpu.SemaphoreType.DMA],
        compiler_params=params,
        cost_estimate=cheap,
        name="take",
    )(from_hbm(holograms[0]), table)
    pieces = pl.pallas_call(
        lambda *refs: row_kernel(inner, *refs),
        out_shape=[shaped(dists, rows_dev, block)] * (own * inner),
        in_specs=vmem(3),
        out_specs=vmem(own * inner),
        compiler_params=params,
        cost_estimate=cheap,
        name="row_spectra",
    )(mine, partner, table)
    arrived = [
        spread(pieces[chunk * inner : (chunk + 1) * inner], send_order) for chunk in range(own)
    ]

    gain = pl.pallas_call(
        lambda *refs: filter_kernel(inner, dist_dev, *refs),
        out_shape=shaped(dists, width, block),
        in_specs=smem(1) + unread(1),
        out_specs=one_out,
        compiler_params=params,
        cost_estimate=cheap,
        name="filters",
    )(from_hbm(propagation), pieces[0])

    sums = []
    for chunk in range(own):
        blocks = pl.pallas_call(
            lambda *refs: column_kernel(inner, outer, *refs),
            out_shape=[shaped(depth, block)] * outer,
            in_specs=vmem(2 + inner),
            out_specs=vmem(outer),
            scratch_shapes=[
                pltpu.VMEM((dists, depth, block), bf16),
                pltpu.VMEM((width, block), f32),
                pltpu.VMEM((width, block), bf16),
            ],
            compiler_params=params,
            cost_estimate=cheap,
            name="columns",
        )(table, gain, *arrived[chunk])
        ours, first, second, third = blocks
        near = sent(first, to_plane(1))
        others = [sent(second, to_plane(1)), sent(second, to_middle)]
        earlier = sums[-1][3:] if sums else others
        message = pl.pallas_call(
            lambda *refs: far_kernel(inner, *refs),
            out_shape=shaped(depth, block),
            in_specs=unread(len(earlier)) + vmem(2),
            out_specs=one_out,
            compiler_params=params,
            cost_estimate=cheap,
            name="far",
        )(*earlier, third, near)
        far = sent(message, to_plane(2))
        sums.append([ours, far, near, *others])

    phases = []
    for chunk in range(own):
        second, first, again = pl.pallas_call(
            lambda *refs: half_kernel(inner, *refs),
            out_shape=[shaped(capacity, block)] * 3,
            in_specs=vmem(5),
            out_specs=vmem(3),
            compiler_params=params,
            cost_estimate=cheap,
            name="half",
        )(*sums[chunk])
        pieces = spread([first, first, second, again], tail_order)
        phase = pl.pallas_call(
            lambda *refs: phase_kernel(inner, *refs),
            out_shape=shaped(capacity, width),
            in_specs=vmem(1 + inner),
            out_specs=one_out,
            scratch_shapes=[pltpu.VMEM((capacity, width), bf16)],
            compiler_params=params,
            cost_estimate=cheap,
            name="phase",
        )(table, *pieces)
        phases += [phase, sent(phase, to_other_core)]

    total, chosen, select = pl.pallas_call(
        lambda *refs: recon_kernel(own, *refs),
        out_shape=[
            jax.ShapeDtypeStruct((capacity, pixels), f32),
            shaped(width, pixels),
            shaped(capacity, capacity),
        ],
        in_specs=smem(2) + vmem(2 * own),
        out_specs=vmem(3),
        compiler_params=params,
        cost_estimate=cheap,
        name="recon",
    )(angle_order, slab_rows, weights, *phases[:-1])
    return pl.pallas_call(
        recon_last_kernel,
        out_shape=shaped(capacity, pixels),
        in_specs=vmem(4),
        out_specs=one_out,
        compiler_params=params,
        cost_estimate=cheap,
        name="recon",
    )(chosen, phases[-1], total, select)


def on_device(holograms, propagation, weights, angle_order, slab_rows):
    mbatch, angles, dist_dev, rows_dev, width = holograms.shape
    groups = lax.axis_size("rows")
    inner = 2 ** (int(math.log2(groups)) // 2)
    block = width // inner
    fits = (
        inner * (groups // inner) == groups
        and rows_dev % 16 == 0
        and block % 128 == 0
        and inner * rows_dev % 128 == 0
        and inner == 4
        and groups == inner * inner
        and lax.axis_size("dist") == 2
        and angles == 2 * lax.axis_size("dist")
    )
    if fits:
        return plane_plan(inner, holograms, propagation, weights, angle_order, slab_rows)
    return flat_plan(holograms, propagation, weights, angle_order, slab_rows)


def solution(mesh):
    return jax.shard_map(
        on_device,
        mesh=mesh,
        in_specs=(P(None, None, "dist", "rows", None), P(), P(None, None, "dist"), P(), P()),
        out_specs=P("rows", "dist"),
        check_vma=False,
    )
```

```python
import math

import jax
import jax.numpy as jnp
import numpy as np
from jax import lax
from jax.experimental import pallas as pl
from jax.experimental.pallas import tpu as pltpu
from jax.sharding import PartitionSpec as P

absorb_ratio = 0.1
regularizer = 0.05
bf16 = jnp.bfloat16
f32 = jnp.float32
send_order = (0, 2, 1, 3)
tail_order = (0, 2, 3, 1)


def hartley(length):
    index = np.arange(length)
    turned = (index[:, None] * index[None, :] % length) * (2.0 * math.pi / length)
    table = (np.cos(turned) + np.sin(turned)) / math.sqrt(length)
    return table.astype(bf16)


def signed_square(index, length):
    signed = jnp.where(index < length // 2, index, index - length).astype(f32)
    return signed * signed / float(length * length)


def filters(propagation, rows_sq, cols_sq):
    first = propagation[:, None] * rows_sq[None]
    second = propagation[:, None] * cols_sq[None]
    sin_b, cos_b = jnp.sin(second), jnp.cos(second)
    with_sin = 2.0 * (cos_b - absorb_ratio * sin_b)
    with_cos = 2.0 * (sin_b + absorb_ratio * cos_b)
    transfer = (
        jnp.sin(first)[:, :, None] * with_sin[:, None, :]
        + jnp.cos(first)[:, :, None] * with_cos[:, None, :]
    )
    denom = jnp.sum(transfer * transfer, axis=0) + regularizer
    return transfer / denom


def flat_plan(holograms, propagation, weights, angle_order, slab_rows):
    mbatch, angles, dist_dev, rows_dev, width = holograms.shape
    groups = lax.axis_size("rows")
    cores = lax.axis_size("dist")
    capacity = 2 * rows_dev
    own = angles // cores
    cols = width // groups
    dists = dist_dev * cores
    device = lax.axis_index("rows")
    table = jnp.asarray(hartley(width))
    index = jnp.arange(width, dtype=jnp.int32)
    my_cols = device * cols + jnp.arange(cols, dtype=jnp.int32)
    gain = filters(propagation, signed_square(my_cols, width), signed_square(index, width))

    mine = lax.all_to_all(holograms[0], "dist", split_axis=0, concat_axis=1, tiled=True)
    flat = mine.reshape(own * dists * rows_dev, width)
    spec = jnp.einsum("kx,mx->km", table, flat, preferred_element_type=f32)
    spec = spec.astype(bf16).reshape(groups, cols, own * dists * rows_dev)
    spec = lax.all_to_all(spec, "rows", split_axis=0, concat_axis=0, tiled=True)
    spec = spec.reshape(groups, cols, own, dists, rows_dev).transpose(1, 2, 3, 0, 4)
    spec = spec.reshape(cols * own * dists, width)
    full = jnp.dot(spec, table, preferred_element_type=f32)
    full = full.reshape(cols, own, dists, width)
    full = jnp.sum(full * gain.transpose(1, 0, 2)[:, None], axis=2).astype(bf16)
    half = jnp.einsum("yq,akq->yak", table, full.transpose(1, 0, 2), preferred_element_type=f32)
    half = half.astype(bf16).reshape(groups, rows_dev, own * cols)
    half = lax.all_to_all(half, "rows", split_axis=0, concat_axis=0, tiled=True)
    half = half.reshape(groups, rows_dev, own, cols).transpose(2, 1, 0, 3)
    half = half.reshape(own * rows_dev, width)
    phase = jnp.dot(half, table, preferred_element_type=f32)
    phase = phase.astype(bf16).reshape(own, rows_dev, width)
    phase = lax.all_gather(phase, "dist", axis=0, tiled=True)
    place = (angle_order[0][None, :] == jnp.arange(angles)[:, None]).astype(bf16)
    phase = jnp.einsum("wa,ayx->wyx", place, phase, preferred_element_type=f32)
    recon = jnp.einsum(
        "wyx,wxp->yp", phase.astype(bf16), weights, preferred_element_type=f32
    ).astype(bf16)
    parity = device % 2
    offset = parity * slab_rows[device - parity]
    count = slab_rows[device]
    pairs = [(source, source ^ 1) for source in range(groups)]
    partner = lax.ppermute(recon, "rows", pairs)
    lower = jnp.where(parity == 1, partner, recon)
    upper = jnp.where(parity == 1, recon, partner)
    paired = jnp.concatenate([lower, upper], axis=0)
    slot = jnp.arange(capacity, dtype=jnp.int32)[:, None]
    source = jnp.arange(capacity, dtype=jnp.int32)[None, :]
    select = ((source == offset + slot) & (slot < count)).astype(bf16)
    return jnp.dot(select, paired, preferred_element_type=f32).astype(bf16)


def position(inner):
    device = lax.axis_index("rows")
    return lax.axis_index("dist"), device // inner, device % inner


def row_kernel(inner, holo, there, table, after, *refs):
    outs, mine, loaded = refs[:-2], refs[-2], refs[-1]
    own = len(outs) // inner
    core, _, spot = position(inner)
    _, dist_dev, rows_dev, width = there.shape
    block = width // inner
    copies = [
        pltpu.make_async_copy(
            holo.at[core * own + chunk, d], mine.at[chunk, d], loaded.at[chunk * dist_dev + d]
        )
        for chunk in range(own)
        for d in range(dist_dev)
    ]
    for copy in copies:
        copy.start()
    for first, source in ((dist_dev, there.at[pl.ds(core * own, own)]), (0, mine)):
        if first == 0:
            for copy in copies:
                copy.wait()
        rows = source[...].reshape(own * dist_dev * rows_dev, width)
        for rel in range(inner):
            part = table[:, pl.ds(pl.multiple_of((spot ^ rel) * block, block), block)]
            got = jnp.dot(rows, part, preferred_element_type=f32).astype(bf16)
            got = got.reshape(own, dist_dev, rows_dev, block)
            for chunk in range(own):
                outs[chunk * inner + rel][first : first + dist_dev] = got[chunk]


def sine_of_turns(turns):
    turns = turns - jnp.round(turns)
    folded = jnp.where(jnp.abs(turns) > 0.25, jnp.where(turns > 0, 0.5, -0.5) - turns, turns)
    angle = folded * (2.0 * math.pi)
    square = angle * angle
    series = jnp.full_like(angle, 1.0 / math.factorial(13))
    for order in range(11, 0, -2):
        series = series * -square + 1.0 / math.factorial(order)
    return angle * series


def filter_kernel(inner, dist_dev, propagation, out):
    dists, width, block = out.shape
    core, _, spot = position(inner)

    def square(first, length):
        index = lax.broadcasted_iota(jnp.int32, (1, length), 1) + first
        signed = jnp.where(index < width // 2, index, index - width).astype(f32)
        return signed * signed * (1.0 / (width * width))

    def phases(first, length):
        values = square(first, length)
        rows = []
        for d in range(dists):
            other = d // dist_dev
            scale = propagation[(core ^ other) * dist_dev + d % dist_dev]
            rows.append(scale * values * (0.5 / math.pi))
        turns = jnp.concatenate(rows, axis=0)
        return sine_of_turns(jnp.concatenate([turns, turns + 0.25], axis=0))

    along = phases(0, width)
    across = phases(spot * block, block)
    sin_b, cos_b = across[:dists], across[dists:]
    with_sin = 2.0 * (cos_b - absorb_ratio * sin_b)
    with_cos = 2.0 * (sin_b + absorb_ratio * cos_b)
    turned = along.T
    step = 128
    for at in range(0, width, step):
        rows = turned[at : at + step]
        transfer = [
            rows[:, d : d + 1] * with_sin[d : d + 1, :]
            + rows[:, dists + d : dists + d + 1] * with_cos[d : d + 1, :]
            for d in range(dists)
        ]
        denom = transfer[0] * transfer[0]
        for value in transfer[1:]:
            denom = denom + value * value
        scale = 1.0 / (denom + regularizer)
        for d in range(dists):
            out[d, at : at + step, :] = (transfer[d] * scale).astype(bf16)


def column_kernel(inner, outer, table, gain, *refs):
    pieces = dict(zip(send_order, refs[:inner]))
    *outs, stack, total, spectrum = refs[inner:]
    _, plane, spot = position(inner)
    dists, rows_dev, block = pieces[0].shape
    depth = inner * rows_dev
    for rel in range(inner):
        start = pl.multiple_of((spot ^ rel) * rows_dev, rows_dev)
        for d in range(dists):
            stack[d, pl.ds(start, rows_dev), :] = pieces[rel][d]
    part = table[:, pl.ds(pl.multiple_of(plane * depth, depth), depth)]
    for d in range(dists):
        got = jnp.dot(part, stack[d], preferred_element_type=f32) * gain[d].astype(f32)
        if d == 0:
            total[...] = got
        else:
            total[...] += got
    spectrum[...] = total[...].astype(bf16)
    middle = (plane == 1) | (plane == 2)
    first = jnp.where(middle, 1, 3)
    for rel, out in zip((0, first, 4 - first, 2), outs):
        rows = pl.ds(pl.multiple_of((plane ^ rel) * depth, depth), depth)
        value = jnp.dot(table[rows, :], spectrum[...], preferred_element_type=f32)
        out[...] = value.astype(bf16)


def far_kernel(inner, *refs):
    ours, got, out = refs[-3:]
    _, plane, _ = position(inner)
    middle = (plane == 1) | (plane == 2)
    more = jnp.where(middle, got[...].astype(f32), 0.0)
    out[...] = (ours[...].astype(f32) + more).astype(bf16)


def half_kernel(inner, ours, far, near, next_near, across, other, mine, again):
    _, plane, spot = position(inner)
    middle = (plane == 1) | (plane == 2)
    capacity = mine.shape[0]
    for out, pair in ((mine, spot // 2), (other, 1 - spot // 2)):
        rows = pl.ds(pl.multiple_of(pair * capacity, capacity), capacity)
        inside = next_near[rows, :].astype(f32) + across[rows, :].astype(f32)
        more = jnp.where(middle, inside, near[rows, :].astype(f32))
        got = ours[rows, :].astype(f32) + far[rows, :].astype(f32) + more
        out[...] = got.astype(bf16)
    again[...] = other[...]


def phase_kernel(inner, table, *refs):
    pieces = dict(zip(tail_order, refs[:inner]))
    out, joined = refs[-2:]
    _, _, spot = position(inner)
    block = refs[0].shape[1]
    for rel in range(inner):
        columns = pl.ds(pl.multiple_of((spot ^ rel) * block, block), block)
        joined[:, columns] = pieces[rel][...]
    out[...] = jnp.dot(joined[...], table[...], preferred_element_type=f32).astype(bf16)


def recon_kernel(own, order, slabs, weights, *refs):
    phases = refs[: 2 * own - 1]
    out, chosen, select = refs[2 * own - 1 :]
    core = lax.axis_index("dist")
    device = lax.axis_index("rows")
    total = None
    for step, phase in enumerate(phases):
        here = weights[order[0, (core ^ (step % 2)) * own + step // 2]]
        got = jnp.dot(phase[...], here, preferred_element_type=f32)
        total = got if total is None else total + got
    out[...] = total
    chosen[...] = weights[order[0, (core ^ 1) * own + own - 1]]
    parity = device % 2
    offset = parity * slabs[device - parity]
    slot = lax.broadcasted_iota(jnp.int32, select.shape, 0)
    source = lax.broadcasted_iota(jnp.int32, select.shape, 1)
    picked = (source == slot + offset) & (slot < slabs[device])
    select[...] = jnp.where(picked, 1.0, 0.0).astype(bf16)


def recon_last_kernel(weights, phase, before, select, out):
    total = before[...] + jnp.dot(phase[...], weights[...], preferred_element_type=f32)
    got = jnp.dot(select[...], total.astype(bf16), preferred_element_type=f32)
    out[...] = got.astype(bf16)


def vmem(count):
    return [pl.BlockSpec(memory_space=pltpu.VMEM)] * count


def from_hbm(value):
    return pltpu.with_memory_space_constraint(value, pltpu.HBM)


def in_hbm(count):
    return [pl.BlockSpec(memory_space=pltpu.HBM)] * count


def unread(count):
    return [pl.BlockSpec(memory_space=pl.ANY)] * count


def smem(count):
    return [pl.BlockSpec(memory_space=pltpu.SMEM)] * count


def plane_plan(inner, holograms, propagation, weights, angle_order, slab_rows):
    mbatch, angles, dist_dev, rows_dev, width = holograms.shape
    groups = lax.axis_size("rows")
    cores = lax.axis_size("dist")
    outer = groups // inner
    own = angles // cores
    block = width // inner
    depth = inner * rows_dev
    dists = cores * dist_dev
    pixels = weights.shape[2]
    capacity = 2 * rows_dev
    params = pltpu.CompilerParams(vmem_limit_bytes=16 * 2**20)
    one_out = pl.BlockSpec(memory_space=pltpu.VMEM)

    cheap = pl.CostEstimate(flops=1, bytes_accessed=1, transcendentals=0)

    def shaped(*shape):
        return jax.ShapeDtypeStruct(shape, bf16)

    table = jnp.asarray(hartley(width))

    def sent(value, target):
        pairs = []
        for c in range(cores):
            for r in range(groups):
                to_core, to_row = target(c, r)
                pairs.append((c * groups + r, to_core * groups + to_row))
        return lax.ppermute(value, ("dist", "rows"), pairs)

    def to_other_core(c, r):
        return c ^ 1, r

    def to_spot(rel):
        return lambda c, r: (c, r ^ rel)

    def spread(pieces, order):
        return [sent(pieces[rel], to_spot(rel)) if rel else pieces[rel] for rel in order]

    def to_plane(rel):
        return lambda c, r: (c, (r // inner ^ rel) * inner + r % inner)

    def to_middle(c, r):
        z = r // inner
        return (c, (3 - z) * inner + r % inner) if z in (1, 2) else (c ^ 1, r)

    partner = sent(holograms[0], to_other_core)
    gain = pl.pallas_call(
        lambda *refs: filter_kernel(inner, dist_dev, *refs),
        out_shape=shaped(dists, width, block),
        in_specs=smem(1),
        out_specs=one_out,
        compiler_params=params,
        cost_estimate=cheap,
        name="filters",
    )(from_hbm(propagation))
    pieces = pl.pallas_call(
        lambda *refs: row_kernel(inner, *refs),
        out_shape=[shaped(dists, rows_dev, block)] * (own * inner),
        in_specs=in_hbm(1) + vmem(2) + unread(1),
        out_specs=vmem(own * inner),
        scratch_shapes=[
            pltpu.VMEM((own, dist_dev, rows_dev, width), bf16),
            pltpu.SemaphoreType.DMA((own * dist_dev,)),
        ],
        compiler_params=params,
        cost_estimate=cheap,
        name="row_spectra",
    )(from_hbm(holograms[0]), partner, table, gain)
    arrived = [
        spread(pieces[chunk * inner : (chunk + 1) * inner], send_order) for chunk in range(own)
    ]

    sums = []
    for chunk in range(own):
        blocks = pl.pallas_call(
            lambda *refs: column_kernel(inner, outer, *refs),
            out_shape=[shaped(depth, block)] * outer,
            in_specs=vmem(2 + inner),
            out_specs=vmem(outer),
            scratch_shapes=[
                pltpu.VMEM((dists, depth, block), bf16),
                pltpu.VMEM((width, block), f32),
                pltpu.VMEM((width, block), bf16),
            ],
            compiler_params=params,
            cost_estimate=cheap,
            name="columns",
        )(table, gain, *arrived[chunk])
        ours, first, second, third = blocks
        near = sent(first, to_plane(1))
        earlier = sums[-1][3:] if sums else []
        message = pl.pallas_call(
            lambda *refs: far_kernel(inner, *refs),
            out_shape=shaped(depth, block),
            in_specs=unread(len(earlier)) + vmem(2),
            out_specs=one_out,
            compiler_params=params,
            cost_estimate=cheap,
            name="far",
        )(*earlier, third, near)
        far = sent(message, to_plane(2))
        sums.append([ours, far, near, sent(second, to_plane(1)), sent(second, to_middle)])

    phases = []
    for chunk in range(own):
        second, first, again = pl.pallas_call(
            lambda *refs: half_kernel(inner, *refs),
            out_shape=[shaped(capacity, block)] * 3,
            in_specs=vmem(5),
            out_specs=vmem(3),
            compiler_params=params,
            cost_estimate=cheap,
            name="half",
        )(*sums[chunk])
        pieces = spread([first, first, second, again], tail_order)
        phase = pl.pallas_call(
            lambda *refs: phase_kernel(inner, *refs),
            out_shape=shaped(capacity, width),
            in_specs=vmem(1 + inner),
            out_specs=one_out,
            scratch_shapes=[pltpu.VMEM((capacity, width), bf16)],
            compiler_params=params,
            cost_estimate=cheap,
            name="phase",
        )(table, *pieces)
        phases += [phase, sent(phase, to_other_core)]

    total, chosen, select = pl.pallas_call(
        lambda *refs: recon_kernel(own, *refs),
        out_shape=[
            jax.ShapeDtypeStruct((capacity, pixels), f32),
            shaped(width, pixels),
            shaped(capacity, capacity),
        ],
        in_specs=smem(2) + vmem(2 * own),
        out_specs=vmem(3),
        compiler_params=params,
        cost_estimate=cheap,
        name="recon",
    )(angle_order, slab_rows, weights, *phases[:-1])
    return pl.pallas_call(
        recon_last_kernel,
        out_shape=shaped(capacity, pixels),
        in_specs=vmem(4),
        out_specs=one_out,
        compiler_params=params,
        cost_estimate=cheap,
        name="recon",
    )(chosen, phases[-1], total, select)


def on_device(holograms, propagation, weights, angle_order, slab_rows):
    mbatch, angles, dist_dev, rows_dev, width = holograms.shape
    groups = lax.axis_size("rows")
    inner = 2 ** (int(math.log2(groups)) // 2)
    block = width // inner
    fits = (
        inner * (groups // inner) == groups
        and rows_dev % 16 == 0
        and block % 128 == 0
        and inner * rows_dev % 128 == 0
        and inner == 4
        and groups == inner * inner
        and lax.axis_size("dist") == 2
        and angles == 2 * lax.axis_size("dist")
    )
    if fits:
        return plane_plan(inner, holograms, propagation, weights, angle_order, slab_rows)
    return flat_plan(holograms, propagation, weights, angle_order, slab_rows)


def solution(mesh):
    return jax.shard_map(
        on_device,
        mesh=mesh,
        in_specs=(P(None, None, "dist", "rows", None), P(), P(None, None, "dist"), P(), P()),
        out_specs=P("rows", "dist"),
        check_vma=False,
    )
```

```python
import math

import jax
import jax.numpy as jnp
import numpy as np
from jax import lax
from jax.experimental import pallas as pl
from jax.experimental.pallas import tpu as pltpu
from jax.sharding import PartitionSpec as P

absorb_ratio = 0.1
regularizer = 0.05
bf16 = jnp.bfloat16
f32 = jnp.float32
send_order = (0, 2, 1, 3)
tail_order = (0, 2, 3, 1)


def hartley(length):
    index = np.arange(length)
    turned = (index[:, None] * index[None, :] % length) * (2.0 * math.pi / length)
    table = (np.cos(turned) + np.sin(turned)) / math.sqrt(length)
    return table.astype(bf16)


def signed_square(index, length):
    signed = jnp.where(index < length // 2, index, index - length).astype(f32)
    return signed * signed / float(length * length)


def filters(propagation, rows_sq, cols_sq):
    first = propagation[:, None] * rows_sq[None]
    second = propagation[:, None] * cols_sq[None]
    sin_b, cos_b = jnp.sin(second), jnp.cos(second)
    with_sin = 2.0 * (cos_b - absorb_ratio * sin_b)
    with_cos = 2.0 * (sin_b + absorb_ratio * cos_b)
    transfer = (
        jnp.sin(first)[:, :, None] * with_sin[:, None, :]
        + jnp.cos(first)[:, :, None] * with_cos[:, None, :]
    )
    denom = jnp.sum(transfer * transfer, axis=0) + regularizer
    return transfer / denom


def flat_plan(holograms, propagation, weights, angle_order, slab_rows):
    mbatch, angles, dist_dev, rows_dev, width = holograms.shape
    groups = lax.axis_size("rows")
    cores = lax.axis_size("dist")
    capacity = 2 * rows_dev
    own = angles // cores
    cols = width // groups
    dists = dist_dev * cores
    device = lax.axis_index("rows")
    table = jnp.asarray(hartley(width))
    index = jnp.arange(width, dtype=jnp.int32)
    my_cols = device * cols + jnp.arange(cols, dtype=jnp.int32)
    gain = filters(propagation, signed_square(my_cols, width), signed_square(index, width))

    mine = lax.all_to_all(holograms[0], "dist", split_axis=0, concat_axis=1, tiled=True)
    flat = mine.reshape(own * dists * rows_dev, width)
    spec = jnp.einsum("kx,mx->km", table, flat, preferred_element_type=f32)
    spec = spec.astype(bf16).reshape(groups, cols, own * dists * rows_dev)
    spec = lax.all_to_all(spec, "rows", split_axis=0, concat_axis=0, tiled=True)
    spec = spec.reshape(groups, cols, own, dists, rows_dev).transpose(1, 2, 3, 0, 4)
    spec = spec.reshape(cols * own * dists, width)
    full = jnp.dot(spec, table, preferred_element_type=f32)
    full = full.reshape(cols, own, dists, width)
    full = jnp.sum(full * gain.transpose(1, 0, 2)[:, None], axis=2).astype(bf16)
    half = jnp.einsum("yq,akq->yak", table, full.transpose(1, 0, 2), preferred_element_type=f32)
    half = half.astype(bf16).reshape(groups, rows_dev, own * cols)
    half = lax.all_to_all(half, "rows", split_axis=0, concat_axis=0, tiled=True)
    half = half.reshape(groups, rows_dev, own, cols).transpose(2, 1, 0, 3)
    half = half.reshape(own * rows_dev, width)
    phase = jnp.dot(half, table, preferred_element_type=f32)
    phase = phase.astype(bf16).reshape(own, rows_dev, width)
    phase = lax.all_gather(phase, "dist", axis=0, tiled=True)
    place = (angle_order[0][None, :] == jnp.arange(angles)[:, None]).astype(bf16)
    phase = jnp.einsum("wa,ayx->wyx", place, phase, preferred_element_type=f32)
    recon = jnp.einsum(
        "wyx,wxp->yp", phase.astype(bf16), weights, preferred_element_type=f32
    ).astype(bf16)
    parity = device % 2
    offset = parity * slab_rows[device - parity]
    count = slab_rows[device]
    pairs = [(source, source ^ 1) for source in range(groups)]
    partner = lax.ppermute(recon, "rows", pairs)
    lower = jnp.where(parity == 1, partner, recon)
    upper = jnp.where(parity == 1, recon, partner)
    paired = jnp.concatenate([lower, upper], axis=0)
    slot = jnp.arange(capacity, dtype=jnp.int32)[:, None]
    source = jnp.arange(capacity, dtype=jnp.int32)[None, :]
    select = ((source == offset + slot) & (slot < count)).astype(bf16)
    return jnp.dot(select, paired, preferred_element_type=f32).astype(bf16)


def position(inner):
    device = lax.axis_index("rows")
    return lax.axis_index("dist"), device // inner, device % inner


def row_kernel(inner, holo, there, table, after, *refs):
    outs, mine, loaded = refs[:-2], refs[-2], refs[-1]
    own = len(outs) // inner
    core, _, spot = position(inner)
    _, dist_dev, rows_dev, width = there.shape
    block = width // inner
    copy = pltpu.make_async_copy(holo.at[pl.ds(core * own, own)], mine, loaded)
    copy.start()
    for first, source in ((dist_dev, there.at[pl.ds(core * own, own)]), (0, mine)):
        if first == 0:
            copy.wait()
        rows = source[...].reshape(own * dist_dev * rows_dev, width)
        for rel in range(inner):
            part = table[:, pl.ds(pl.multiple_of((spot ^ rel) * block, block), block)]
            got = jnp.dot(rows, part, preferred_element_type=f32).astype(bf16)
            got = got.reshape(own, dist_dev, rows_dev, block)
            for chunk in range(own):
                outs[chunk * inner + rel][first : first + dist_dev] = got[chunk]


def whole_turns(scale, square):
    turns = scale * square * (0.5 / math.pi)
    return (turns - jnp.round(turns)) * (2.0 * math.pi)


def filter_kernel(inner, dist_dev, turns, out):
    dists, width, block = out.shape
    core, _, spot = position(inner)

    def square(first, length):
        index = lax.broadcasted_iota(jnp.int32, (1, length), 1) + first
        signed = jnp.where(index < width // 2, index, index - width).astype(f32)
        return signed * signed * (1.0 / (width * width))

    def phases(first, length):
        values = square(first, length)
        rows = []
        for d in range(dists):
            other = d // dist_dev
            scale = turns[(core ^ other) * dist_dev + d % dist_dev]
            rows.append(whole_turns(scale, values))
        return jnp.concatenate(rows, axis=0)

    along = phases(0, width)
    across = phases(spot * block, block)
    sin_b, cos_b = jnp.sin(across), jnp.cos(across)
    with_sin = 2.0 * (cos_b - absorb_ratio * sin_b)
    with_cos = 2.0 * (sin_b + absorb_ratio * cos_b)
    turned = jnp.concatenate([jnp.sin(along), jnp.cos(along)], axis=0).T
    step = 128
    for at in range(0, width, step):
        rows = turned[at : at + step]
        transfer = [
            rows[:, d : d + 1] * with_sin[d : d + 1, :]
            + rows[:, dists + d : dists + d + 1] * with_cos[d : d + 1, :]
            for d in range(dists)
        ]
        denom = transfer[0] * transfer[0]
        for value in transfer[1:]:
            denom = denom + value * value
        scale = 1.0 / (denom + regularizer)
        for d in range(dists):
            out[d, at : at + step, :] = (transfer[d] * scale).astype(bf16)


def column_kernel(inner, outer, table, gain, *refs):
    pieces = dict(zip(send_order, refs[:inner]))
    ours, second, *halves, stack, total, spectrum = refs[inner:]
    _, plane, spot = position(inner)
    dists, rows_dev, block = pieces[0].shape
    depth = inner * rows_dev
    for rel in range(inner):
        start = pl.multiple_of((spot ^ rel) * rows_dev, rows_dev)
        for d in range(dists):
            stack[d, pl.ds(start, rows_dev), :] = pieces[rel][d]
    part = table[:, pl.ds(pl.multiple_of(plane * depth, depth), depth)]
    for d in range(dists):
        got = jnp.dot(part, stack[d], preferred_element_type=f32) * gain[d].astype(f32)
        if d == 0:
            total[...] = got
        else:
            total[...] += got
    spectrum[...] = total[...].astype(bf16)
    middle = (plane == 1) | (plane == 2)
    first = jnp.where(middle, 1, 3)
    splits = len(halves) // 2
    wide = block // splits
    for rel, targets in (
        (first, halves[:splits]),
        (4 - first, [second]),
        (2, halves[splits:]),
        (0, [ours]),
    ):
        rows = pl.ds(pl.multiple_of((plane ^ rel) * depth, depth), depth)
        value = jnp.dot(table[rows, :], spectrum[...], preferred_element_type=f32).astype(bf16)
        for split, out in enumerate(targets):
            width_here = out.shape[1]
            out[...] = value[:, split * wide : split * wide + width_here]


def far_kernel(inner, *refs):
    ours, got, out = refs[-3:]
    _, plane, _ = position(inner)
    middle = (plane == 1) | (plane == 2)
    more = jnp.where(middle, got[...].astype(f32), 0.0)
    out[...] = (ours[...].astype(f32) + more).astype(bf16)


def half_kernel(inner, splits, ours, next_near, across, *refs):
    fars, nears = refs[:splits], refs[splits : 2 * splits]
    other, mine, again = refs[-3:]
    _, plane, spot = position(inner)
    middle = (plane == 1) | (plane == 2)
    capacity, block = mine.shape
    wide = block // splits
    for out, pair in ((mine, spot // 2), (other, 1 - spot // 2)):
        rows = pl.ds(pl.multiple_of(pair * capacity, capacity), capacity)
        for split in range(splits):
            lanes = slice(split * wide, (split + 1) * wide)
            inside = next_near[rows, lanes].astype(f32) + across[rows, lanes].astype(f32)
            more = jnp.where(middle, inside, nears[split][rows, :].astype(f32))
            got = ours[rows, lanes].astype(f32) + fars[split][rows, :].astype(f32) + more
            out[:, lanes] = got.astype(bf16)
    again[...] = other[...]


def phase_kernel(inner, table, *refs):
    pieces = dict(zip(tail_order, refs[:inner]))
    out, joined = refs[-2:]
    _, _, spot = position(inner)
    block = refs[0].shape[1]
    for rel in range(inner):
        columns = pl.ds(pl.multiple_of((spot ^ rel) * block, block), block)
        joined[:, columns] = pieces[rel][...]
    out[...] = jnp.dot(joined[...], table[...], preferred_element_type=f32).astype(bf16)


def recon_kernel(own, order, slabs, weights, *refs):
    phases = refs[: 2 * own - 1]
    out, chosen, select = refs[2 * own - 1 :]
    core = lax.axis_index("dist")
    device = lax.axis_index("rows")
    total = None
    for step, phase in enumerate(phases):
        here = weights[order[0, (core ^ (step % 2)) * own + step // 2]]
        got = jnp.dot(phase[...], here, preferred_element_type=f32)
        total = got if total is None else total + got
    out[...] = total
    chosen[...] = weights[order[0, (core ^ 1) * own + own - 1]]
    parity = device % 2
    offset = parity * slabs[device - parity]
    slot = lax.broadcasted_iota(jnp.int32, select.shape, 0)
    source = lax.broadcasted_iota(jnp.int32, select.shape, 1)
    picked = (source == slot + offset) & (slot < slabs[device])
    select[...] = jnp.where(picked, 1.0, 0.0).astype(bf16)


def recon_last_kernel(weights, phase, before, select, out):
    total = before[...] + jnp.dot(phase[...], weights[...], preferred_element_type=f32)
    got = jnp.dot(select[...], total.astype(bf16), preferred_element_type=f32)
    out[...] = got.astype(bf16)


def vmem(count):
    return [pl.BlockSpec(memory_space=pltpu.VMEM)] * count


def from_hbm(value):
    return pltpu.with_memory_space_constraint(value, pltpu.HBM)


def in_hbm(count):
    return [pl.BlockSpec(memory_space=pltpu.HBM)] * count


def unread(count):
    return [pl.BlockSpec(memory_space=pl.ANY)] * count


def smem(count):
    return [pl.BlockSpec(memory_space=pltpu.SMEM)] * count


def plane_plan(inner, holograms, propagation, weights, angle_order, slab_rows):
    mbatch, angles, dist_dev, rows_dev, width = holograms.shape
    groups = lax.axis_size("rows")
    cores = lax.axis_size("dist")
    outer = groups // inner
    own = angles // cores
    block = width // inner
    depth = inner * rows_dev
    dists = cores * dist_dev
    pixels = weights.shape[2]
    capacity = 2 * rows_dev
    params = pltpu.CompilerParams(vmem_limit_bytes=16 * 2**20)
    one_out = pl.BlockSpec(memory_space=pltpu.VMEM)

    cheap = pl.CostEstimate(flops=1, bytes_accessed=1, transcendentals=0)

    def shaped(*shape):
        return jax.ShapeDtypeStruct(shape, bf16)

    table = jnp.asarray(hartley(width))

    def sent(value, target):
        pairs = []
        for c in range(cores):
            for r in range(groups):
                to_core, to_row = target(c, r)
                pairs.append((c * groups + r, to_core * groups + to_row))
        return lax.ppermute(value, ("dist", "rows"), pairs)

    def to_other_core(c, r):
        return c ^ 1, r

    def to_spot(rel):
        return lambda c, r: (c, r ^ rel)

    def spread(pieces, order):
        return [sent(pieces[rel], to_spot(rel)) if rel else pieces[rel] for rel in order]

    def to_plane(rel):
        return lambda c, r: (c, (r // inner ^ rel) * inner + r % inner)

    def to_middle(c, r):
        z = r // inner
        return (c, (3 - z) * inner + r % inner) if z in (1, 2) else (c ^ 1, r)

    partner = sent(holograms[0], to_other_core)
    gain = pl.pallas_call(
        lambda *refs: filter_kernel(inner, dist_dev, *refs),
        out_shape=shaped(dists, width, block),
        in_specs=smem(1),
        out_specs=one_out,
        compiler_params=params,
        cost_estimate=cheap,
        name="filters",
    )(from_hbm(propagation))
    pieces = pl.pallas_call(
        lambda *refs: row_kernel(inner, *refs),
        out_shape=[shaped(dists, rows_dev, block)] * (own * inner),
        in_specs=in_hbm(1) + vmem(2) + unread(1),
        out_specs=vmem(own * inner),
        scratch_shapes=[
            pltpu.VMEM((own, dist_dev, rows_dev, width), bf16),
            pltpu.SemaphoreType.DMA,
        ],
        compiler_params=params,
        cost_estimate=cheap,
        name="row_spectra",
    )(from_hbm(holograms[0]), partner, table, gain)
    arrived = [
        spread(pieces[chunk * inner : (chunk + 1) * inner], send_order) for chunk in range(own)
    ]

    def parts_of(chunk):
        return 2 if chunk == own - 1 and block % 256 == 0 else 1

    sums = []
    for chunk in range(own):
        splits = parts_of(chunk)
        blocks = pl.pallas_call(
            lambda *refs: column_kernel(inner, outer, *refs),
            out_shape=[shaped(depth, block)] * 2
            + [shaped(depth, block // splits)] * (2 * splits),
            in_specs=vmem(2 + inner),
            out_specs=vmem(2 + 2 * splits),
            scratch_shapes=[
                pltpu.VMEM((dists, depth, block), bf16),
                pltpu.VMEM((width, block), f32),
                pltpu.VMEM((width, block), bf16),
            ],
            compiler_params=params,
            cost_estimate=cheap,
            name="columns",
        )(table, gain, *arrived[chunk])
        ours, second, *halves = blocks
        earlier = sums[-1][1:3] if sums else []
        nears = [sent(half, to_plane(1)) for half in halves[:splits]]
        fars = []
        for split in range(splits):
            message = pl.pallas_call(
                lambda *refs: far_kernel(inner, *refs),
                out_shape=shaped(depth, block // splits),
                in_specs=unread(len(earlier)) + vmem(2),
                out_specs=one_out,
                compiler_params=params,
                cost_estimate=cheap,
                name="far",
            )(*earlier, halves[splits + split], nears[split])
            fars.append(sent(message, to_plane(2)))
        sums.append(
            [ours, sent(second, to_plane(1)), sent(second, to_middle), *fars, *nears]
        )

    phases = []
    for chunk in range(own):
        sent_before = pieces[2:3] if chunk else []
        second, first, again = pl.pallas_call(
            lambda *refs, chunk=chunk: half_kernel(inner, parts_of(chunk), *refs),
            out_shape=[shaped(capacity, block)] * 3,
            in_specs=vmem(len(sums[chunk])) + unread(len(sent_before)),
            out_specs=vmem(3),
            compiler_params=params,
            cost_estimate=cheap,
            name="half",
        )(*sums[chunk], *sent_before)
        pieces = spread([first, first, second, again], tail_order)
        phase = pl.pallas_call(
            lambda *refs: phase_kernel(inner, *refs),
            out_shape=shaped(capacity, width),
            in_specs=vmem(1 + inner),
            out_specs=one_out,
            scratch_shapes=[pltpu.VMEM((capacity, width), bf16)],
            compiler_params=params,
            cost_estimate=cheap,
            name="phase",
        )(table, *pieces)
        phases += [phase, sent(phase, to_other_core)]

    total, chosen, select = pl.pallas_call(
        lambda *refs: recon_kernel(own, *refs),
        out_shape=[
            jax.ShapeDtypeStruct((capacity, pixels), f32),
            shaped(width, pixels),
            shaped(capacity, capacity),
        ],
        in_specs=smem(2) + vmem(2 * own),
        out_specs=vmem(3),
        compiler_params=params,
        cost_estimate=cheap,
        name="recon",
    )(angle_order, slab_rows, weights, *phases[:-1])
    return pl.pallas_call(
        recon_last_kernel,
        out_shape=shaped(capacity, pixels),
        in_specs=vmem(4),
        out_specs=one_out,
        compiler_params=params,
        cost_estimate=cheap,
        name="recon",
    )(chosen, phases[-1], total, select)


def on_device(holograms, propagation, weights, angle_order, slab_rows):
    mbatch, angles, dist_dev, rows_dev, width = holograms.shape
    groups = lax.axis_size("rows")
    inner = 2 ** (int(math.log2(groups)) // 2)
    block = width // inner
    fits = (
        inner * (groups // inner) == groups
        and rows_dev % 16 == 0
        and block % 128 == 0
        and inner * rows_dev % 128 == 0
        and inner == 4
        and groups == inner * inner
        and lax.axis_size("dist") == 2
        and angles == 2 * lax.axis_size("dist")
    )
    if fits:
        return plane_plan(inner, holograms, propagation, weights, angle_order, slab_rows)
    return flat_plan(holograms, propagation, weights, angle_order, slab_rows)


def solution(mesh):
    return jax.shard_map(
        on_device,
        mesh=mesh,
        in_specs=(P(None, None, "dist", "rows", None), P(), P(None, None, "dist"), P(), P()),
        out_specs=P("rows", "dist"),
        check_vma=False,
    )
```

```python
import math

import jax
import jax.numpy as jnp
import numpy as np
from jax import lax
from jax.experimental import pallas as pl
from jax.experimental.pallas import tpu as pltpu
from jax.sharding import PartitionSpec as P

absorb_ratio = 0.1
regularizer = 0.05
bf16 = jnp.bfloat16
f32 = jnp.float32
send_order = (0, 2, 1, 3)
tail_order = (0, 2, 3, 1)


def hartley(length):
    index = np.arange(length)
    turned = (index[:, None] * index[None, :] % length) * (2.0 * math.pi / length)
    table = (np.cos(turned) + np.sin(turned)) / math.sqrt(length)
    return table.astype(bf16)


def signed_square(index, length):
    signed = jnp.where(index < length // 2, index, index - length).astype(f32)
    return signed * signed / float(length * length)


def filters(propagation, rows_sq, cols_sq):
    first = propagation[:, None] * rows_sq[None]
    second = propagation[:, None] * cols_sq[None]
    sin_b, cos_b = jnp.sin(second), jnp.cos(second)
    with_sin = 2.0 * (cos_b - absorb_ratio * sin_b)
    with_cos = 2.0 * (sin_b + absorb_ratio * cos_b)
    transfer = (
        jnp.sin(first)[:, :, None] * with_sin[:, None, :]
        + jnp.cos(first)[:, :, None] * with_cos[:, None, :]
    )
    denom = jnp.sum(transfer * transfer, axis=0) + regularizer
    return transfer / denom


def flat_plan(holograms, propagation, weights, angle_order, slab_rows):
    mbatch, angles, dist_dev, rows_dev, width = holograms.shape
    groups = lax.axis_size("rows")
    cores = lax.axis_size("dist")
    capacity = 2 * rows_dev
    own = angles // cores
    cols = width // groups
    dists = dist_dev * cores
    device = lax.axis_index("rows")
    table = jnp.asarray(hartley(width))
    index = jnp.arange(width, dtype=jnp.int32)
    my_cols = device * cols + jnp.arange(cols, dtype=jnp.int32)
    gain = filters(propagation, signed_square(my_cols, width), signed_square(index, width))

    mine = lax.all_to_all(holograms[0], "dist", split_axis=0, concat_axis=1, tiled=True)
    flat = mine.reshape(own * dists * rows_dev, width)
    spec = jnp.einsum("kx,mx->km", table, flat, preferred_element_type=f32)
    spec = spec.astype(bf16).reshape(groups, cols, own * dists * rows_dev)
    spec = lax.all_to_all(spec, "rows", split_axis=0, concat_axis=0, tiled=True)
    spec = spec.reshape(groups, cols, own, dists, rows_dev).transpose(1, 2, 3, 0, 4)
    spec = spec.reshape(cols * own * dists, width)
    full = jnp.dot(spec, table, preferred_element_type=f32)
    full = full.reshape(cols, own, dists, width)
    full = jnp.sum(full * gain.transpose(1, 0, 2)[:, None], axis=2).astype(bf16)
    half = jnp.einsum("yq,akq->yak", table, full.transpose(1, 0, 2), preferred_element_type=f32)
    half = half.astype(bf16).reshape(groups, rows_dev, own * cols)
    half = lax.all_to_all(half, "rows", split_axis=0, concat_axis=0, tiled=True)
    half = half.reshape(groups, rows_dev, own, cols).transpose(2, 1, 0, 3)
    half = half.reshape(own * rows_dev, width)
    phase = jnp.dot(half, table, preferred_element_type=f32)
    phase = phase.astype(bf16).reshape(own, rows_dev, width)
    phase = lax.all_gather(phase, "dist", axis=0, tiled=True)
    place = (angle_order[0][None, :] == jnp.arange(angles)[:, None]).astype(bf16)
    phase = jnp.einsum("wa,ayx->wyx", place, phase, preferred_element_type=f32)
    recon = jnp.einsum(
        "wyx,wxp->yp", phase.astype(bf16), weights, preferred_element_type=f32
    ).astype(bf16)
    parity = device % 2
    offset = parity * slab_rows[device - parity]
    count = slab_rows[device]
    pairs = [(source, source ^ 1) for source in range(groups)]
    partner = lax.ppermute(recon, "rows", pairs)
    lower = jnp.where(parity == 1, partner, recon)
    upper = jnp.where(parity == 1, recon, partner)
    paired = jnp.concatenate([lower, upper], axis=0)
    slot = jnp.arange(capacity, dtype=jnp.int32)[:, None]
    source = jnp.arange(capacity, dtype=jnp.int32)[None, :]
    select = ((source == offset + slot) & (slot < count)).astype(bf16)
    return jnp.dot(select, paired, preferred_element_type=f32).astype(bf16)


def position(inner):
    device = lax.axis_index("rows")
    return lax.axis_index("dist"), device // inner, device % inner


def row_kernel(inner, holo, there, table, after, *refs):
    outs, mine, loaded = refs[:-2], refs[-2], refs[-1]
    own = len(outs) // inner
    core, _, spot = position(inner)
    _, dist_dev, rows_dev, width = there.shape
    block = width // inner
    copy = pltpu.make_async_copy(holo.at[pl.ds(core * own, own)], mine, loaded)
    copy.start()
    for first, source in ((dist_dev, there.at[pl.ds(core * own, own)]), (0, mine)):
        if first == 0:
            copy.wait()
        rows = source[...].reshape(own * dist_dev * rows_dev, width)
        for rel in range(inner):
            part = table[:, pl.ds(pl.multiple_of((spot ^ rel) * block, block), block)]
            got = jnp.dot(rows, part, preferred_element_type=f32).astype(bf16)
            got = got.reshape(own, dist_dev, rows_dev, block)
            for chunk in range(own):
                outs[chunk * inner + rel][first : first + dist_dev] = got[chunk]


def whole_turns(scale, square):
    turns = scale * square * (0.5 / math.pi)
    return (turns - jnp.round(turns)) * (2.0 * math.pi)


def filter_kernel(inner, dist_dev, turns, out):
    dists, width, block = out.shape
    core, _, spot = position(inner)

    def square(first, length):
        index = lax.broadcasted_iota(jnp.int32, (1, length), 1) + first
        signed = jnp.where(index < width // 2, index, index - width).astype(f32)
        return signed * signed * (1.0 / (width * width))

    def phases(first, length):
        values = square(first, length)
        rows = []
        for d in range(dists):
            other = d // dist_dev
            scale = turns[(core ^ other) * dist_dev + d % dist_dev]
            rows.append(whole_turns(scale, values))
        return jnp.concatenate(rows, axis=0)

    along = phases(0, width)
    across = phases(spot * block, block)
    sin_b, cos_b = jnp.sin(across), jnp.cos(across)
    with_sin = 2.0 * (cos_b - absorb_ratio * sin_b)
    with_cos = 2.0 * (sin_b + absorb_ratio * cos_b)
    turned = jnp.concatenate([jnp.sin(along), jnp.cos(along)], axis=0).T
    step = 128
    for at in range(0, width, step):
        rows = turned[at : at + step]
        transfer = [
            rows[:, d : d + 1] * with_sin[d : d + 1, :]
            + rows[:, dists + d : dists + d + 1] * with_cos[d : d + 1, :]
            for d in range(dists)
        ]
        denom = transfer[0] * transfer[0]
        for value in transfer[1:]:
            denom = denom + value * value
        scale = 1.0 / (denom + regularizer)
        for d in range(dists):
            out[d, at : at + step, :] = (transfer[d] * scale).astype(bf16)


def column_kernel(inner, outer, table, gain, *refs):
    pieces = dict(zip(send_order, refs[:inner]))
    *outs, stack, total, spectrum = refs[inner:]
    _, plane, spot = position(inner)
    dists, rows_dev, block = pieces[0].shape
    depth = inner * rows_dev
    for rel in range(inner):
        start = pl.multiple_of((spot ^ rel) * rows_dev, rows_dev)
        for d in range(dists):
            stack[d, pl.ds(start, rows_dev), :] = pieces[rel][d]
    part = table[:, pl.ds(pl.multiple_of(plane * depth, depth), depth)]
    for d in range(dists):
        got = jnp.dot(part, stack[d], preferred_element_type=f32) * gain[d].astype(f32)
        if d == 0:
            total[...] = got
        else:
            total[...] += got
    spectrum[...] = total[...].astype(bf16)
    middle = (plane == 1) | (plane == 2)
    first = jnp.where(middle, 1, 3)
    for rel, out in zip((0, first, 4 - first, 2), outs):
        rows = pl.ds(pl.multiple_of((plane ^ rel) * depth, depth), depth)
        value = jnp.dot(table[rows, :], spectrum[...], preferred_element_type=f32)
        out[...] = value.astype(bf16)


def far_kernel(inner, *refs):
    ours, got, out = refs[-3:]
    _, plane, _ = position(inner)
    middle = (plane == 1) | (plane == 2)
    more = jnp.where(middle, got[...].astype(f32), 0.0)
    out[...] = (ours[...].astype(f32) + more).astype(bf16)


def half_kernel(inner, ours, far, near, next_near, across, other, mine, again):
    _, plane, spot = position(inner)
    middle = (plane == 1) | (plane == 2)
    capacity = mine.shape[0]
    for out, pair in ((mine, spot // 2), (other, 1 - spot // 2)):
        rows = pl.ds(pl.multiple_of(pair * capacity, capacity), capacity)
        inside = next_near[rows, :].astype(f32) + across[rows, :].astype(f32)
        more = jnp.where(middle, inside, near[rows, :].astype(f32))
        got = ours[rows, :].astype(f32) + far[rows, :].astype(f32) + more
        out[...] = got.astype(bf16)
    again[...] = other[...]


def phase_kernel(inner, table, *refs):
    pieces = dict(zip(tail_order, refs[:inner]))
    out, joined = refs[-2:]
    _, _, spot = position(inner)
    block = refs[0].shape[1]
    for rel in range(inner):
        columns = pl.ds(pl.multiple_of((spot ^ rel) * block, block), block)
        joined[:, columns] = pieces[rel][...]
    out[...] = jnp.dot(joined[...], table[...], preferred_element_type=f32).astype(bf16)


def recon_kernel(own, order, slabs, weights, *refs):
    phases = refs[: 2 * own - 1]
    out, chosen, select = refs[2 * own - 1 :]
    core = lax.axis_index("dist")
    device = lax.axis_index("rows")
    total = None
    for step, phase in enumerate(phases):
        here = weights[order[0, (core ^ (step % 2)) * own + step // 2]]
        got = jnp.dot(phase[...], here, preferred_element_type=f32)
        total = got if total is None else total + got
    out[...] = total
    chosen[...] = weights[order[0, (core ^ 1) * own + own - 1]]
    parity = device % 2
    offset = parity * slabs[device - parity]
    slot = lax.broadcasted_iota(jnp.int32, select.shape, 0)
    source = lax.broadcasted_iota(jnp.int32, select.shape, 1)
    picked = (source == slot + offset) & (slot < slabs[device])
    select[...] = jnp.where(picked, 1.0, 0.0).astype(bf16)


def recon_last_kernel(weights, phase, before, select, out):
    total = before[...] + jnp.dot(phase[...], weights[...], preferred_element_type=f32)
    got = jnp.dot(select[...], total.astype(bf16), preferred_element_type=f32)
    out[...] = got.astype(bf16)


def vmem(count):
    return [pl.BlockSpec(memory_space=pltpu.VMEM)] * count


def from_hbm(value):
    return pltpu.with_memory_space_constraint(value, pltpu.HBM)


def in_hbm(count):
    return [pl.BlockSpec(memory_space=pltpu.HBM)] * count


def unread(count):
    return [pl.BlockSpec(memory_space=pl.ANY)] * count


def smem(count):
    return [pl.BlockSpec(memory_space=pltpu.SMEM)] * count


def plane_plan(inner, holograms, propagation, weights, angle_order, slab_rows):
    mbatch, angles, dist_dev, rows_dev, width = holograms.shape
    groups = lax.axis_size("rows")
    cores = lax.axis_size("dist")
    outer = groups // inner
    own = angles // cores
    block = width // inner
    depth = inner * rows_dev
    dists = cores * dist_dev
    pixels = weights.shape[2]
    capacity = 2 * rows_dev
    params = pltpu.CompilerParams(vmem_limit_bytes=16 * 2**20)
    one_out = pl.BlockSpec(memory_space=pltpu.VMEM)

    cheap = pl.CostEstimate(flops=1, bytes_accessed=1, transcendentals=0)

    def shaped(*shape):
        return jax.ShapeDtypeStruct(shape, bf16)

    table = jnp.asarray(hartley(width))

    def sent(value, target):
        pairs = []
        for c in range(cores):
            for r in range(groups):
                to_core, to_row = target(c, r)
                if to_row is not None:
                    pairs.append((c * groups + r, to_core * groups + to_row))
        return lax.ppermute(value, ("dist", "rows"), pairs)

    def to_other_core(c, r):
        return c ^ 1, r

    def to_spot(rel):
        return lambda c, r: (c, r ^ rel)

    def spread(pieces, order):
        return [sent(pieces[rel], to_spot(rel)) if rel else pieces[rel] for rel in order]

    def to_plane(rel):
        return lambda c, r: (c, (r // inner ^ rel) * inner + r % inner)

    def from_ends(c, r):
        z = r // inner
        return c, None if z in (1, 2) else (z ^ 1) * inner + r % inner

    def to_middle(c, r):
        z = r // inner
        return (c, (3 - z) * inner + r % inner) if z in (1, 2) else (c ^ 1, r)

    partner = sent(holograms[0], to_other_core)
    gain = pl.pallas_call(
        lambda *refs: filter_kernel(inner, dist_dev, *refs),
        out_shape=shaped(dists, width, block),
        in_specs=smem(1),
        out_specs=one_out,
        compiler_params=params,
        cost_estimate=cheap,
        name="filters",
    )(from_hbm(propagation))
    pieces = pl.pallas_call(
        lambda *refs: row_kernel(inner, *refs),
        out_shape=[shaped(dists, rows_dev, block)] * (own * inner),
        in_specs=in_hbm(1) + vmem(2) + unread(1),
        out_specs=vmem(own * inner),
        scratch_shapes=[
            pltpu.VMEM((own, dist_dev, rows_dev, width), bf16),
            pltpu.SemaphoreType.DMA,
        ],
        compiler_params=params,
        cost_estimate=cheap,
        name="row_spectra",
    )(from_hbm(holograms[0]), partner, table, gain)
    arrived = [
        spread(pieces[chunk * inner : (chunk + 1) * inner], send_order) for chunk in range(own)
    ]

    sums = []
    for chunk in range(own):
        blocks = pl.pallas_call(
            lambda *refs: column_kernel(inner, outer, *refs),
            out_shape=[shaped(depth, block)] * outer,
            in_specs=vmem(2 + inner),
            out_specs=vmem(outer),
            scratch_shapes=[
                pltpu.VMEM((dists, depth, block), bf16),
                pltpu.VMEM((width, block), f32),
                pltpu.VMEM((width, block), bf16),
            ],
            compiler_params=params,
            cost_estimate=cheap,
            name="columns",
        )(table, gain, *arrived[chunk])
        ours, first, second, third = blocks
        near = sent(first, to_plane(1))
        earlier = sums[-1][3:] if sums else []
        message = pl.pallas_call(
            lambda *refs: far_kernel(inner, *refs),
            out_shape=shaped(depth, block),
            in_specs=unread(len(earlier)) + vmem(2),
            out_specs=one_out,
            compiler_params=params,
            cost_estimate=cheap,
            name="far",
        )(*earlier, third, near)
        far = sent(message, to_plane(2))
        to_next = from_ends if sums else to_plane(1)
        sums.append([ours, far, near, sent(second, to_next), sent(second, to_middle)])

    phases = []
    for chunk in range(own):
        second, first, again = pl.pallas_call(
            lambda *refs: half_kernel(inner, *refs),
            out_shape=[shaped(capacity, block)] * 3,
            in_specs=vmem(5),
            out_specs=vmem(3),
            compiler_params=params,
            cost_estimate=cheap,
            name="half",
        )(*sums[chunk])
        pieces = spread([first, first, second, again], tail_order)
        phase = pl.pallas_call(
            lambda *refs: phase_kernel(inner, *refs),
            out_shape=shaped(capacity, width),
            in_specs=vmem(1 + inner),
            out_specs=one_out,
            scratch_shapes=[pltpu.VMEM((capacity, width), bf16)],
            compiler_params=params,
            cost_estimate=cheap,
            name="phase",
        )(table, *pieces)
        phases += [phase, sent(phase, to_other_core)]

    total, chosen, select = pl.pallas_call(
        lambda *refs: recon_kernel(own, *refs),
        out_shape=[
            jax.ShapeDtypeStruct((capacity, pixels), f32),
            shaped(width, pixels),
            shaped(capacity, capacity),
        ],
        in_specs=smem(2) + vmem(2 * own),
        out_specs=vmem(3),
        compiler_params=params,
        cost_estimate=cheap,
        name="recon",
    )(angle_order, slab_rows, weights, *phases[:-1])
    return pl.pallas_call(
        recon_last_kernel,
        out_shape=shaped(capacity, pixels),
        in_specs=vmem(4),
        out_specs=one_out,
        compiler_params=params,
        cost_estimate=cheap,
        name="recon",
    )(chosen, phases[-1], total, select)


def on_device(holograms, propagation, weights, angle_order, slab_rows):
    mbatch, angles, dist_dev, rows_dev, width = holograms.shape
    groups = lax.axis_size("rows")
    inner = 2 ** (int(math.log2(groups)) // 2)
    block = width // inner
    fits = (
        inner * (groups // inner) == groups
        and rows_dev % 16 == 0
        and block % 128 == 0
        and inner * rows_dev % 128 == 0
        and inner == 4
        and groups == inner * inner
        and lax.axis_size("dist") == 2
        and angles == 2 * lax.axis_size("dist")
    )
    if fits:
        return plane_plan(inner, holograms, propagation, weights, angle_order, slab_rows)
    return flat_plan(holograms, propagation, weights, angle_order, slab_rows)


def solution(mesh):
    return jax.shard_map(
        on_device,
        mesh=mesh,
        in_specs=(P(None, None, "dist", "rows", None), P(), P(None, None, "dist"), P(), P()),
        out_specs=P("rows", "dist"),
        check_vma=False,
    )
```

```python
import math

import jax
import jax.numpy as jnp
import numpy as np
from jax import lax
from jax.experimental import pallas as pl
from jax.experimental.pallas import tpu as pltpu
from jax.sharding import PartitionSpec as P

absorb_ratio = 0.1
regularizer = 0.05
bf16 = jnp.bfloat16
f32 = jnp.float32
send_order = (0, 2, 1, 3)
tail_order = (0, 2, 3, 1)


def hartley(length):
    index = np.arange(length)
    turned = (index[:, None] * index[None, :] % length) * (2.0 * math.pi / length)
    table = (np.cos(turned) + np.sin(turned)) / math.sqrt(length)
    return table.astype(bf16)


def signed_square(index, length):
    signed = jnp.where(index < length // 2, index, index - length).astype(f32)
    return signed * signed / float(length * length)


def filters(propagation, rows_sq, cols_sq):
    first = propagation[:, None] * rows_sq[None]
    second = propagation[:, None] * cols_sq[None]
    sin_b, cos_b = jnp.sin(second), jnp.cos(second)
    with_sin = 2.0 * (cos_b - absorb_ratio * sin_b)
    with_cos = 2.0 * (sin_b + absorb_ratio * cos_b)
    transfer = (
        jnp.sin(first)[:, :, None] * with_sin[:, None, :]
        + jnp.cos(first)[:, :, None] * with_cos[:, None, :]
    )
    denom = jnp.sum(transfer * transfer, axis=0) + regularizer
    return transfer / denom


def flat_plan(holograms, propagation, weights, angle_order, slab_rows):
    mbatch, angles, dist_dev, rows_dev, width = holograms.shape
    groups = lax.axis_size("rows")
    cores = lax.axis_size("dist")
    capacity = 2 * rows_dev
    own = angles // cores
    cols = width // groups
    dists = dist_dev * cores
    device = lax.axis_index("rows")
    table = jnp.asarray(hartley(width))
    index = jnp.arange(width, dtype=jnp.int32)
    my_cols = device * cols + jnp.arange(cols, dtype=jnp.int32)
    gain = filters(propagation, signed_square(my_cols, width), signed_square(index, width))

    mine = lax.all_to_all(holograms[0], "dist", split_axis=0, concat_axis=1, tiled=True)
    flat = mine.reshape(own * dists * rows_dev, width)
    spec = jnp.einsum("kx,mx->km", table, flat, preferred_element_type=f32)
    spec = spec.astype(bf16).reshape(groups, cols, own * dists * rows_dev)
    spec = lax.all_to_all(spec, "rows", split_axis=0, concat_axis=0, tiled=True)
    spec = spec.reshape(groups, cols, own, dists, rows_dev).transpose(1, 2, 3, 0, 4)
    spec = spec.reshape(cols * own * dists, width)
    full = jnp.dot(spec, table, preferred_element_type=f32)
    full = full.reshape(cols, own, dists, width)
    full = jnp.sum(full * gain.transpose(1, 0, 2)[:, None], axis=2).astype(bf16)
    half = jnp.einsum("yq,akq->yak", table, full.transpose(1, 0, 2), preferred_element_type=f32)
    half = half.astype(bf16).reshape(groups, rows_dev, own * cols)
    half = lax.all_to_all(half, "rows", split_axis=0, concat_axis=0, tiled=True)
    half = half.reshape(groups, rows_dev, own, cols).transpose(2, 1, 0, 3)
    half = half.reshape(own * rows_dev, width)
    phase = jnp.dot(half, table, preferred_element_type=f32)
    phase = phase.astype(bf16).reshape(own, rows_dev, width)
    phase = lax.all_gather(phase, "dist", axis=0, tiled=True)
    place = (angle_order[0][None, :] == jnp.arange(angles)[:, None]).astype(bf16)
    phase = jnp.einsum("wa,ayx->wyx", place, phase, preferred_element_type=f32)
    recon = jnp.einsum(
        "wyx,wxp->yp", phase.astype(bf16), weights, preferred_element_type=f32
    ).astype(bf16)
    parity = device % 2
    offset = parity * slab_rows[device - parity]
    count = slab_rows[device]
    pairs = [(source, source ^ 1) for source in range(groups)]
    partner = lax.ppermute(recon, "rows", pairs)
    lower = jnp.where(parity == 1, partner, recon)
    upper = jnp.where(parity == 1, recon, partner)
    paired = jnp.concatenate([lower, upper], axis=0)
    slot = jnp.arange(capacity, dtype=jnp.int32)[:, None]
    source = jnp.arange(capacity, dtype=jnp.int32)[None, :]
    select = ((source == offset + slot) & (slot < count)).astype(bf16)
    return jnp.dot(select, paired, preferred_element_type=f32).astype(bf16)


def position(inner):
    device = lax.axis_index("rows")
    return lax.axis_index("dist"), device // inner, device % inner


def row_kernel(inner, holo, there, table, after, *refs):
    outs, mine, loaded = refs[:-2], refs[-2], refs[-1]
    own = len(outs) // inner
    core, _, spot = position(inner)
    _, dist_dev, rows_dev, width = there.shape
    block = width // inner
    copy = pltpu.make_async_copy(holo.at[pl.ds(core * own, own)], mine, loaded)
    copy.start()
    for first, source in ((dist_dev, there.at[pl.ds(core * own, own)]), (0, mine)):
        if first == 0:
            copy.wait()
        rows = source[...].reshape(own * dist_dev * rows_dev, width)
        for rel in range(inner):
            part = table[:, pl.ds(pl.multiple_of((spot ^ rel) * block, block), block)]
            got = jnp.dot(rows, part, preferred_element_type=f32).astype(bf16)
            got = got.reshape(own, dist_dev, rows_dev, block)
            for chunk in range(own):
                outs[chunk * inner + rel][first : first + dist_dev] = got[chunk]


def whole_turns(scale, square):
    turns = scale * square * (0.5 / math.pi)
    return (turns - jnp.round(turns)) * (2.0 * math.pi)


def filter_kernel(inner, dist_dev, turns, out):
    dists, width, block = out.shape
    core, _, spot = position(inner)

    def square(first, length):
        index = lax.broadcasted_iota(jnp.int32, (1, length), 1) + first
        signed = jnp.where(index < width // 2, index, index - width).astype(f32)
        return signed * signed * (1.0 / (width * width))

    def phases(first, length):
        values = square(first, length)
        rows = []
        for d in range(dists):
            other = d // dist_dev
            scale = turns[(core ^ other) * dist_dev + d % dist_dev]
            rows.append(whole_turns(scale, values))
        return jnp.concatenate(rows, axis=0)

    along = phases(0, width)
    across = phases(spot * block, block)
    sin_b, cos_b = jnp.sin(across), jnp.cos(across)
    with_sin = 2.0 * (cos_b - absorb_ratio * sin_b)
    with_cos = 2.0 * (sin_b + absorb_ratio * cos_b)
    turned = jnp.concatenate([jnp.sin(along), jnp.cos(along)], axis=0).T
    step = 128
    for at in range(0, width, step):
        rows = turned[at : at + step]
        transfer = [
            rows[:, d : d + 1] * with_sin[d : d + 1, :]
            + rows[:, dists + d : dists + d + 1] * with_cos[d : d + 1, :]
            for d in range(dists)
        ]
        denom = transfer[0] * transfer[0]
        for value in transfer[1:]:
            denom = denom + value * value
        scale = 1.0 / (denom + regularizer)
        for d in range(dists):
            out[d, at : at + step, :] = (transfer[d] * scale).astype(bf16)


def column_kernel(inner, outer, table, gain, *refs):
    pieces = dict(zip(send_order, refs[:inner]))
    spectrum, stack, total = refs[inner:]
    _, plane, spot = position(inner)
    dists, rows_dev, block = pieces[0].shape
    depth = inner * rows_dev
    for rel in range(inner):
        start = pl.multiple_of((spot ^ rel) * rows_dev, rows_dev)
        for d in range(dists):
            stack[d, pl.ds(start, rows_dev), :] = pieces[rel][d]
    part = table[:, pl.ds(pl.multiple_of(plane * depth, depth), depth)]
    for d in range(dists):
        got = jnp.dot(part, stack[d], preferred_element_type=f32) * gain[d].astype(f32)
        if d == 0:
            total[...] = got
        else:
            total[...] += got
    spectrum[...] = total[...].astype(bf16)


def block_kernel(inner, table, spectrum, *refs):
    outs = refs[-4:]
    _, plane, _ = position(inner)
    depth = outs[0].shape[0]
    middle = (plane == 1) | (plane == 2)
    first = jnp.where(middle, 1, 3)
    for rel, out in zip((0, first, 4 - first, 2), outs):
        rows = pl.ds(pl.multiple_of((plane ^ rel) * depth, depth), depth)
        value = jnp.dot(table[rows, :], spectrum[...], preferred_element_type=f32)
        out[...] = value.astype(bf16)


def far_kernel(inner, *refs):
    ours, got, out = refs[-3:]
    _, plane, _ = position(inner)
    middle = (plane == 1) | (plane == 2)
    more = jnp.where(middle, got[...].astype(f32), 0.0)
    out[...] = (ours[...].astype(f32) + more).astype(bf16)


def half_kernel(inner, ours, far, near, next_near, across, other, mine, again):
    _, plane, spot = position(inner)
    middle = (plane == 1) | (plane == 2)
    capacity = mine.shape[0]
    for out, pair in ((mine, spot // 2), (other, 1 - spot // 2)):
        rows = pl.ds(pl.multiple_of(pair * capacity, capacity), capacity)
        inside = next_near[rows, :].astype(f32) + across[rows, :].astype(f32)
        more = jnp.where(middle, inside, near[rows, :].astype(f32))
        got = ours[rows, :].astype(f32) + far[rows, :].astype(f32) + more
        out[...] = got.astype(bf16)
    again[...] = other[...]


def phase_kernel(inner, table, *refs):
    pieces = dict(zip(tail_order, refs[:inner]))
    out, joined = refs[-2:]
    _, _, spot = position(inner)
    block = refs[0].shape[1]
    for rel in range(inner):
        columns = pl.ds(pl.multiple_of((spot ^ rel) * block, block), block)
        joined[:, columns] = pieces[rel][...]
    out[...] = jnp.dot(joined[...], table[...], preferred_element_type=f32).astype(bf16)


def recon_kernel(own, order, slabs, weights, *refs):
    phases = refs[: 2 * own - 1]
    out, chosen, select = refs[2 * own - 1 :]
    core = lax.axis_index("dist")
    device = lax.axis_index("rows")
    total = None
    for step, phase in enumerate(phases):
        here = weights[order[0, (core ^ (step % 2)) * own + step // 2]]
        got = jnp.dot(phase[...], here, preferred_element_type=f32)
        total = got if total is None else total + got
    out[...] = total
    chosen[...] = weights[order[0, (core ^ 1) * own + own - 1]]
    parity = device % 2
    offset = parity * slabs[device - parity]
    slot = lax.broadcasted_iota(jnp.int32, select.shape, 0)
    source = lax.broadcasted_iota(jnp.int32, select.shape, 1)
    picked = (source == slot + offset) & (slot < slabs[device])
    select[...] = jnp.where(picked, 1.0, 0.0).astype(bf16)


def recon_last_kernel(weights, phase, before, select, out):
    total = before[...] + jnp.dot(phase[...], weights[...], preferred_element_type=f32)
    got = jnp.dot(select[...], total.astype(bf16), preferred_element_type=f32)
    out[...] = got.astype(bf16)


def vmem(count):
    return [pl.BlockSpec(memory_space=pltpu.VMEM)] * count


def from_hbm(value):
    return pltpu.with_memory_space_constraint(value, pltpu.HBM)


def in_hbm(count):
    return [pl.BlockSpec(memory_space=pltpu.HBM)] * count


def unread(count):
    return [pl.BlockSpec(memory_space=pl.ANY)] * count


def smem(count):
    return [pl.BlockSpec(memory_space=pltpu.SMEM)] * count


def plane_plan(inner, holograms, propagation, weights, angle_order, slab_rows):
    mbatch, angles, dist_dev, rows_dev, width = holograms.shape
    groups = lax.axis_size("rows")
    cores = lax.axis_size("dist")
    outer = groups // inner
    own = angles // cores
    block = width // inner
    depth = inner * rows_dev
    dists = cores * dist_dev
    pixels = weights.shape[2]
    capacity = 2 * rows_dev
    params = pltpu.CompilerParams(vmem_limit_bytes=16 * 2**20)
    one_out = pl.BlockSpec(memory_space=pltpu.VMEM)

    cheap = pl.CostEstimate(flops=1, bytes_accessed=1, transcendentals=0)

    def shaped(*shape):
        return jax.ShapeDtypeStruct(shape, bf16)

    table = jnp.asarray(hartley(width))

    def sent(value, target):
        pairs = []
        for c in range(cores):
            for r in range(groups):
                to_core, to_row = target(c, r)
                if to_row is not None:
                    pairs.append((c * groups + r, to_core * groups + to_row))
        return lax.ppermute(value, ("dist", "rows"), pairs)

    def to_other_core(c, r):
        return c ^ 1, r

    def to_spot(rel):
        return lambda c, r: (c, r ^ rel)

    def spread(pieces, order):
        return [sent(pieces[rel], to_spot(rel)) if rel else pieces[rel] for rel in order]

    def to_plane(rel):
        return lambda c, r: (c, (r // inner ^ rel) * inner + r % inner)

    def from_ends(c, r):
        z = r // inner
        return c, None if z in (1, 2) else (z ^ 1) * inner + r % inner

    def to_middle(c, r):
        z = r // inner
        return (c, (3 - z) * inner + r % inner) if z in (1, 2) else (c ^ 1, r)

    partner = sent(holograms[0], to_other_core)
    gain = pl.pallas_call(
        lambda *refs: filter_kernel(inner, dist_dev, *refs),
        out_shape=shaped(dists, width, block),
        in_specs=smem(1),
        out_specs=one_out,
        compiler_params=params,
        cost_estimate=cheap,
        name="filters",
    )(from_hbm(propagation))
    pieces = pl.pallas_call(
        lambda *refs: row_kernel(inner, *refs),
        out_shape=[shaped(dists, rows_dev, block)] * (own * inner),
        in_specs=in_hbm(1) + vmem(2) + unread(1),
        out_specs=vmem(own * inner),
        scratch_shapes=[
            pltpu.VMEM((own, dist_dev, rows_dev, width), bf16),
            pltpu.SemaphoreType.DMA,
        ],
        compiler_params=params,
        cost_estimate=cheap,
        name="row_spectra",
    )(from_hbm(holograms[0]), partner, table, gain)
    arrived = [
        spread(pieces[chunk * inner : (chunk + 1) * inner], send_order) for chunk in range(own)
    ]

    sums = []
    for chunk in range(own):
        spectrum = pl.pallas_call(
            lambda *refs: column_kernel(inner, outer, *refs),
            out_shape=shaped(width, block),
            in_specs=vmem(2 + inner),
            out_specs=one_out,
            scratch_shapes=[
                pltpu.VMEM((dists, depth, block), bf16),
                pltpu.VMEM((width, block), f32),
            ],
            compiler_params=params,
            cost_estimate=cheap,
            name="columns",
        )(table, gain, *arrived[chunk])
        before = [message] if sums else []
        blocks = pl.pallas_call(
            lambda *refs: block_kernel(inner, *refs),
            out_shape=[shaped(depth, block)] * outer,
            in_specs=vmem(2) + unread(len(before)),
            out_specs=vmem(outer),
            compiler_params=params,
            cost_estimate=cheap,
            name="blocks",
        )(table, spectrum, *before)
        ours, first, second, third = blocks
        near = sent(first, to_plane(1))
        earlier = sums[-1][1:2] + sums[-1][3:] if sums else []
        message = pl.pallas_call(
            lambda *refs: far_kernel(inner, *refs),
            out_shape=shaped(depth, block),
            in_specs=unread(len(earlier)) + vmem(2),
            out_specs=one_out,
            compiler_params=params,
            cost_estimate=cheap,
            name="far",
        )(*earlier, third, near)
        far = sent(message, to_plane(2))
        to_next = from_ends if sums else to_plane(1)
        sums.append([ours, far, near, sent(second, to_next), sent(second, to_middle)])

    phases = []
    for chunk in range(own):
        second, first, again = pl.pallas_call(
            lambda *refs: half_kernel(inner, *refs),
            out_shape=[shaped(capacity, block)] * 3,
            in_specs=vmem(5),
            out_specs=vmem(3),
            compiler_params=params,
            cost_estimate=cheap,
            name="half",
        )(*sums[chunk])
        pieces = spread([first, first, second, again], tail_order)
        phase = pl.pallas_call(
            lambda *refs: phase_kernel(inner, *refs),
            out_shape=shaped(capacity, width),
            in_specs=vmem(1 + inner),
            out_specs=one_out,
            scratch_shapes=[pltpu.VMEM((capacity, width), bf16)],
            compiler_params=params,
            cost_estimate=cheap,
            name="phase",
        )(table, *pieces)
        phases += [phase, sent(phase, to_other_core)]

    total, chosen, select = pl.pallas_call(
        lambda *refs: recon_kernel(own, *refs),
        out_shape=[
            jax.ShapeDtypeStruct((capacity, pixels), f32),
            shaped(width, pixels),
            shaped(capacity, capacity),
        ],
        in_specs=smem(2) + vmem(2 * own),
        out_specs=vmem(3),
        compiler_params=params,
        cost_estimate=cheap,
        name="recon",
    )(angle_order, slab_rows, weights, *phases[:-1])
    return pl.pallas_call(
        recon_last_kernel,
        out_shape=shaped(capacity, pixels),
        in_specs=vmem(4),
        out_specs=one_out,
        compiler_params=params,
        cost_estimate=cheap,
        name="recon",
    )(chosen, phases[-1], total, select)


def on_device(holograms, propagation, weights, angle_order, slab_rows):
    mbatch, angles, dist_dev, rows_dev, width = holograms.shape
    groups = lax.axis_size("rows")
    inner = 2 ** (int(math.log2(groups)) // 2)
    block = width // inner
    fits = (
        inner * (groups // inner) == groups
        and rows_dev % 16 == 0
        and block % 128 == 0
        and inner * rows_dev % 128 == 0
        and inner == 4
        and groups == inner * inner
        and lax.axis_size("dist") == 2
        and angles == 2 * lax.axis_size("dist")
    )
    if fits:
        return plane_plan(inner, holograms, propagation, weights, angle_order, slab_rows)
    return flat_plan(holograms, propagation, weights, angle_order, slab_rows)


def solution(mesh):
    return jax.shard_map(
        on_device,
        mesh=mesh,
        in_specs=(P(None, None, "dist", "rows", None), P(), P(None, None, "dist"), P(), P()),
        out_specs=P("rows", "dist"),
        check_vma=False,
    )
```

```python
import math

import jax
import jax.numpy as jnp
import numpy as np
from jax import lax
from jax.experimental import pallas as pl
from jax.experimental.pallas import tpu as pltpu
from jax.sharding import PartitionSpec as P

absorb_ratio = 0.1
regularizer = 0.05
bf16 = jnp.bfloat16
f32 = jnp.float32
send_order = (0, 2, 1, 3)
tail_order = (0, 2, 3, 1)


def hartley(length):
    index = np.arange(length)
    turned = (index[:, None] * index[None, :] % length) * (2.0 * math.pi / length)
    table = (np.cos(turned) + np.sin(turned)) / math.sqrt(length)
    return table.astype(bf16)


def signed_square(index, length):
    signed = jnp.where(index < length // 2, index, index - length).astype(f32)
    return signed * signed / float(length * length)


def filters(propagation, rows_sq, cols_sq):
    first = propagation[:, None] * rows_sq[None]
    second = propagation[:, None] * cols_sq[None]
    sin_b, cos_b = jnp.sin(second), jnp.cos(second)
    with_sin = 2.0 * (cos_b - absorb_ratio * sin_b)
    with_cos = 2.0 * (sin_b + absorb_ratio * cos_b)
    transfer = (
        jnp.sin(first)[:, :, None] * with_sin[:, None, :]
        + jnp.cos(first)[:, :, None] * with_cos[:, None, :]
    )
    denom = jnp.sum(transfer * transfer, axis=0) + regularizer
    return transfer / denom


def flat_plan(holograms, propagation, weights, angle_order, slab_rows):
    mbatch, angles, dist_dev, rows_dev, width = holograms.shape
    groups = lax.axis_size("rows")
    cores = lax.axis_size("dist")
    capacity = 2 * rows_dev
    own = angles // cores
    cols = width // groups
    dists = dist_dev * cores
    device = lax.axis_index("rows")
    table = jnp.asarray(hartley(width))
    index = jnp.arange(width, dtype=jnp.int32)
    my_cols = device * cols + jnp.arange(cols, dtype=jnp.int32)
    gain = filters(propagation, signed_square(my_cols, width), signed_square(index, width))

    mine = lax.all_to_all(holograms[0], "dist", split_axis=0, concat_axis=1, tiled=True)
    flat = mine.reshape(own * dists * rows_dev, width)
    spec = jnp.einsum("kx,mx->km", table, flat, preferred_element_type=f32)
    spec = spec.astype(bf16).reshape(groups, cols, own * dists * rows_dev)
    spec = lax.all_to_all(spec, "rows", split_axis=0, concat_axis=0, tiled=True)
    spec = spec.reshape(groups, cols, own, dists, rows_dev).transpose(1, 2, 3, 0, 4)
    spec = spec.reshape(cols * own * dists, width)
    full = jnp.dot(spec, table, preferred_element_type=f32)
    full = full.reshape(cols, own, dists, width)
    full = jnp.sum(full * gain.transpose(1, 0, 2)[:, None], axis=2).astype(bf16)
    half = jnp.einsum("yq,akq->yak", table, full.transpose(1, 0, 2), preferred_element_type=f32)
    half = half.astype(bf16).reshape(groups, rows_dev, own * cols)
    half = lax.all_to_all(half, "rows", split_axis=0, concat_axis=0, tiled=True)
    half = half.reshape(groups, rows_dev, own, cols).transpose(2, 1, 0, 3)
    half = half.reshape(own * rows_dev, width)
    phase = jnp.dot(half, table, preferred_element_type=f32)
    phase = phase.astype(bf16).reshape(own, rows_dev, width)
    phase = lax.all_gather(phase, "dist", axis=0, tiled=True)
    place = (angle_order[0][None, :] == jnp.arange(angles)[:, None]).astype(bf16)
    phase = jnp.einsum("wa,ayx->wyx", place, phase, preferred_element_type=f32)
    recon = jnp.einsum(
        "wyx,wxp->yp", phase.astype(bf16), weights, preferred_element_type=f32
    ).astype(bf16)
    parity = device % 2
    offset = parity * slab_rows[device - parity]
    count = slab_rows[device]
    pairs = [(source, source ^ 1) for source in range(groups)]
    partner = lax.ppermute(recon, "rows", pairs)
    lower = jnp.where(parity == 1, partner, recon)
    upper = jnp.where(parity == 1, recon, partner)
    paired = jnp.concatenate([lower, upper], axis=0)
    slot = jnp.arange(capacity, dtype=jnp.int32)[:, None]
    source = jnp.arange(capacity, dtype=jnp.int32)[None, :]
    select = ((source == offset + slot) & (slot < count)).astype(bf16)
    return jnp.dot(select, paired, preferred_element_type=f32).astype(bf16)


def position(inner):
    device = lax.axis_index("rows")
    return lax.axis_index("dist"), device // inner, device % inner


def row_kernel(inner, holo, there, table, after, *refs):
    outs, mine, loaded = refs[:-2], refs[-2], refs[-1]
    own = len(outs) // inner
    core, _, spot = position(inner)
    _, dist_dev, rows_dev, width = there.shape
    block = width // inner
    copy = pltpu.make_async_copy(holo.at[pl.ds(core * own, own)], mine, loaded)
    copy.start()
    for first, source in ((dist_dev, there.at[pl.ds(core * own, own)]), (0, mine)):
        if first == 0:
            copy.wait()
        rows = source[...].reshape(own * dist_dev * rows_dev, width)
        for rel in range(inner):
            part = table[:, pl.ds(pl.multiple_of((spot ^ rel) * block, block), block)]
            got = jnp.dot(rows, part, preferred_element_type=f32).astype(bf16)
            got = got.reshape(own, dist_dev, rows_dev, block)
            for chunk in range(own):
                outs[chunk * inner + rel][first : first + dist_dev] = got[chunk]


def whole_turns(scale, square):
    turns = scale * square * (0.5 / math.pi)
    return (turns - jnp.round(turns)) * (2.0 * math.pi)


def filter_kernel(inner, dist_dev, turns, out):
    dists, width, block = out.shape
    core, _, spot = position(inner)

    def square(first, length):
        index = lax.broadcasted_iota(jnp.int32, (1, length), 1) + first
        signed = jnp.where(index < width // 2, index, index - width).astype(f32)
        return signed * signed * (1.0 / (width * width))

    def phases(first, length):
        values = square(first, length)
        rows = []
        for d in range(dists):
            other = d // dist_dev
            scale = turns[(core ^ other) * dist_dev + d % dist_dev]
            rows.append(whole_turns(scale, values))
        return jnp.concatenate(rows, axis=0)

    along = phases(0, width)
    across = phases(spot * block, block)
    sin_b, cos_b = jnp.sin(across), jnp.cos(across)
    with_sin = 2.0 * (cos_b - absorb_ratio * sin_b)
    with_cos = 2.0 * (sin_b + absorb_ratio * cos_b)
    turned = jnp.concatenate([jnp.sin(along), jnp.cos(along)], axis=0).T
    step = 128
    for at in range(0, width, step):
        rows = turned[at : at + step]
        transfer = [
            rows[:, d : d + 1] * with_sin[d : d + 1, :]
            + rows[:, dists + d : dists + d + 1] * with_cos[d : d + 1, :]
            for d in range(dists)
        ]
        denom = transfer[0] * transfer[0]
        for value in transfer[1:]:
            denom = denom + value * value
        scale = 1.0 / (denom + regularizer)
        for d in range(dists):
            out[d, at : at + step, :] = (transfer[d] * scale).astype(bf16)


def column_kernel(inner, outer, table, gain, *refs):
    pieces = dict(zip(send_order, refs[:inner]))
    *outs, stack, total, spectrum = refs[inner:]
    _, plane, spot = position(inner)
    dists, rows_dev, block = pieces[0].shape
    depth = inner * rows_dev
    for rel in range(inner):
        start = pl.multiple_of((spot ^ rel) * rows_dev, rows_dev)
        for d in range(dists):
            stack[d, pl.ds(start, rows_dev), :] = pieces[rel][d]
    part = table[:, pl.ds(pl.multiple_of(plane * depth, depth), depth)]
    for d in range(dists):
        got = jnp.dot(part, stack[d], preferred_element_type=f32) * gain[d].astype(f32)
        if d == 0:
            total[...] = got
        else:
            total[...] += got
    spectrum[...] = total[...].astype(bf16)
    middle = (plane == 1) | (plane == 2)
    first = jnp.where(middle, 1, 3)
    for rel, out in zip((0, first, 4 - first, 2), outs):
        rows = pl.ds(pl.multiple_of((plane ^ rel) * depth, depth), depth)
        value = jnp.dot(table[rows, :], spectrum[...], preferred_element_type=f32)
        out[...] = value.astype(bf16)


def far_kernel(inner, *refs):
    ours, got, out = refs[-3:]
    _, plane, _ = position(inner)
    middle = (plane == 1) | (plane == 2)
    more = jnp.where(middle, got[...].astype(f32), 0.0)
    out[...] = (ours[...].astype(f32) + more).astype(bf16)


def half_kernel(inner, ours, far, near, next_near, across, other, mine, again):
    _, plane, spot = position(inner)
    middle = (plane == 1) | (plane == 2)
    capacity = mine.shape[0]
    for out, pair in ((mine, spot // 2), (other, 1 - spot // 2)):
        rows = pl.ds(pl.multiple_of(pair * capacity, capacity), capacity)
        inside = next_near[rows, :].astype(f32) + across[rows, :].astype(f32)
        more = jnp.where(middle, inside, near[rows, :].astype(f32))
        got = ours[rows, :].astype(f32) + far[rows, :].astype(f32) + more
        out[...] = got.astype(bf16)
    again[...] = other[...]


def phase_kernel(inner, table, *refs):
    pieces = dict(zip(tail_order, refs[:inner]))
    out, joined = refs[-2:]
    _, _, spot = position(inner)
    block = refs[0].shape[1]
    for rel in range(inner):
        columns = pl.ds(pl.multiple_of((spot ^ rel) * block, block), block)
        joined[:, columns] = pieces[rel][...]
    out[...] = jnp.dot(joined[...], table[...], preferred_element_type=f32).astype(bf16)


def recon_kernel(own, order, slabs, weights, *refs):
    phases = refs[: 2 * own - 2]
    out, chosen, select = refs[2 * own - 2 :]
    core = lax.axis_index("dist")
    device = lax.axis_index("rows")
    total = None
    for step, phase in enumerate(phases):
        here = weights[order[0, (core ^ (step % 2)) * own + step // 2]]
        got = jnp.dot(phase[...], here, preferred_element_type=f32)
        total = got if total is None else total + got
    out[...] = total
    for other in range(2):
        chosen[other] = weights[order[0, (core ^ other) * own + own - 1]]
    parity = device % 2
    offset = parity * slabs[device - parity]
    slot = lax.broadcasted_iota(jnp.int32, select.shape, 0)
    source = lax.broadcasted_iota(jnp.int32, select.shape, 1)
    picked = (source == slot + offset) & (slot < slabs[device])
    select[...] = jnp.where(picked, 1.0, 0.0).astype(bf16)


def recon_last_kernel(inner, table, weights, before, select, *refs):
    out, joined = refs[-2:]
    _, _, spot = position(inner)
    capacity, block = refs[0].shape
    for other in range(2):
        pieces = dict(zip(tail_order, refs[other * inner : (other + 1) * inner]))
        for rel in range(inner):
            columns = pl.ds(pl.multiple_of((spot ^ rel) * block, block), block)
            joined[other * capacity : (other + 1) * capacity, columns] = pieces[rel][...]
    phase = jnp.dot(joined[...], table[...], preferred_element_type=f32).astype(bf16)
    total = before[...]
    for other in range(2):
        ours = phase[other * capacity : (other + 1) * capacity]
        total = total + jnp.dot(ours, weights[other], preferred_element_type=f32)
    got = jnp.dot(select[...], total.astype(bf16), preferred_element_type=f32)
    out[...] = got.astype(bf16)


def vmem(count):
    return [pl.BlockSpec(memory_space=pltpu.VMEM)] * count


def from_hbm(value):
    return pltpu.with_memory_space_constraint(value, pltpu.HBM)


def in_hbm(count):
    return [pl.BlockSpec(memory_space=pltpu.HBM)] * count


def unread(count):
    return [pl.BlockSpec(memory_space=pl.ANY)] * count


def smem(count):
    return [pl.BlockSpec(memory_space=pltpu.SMEM)] * count


def plane_plan(inner, holograms, propagation, weights, angle_order, slab_rows):
    mbatch, angles, dist_dev, rows_dev, width = holograms.shape
    groups = lax.axis_size("rows")
    cores = lax.axis_size("dist")
    outer = groups // inner
    own = angles // cores
    block = width // inner
    depth = inner * rows_dev
    dists = cores * dist_dev
    pixels = weights.shape[2]
    capacity = 2 * rows_dev
    params = pltpu.CompilerParams(vmem_limit_bytes=16 * 2**20)
    one_out = pl.BlockSpec(memory_space=pltpu.VMEM)

    cheap = pl.CostEstimate(flops=1, bytes_accessed=1, transcendentals=0)

    def shaped(*shape):
        return jax.ShapeDtypeStruct(shape, bf16)

    table = jnp.asarray(hartley(width))

    def sent(value, target):
        pairs = []
        for c in range(cores):
            for r in range(groups):
                to_core, to_row = target(c, r)
                if to_row is not None:
                    pairs.append((c * groups + r, to_core * groups + to_row))
        return lax.ppermute(value, ("dist", "rows"), pairs)

    def to_other_core(c, r):
        return c ^ 1, r

    def to_spot(rel):
        return lambda c, r: (c, r ^ rel)

    def spread(pieces, order):
        return [sent(pieces[rel], to_spot(rel)) if rel else pieces[rel] for rel in order]

    def to_plane(rel):
        return lambda c, r: (c, (r // inner ^ rel) * inner + r % inner)

    def from_ends(c, r):
        z = r // inner
        return c, None if z in (1, 2) else (z ^ 1) * inner + r % inner

    def to_middle(c, r):
        z = r // inner
        return (c, (3 - z) * inner + r % inner) if z in (1, 2) else (c ^ 1, r)

    partner = sent(holograms[0], to_other_core)
    gain = pl.pallas_call(
        lambda *refs: filter_kernel(inner, dist_dev, *refs),
        out_shape=shaped(dists, width, block),
        in_specs=smem(1),
        out_specs=one_out,
        compiler_params=params,
        cost_estimate=cheap,
        name="filters",
    )(from_hbm(propagation))
    pieces = pl.pallas_call(
        lambda *refs: row_kernel(inner, *refs),
        out_shape=[shaped(dists, rows_dev, block)] * (own * inner),
        in_specs=in_hbm(1) + vmem(2) + unread(1),
        out_specs=vmem(own * inner),
        scratch_shapes=[
            pltpu.VMEM((own, dist_dev, rows_dev, width), bf16),
            pltpu.SemaphoreType.DMA,
        ],
        compiler_params=params,
        cost_estimate=cheap,
        name="row_spectra",
    )(from_hbm(holograms[0]), partner, table, gain)
    arrived = [
        spread(pieces[chunk * inner : (chunk + 1) * inner], send_order) for chunk in range(own)
    ]

    sums = []
    for chunk in range(own):
        blocks = pl.pallas_call(
            lambda *refs: column_kernel(inner, outer, *refs),
            out_shape=[shaped(depth, block)] * outer,
            in_specs=vmem(2 + inner),
            out_specs=vmem(outer),
            scratch_shapes=[
                pltpu.VMEM((dists, depth, block), bf16),
                pltpu.VMEM((width, block), f32),
                pltpu.VMEM((width, block), bf16),
            ],
            compiler_params=params,
            cost_estimate=cheap,
            name="columns",
        )(table, gain, *arrived[chunk])
        ours, first, second, third = blocks
        near = sent(first, to_plane(1))
        earlier = sums[-1][3:] if sums else []
        message = pl.pallas_call(
            lambda *refs: far_kernel(inner, *refs),
            out_shape=shaped(depth, block),
            in_specs=unread(len(earlier)) + vmem(2),
            out_specs=one_out,
            compiler_params=params,
            cost_estimate=cheap,
            name="far",
        )(*earlier, third, near)
        far = sent(message, to_plane(2))
        to_next = from_ends if sums else to_plane(1)
        sums.append([ours, far, near, sent(second, to_next), sent(second, to_middle)])

    phases = []
    for chunk in range(own):
        second, first, again = pl.pallas_call(
            lambda *refs: half_kernel(inner, *refs),
            out_shape=[shaped(capacity, block)] * 3,
            in_specs=vmem(5),
            out_specs=vmem(3),
            compiler_params=params,
            cost_estimate=cheap,
            name="half",
        )(*sums[chunk])
        pieces = spread([first, first, second, again], tail_order)
        if chunk == own - 1:
            break
        phase = pl.pallas_call(
            lambda *refs: phase_kernel(inner, *refs),
            out_shape=shaped(capacity, width),
            in_specs=vmem(1 + inner),
            out_specs=one_out,
            scratch_shapes=[pltpu.VMEM((capacity, width), bf16)],
            compiler_params=params,
            cost_estimate=cheap,
            name="phase",
        )(table, *pieces)
        phases += [phase, sent(phase, to_other_core)]

    total, chosen, select = pl.pallas_call(
        lambda *refs: recon_kernel(own, *refs),
        out_shape=[
            jax.ShapeDtypeStruct((capacity, pixels), f32),
            shaped(2, width, pixels),
            shaped(capacity, capacity),
        ],
        in_specs=smem(2) + vmem(1 + len(phases)),
        out_specs=vmem(3),
        compiler_params=params,
        cost_estimate=cheap,
        name="recon",
    )(angle_order, slab_rows, weights, *phases)
    there = [sent(piece, to_other_core) for piece in pieces]
    return pl.pallas_call(
        lambda *refs: recon_last_kernel(inner, *refs),
        out_shape=shaped(capacity, pixels),
        in_specs=vmem(4 + 2 * inner),
        out_specs=one_out,
        scratch_shapes=[pltpu.VMEM((2 * capacity, width), bf16)],
        compiler_params=params,
        cost_estimate=cheap,
        name="recon",
    )(table, chosen, total, select, *pieces, *there)


def on_device(holograms, propagation, weights, angle_order, slab_rows):
    mbatch, angles, dist_dev, rows_dev, width = holograms.shape
    groups = lax.axis_size("rows")
    inner = 2 ** (int(math.log2(groups)) // 2)
    block = width // inner
    fits = (
        inner * (groups // inner) == groups
        and rows_dev % 16 == 0
        and block % 128 == 0
        and inner * rows_dev % 128 == 0
        and inner == 4
        and groups == inner * inner
        and lax.axis_size("dist") == 2
        and angles == 2 * lax.axis_size("dist")
    )
    if fits:
        return plane_plan(inner, holograms, propagation, weights, angle_order, slab_rows)
    return flat_plan(holograms, propagation, weights, angle_order, slab_rows)


def solution(mesh):
    return jax.shard_map(
        on_device,
        mesh=mesh,
        in_specs=(P(None, None, "dist", "rows", None), P(), P(None, None, "dist"), P(), P()),
        out_specs=P("rows", "dist"),
        check_vma=False,
    )
```

```python
import math

import jax
import jax.numpy as jnp
import numpy as np
from jax import lax
from jax.experimental import pallas as pl
from jax.experimental.pallas import tpu as pltpu
from jax.sharding import PartitionSpec as P

absorb_ratio = 0.1
regularizer = 0.05
bf16 = jnp.bfloat16
f32 = jnp.float32
send_order = (0, 2, 1, 3)
tail_order = (0, 2, 3, 1)


def hartley(length):
    index = np.arange(length)
    turned = (index[:, None] * index[None, :] % length) * (2.0 * math.pi / length)
    table = (np.cos(turned) + np.sin(turned)) / math.sqrt(length)
    return table.astype(bf16)


def signed_square(index, length):
    signed = jnp.where(index < length // 2, index, index - length).astype(f32)
    return signed * signed / float(length * length)


def filters(propagation, rows_sq, cols_sq):
    first = propagation[:, None] * rows_sq[None]
    second = propagation[:, None] * cols_sq[None]
    sin_b, cos_b = jnp.sin(second), jnp.cos(second)
    with_sin = 2.0 * (cos_b - absorb_ratio * sin_b)
    with_cos = 2.0 * (sin_b + absorb_ratio * cos_b)
    transfer = (
        jnp.sin(first)[:, :, None] * with_sin[:, None, :]
        + jnp.cos(first)[:, :, None] * with_cos[:, None, :]
    )
    denom = jnp.sum(transfer * transfer, axis=0) + regularizer
    return transfer / denom


def flat_plan(holograms, propagation, weights, angle_order, slab_rows):
    mbatch, angles, dist_dev, rows_dev, width = holograms.shape
    groups = lax.axis_size("rows")
    cores = lax.axis_size("dist")
    capacity = 2 * rows_dev
    own = angles // cores
    cols = width // groups
    dists = dist_dev * cores
    device = lax.axis_index("rows")
    table = jnp.asarray(hartley(width))
    index = jnp.arange(width, dtype=jnp.int32)
    my_cols = device * cols + jnp.arange(cols, dtype=jnp.int32)
    gain = filters(propagation, signed_square(my_cols, width), signed_square(index, width))

    mine = lax.all_to_all(holograms[0], "dist", split_axis=0, concat_axis=1, tiled=True)
    flat = mine.reshape(own * dists * rows_dev, width)
    spec = jnp.einsum("kx,mx->km", table, flat, preferred_element_type=f32)
    spec = spec.astype(bf16).reshape(groups, cols, own * dists * rows_dev)
    spec = lax.all_to_all(spec, "rows", split_axis=0, concat_axis=0, tiled=True)
    spec = spec.reshape(groups, cols, own, dists, rows_dev).transpose(1, 2, 3, 0, 4)
    spec = spec.reshape(cols * own * dists, width)
    full = jnp.dot(spec, table, preferred_element_type=f32)
    full = full.reshape(cols, own, dists, width)
    full = jnp.sum(full * gain.transpose(1, 0, 2)[:, None], axis=2).astype(bf16)
    half = jnp.einsum("yq,akq->yak", table, full.transpose(1, 0, 2), preferred_element_type=f32)
    half = half.astype(bf16).reshape(groups, rows_dev, own * cols)
    half = lax.all_to_all(half, "rows", split_axis=0, concat_axis=0, tiled=True)
    half = half.reshape(groups, rows_dev, own, cols).transpose(2, 1, 0, 3)
    half = half.reshape(own * rows_dev, width)
    phase = jnp.dot(half, table, preferred_element_type=f32)
    phase = phase.astype(bf16).reshape(own, rows_dev, width)
    phase = lax.all_gather(phase, "dist", axis=0, tiled=True)
    place = (angle_order[0][None, :] == jnp.arange(angles)[:, None]).astype(bf16)
    phase = jnp.einsum("wa,ayx->wyx", place, phase, preferred_element_type=f32)
    recon = jnp.einsum(
        "wyx,wxp->yp", phase.astype(bf16), weights, preferred_element_type=f32
    ).astype(bf16)
    parity = device % 2
    offset = parity * slab_rows[device - parity]
    count = slab_rows[device]
    pairs = [(source, source ^ 1) for source in range(groups)]
    partner = lax.ppermute(recon, "rows", pairs)
    lower = jnp.where(parity == 1, partner, recon)
    upper = jnp.where(parity == 1, recon, partner)
    paired = jnp.concatenate([lower, upper], axis=0)
    slot = jnp.arange(capacity, dtype=jnp.int32)[:, None]
    source = jnp.arange(capacity, dtype=jnp.int32)[None, :]
    select = ((source == offset + slot) & (slot < count)).astype(bf16)
    return jnp.dot(select, paired, preferred_element_type=f32).astype(bf16)


def position(inner):
    device = lax.axis_index("rows")
    return lax.axis_index("dist"), device // inner, device % inner


def row_kernel(inner, holo, there, table, after, *refs):
    outs, mine, loaded = refs[:-2], refs[-2], refs[-1]
    own = len(outs) // inner
    core, _, spot = position(inner)
    _, dist_dev, rows_dev, width = there.shape
    block = width // inner
    copies = [
        pltpu.make_async_copy(
            holo.at[core * own + chunk, d], mine.at[chunk, d], loaded.at[chunk * dist_dev + d]
        )
        for chunk in range(own)
        for d in range(dist_dev)
    ]
    for copy in copies:
        copy.start()
    partner = there[pl.ds(core * own, own)].reshape(own * dist_dev * rows_dev, width)
    for copy in copies:
        copy.wait()
    ours = mine[...].reshape(own * dist_dev * rows_dev, width)
    rows = jnp.concatenate([ours, partner], axis=0)
    for rel in range(inner):
        part = table[:, pl.ds(pl.multiple_of((spot ^ rel) * block, block), block)]
        got = jnp.dot(rows, part, preferred_element_type=f32).astype(bf16)
        got = got.reshape(2, own, dist_dev, rows_dev, block)
        for chunk in range(own):
            out = outs[chunk * inner + rel]
            out[0:dist_dev] = got[0, chunk]
            out[dist_dev:] = got[1, chunk]


def whole_turns(scale, square):
    turns = scale * square * (0.5 / math.pi)
    return (turns - jnp.round(turns)) * (2.0 * math.pi)


def filter_kernel(inner, dist_dev, turns, out):
    dists, width, block = out.shape
    core, _, spot = position(inner)

    def square(first, length):
        index = lax.broadcasted_iota(jnp.int32, (1, length), 1) + first
        signed = jnp.where(index < width // 2, index, index - width).astype(f32)
        return signed * signed * (1.0 / (width * width))

    def phases(first, length):
        values = square(first, length)
        rows = []
        for d in range(dists):
            other = d // dist_dev
            scale = turns[(core ^ other) * dist_dev + d % dist_dev]
            rows.append(whole_turns(scale, values))
        return jnp.concatenate(rows, axis=0)

    along = phases(0, width)
    across = phases(spot * block, block)
    sin_b, cos_b = jnp.sin(across), jnp.cos(across)
    with_sin = 2.0 * (cos_b - absorb_ratio * sin_b)
    with_cos = 2.0 * (sin_b + absorb_ratio * cos_b)
    turned = jnp.concatenate([jnp.sin(along), jnp.cos(along)], axis=0).T
    step = 128
    for at in range(0, width, step):
        rows = turned[at : at + step]
        transfer = [
            rows[:, d : d + 1] * with_sin[d : d + 1, :]
            + rows[:, dists + d : dists + d + 1] * with_cos[d : d + 1, :]
            for d in range(dists)
        ]
        denom = transfer[0] * transfer[0]
        for value in transfer[1:]:
            denom = denom + value * value
        scale = 1.0 / (denom + regularizer)
        for d in range(dists):
            out[d, at : at + step, :] = (transfer[d] * scale).astype(bf16)


def column_kernel(inner, outer, table, gain, *refs):
    pieces = dict(zip(send_order, refs[:inner]))
    *outs, stack, total, spectrum = refs[inner:]
    _, plane, spot = position(inner)
    dists, rows_dev, block = pieces[0].shape
    depth = inner * rows_dev
    for rel in range(inner):
        start = pl.multiple_of((spot ^ rel) * rows_dev, rows_dev)
        for d in range(dists):
            stack[d, pl.ds(start, rows_dev), :] = pieces[rel][d]
    part = table[:, pl.ds(pl.multiple_of(plane * depth, depth), depth)]
    for d in range(dists):
        got = jnp.dot(part, stack[d], preferred_element_type=f32) * gain[d].astype(f32)
        if d == 0:
            total[...] = got
        else:
            total[...] += got
    spectrum[...] = total[...].astype(bf16)
    middle = (plane == 1) | (plane == 2)
    first = jnp.where(middle, 1, 3)
    for rel, out in zip((0, first, 4 - first, 2), outs):
        rows = pl.ds(pl.multiple_of((plane ^ rel) * depth, depth), depth)
        value = jnp.dot(table[rows, :], spectrum[...], preferred_element_type=f32)
        out[...] = value.astype(bf16)


def far_kernel(inner, *refs):
    ours, got, out = refs[-3:]
    _, plane, _ = position(inner)
    middle = (plane == 1) | (plane == 2)
    more = jnp.where(middle, got[...].astype(f32), 0.0)
    out[...] = (ours[...].astype(f32) + more).astype(bf16)


def half_kernel(inner, ours, far, near, next_near, across, other, mine, again):
    _, plane, spot = position(inner)
    middle = (plane == 1) | (plane == 2)
    capacity = mine.shape[0]
    for out, pair in ((mine, spot // 2), (other, 1 - spot // 2)):
        rows = pl.ds(pl.multiple_of(pair * capacity, capacity), capacity)
        inside = next_near[rows, :].astype(f32) + across[rows, :].astype(f32)
        more = jnp.where(middle, inside, near[rows, :].astype(f32))
        got = ours[rows, :].astype(f32) + far[rows, :].astype(f32) + more
        out[...] = got.astype(bf16)
    again[...] = other[...]


def phase_kernel(inner, table, *refs):
    pieces = dict(zip(tail_order, refs[:inner]))
    out, joined = refs[-2:]
    _, _, spot = position(inner)
    block = refs[0].shape[1]
    for rel in range(inner):
        columns = pl.ds(pl.multiple_of((spot ^ rel) * block, block), block)
        joined[:, columns] = pieces[rel][...]
    out[...] = jnp.dot(joined[...], table[...], preferred_element_type=f32).astype(bf16)


def recon_kernel(own, order, slabs, weights, *refs):
    phases = refs[: 2 * own - 1]
    out, chosen, select = refs[2 * own - 1 :]
    core = lax.axis_index("dist")
    device = lax.axis_index("rows")
    total = None
    for step, phase in enumerate(phases):
        here = weights[order[0, (core ^ (step % 2)) * own + step // 2]]
        got = jnp.dot(phase[...], here, preferred_element_type=f32)
        total = got if total is None else total + got
    out[...] = total
    chosen[...] = weights[order[0, (core ^ 1) * own + own - 1]]
    parity = device % 2
    offset = parity * slabs[device - parity]
    slot = lax.broadcasted_iota(jnp.int32, select.shape, 0)
    source = lax.broadcasted_iota(jnp.int32, select.shape, 1)
    picked = (source == slot + offset) & (slot < slabs[device])
    select[...] = jnp.where(picked, 1.0, 0.0).astype(bf16)


def recon_last_kernel(weights, phase, before, select, out):
    total = before[...] + jnp.dot(phase[...], weights[...], preferred_element_type=f32)
    got = jnp.dot(select[...], total.astype(bf16), preferred_element_type=f32)
    out[...] = got.astype(bf16)


def vmem(count):
    return [pl.BlockSpec(memory_space=pltpu.VMEM)] * count


def from_hbm(value):
    return pltpu.with_memory_space_constraint(value, pltpu.HBM)


def in_hbm(count):
    return [pl.BlockSpec(memory_space=pltpu.HBM)] * count


def unread(count):
    return [pl.BlockSpec(memory_space=pl.ANY)] * count


def smem(count):
    return [pl.BlockSpec(memory_space=pltpu.SMEM)] * count


def plane_plan(inner, holograms, propagation, weights, angle_order, slab_rows):
    mbatch, angles, dist_dev, rows_dev, width = holograms.shape
    groups = lax.axis_size("rows")
    cores = lax.axis_size("dist")
    outer = groups // inner
    own = angles // cores
    block = width // inner
    depth = inner * rows_dev
    dists = cores * dist_dev
    pixels = weights.shape[2]
    capacity = 2 * rows_dev
    params = pltpu.CompilerParams(vmem_limit_bytes=16 * 2**20)
    one_out = pl.BlockSpec(memory_space=pltpu.VMEM)

    cheap = pl.CostEstimate(flops=1, bytes_accessed=1, transcendentals=0)

    def shaped(*shape):
        return jax.ShapeDtypeStruct(shape, bf16)

    table = jnp.asarray(hartley(width))

    def sent(value, target):
        pairs = []
        for c in range(cores):
            for r in range(groups):
                to_core, to_row = target(c, r)
                if to_row is not None:
                    pairs.append((c * groups + r, to_core * groups + to_row))
        return lax.ppermute(value, ("dist", "rows"), pairs)

    def to_other_core(c, r):
        return c ^ 1, r

    def to_spot(rel):
        return lambda c, r: (c, r ^ rel)

    def spread(pieces, order):
        return [sent(pieces[rel], to_spot(rel)) if rel else pieces[rel] for rel in order]

    def to_plane(rel):
        return lambda c, r: (c, (r // inner ^ rel) * inner + r % inner)

    def from_ends(c, r):
        z = r // inner
        return c, None if z in (1, 2) else (z ^ 1) * inner + r % inner

    def to_middle(c, r):
        z = r // inner
        return (c, (3 - z) * inner + r % inner) if z in (1, 2) else (c ^ 1, r)

    partner = sent(holograms[0], to_other_core)
    gain = pl.pallas_call(
        lambda *refs: filter_kernel(inner, dist_dev, *refs),
        out_shape=shaped(dists, width, block),
        in_specs=smem(1),
        out_specs=one_out,
        compiler_params=params,
        cost_estimate=cheap,
        name="filters",
    )(from_hbm(propagation))
    pieces = pl.pallas_call(
        lambda *refs: row_kernel(inner, *refs),
        out_shape=[shaped(dists, rows_dev, block)] * (own * inner),
        in_specs=in_hbm(1) + vmem(2) + unread(1),
        out_specs=vmem(own * inner),
        scratch_shapes=[
            pltpu.VMEM((own, dist_dev, rows_dev, width), bf16),
            pltpu.SemaphoreType.DMA((own * dist_dev,)),
        ],
        compiler_params=params,
        cost_estimate=cheap,
        name="row_spectra",
    )(from_hbm(holograms[0]), partner, table, gain)
    arrived = [
        spread(pieces[chunk * inner : (chunk + 1) * inner], send_order) for chunk in range(own)
    ]

    sums = []
    for chunk in range(own):
        blocks = pl.pallas_call(
            lambda *refs: column_kernel(inner, outer, *refs),
            out_shape=[shaped(depth, block)] * outer,
            in_specs=vmem(2 + inner),
            out_specs=vmem(outer),
            scratch_shapes=[
                pltpu.VMEM((dists, depth, block), bf16),
                pltpu.VMEM((width, block), f32),
                pltpu.VMEM((width, block), bf16),
            ],
            compiler_params=params,
            cost_estimate=cheap,
            name="columns",
        )(table, gain, *arrived[chunk])
        ours, first, second, third = blocks
        near = sent(first, to_plane(1))
        earlier = sums[-1][3:] if sums else []
        message = pl.pallas_call(
            lambda *refs: far_kernel(inner, *refs),
            out_shape=shaped(depth, block),
            in_specs=unread(len(earlier)) + vmem(2),
            out_specs=one_out,
            compiler_params=params,
            cost_estimate=cheap,
            name="far",
        )(*earlier, third, near)
        far = sent(message, to_plane(2))
        to_next = from_ends if sums else to_plane(1)
        sums.append([ours, far, near, sent(second, to_next), sent(second, to_middle)])

    phases = []
    for chunk in range(own):
        second, first, again = pl.pallas_call(
            lambda *refs: half_kernel(inner, *refs),
            out_shape=[shaped(capacity, block)] * 3,
            in_specs=vmem(5),
            out_specs=vmem(3),
            compiler_params=params,
            cost_estimate=cheap,
            name="half",
        )(*sums[chunk])
        pieces = spread([first, first, second, again], tail_order)
        phase = pl.pallas_call(
            lambda *refs: phase_kernel(inner, *refs),
            out_shape=shaped(capacity, width),
            in_specs=vmem(1 + inner),
            out_specs=one_out,
            scratch_shapes=[pltpu.VMEM((capacity, width), bf16)],
            compiler_params=params,
            cost_estimate=cheap,
            name="phase",
        )(table, *pieces)
        phases += [phase, sent(phase, to_other_core)]

    total, chosen, select = pl.pallas_call(
        lambda *refs: recon_kernel(own, *refs),
        out_shape=[
            jax.ShapeDtypeStruct((capacity, pixels), f32),
            shaped(width, pixels),
            shaped(capacity, capacity),
        ],
        in_specs=smem(2) + vmem(2 * own),
        out_specs=vmem(3),
        compiler_params=params,
        cost_estimate=cheap,
        name="recon",
    )(angle_order, slab_rows, weights, *phases[:-1])
    return pl.pallas_call(
        recon_last_kernel,
        out_shape=shaped(capacity, pixels),
        in_specs=vmem(4),
        out_specs=one_out,
        compiler_params=params,
        cost_estimate=cheap,
        name="recon",
    )(chosen, phases[-1], total, select)


def on_device(holograms, propagation, weights, angle_order, slab_rows):
    mbatch, angles, dist_dev, rows_dev, width = holograms.shape
    groups = lax.axis_size("rows")
    inner = 2 ** (int(math.log2(groups)) // 2)
    block = width // inner
    fits = (
        inner * (groups // inner) == groups
        and rows_dev % 16 == 0
        and block % 128 == 0
        and inner * rows_dev % 128 == 0
        and inner == 4
        and groups == inner * inner
        and lax.axis_size("dist") == 2
        and angles == 2 * lax.axis_size("dist")
    )
    if fits:
        return plane_plan(inner, holograms, propagation, weights, angle_order, slab_rows)
    return flat_plan(holograms, propagation, weights, angle_order, slab_rows)


def solution(mesh):
    return jax.shard_map(
        on_device,
        mesh=mesh,
        in_specs=(P(None, None, "dist", "rows", None), P(), P(None, None, "dist"), P(), P()),
        out_specs=P("rows", "dist"),
        check_vma=False,
    )
```

```python
import math

import jax
import jax.numpy as jnp
import numpy as np
from jax import lax
from jax.experimental import pallas as pl
from jax.experimental.pallas import tpu as pltpu
from jax.sharding import PartitionSpec as P

absorb_ratio = 0.1
regularizer = 0.05
bf16 = jnp.bfloat16
f32 = jnp.float32
send_order = (0, 2, 1, 3)
tail_order = (0, 3, 2, 1)


def hartley(length):
    index = np.arange(length)
    turned = (index[:, None] * index[None, :] % length) * (2.0 * math.pi / length)
    table = (np.cos(turned) + np.sin(turned)) / math.sqrt(length)
    return table.astype(bf16)


def signed_square(index, length):
    signed = jnp.where(index < length // 2, index, index - length).astype(f32)
    return signed * signed / float(length * length)


def filters(propagation, rows_sq, cols_sq):
    first = propagation[:, None] * rows_sq[None]
    second = propagation[:, None] * cols_sq[None]
    sin_b, cos_b = jnp.sin(second), jnp.cos(second)
    with_sin = 2.0 * (cos_b - absorb_ratio * sin_b)
    with_cos = 2.0 * (sin_b + absorb_ratio * cos_b)
    transfer = (
        jnp.sin(first)[:, :, None] * with_sin[:, None, :]
        + jnp.cos(first)[:, :, None] * with_cos[:, None, :]
    )
    denom = jnp.sum(transfer * transfer, axis=0) + regularizer
    return transfer / denom


def flat_plan(holograms, propagation, weights, angle_order, slab_rows):
    mbatch, angles, dist_dev, rows_dev, width = holograms.shape
    groups = lax.axis_size("rows")
    cores = lax.axis_size("dist")
    capacity = 2 * rows_dev
    own = angles // cores
    cols = width // groups
    dists = dist_dev * cores
    device = lax.axis_index("rows")
    table = jnp.asarray(hartley(width))
    index = jnp.arange(width, dtype=jnp.int32)
    my_cols = device * cols + jnp.arange(cols, dtype=jnp.int32)
    gain = filters(propagation, signed_square(my_cols, width), signed_square(index, width))

    mine = lax.all_to_all(holograms[0], "dist", split_axis=0, concat_axis=1, tiled=True)
    flat = mine.reshape(own * dists * rows_dev, width)
    spec = jnp.einsum("kx,mx->km", table, flat, preferred_element_type=f32)
    spec = spec.astype(bf16).reshape(groups, cols, own * dists * rows_dev)
    spec = lax.all_to_all(spec, "rows", split_axis=0, concat_axis=0, tiled=True)
    spec = spec.reshape(groups, cols, own, dists, rows_dev).transpose(1, 2, 3, 0, 4)
    spec = spec.reshape(cols * own * dists, width)
    full = jnp.dot(spec, table, preferred_element_type=f32)
    full = full.reshape(cols, own, dists, width)
    full = jnp.sum(full * gain.transpose(1, 0, 2)[:, None], axis=2).astype(bf16)
    half = jnp.einsum("yq,akq->yak", table, full.transpose(1, 0, 2), preferred_element_type=f32)
    half = half.astype(bf16).reshape(groups, rows_dev, own * cols)
    half = lax.all_to_all(half, "rows", split_axis=0, concat_axis=0, tiled=True)
    half = half.reshape(groups, rows_dev, own, cols).transpose(2, 1, 0, 3)
    half = half.reshape(own * rows_dev, width)
    phase = jnp.dot(half, table, preferred_element_type=f32)
    phase = phase.astype(bf16).reshape(own, rows_dev, width)
    phase = lax.all_gather(phase, "dist", axis=0, tiled=True)
    place = (angle_order[0][None, :] == jnp.arange(angles)[:, None]).astype(bf16)
    phase = jnp.einsum("wa,ayx->wyx", place, phase, preferred_element_type=f32)
    recon = jnp.einsum(
        "wyx,wxp->yp", phase.astype(bf16), weights, preferred_element_type=f32
    ).astype(bf16)
    parity = device % 2
    offset = parity * slab_rows[device - parity]
    count = slab_rows[device]
    pairs = [(source, source ^ 1) for source in range(groups)]
    partner = lax.ppermute(recon, "rows", pairs)
    lower = jnp.where(parity == 1, partner, recon)
    upper = jnp.where(parity == 1, recon, partner)
    paired = jnp.concatenate([lower, upper], axis=0)
    slot = jnp.arange(capacity, dtype=jnp.int32)[:, None]
    source = jnp.arange(capacity, dtype=jnp.int32)[None, :]
    select = ((source == offset + slot) & (slot < count)).astype(bf16)
    return jnp.dot(select, paired, preferred_element_type=f32).astype(bf16)


def position(inner):
    device = lax.axis_index("rows")
    return lax.axis_index("dist"), device // inner, device % inner


def row_kernel(inner, holo, there, table, after, *refs):
    outs, mine, loaded = refs[:-2], refs[-2], refs[-1]
    own = len(outs) // inner
    core, _, spot = position(inner)
    _, dist_dev, rows_dev, width = there.shape
    block = width // inner
    copy = pltpu.make_async_copy(holo.at[pl.ds(core * own, own)], mine, loaded)
    copy.start()
    for first, source in ((dist_dev, there.at[pl.ds(core * own, own)]), (0, mine)):
        if first == 0:
            copy.wait()
        rows = source[...].reshape(own * dist_dev * rows_dev, width)
        for rel in range(inner):
            part = table[:, pl.ds(pl.multiple_of((spot ^ rel) * block, block), block)]
            got = jnp.dot(rows, part, preferred_element_type=f32).astype(bf16)
            got = got.reshape(own, dist_dev, rows_dev, block)
            for chunk in range(own):
                outs[chunk * inner + rel][first : first + dist_dev] = got[chunk]


def whole_turns(scale, square):
    turns = scale * square * (0.5 / math.pi)
    return (turns - jnp.round(turns)) * (2.0 * math.pi)


def filter_kernel(inner, dist_dev, turns, out):
    dists, width, block = out.shape
    core, _, spot = position(inner)

    def square(first, length):
        index = lax.broadcasted_iota(jnp.int32, (1, length), 1) + first
        signed = jnp.where(index < width // 2, index, index - width).astype(f32)
        return signed * signed * (1.0 / (width * width))

    def phases(first, length):
        values = square(first, length)
        rows = []
        for d in range(dists):
            other = d // dist_dev
            scale = turns[(core ^ other) * dist_dev + d % dist_dev]
            rows.append(whole_turns(scale, values))
        return jnp.concatenate(rows, axis=0)

    along = phases(0, width)
    across = phases(spot * block, block)
    sin_b, cos_b = jnp.sin(across), jnp.cos(across)
    with_sin = 2.0 * (cos_b - absorb_ratio * sin_b)
    with_cos = 2.0 * (sin_b + absorb_ratio * cos_b)
    turned = jnp.concatenate([jnp.sin(along), jnp.cos(along)], axis=0).T
    step = 128
    for at in range(0, width, step):
        rows = turned[at : at + step]
        transfer = [
            rows[:, d : d + 1] * with_sin[d : d + 1, :]
            + rows[:, dists + d : dists + d + 1] * with_cos[d : d + 1, :]
            for d in range(dists)
        ]
        denom = transfer[0] * transfer[0]
        for value in transfer[1:]:
            denom = denom + value * value
        scale = 1.0 / (denom + regularizer)
        for d in range(dists):
            out[d, at : at + step, :] = (transfer[d] * scale).astype(bf16)


def column_kernel(inner, outer, table, gain, *refs):
    pieces = dict(zip(send_order, refs[:inner]))
    *outs, stack, total, spectrum = refs[inner:]
    _, plane, spot = position(inner)
    dists, rows_dev, block = pieces[0].shape
    depth = inner * rows_dev
    for rel in range(inner):
        start = pl.multiple_of((spot ^ rel) * rows_dev, rows_dev)
        for d in range(dists):
            stack[d, pl.ds(start, rows_dev), :] = pieces[rel][d]
    part = table[:, pl.ds(pl.multiple_of(plane * depth, depth), depth)]
    for d in range(dists):
        got = jnp.dot(part, stack[d], preferred_element_type=f32) * gain[d].astype(f32)
        if d == 0:
            total[...] = got
        else:
            total[...] += got
    spectrum[...] = total[...].astype(bf16)
    middle = (plane == 1) | (plane == 2)
    first = jnp.where(middle, 1, 3)
    for rel, out in zip((0, first, 4 - first, 2), outs):
        rows = pl.ds(pl.multiple_of((plane ^ rel) * depth, depth), depth)
        value = jnp.dot(table[rows, :], spectrum[...], preferred_element_type=f32)
        out[...] = value.astype(bf16)


def far_kernel(inner, *refs):
    ours, got, out = refs[-3:]
    _, plane, _ = position(inner)
    middle = (plane == 1) | (plane == 2)
    more = jnp.where(middle, got[...].astype(f32), 0.0)
    out[...] = (ours[...].astype(f32) + more).astype(bf16)


def half_kernel(inner, ours, far, near, next_near, across, other, mine, again):
    _, plane, spot = position(inner)
    middle = (plane == 1) | (plane == 2)
    capacity = mine.shape[0]
    for out, pair in ((mine, spot // 2), (other, 1 - spot // 2)):
        rows = pl.ds(pl.multiple_of(pair * capacity, capacity), capacity)
        inside = next_near[rows, :].astype(f32) + across[rows, :].astype(f32)
        more = jnp.where(middle, inside, near[rows, :].astype(f32))
        got = ours[rows, :].astype(f32) + far[rows, :].astype(f32) + more
        out[...] = got.astype(bf16)
    again[...] = other[...]


def phase_kernel(inner, table, *refs):
    pieces = dict(zip(tail_order, refs[:inner]))
    out, joined = refs[-2:]
    _, _, spot = position(inner)
    block = refs[0].shape[1]
    for rel in range(inner):
        columns = pl.ds(pl.multiple_of((spot ^ rel) * block, block), block)
        joined[:, columns] = pieces[rel][...]
    out[...] = jnp.dot(joined[...], table[...], preferred_element_type=f32).astype(bf16)


def recon_kernel(own, order, slabs, weights, *refs):
    phases = refs[: 2 * own - 1]
    out, chosen, select = refs[2 * own - 1 :]
    core = lax.axis_index("dist")
    device = lax.axis_index("rows")
    total = None
    for step, phase in enumerate(phases):
        here = weights[order[0, (core ^ (step % 2)) * own + step // 2]]
        got = jnp.dot(phase[...], here, preferred_element_type=f32)
        total = got if total is None else total + got
    out[...] = total
    chosen[...] = weights[order[0, (core ^ 1) * own + own - 1]]
    parity = device % 2
    offset = parity * slabs[device - parity]
    slot = lax.broadcasted_iota(jnp.int32, select.shape, 0)
    source = lax.broadcasted_iota(jnp.int32, select.shape, 1)
    picked = (source == slot + offset) & (slot < slabs[device])
    select[...] = jnp.where(picked, 1.0, 0.0).astype(bf16)


def recon_last_kernel(weights, phase, before, select, out):
    total = before[...] + jnp.dot(phase[...], weights[...], preferred_element_type=f32)
    got = jnp.dot(select[...], total.astype(bf16), preferred_element_type=f32)
    out[...] = got.astype(bf16)


def vmem(count):
    return [pl.BlockSpec(memory_space=pltpu.VMEM)] * count


def from_hbm(value):
    return pltpu.with_memory_space_constraint(value, pltpu.HBM)


def in_hbm(count):
    return [pl.BlockSpec(memory_space=pltpu.HBM)] * count


def unread(count):
    return [pl.BlockSpec(memory_space=pl.ANY)] * count


def smem(count):
    return [pl.BlockSpec(memory_space=pltpu.SMEM)] * count


def plane_plan(inner, holograms, propagation, weights, angle_order, slab_rows):
    mbatch, angles, dist_dev, rows_dev, width = holograms.shape
    groups = lax.axis_size("rows")
    cores = lax.axis_size("dist")
    outer = groups // inner
    own = angles // cores
    block = width // inner
    depth = inner * rows_dev
    dists = cores * dist_dev
    pixels = weights.shape[2]
    capacity = 2 * rows_dev
    params = pltpu.CompilerParams(vmem_limit_bytes=16 * 2**20)
    one_out = pl.BlockSpec(memory_space=pltpu.VMEM)

    cheap = pl.CostEstimate(flops=1, bytes_accessed=1, transcendentals=0)

    def shaped(*shape):
        return jax.ShapeDtypeStruct(shape, bf16)

    table = jnp.asarray(hartley(width))

    def sent(value, target):
        pairs = []
        for c in range(cores):
            for r in range(groups):
                to_core, to_row = target(c, r)
                if to_row is not None:
                    pairs.append((c * groups + r, to_core * groups + to_row))
        return lax.ppermute(value, ("dist", "rows"), pairs)

    def to_other_core(c, r):
        return c ^ 1, r

    def to_spot(rel):
        return lambda c, r: (c, r ^ rel)

    def spread(pieces, order):
        return [sent(pieces[rel], to_spot(rel)) if rel else pieces[rel] for rel in order]

    def to_plane(rel):
        return lambda c, r: (c, (r // inner ^ rel) * inner + r % inner)

    def from_ends(c, r):
        z = r // inner
        return c, None if z in (1, 2) else (z ^ 1) * inner + r % inner

    def to_middle(c, r):
        z = r // inner
        return (c, (3 - z) * inner + r % inner) if z in (1, 2) else (c ^ 1, r)

    partner = sent(holograms[0], to_other_core)
    gain = pl.pallas_call(
        lambda *refs: filter_kernel(inner, dist_dev, *refs),
        out_shape=shaped(dists, width, block),
        in_specs=smem(1),
        out_specs=one_out,
        compiler_params=params,
        cost_estimate=cheap,
        name="filters",
    )(from_hbm(propagation))
    pieces = pl.pallas_call(
        lambda *refs: row_kernel(inner, *refs),
        out_shape=[shaped(dists, rows_dev, block)] * (own * inner),
        in_specs=in_hbm(1) + vmem(2) + unread(1),
        out_specs=vmem(own * inner),
        scratch_shapes=[
            pltpu.VMEM((own, dist_dev, rows_dev, width), bf16),
            pltpu.SemaphoreType.DMA,
        ],
        compiler_params=params,
        cost_estimate=cheap,
        name="row_spectra",
    )(from_hbm(holograms[0]), partner, table, gain)
    arrived = [
        spread(pieces[chunk * inner : (chunk + 1) * inner], send_order) for chunk in range(own)
    ]

    sums = []
    for chunk in range(own):
        blocks = pl.pallas_call(
            lambda *refs: column_kernel(inner, outer, *refs),
            out_shape=[shaped(depth, block)] * outer,
            in_specs=vmem(2 + inner),
            out_specs=vmem(outer),
            scratch_shapes=[
                pltpu.VMEM((dists, depth, block), bf16),
                pltpu.VMEM((width, block), f32),
                pltpu.VMEM((width, block), bf16),
            ],
            compiler_params=params,
            cost_estimate=cheap,
            name="columns",
        )(table, gain, *arrived[chunk])
        ours, first, second, third = blocks
        near = sent(first, to_plane(1))
        earlier = sums[-1][3:] if sums else []
        message = pl.pallas_call(
            lambda *refs: far_kernel(inner, *refs),
            out_shape=shaped(depth, block),
            in_specs=unread(len(earlier)) + vmem(2),
            out_specs=one_out,
            compiler_params=params,
            cost_estimate=cheap,
            name="far",
        )(*earlier, third, near)
        far = sent(message, to_plane(2))
        to_next = from_ends if sums else to_plane(1)
        sums.append([ours, far, near, sent(second, to_next), sent(second, to_middle)])

    phases = []
    for chunk in range(own):
        second, first, again = pl.pallas_call(
            lambda *refs: half_kernel(inner, *refs),
            out_shape=[shaped(capacity, block)] * 3,
            in_specs=vmem(5),
            out_specs=vmem(3),
            compiler_params=params,
            cost_estimate=cheap,
            name="half",
        )(*sums[chunk])
        pieces = spread([first, first, second, again], tail_order)
        phase = pl.pallas_call(
            lambda *refs: phase_kernel(inner, *refs),
            out_shape=shaped(capacity, width),
            in_specs=vmem(1 + inner),
            out_specs=one_out,
            scratch_shapes=[pltpu.VMEM((capacity, width), bf16)],
            compiler_params=params,
            cost_estimate=cheap,
            name="phase",
        )(table, *pieces)
        phases += [phase, sent(phase, to_other_core)]

    total, chosen, select = pl.pallas_call(
        lambda *refs: recon_kernel(own, *refs),
        out_shape=[
            jax.ShapeDtypeStruct((capacity, pixels), f32),
            shaped(width, pixels),
            shaped(capacity, capacity),
        ],
        in_specs=smem(2) + vmem(2 * own),
        out_specs=vmem(3),
        compiler_params=params,
        cost_estimate=cheap,
        name="recon",
    )(angle_order, slab_rows, weights, *phases[:-1])
    return pl.pallas_call(
        recon_last_kernel,
        out_shape=shaped(capacity, pixels),
        in_specs=vmem(4),
        out_specs=one_out,
        compiler_params=params,
        cost_estimate=cheap,
        name="recon",
    )(chosen, phases[-1], total, select)


def on_device(holograms, propagation, weights, angle_order, slab_rows):
    mbatch, angles, dist_dev, rows_dev, width = holograms.shape
    groups = lax.axis_size("rows")
    inner = 2 ** (int(math.log2(groups)) // 2)
    block = width // inner
    fits = (
        inner * (groups // inner) == groups
        and rows_dev % 16 == 0
        and block % 128 == 0
        and inner * rows_dev % 128 == 0
        and inner == 4
        and groups == inner * inner
        and lax.axis_size("dist") == 2
        and angles == 2 * lax.axis_size("dist")
    )
    if fits:
        return plane_plan(inner, holograms, propagation, weights, angle_order, slab_rows)
    return flat_plan(holograms, propagation, weights, angle_order, slab_rows)


def solution(mesh):
    return jax.shard_map(
        on_device,
        mesh=mesh,
        in_specs=(P(None, None, "dist", "rows", None), P(), P(None, None, "dist"), P(), P()),
        out_specs=P("rows", "dist"),
        check_vma=False,
    )
```
